32 devices in a mesh: dp: 8 (over z, x), fsdp: 4 (over y, core).
Axes of the slice: x: 2, y: 2, z: 4, core: 2. Of those that a mesh axis runs over, the one named last changes fastest.
Arguments:
- token_identifiers: int32 [2, 32, 1024], P(None, ('dp', 'fsdp')), may hold values from 0 to 50256
- lengths: int32 [2, 32], P(None, ('dp', 'fsdp')), may hold values from 64 to 1024, as said below
- loss_positions: int32 [2, 32, 32], P(None, ('dp', 'fsdp')), may hold values from 0 to 1022, as said below
- token_embedding_table: bfloat16 [50304, 1024], P(('dp', 'fsdp'))
- positions: bfloat16 [1024, 1024], P(('dp', 'fsdp')), may hold values from -0.59765625 to 0.59765625
- query_key_value_matrix: bfloat16 [1024, 3072], P(('dp', 'fsdp')), may hold values from -0.1875 to 0.1875
- output_weight: bfloat16 [1024, 1024], P(('dp', 'fsdp')), may hold values from -0.75 to 0.75
- up_weight: bfloat16 [1024, 4096], P(('dp', 'fsdp')), may hold values from -0.1875 to 0.1875
- down_weight: bfloat16 [4096, 1024], P(('dp', 'fsdp')), may hold values from -0.09375 to 0.09375
- vectors: bfloat16 [15360], P(('dp', 'fsdp'))
- adapter_down_weight: float32 [1024, 8], replicated, may hold values from -0.1875 to 0.1875
- adapter_up_weight: float32 [8, 1024], replicated, may hold values from -0.12 to 0.12
- left_statistics: float32 [16, 256, 256], P('fsdp')
- right_statistics: float32 [16, 4, 4], P('fsdp')
Outputs:
- loss: float32 [2], replicated
- adapter_gradient_norm: float32 [], replicated
- lora_a_grad: float32 [1024, 8], replicated
- lora_b_grad: float32 [8, 1024], replicated
- left_stats_new: float32 [16, 256, 256], P('fsdp')
- right_stats_new: float32 [16, 4, 4], P('fsdp')
- adapter_down_updated: float32 [1024, 8], replicated
- adapter_up_updated: float32 [8, 1024], replicated
The draws below stay inside these ranges and needn't reach their ends.
Inputs may be any that keep to these rules, and one draw needn't show every extreme that they name: `lengths`: in each micro-batch one sequence holds all 1024 slots and at most one holds 64. `loss_positions`: the slots of one sequence are distinct.
All inputs are finite; a program needn't handle non-finite values.
Results may differ from the reference program's by a relative error of at most 0.009.
Values may be sent and summed in bfloat16 or wider, within the bound.
A program may use at most 256 MiB of HBM per device.

```python
import math
import jax
import jax.numpy as jnp
import numpy as np
from jax import lax

MODEL_WIDTH = 1024
ATTENTION_HEADS = 16
FF = 4096
VOCAB = 50304
SLOT_LENGTH = 1024
ADAPTER_RANK = 4
MICRO = 2
LOSS = 32
STATS_BLOCK_ROWS = 256
NEWTON = 8
SEQS = 32
VEC = 15360
NB = 16


clip_level = 0.01


state_share = 0.0526


def draw_lengths(key, part):
    key = jax.random.fold_in(key, 11)
    key_jitter, key_long, key_short = jax.random.split(key, 3)
    sequence = jnp.arange(SEQS, dtype=jnp.int32)
    baseline = SLOT_LENGTH // 4 + SLOT_LENGTH * 9 // 16 * sequence // max(SEQS - 1, 1)
    jitter = jax.random.randint(key_jitter, (MICRO, SEQS), -(SLOT_LENGTH // 8), SLOT_LENGTH // 8 + 1)
    value_rows = jnp.clip(baseline[None, :] + jitter, SLOT_LENGTH // 8, SLOT_LENGTH)
    longest = jax.random.randint(key_long, (MICRO, 1), 0, SEQS)
    shortest = jax.random.randint(key_short, (MICRO, 1), 0, SEQS)
    value_rows = jnp.where(sequence[None, :] == shortest, SLOT_LENGTH // 16, value_rows)
    value_rows = jnp.where(sequence[None, :] == longest, SLOT_LENGTH, value_rows)
    return value_rows.astype(jnp.int32)


def draw_loss_positions(key, part):
    key = jax.random.fold_in(key, 12)
    streams = jax.random.split(key, MICRO * SEQS)
    picked = jax.vmap(lambda stream: jax.random.permutation(stream, SLOT_LENGTH - 1)[:LOSS])(streams)
    return picked.reshape(MICRO, SEQS, LOSS).astype(jnp.int32)


def draw_token_embedding_table(key, part):
    key = jax.random.fold_in(key, 13)
    place = jnp.arange(VOCAB, dtype=jnp.float32)[:, None] / (VOCAB - 1)
    noise = jax.random.normal(key, (VOCAB, MODEL_WIDTH), jnp.float32)
    rising = 1.0 + 2.0 * place
    return (noise * rising * MODEL_WIDTH ** (-0.5)).astype(jnp.bfloat16)


def draw_vectors(key, part):
    key = jax.random.fold_in(key, 14)
    index = jnp.arange(VEC, dtype=jnp.int32)
    noise = jax.random.normal(key, (VEC,), jnp.float32)
    is_gain = (index < 6 * MODEL_WIDTH) & (index // MODEL_WIDTH % 2 == 0)
    return jnp.where(is_gain, 1.0 + 0.1 * noise, 0.1 * noise).astype(jnp.bfloat16)


def stats_matrix(key, size, scale):
    key_diag, key_off = jax.random.split(key)
    identity = jnp.eye(size, dtype=jnp.float32)
    diagonal = jnp.exp(jax.random.uniform(key_diag, (NB, size), jnp.float32, 0.0, 1.3862944))
    spread = jax.random.uniform(key_off, (NB, size, size), jnp.float32, -1.0, 1.0)
    spread = 0.5 * (spread + jnp.swapaxes(spread, 1, 2)) * (0.3 * size ** (-0.5))
    return scale * (identity * diagonal[:, :, None] + (1.0 - identity) * spread)


def draw_left_statistics(key, part):
    key = jax.random.fold_in(key, 15)
    return stats_matrix(key, STATS_BLOCK_ROWS, state_share * clip_level ** 2 / (4.0 * MODEL_WIDTH))


def draw_right_statistics(key, part):
    key = jax.random.fold_in(key, 16)
    return stats_matrix(key, ADAPTER_RANK, state_share * STATS_BLOCK_ROWS * clip_level ** 2 / (4.0 * MODEL_WIDTH * ADAPTER_RANK))


def touch_ends(values, key, least, largest):
    longest = values.shape.index(max(values.shape))
    spots = []
    for shift in (0, 1):
        where = [jax.random.randint(jax.random.fold_in(key, axis), (), 0, length) for axis, length in enumerate(values.shape)]
        where[longest] = (where[longest] + shift) % values.shape[longest]
        spots.append(tuple(where))
    return values.at[spots[0]].set(least).at[spots[1]].set(largest)


def steps_of(key, extent, shards, least, top_value):
    loudness = 1.0
    for position, shards_of in shards:
        draws = jax.random.uniform(jax.random.fold_in(jax.random.fold_in(key, 6), position), (shards_of,), jnp.float32, least / len(shards), top_value / len(shards))
        loudness = loudness * jnp.repeat(jnp.exp(draws), extent[position] // shards_of).reshape((-1,) + (1,) * (len(extent) - 1 - position))
    return loudness


def rank_bounds(count, slope):
    portions = [(1 << 20) // math.isqrt(standing ** slope) + 1 for standing in range(1, count + 1)]
    scale = 1 + sum(portions) // (1 << 30)
    return np.cumsum(np.array([max(1, weight // scale) for weight in portions]))


def skewed_ids(own_key, extent, count, skew):
    listing = rank_bounds(count, skew)
    lot = jax.random.randint(jax.random.fold_in(own_key, 1), extent, 0, int(listing[count - 1]))
    grade = jnp.searchsorted(jnp.asarray(listing, jnp.int32), lot, side="right")
    return jax.random.permutation(jax.random.fold_in(own_key, 2), count)[grade].astype(jnp.int32)


def normal_values(own_key, dims, deviation, bound, cuts=(), kind=jnp.bfloat16):
    values = jax.random.normal(own_key, dims, jnp.float32) * deviation
    if len(cuts) > 0:
        values = steps_of(own_key, dims, cuts, -0.22, 0.18) * values
    return jnp.clip(values, min=-bound, max=bound).astype(kind)


def setup_inputs(seed: int = 0) -> dict:
    arg_keys = jax.random.split(jax.random.key(seed), 15)
    return {
        "token_identifiers": touch_ends(skewed_ids(arg_keys[0], (MICRO, SEQS, SLOT_LENGTH), min(VOCAB, 50257), 2), jax.random.fold_in(arg_keys[0], 3), 0, (min(VOCAB, 50257)) - 1).astype(jnp.int32),
        "lengths": draw_lengths(jax.random.fold_in(arg_keys[14], 71), 0),
        "loss_positions": draw_loss_positions(jax.random.fold_in(arg_keys[14], 71), 0),
        "token_embedding_table": draw_token_embedding_table(jax.random.fold_in(arg_keys[14], 71), 0),
        "positions": normal_values(arg_keys[4], (SLOT_LENGTH, MODEL_WIDTH), 0.1, 0.59765625, ((0, 32),)),
        "query_key_value_matrix": normal_values(arg_keys[5], (MODEL_WIDTH, 3 * MODEL_WIDTH), MODEL_WIDTH ** -0.5, 0.1875, ((0, 32),)),
        "output_weight": normal_values(arg_keys[6], (MODEL_WIDTH, MODEL_WIDTH), (MODEL_WIDTH // 16) ** -0.5, 0.75, ((0, 32),)),
        "up_weight": normal_values(arg_keys[7], (MODEL_WIDTH, FF), MODEL_WIDTH ** -0.5, 0.1875, ((0, 32),)),
        "down_weight": normal_values(arg_keys[8], (FF, MODEL_WIDTH), FF ** -0.5, 0.09375, ((0, 32),)),
        "vectors": draw_vectors(jax.random.fold_in(arg_keys[14], 71), 0),
        "adapter_down_weight": normal_values(arg_keys[10], (MODEL_WIDTH, 2 * ADAPTER_RANK), MODEL_WIDTH ** -0.5, 0.1875, (), jnp.float32),
        "adapter_up_weight": normal_values(arg_keys[11], (2 * ADAPTER_RANK, MODEL_WIDTH), 0.02, 0.12, (), jnp.float32),
        "left_statistics": draw_left_statistics(jax.random.fold_in(arg_keys[14], 71), 0),
        "right_statistics": draw_right_statistics(jax.random.fold_in(arg_keys[14], 71), 0),
    }


ln_eps = 1e-05
adapter_alpha = 32.0
beta_stats = 0.95
root_eps = 1e-12
clip_level = 0.01
learn_rate = 0.05
masked_score = -1e+30

@jax.custom_vjp
def lowrank_output(v):
    return lax.optimization_barrier(v.astype(jnp.bfloat16)).astype(jnp.float32)

@jax.custom_vjp
def lowrank_backward(v):
    return v

def low_keep(v):
    return (lowrank_output(v), None)

def low_pass(kept, grad):
    return (grad,)

def back_keep(v):
    return (v, None)

def back_low(kept, grad):
    return (lowrank_output(grad),)
lowrank_output.defvjp(low_keep, low_pass)
lowrank_backward.defvjp(back_keep, back_low)

def layer_norm(value_rows, norm_gain, norm_shift):
    centred = value_rows - lax.optimization_barrier(jnp.mean(value_rows, axis=-1, keepdims=True))
    inverse = lax.rsqrt(lax.optimization_barrier(jnp.mean(centred * centred, axis=-1, keepdims=True)) + ln_eps)
    return centred * inverse * norm_gain + norm_shift

def split_vectors(vectors, model_width_size, hidden_width):
    piece_sizes = [model_width_size] * 6 + [3 * model_width_size, model_width_size, hidden_width, model_width_size]
    pieces = []
    offset = 0
    for amount in piece_sizes:
        pieces.append(vectors[offset:offset + amount].astype(jnp.float32))
        offset = offset + amount
    return pieces

def dense_matrix(left_side, right_side):
    return jnp.dot(left_side, right_side, precision=lax.Precision.HIGHEST)

def batched(left_side, right_side):
    return jnp.einsum('bij,bjk->bik', left_side, right_side, precision=lax.Precision.HIGHEST)

def inverse_root(matrix):
    identity = jnp.eye(matrix.shape[-1], dtype=jnp.float32)
    trace_sum = lax.optimization_barrier(jnp.sum(matrix * identity, axis=(1, 2), keepdims=True))
    current = matrix / trace_sum
    root_now = identity * lax.rsqrt(jnp.sqrt(trace_sum))
    for iteration in range(NEWTON):
        factor = (5.0 * identity - current) * 0.25
        root_now = batched(root_now, factor)
        square = batched(factor, factor)
        current = batched(batched(square, square), current)
    return root_now

def shampoo_update(gradient, weights, left_statistics, right_statistics):
    left_renewed = beta_stats * left_statistics + (1.0 - beta_stats) * jnp.einsum('bir,bjr->bij', gradient, gradient, precision=lax.Precision.HIGHEST)
    right_renewed = beta_stats * right_statistics + (1.0 - beta_stats) * jnp.einsum('bir,bis->brs', gradient, gradient, precision=lax.Precision.HIGHEST)
    left_root = inverse_root(left_renewed + root_eps * jnp.eye(left_renewed.shape[-1], dtype=jnp.float32))
    right_root = inverse_root(right_renewed + root_eps * jnp.eye(right_renewed.shape[-1], dtype=jnp.float32))
    update = batched(batched(left_root, gradient), right_root)
    return (weights - learn_rate * update, left_renewed, right_renewed)

def split_into_blocks(down_portion, up_portion, statistics_block_rows):
    adapter_rank_size = up_portion.shape[0] // 2
    stacked_rows = jnp.stack([down_portion[:, :adapter_rank_size], down_portion[:, adapter_rank_size:], up_portion[:adapter_rank_size].T, up_portion[adapter_rank_size:].T])
    return stacked_rows.reshape(-1, statistics_block_rows, adapter_rank_size)

def merge_from_blocks(blocks, model_width_size):
    stacked_rows = blocks.reshape(4, model_width_size, blocks.shape[-1])
    return (jnp.concatenate([stacked_rows[0], stacked_rows[1]], axis=1), jnp.concatenate([stacked_rows[2].T, stacked_rows[3].T], axis=0))

def reference(token_identifiers, lengths, loss_positions, token_embedding_table, positions, query_key_value_matrix, output_weight, up_weight, down_weight, vectors, adapter_down_weight, adapter_up_weight, left_statistics, right_statistics):
    embed_table = token_embedding_table.astype(jnp.float32)
    pos_table = positions.astype(jnp.float32)
    query_key_value_weight = query_key_value_matrix.astype(jnp.float32)
    out_w = output_weight.astype(jnp.float32)
    up_w = up_weight.astype(jnp.float32)
    down_w = down_weight.astype(jnp.float32)
    norm_values = split_vectors(vectors, MODEL_WIDTH, FF)
    head_width = MODEL_WIDTH // ATTENTION_HEADS
    inv_scale = head_width ** (-0.5)
    adapter_scale = adapter_alpha / ADAPTER_RANK
    seq_ids = token_identifiers.reshape(-1, SLOT_LENGTH)
    seq_len = lengths.reshape(-1)
    seq_pos = loss_positions.reshape(-1, LOSS)

    def sequence(down_portion, up_portion, seq_data):
        ids_row, seq_length, picked_rows = seq_data
        start_x = embed_table[ids_row] + pos_table
        norm_one = lowrank_output(layer_norm(start_x, norm_values[0], norm_values[1]))
        lowrank_projection = lowrank_backward(lowrank_output(dense_matrix(norm_one, lowrank_output(down_portion))))
        up_lowrank = lowrank_output(up_portion)
        key_value_pair = dense_matrix(norm_one, query_key_value_weight[:, MODEL_WIDTH:]) + norm_values[6][MODEL_WIDTH:]
        keys = lowrank_output(key_value_pair[:, :MODEL_WIDTH]).reshape(SLOT_LENGTH, ATTENTION_HEADS, head_width)
        value_rows = lowrank_backward(lowrank_output(key_value_pair[:, MODEL_WIDTH:] + adapter_scale * dense_matrix(lowrank_projection[:, ADAPTER_RANK:], up_lowrank[ADAPTER_RANK:]))).reshape(SLOT_LENGTH, ATTENTION_HEADS, head_width)
        selected_norm = norm_one[picked_rows]
        selected_lowrank = lowrank_projection[picked_rows]
        query_rows = dense_matrix(selected_norm, query_key_value_weight[:, :MODEL_WIDTH]) + norm_values[6][:MODEL_WIDTH] + adapter_scale * dense_matrix(selected_lowrank[:, :ADAPTER_RANK], up_lowrank[:ADAPTER_RANK])
        query_rows = lowrank_backward(lowrank_output(query_rows)).reshape(LOSS, ATTENTION_HEADS, head_width)
        raw = lowrank_backward(jnp.einsum('qhd,khd->hqk', query_rows, keys, precision=lax.Precision.HIGHEST) * inv_scale)
        key_index = jnp.arange(SLOT_LENGTH, dtype=jnp.int32)
        allowed = (key_index[None, :] <= picked_rows[:, None]) & (key_index[None, :] < seq_length)
        probs = lowrank_output(jax.nn.softmax(jnp.where(allowed[None], raw, masked_score), axis=2))
        attended = jnp.einsum('hqk,khd->qhd', probs, value_rows, precision=lax.Precision.HIGHEST).reshape(LOSS, MODEL_WIDTH)
        attended = lowrank_backward(lowrank_output(attended))
        middle = start_x[picked_rows] + lowrank_backward(dense_matrix(attended, out_w) + norm_values[7])
        norm_two = lowrank_output(layer_norm(middle, norm_values[2], norm_values[3]))
        before = lowrank_backward(dense_matrix(norm_two, up_w) + norm_values[8])
        activated = lowrank_output(jax.nn.gelu(before, approximate=True))
        final_x = middle + lowrank_backward(dense_matrix(activated, down_w) + norm_values[9])
        final_n = lowrank_output(layer_norm(final_x, norm_values[4], norm_values[5]))
        logits = lowrank_backward(jnp.dot(final_n, embed_table.T, precision=lax.Precision.HIGHEST))
        targets = ids_row[picked_rows + 1]
        valid = (picked_rows + 1 < seq_length).astype(jnp.float32)
        chosen = jnp.take_along_axis(logits, targets[:, None], axis=1)[:, 0]
        return jnp.sum(valid * (jax.nn.logsumexp(logits, axis=1) - chosen))

    def total_amount(down_portion, up_portion):

        def advance(running, seq_data):
            return (running + jax.checkpoint(sequence)(down_portion, up_portion, seq_data), None)
        result, unused = lax.scan(advance, jnp.zeros((), jnp.float32), (seq_ids, seq_len, seq_pos))
        return result
    loss_running_sum, backward_function = jax.vjp(total_amount, adapter_down_weight, adapter_up_weight)
    down_gradient, up_gradient = backward_function(jnp.ones((), jnp.float32))
    loss_token_count = jnp.sum((seq_pos + 1 < seq_len[:, None]).astype(jnp.float32))
    adapter_gradient_norm = jnp.sqrt(jnp.sum(down_gradient * down_gradient) + jnp.sum(up_gradient * up_gradient))
    factor = clip_level / jnp.maximum(adapter_gradient_norm, clip_level)
    down_gradient = down_gradient * factor
    up_gradient = up_gradient * factor
    updated_blocks, left_renewed, right_renewed = shampoo_update(split_into_blocks(down_gradient, up_gradient, STATS_BLOCK_ROWS), split_into_blocks(adapter_down_weight, adapter_up_weight, STATS_BLOCK_ROWS), left_statistics, right_statistics)
    adapter_down_updated, adapter_up_updated = merge_from_blocks(updated_blocks, MODEL_WIDTH)
    return (jnp.stack([loss_running_sum, loss_token_count]), adapter_gradient_norm, down_gradient, up_gradient, left_renewed, right_renewed, adapter_down_updated, adapter_up_updated)
```

```python
import functools
import jax
import jax.numpy as jnp
from jax import lax
from jax.experimental import pallas as pl
from jax.experimental.pallas import tpu as pltpu
from jax.sharding import PartitionSpec as P

ATTENTION_HEADS = 16
STATS_BLOCK_ROWS = 256
NEWTON = 8
CAPACITY = 80

ln_eps = 1e-05
adapter_alpha = 32.0
beta_stats = 0.95
root_eps = 1e-12
clip_level = 0.01
learn_rate = 0.05
masked_score = -1e30

BOTH = ("dp", "fsdp")
MESH = pl.DeviceIdType.MESH
VMEM = pl.BlockSpec(memory_space=pltpu.VMEM)
ANY = pl.BlockSpec(memory_space=pl.ANY)
f32 = jnp.float32
bf16 = jnp.bfloat16


def place():
    d, f = lax.axis_index("dp"), lax.axis_index("fsdp")
    return d // 2, lax.rem(d, 2), f // 2, lax.rem(f, 2)


def target(z, x, y, c):
    return (z * 2 + x, y * 2 + c)


def nth(i):
    return (i // 4, lax.rem(i, 4))


def greet_all(count):
    me = lax.axis_index("dp") * 4 + lax.axis_index("fsdp")
    sem = pltpu.get_barrier_semaphore()
    for i in range(1, count):
        pl.semaphore_signal(
            sem, inc=1, device_id=nth(lax.rem(me + i, count)), device_id_type=MESH
        )
    pl.semaphore_wait(sem, count - 1)
    return me


def remote(src, dst, send, recv, device):
    return pltpu.make_async_remote_copy(
        src_ref=src, dst_ref=dst, send_sem=send, recv_sem=recv, device_id=device, device_id_type=MESH
    )


def params(collective=None, vmem=60):
    if collective is None:
        return pltpu.CompilerParams(vmem_limit_bytes=vmem * 2**20)
    return pltpu.CompilerParams(
        vmem_limit_bytes=vmem * 2**20, collective_id=collective, has_side_effects=True
    )


def spread_kernel(count, a_ref, b_ref, a_out, b_out, send, recv):
    me = greet_all(count)
    copies = []
    for i in range(1, count):
        to = nth(lax.rem(me + i, count))
        for k, (src, dst) in enumerate(((a_ref, a_out), (b_ref, b_out))):
            copy = remote(src, dst.at[me], send.at[k, i], recv.at[k, i], to)
            copy.start()
            copies.append(copy)
    a_out[me] = a_ref[...]
    b_out[me] = b_ref[...]
    for copy in copies:
        copy.wait()


def spread(a, b, count, collective):
    return pl.pallas_call(
        functools.partial(spread_kernel, count),
        out_shape=[
            jax.ShapeDtypeStruct((count,) + a.shape, a.dtype),
            jax.ShapeDtypeStruct((count,) + b.shape, b.dtype),
        ],
        in_specs=[VMEM] * 2,
        out_specs=[VMEM] * 2,
        scratch_shapes=[pltpu.SemaphoreType.DMA((2, count))] * 2,
        compiler_params=params(collective),
        name="spread",
    )(a, b)


def iota(shape, dim):
    return lax.broadcasted_iota(jnp.int32, shape, dim)


def marks(condition):
    return jnp.where(condition, 1.0, 0.0).astype(bf16)


def dot(a, b, ca, cb):
    return lax.dot_general(a, b, (((ca,), (cb,)), ((), ())), preferred_element_type=f32)


def ranks(high, low, rows):
    width = low.shape[1]
    count = dot(marks(iota((rows, width), 0) == high), marks(iota((128, width), 0) == low), 1, 1)
    present = marks(count > 0.5)
    through = dot(present, marks(iota((128, 128), 0) <= iota((128, 128), 1)), 1, 0)
    return through - present.astype(f32), through[:, 127:128], present.astype(f32)


def select_kernel(capacity, ids_ref, table_ref, round_ref, rows_ref, most_ref, marks_ref):
    units, width = ids_ref.shape[0], ids_ref.shape[2]
    local_rows = table_ref.shape[0]
    grid_rows = -(-local_rows // 128)
    pad_rows = -(-grid_rows // 16) * 16
    me = lax.axis_index("dp") * lax.axis_size("fsdp") + lax.axis_index("fsdp")
    begin = (round_ref[0] * capacity).astype(f32)
    most = jnp.zeros((1, 1), f32)
    for unit in range(units):
        local = ids_ref[unit] - me * local_rows
        inside = (local >= 0) & (local < local_rows)
        high = jnp.where(inside, local >> 7, -1)
        low = jnp.where(inside, local & 127, -1)
        before, row_total, present = ranks(high, low, pad_rows)
        earlier = marks(iota((pad_rows, pad_rows), 1) < iota((pad_rows, pad_rows), 0))
        offset = dot(earlier, jnp.broadcast_to(row_total, (pad_rows, 128)).astype(bf16), 1, 0)
        rank = jnp.where(present > 0.5, before + offset - begin, -1.0)
        most = jnp.maximum(most, jnp.sum(row_total, axis=0, keepdims=True))
        for row in range(grid_rows):
            columns = min(128, local_rows - row * 128)
            hit = iota((capacity, 128), 0).astype(f32) == rank[row : row + 1, :]
            marks_ref[unit * capacity : (unit + 1) * capacity, row * 128 : row * 128 + columns] = (
                marks(hit)[:, :columns]
            )
    most_ref[...] = jnp.broadcast_to(most, most_ref.shape)
    for unit in range(units):
        rows_ref[unit] = dot(
            marks_ref[unit * capacity : (unit + 1) * capacity, :], table_ref[...], 1, 0
        ).astype(bf16)


def select(unit_ids, table, which_round, capacity):
    units = unit_ids.shape[0]
    return pl.pallas_call(
        functools.partial(select_kernel, capacity),
        out_shape=[
            jax.ShapeDtypeStruct((units, capacity, table.shape[1]), bf16),
            jax.ShapeDtypeStruct((8, 128), f32),
        ],
        in_specs=[VMEM, VMEM, pl.BlockSpec(memory_space=pltpu.SMEM)],
        out_specs=[VMEM] * 2,
        scratch_shapes=[pltpu.VMEM((units * capacity, table.shape[0]), bf16)],
        compiler_params=params(),
        name="select",
    )(unit_ids, table, which_round)


def slots_kernel(capacity, owners, local_rows, ids_ref, round_ref, slot_ref):
    ids = ids_ref[...]
    grid_rows = -(-local_rows // 128)
    pad_rows = -(-owners * grid_rows // 16) * 16
    begin = (round_ref[0] * capacity).astype(f32)
    owner = jnp.floor((ids.astype(f32) + 0.5) * (1.0 / local_rows)).astype(jnp.int32)
    local = ids - owner * local_rows
    high = jnp.where(ids >= 0, owner * grid_rows + (local >> 7), -1)
    low = jnp.where(ids >= 0, local & 127, -1)
    before, row_total, present = ranks(high, low, pad_rows)
    group = lambda dim: jnp.floor(
        (iota((pad_rows, pad_rows), dim).astype(f32) + 0.5) * (1.0 / grid_rows)
    )
    earlier = (iota((pad_rows, pad_rows), 1) < iota((pad_rows, pad_rows), 0)) & (
        group(0) == group(1)
    )
    offset = dot(
        marks(earlier), jnp.broadcast_to(row_total, (pad_rows, 128)).astype(bf16), 1, 0
    )
    rank = before + offset - begin
    rank = jnp.where((present > 0.5) & (rank >= 0.0) & (rank < capacity), rank, -1.0)
    width = ids.shape[1]
    of_low = dot(rank.astype(bf16), marks(iota((pad_rows, width), 0) == high), 0, 0)
    own_rank = jnp.sum(jnp.where(iota((128, width), 0) == low, of_low, 0.0), axis=0, keepdims=True)
    slot = owner * capacity + own_rank.astype(jnp.int32)
    slot_ref[...] = jnp.where((ids >= 0) & (own_rank >= 0.0), slot, -1)


def slots(ids, which_round, capacity, owners, local_rows):
    return pl.pallas_call(
        functools.partial(slots_kernel, capacity, owners, local_rows),
        out_shape=jax.ShapeDtypeStruct(ids.shape, jnp.int32),
        in_specs=[VMEM, pl.BlockSpec(memory_space=pltpu.SMEM)],
        out_specs=VMEM,
        compiler_params=params(),
        name="slots",
    )(ids, which_round)


def send_rows(rows_ref, most_ref, rows_out, most_out, sems, own_sems, start_only=None):
    z, x, y, c = place()
    chip = (z * 2 + x) * 2 + y
    copies = []
    for i in range(1, 16):
        to = lax.rem(chip + i, 16)
        device = target(to // 4, lax.rem(to // 2, 2), lax.rem(to, 2), c)
        for k, (src, dst) in enumerate(
            ((rows_ref.at[to], rows_out.at[chip, c]), (most_ref, most_out.at[chip, c]))
        ):
            copies.append(remote(src, dst, sems.at[0, k, i], sems.at[1, k, i], device))
    return copies


def exchange_kernel(weights, rows_ref, most_ref, *refs):
    w_in, refs = refs[:weights], refs[weights:]
    rows_out, most_out = refs[:2]
    w_out, refs = refs[2 : 2 + weights], refs[2 + weights :]
    sems, mate_sems, own_sems, chain_sems, plane_sems, core_sems = refs
    greet_all(32)
    z, x, y, c = place()
    chip = (z * 2 + x) * 2 + y
    mate = target(z, x, y, 1 - c)

    def chain(a, zz, way):
        src = w_out[a].at[zz, x, y, c]
        k = (way + 1) // 2
        return remote(
            src, src, chain_sems.at[0, a, k, zz], chain_sems.at[1, a, k, zz], target(z + way, x, y, c)
        )

    def halves(a):
        rows = w_out[a].shape[4]
        return pl.ds(0, rows // 2), pl.ds(rows // 2, rows // 2)

    def plane(a, zz, step):
        upper, lower = halves(a)
        over_x, over_y = target(z, 1 - x, y, c), target(z, x, 1 - y, c)
        full = w_out[a]
        if step == 1:
            pairs = (
                (full.at[zz, x, y, c, upper], over_x),
                (full.at[zz, x, y, c, lower], over_y),
            )
        else:
            pairs = (
                (full.at[zz, :, y, c, upper], over_y),
                (full.at[zz, x, :, c, lower], over_x),
            )
        return [
            remote(
                ref, ref, plane_sems.at[0, a, zz, step - 1, k], plane_sems.at[1, a, zz, step - 1, k], to
            )
            for k, (ref, to) in enumerate(pairs)
        ]

    def landed(a, zz, step):
        upper, lower = halves(a)
        full = w_out[a]
        over_x, over_y = target(z, 1 - x, y, c), target(z, x, 1 - y, c)
        if step == 1:
            pairs = (
                (full.at[zz, 1 - x, y, c, upper], over_x),
                (full.at[zz, x, 1 - y, c, lower], over_y),
            )
        else:
            pairs = (
                (full.at[zz, :, 1 - y, c, upper], over_y),
                (full.at[zz, 1 - x, :, c, lower], over_x),
            )
        return [
            remote(
                ref, ref, plane_sems.at[0, a, zz, step - 1, k], plane_sems.at[1, a, zz, step - 1, k], to
            )
            for k, (ref, to) in enumerate(pairs)
        ]

    def to_mate(a, zz):
        ref = w_out[a].at[zz, :, :, c]
        return remote(ref, ref, core_sems.at[0, a, zz], core_sems.at[1, a, zz], mate)

    def from_mate(a, zz):
        ref = w_out[a].at[zz, :, :, 1 - c]
        return remote(ref, ref, core_sems.at[0, a, zz], core_sems.at[1, a, zz], mate)

    def chain_in(a, zz, way):
        ref = w_out[a].at[zz, x, y, c]
        k = (way + 1) // 2
        return remote(
            ref, ref, chain_sems.at[0, a, k, zz], chain_sems.at[1, a, k, zz], target(z - way, x, y, c)
        )

    arrays = range(weights)
    own = [
        pltpu.make_async_copy(w_in[a], w_out[a].at[z, x, y, c], own_sems.at[a]) for a in arrays
    ]
    for copy in own:
        copy.start()
    row_copies = send_rows(rows_ref, most_ref, rows_out, most_out, sems, own_sems)
    for copy in row_copies:
        copy.start()
    own_rows = [
        pltpu.make_async_copy(rows_ref.at[chip], rows_out.at[chip, c], own_sems.at[weights]),
        pltpu.make_async_copy(most_ref, most_out.at[chip, c], own_sems.at[weights + 1]),
    ]
    for copy in own_rows:
        copy.start()
    for copy in own:
        copy.wait()

    def for_each_arrival(step, act):
        for way in (1, -1):
            zz = z - way * (step + 1)

            @pl.when((zz >= 0) & (zz < 4))
            def _(zz=zz, way=way):
                act(zz, way)

    def may_go(way):
        return (z + way >= 0) & (z + way < 4)

    for way in (1, -1):

        @pl.when(may_go(way))
        def _(way=way):
            for a in arrays:
                chain(a, z, way).start()

    for a in arrays:
        for copy in plane(a, z, 1):
            copy.start()

    def second(zz):
        for a in arrays:
            for copy in landed(a, zz, 1):
                copy.wait_recv()
            for copy in plane(a, zz, 2):
                copy.start()

    def third(zz):
        for a in arrays:
            for copy in landed(a, zz, 2):
                copy.wait_recv()
            to_mate(a, zz).start()

    def arrive(zz, way):
        for a in arrays:
            chain_in(a, zz, way).wait_recv()
            for copy in plane(a, zz, 1):
                copy.start()

        @pl.when(may_go(way))
        def _():
            for a in arrays:
                chain(a, zz, way).start()

    for_each_arrival(0, arrive)
    second(z)
    for_each_arrival(1, arrive)
    for_each_arrival(0, lambda zz, way: second(zz))
    third(z)
    for_each_arrival(2, arrive)
    for_each_arrival(1, lambda zz, way: second(zz))
    for_each_arrival(0, lambda zz, way: third(zz))

    def row_mate(k, of, core):
        ref = (rows_out, most_out)[k].at[of, core]
        return remote(ref, ref, mate_sems.at[0, k, of], mate_sems.at[1, k, of], mate)

    for copy in own_rows:
        copy.wait()
    for k in range(2):
        row_mate(k, chip, c).start()
    for i in range(1, 16):
        of = lax.rem(chip + 16 - i, 16)
        for k in range(2):
            row_copies[(i - 1) * 2 + k].wait_recv()
            row_mate(k, of, c).start()

    for_each_arrival(2, lambda zz, way: second(zz))
    for_each_arrival(1, lambda zz, way: third(zz))
    for_each_arrival(2, lambda zz, way: third(zz))

    for i in range(16):
        of = lax.rem(chip + 16 - i, 16)
        for k in range(2):
            row_mate(k, of, c).wait_send()
            row_mate(k, of, 1 - c).wait_recv()
    for copy in row_copies:
        copy.wait_send()
    for a in arrays:
        for zz in range(4):
            for step in (1, 2):
                for copy in plane(a, zz, step):
                    copy.wait_send()
            to_mate(a, zz).wait_send()
            from_mate(a, zz).wait_recv()

    def sent(zz, way):
        for a in arrays:
            chain(a, zz, way).wait_send()

    for way in (1, -1):

        @pl.when(may_go(way))
        def _(way=way):
            sent(z, way)
            for step in range(2):
                zz = z - way * (step + 1)

                @pl.when((zz >= 0) & (zz < 4))
                def _(zz=zz):
                    sent(zz, way)


def exchange(rows, most, weights, collective):
    count = len(weights)
    return pl.pallas_call(
        functools.partial(exchange_kernel, count),
        out_shape=[
            jax.ShapeDtypeStruct((16, 2) + rows.shape[1:], rows.dtype),
            jax.ShapeDtypeStruct((16, 2) + most.shape, most.dtype),
        ]
        + [jax.ShapeDtypeStruct((4, 2, 2, 2) + w.shape, w.dtype) for w in weights],
        in_specs=[VMEM] * 2 + [ANY] * count,
        out_specs=[ANY, VMEM] + [ANY] * count,
        scratch_shapes=[
            pltpu.SemaphoreType.DMA((2, 2, 16)),
            pltpu.SemaphoreType.DMA((2, 2, 16)),
            pltpu.SemaphoreType.DMA((count + 2,)),
            pltpu.SemaphoreType.DMA((2, max(count, 1), 2, 4)),
            pltpu.SemaphoreType.DMA((2, max(count, 1), 4, 2, 2)),
            pltpu.SemaphoreType.DMA((2, max(count, 1), 4)),
        ],
        compiler_params=params(collective),
        name="exchange",
    )(rows, most, *weights)


def layer_norm(v, gain, shift):
    centred = v - jnp.mean(v, axis=-1, keepdims=True)
    inverse = lax.rsqrt(jnp.mean(centred * centred, axis=-1, keepdims=True) + ln_eps)
    normed = centred * inverse
    return normed * gain + shift, normed, inverse


def norm_back(grad_out, gain, normed, inverse):
    scaled = grad_out * gain
    return inverse * (
        scaled
        - jnp.mean(scaled, axis=-1, keepdims=True)
        - normed * jnp.mean(scaled * normed, axis=-1, keepdims=True)
    )


def product(left, right, pattern):
    return jnp.einsum(pattern, left, right, preferred_element_type=f32)


def batched(left, right):
    return jnp.einsum("bij,bjk->bik", left, right, precision=lax.Precision.HIGHEST)


def inverse_root(matrix):
    identity = jnp.eye(matrix.shape[-1], dtype=f32)
    trace_sum = jnp.sum(matrix * identity, axis=(1, 2), keepdims=True)
    current = matrix / trace_sum
    root_now = identity * lax.rsqrt(jnp.sqrt(trace_sum))
    for _ in range(NEWTON):
        factor = (5.0 * identity - current) * 0.25
        root_now = batched(root_now, factor)
        square = batched(factor, factor)
        current = batched(batched(square, square), current)
    return root_now


def shampoo_update(gradient, weights, left_statistics, right_statistics):
    left_renewed = beta_stats * left_statistics + (1.0 - beta_stats) * jnp.einsum(
        "bir,bjr->bij", gradient, gradient, precision=lax.Precision.HIGHEST
    )
    right_renewed = beta_stats * right_statistics + (1.0 - beta_stats) * jnp.einsum(
        "bir,bis->brs", gradient, gradient, precision=lax.Precision.HIGHEST
    )
    left_root = inverse_root(left_renewed + root_eps * jnp.eye(left_renewed.shape[-1], dtype=f32))
    right_root = inverse_root(
        right_renewed + root_eps * jnp.eye(right_renewed.shape[-1], dtype=f32)
    )
    update = batched(batched(left_root, gradient), right_root)
    return (weights - learn_rate * update, left_renewed, right_renewed)


def split_into_blocks(down_part, up_part, block_rows):
    rank = up_part.shape[0] // 2
    stacked = jnp.stack(
        [down_part[:, :rank], down_part[:, rank:], up_part[:rank].T, up_part[rank:].T]
    )
    return stacked.reshape(-1, block_rows, rank)


def merge_from_blocks(blocks, width):
    stacked = blocks.reshape(4, width, blocks.shape[-1])
    return (
        jnp.concatenate([stacked[0], stacked[1]], axis=1),
        jnp.concatenate([stacked[2].T, stacked[3].T], axis=0),
    )


def on_device(
    direct,
    token_identifiers,
    lengths,
    loss_positions,
    token_embedding_table,
    positions,
    query_key_value_matrix,
    output_weight,
    up_weight,
    down_weight,
    vectors,
    adapter_down_weight,
    adapter_up_weight,
    left_statistics,
    right_statistics,
):
    width = adapter_down_weight.shape[0]
    rank = adapter_down_weight.shape[1] // 2
    micros, _, slot_count = token_identifiers.shape
    picks = loss_positions.shape[2]
    ff = up_weight.shape[1]
    head = width // ATTENTION_HEADS
    scale = head ** (-0.5)
    adapter_scale = adapter_alpha / rank
    vocab_slice = token_embedding_table.shape[0]
    devices = lax.axis_size("dp") * lax.axis_size("fsdp")
    me = lax.axis_index(BOTH)
    unit = 2 if direct else 1

    lens = lengths[:, 0]
    ids = token_identifiers[:, 0]
    ids = jnp.where(iota(ids.shape, 1) < lens[:, None], ids, -1)
    packed_ids = ids.reshape(-1, 128)
    amount = vectors.shape[0]
    packed_vec = jnp.pad(vectors.astype(f32), (0, -amount % 1024)).reshape(-1, 128)
    if direct:
        all_ids, all_vec = spread(packed_ids, packed_vec, devices, 0)
    else:
        all_ids, all_vec = (lax.all_gather(v, BOTH) for v in (packed_ids, packed_vec))
    vec = all_vec.reshape(devices, -1)[:, :amount].reshape(-1)
    unit_ids = all_ids.reshape(devices // unit, 1, -1)
    own_ids = lax.dynamic_index_in_dim(unit_ids, me // unit, 0, keepdims=False)

    def own_slots(which):
        both = slots(own_ids, which, CAPACITY, devices, vocab_slice).reshape(unit, -1)
        return lax.dynamic_index_in_dim(both, me % unit, 0, keepdims=False)

    def rows_of(received, slot):
        rows = jnp.take(received.reshape(-1, width), jnp.maximum(slot, 0), axis=0)
        return jnp.where(slot[:, None] >= 0, rows, jnp.zeros((), bf16))

    first = jnp.zeros((1,), jnp.int32)
    slot = own_slots(first)
    rows, most = select(unit_ids, token_embedding_table, first, CAPACITY)
    wide = jnp.concatenate([query_key_value_matrix, up_weight, output_weight, positions], axis=1)
    if direct:
        received, all_most, wide, down_w = exchange(rows, most, [wide, down_weight], 1)
        wide = wide.reshape(-1, wide.shape[-1])
        down_w = down_w.reshape(-1, width)
    else:
        received = lax.all_to_all(rows, BOTH, 0, 0, tiled=True)
        all_most = lax.pmax(most, BOTH)
        wide = lax.all_gather(wide, BOTH, axis=0, tiled=True)
        down_w = lax.all_gather(down_weight, BOTH, axis=0, tiled=True)
    most = jnp.max(all_most)

    def further(state):
        step, rows_sum = state
        which = step.reshape(1)
        rows, most = select(unit_ids, token_embedding_table, which, CAPACITY)
        if direct:
            received = exchange(rows, most, [], 2)[0]
        else:
            received = lax.all_to_all(rows, BOTH, 0, 0, tiled=True)
        return step + 1, rows_sum + rows_of(received, own_slots(which))

    embedded = lax.while_loop(
        lambda state: (state[0] * CAPACITY).astype(f32) < most,
        further,
        (jnp.ones((), jnp.int32), rows_of(received, slot)),
    )[1].reshape(micros, slot_count, width)

    qkv_w = wide[:, : 3 * width]
    up_w = wide[:, 3 * width : 3 * width + ff]
    out_w = wide[:, 3 * width + ff : 4 * width + ff]
    pos_w = wide[:, 4 * width + ff :]
    sizes = [width] * 6 + [3 * width, width, ff, width]
    ends = [sum(sizes[: i + 1]) for i in range(len(sizes))]
    norms = [vec[end - size : end] for size, end in zip(sizes, ends)]

    down_b = adapter_down_weight.astype(bf16)
    up_b = adapter_up_weight.astype(bf16)
    picked = loss_positions[:, 0]
    take = jax.vmap(lambda v, p: jnp.take(v, p, axis=0))
    start_x = embedded.astype(f32) + pos_w.astype(f32)
    h1 = layer_norm(start_x, norms[0], norms[1])[0].astype(bf16)
    low = product(h1, down_b, "btd,dr->btr").astype(bf16)
    pair = product(h1, qkv_w[:, width:], "btd,de->bte") + norms[6][width:]
    keys = pair[..., :width].astype(bf16).reshape(micros, slot_count, -1, head)
    values = pair[..., width:] + adapter_scale * product(low[..., rank:], up_b[rank:], "btr,rm->btm")
    values = values.astype(bf16).reshape(micros, slot_count, -1, head)
    h1_p, low_p = take(h1, picked), take(low, picked)
    queries = product(h1_p, qkv_w[:, :width], "btd,de->bte") + norms[6][:width]
    queries = queries + adapter_scale * product(low_p[..., :rank], up_b[:rank], "btr,rm->btm")
    queries = queries.astype(bf16).reshape(micros, picks, -1, head)
    raw = product(queries, keys, "bqhd,bkhd->bhqk") * scale
    slot_index = jnp.arange(slot_count, dtype=jnp.int32)
    allowed = (slot_index <= picked[:, :, None]) & (slot_index < lens[:, None, None])
    probs = jax.nn.softmax(jnp.where(allowed[:, None], raw, masked_score), axis=-1)
    probs_b = probs.astype(bf16)
    attended = product(probs_b, values, "bhqk,bkhd->bqhd").reshape(-1, width).astype(bf16)
    x_p = take(start_x, picked).reshape(-1, width)
    middle = x_p + product(attended, out_w, "td,de->te") + norms[7]
    norm_two, normed_two, inverse_two = layer_norm(middle, norms[2], norms[3])
    before = product(norm_two.astype(bf16), up_w, "td,df->tf") + norms[8]
    activated, gelu_back = jax.vjp(lambda v: jax.nn.gelu(v, approximate=True), before)
    final = middle + product(activated.astype(bf16), down_w, "tf,fd->td") + norms[9]
    hidden, normed_three, inverse_three = layer_norm(final, norms[4], norms[5])
    hidden = hidden.astype(bf16)

    valid = (picked + 1 < lens[:, None]).astype(f32).reshape(-1)
    wanted = take(embedded, jnp.minimum(picked + 1, slot_count - 1)).reshape(-1, width)
    every = lax.all_gather(hidden, BOTH, axis=0, tiled=True)
    logits = product(every, token_embedding_table, "rd,vd->rv")
    part = jax.nn.logsumexp(logits, axis=1)
    total = jax.nn.logsumexp(lax.all_gather(part, BOTH), axis=0)
    weights = jnp.exp(logits - total[:, None]).astype(bf16)
    mean_row = lax.psum_scatter(
        product(weights, token_embedding_table, "rv,vd->rd"), BOTH, scatter_dimension=0, tiled=True
    )
    own_total = lax.dynamic_slice_in_dim(total, me * valid.shape[0], valid.shape[0], 0)
    chosen = jnp.sum(hidden.astype(f32) * wanted.astype(f32), axis=1)
    loss = jnp.sum(valid * (own_total - chosen))
    d_hidden = valid[:, None] * (mean_row - wanted.astype(f32))

    d_final = norm_back(d_hidden, norms[4], normed_three, inverse_three)
    d_act = product(d_final.astype(bf16), down_w, "td,fd->tf")
    d_before = gelu_back(d_act)[0].astype(bf16)
    d_two = product(d_before, up_w, "tf,df->td")
    d_middle = d_final + norm_back(d_two, norms[2], normed_two, inverse_two)
    d_att = product(d_middle.astype(bf16), out_w, "te,de->td").astype(bf16)
    d_att = d_att.reshape(micros, picks, -1, head)
    d_probs = product(d_att, values, "bqhd,bkhd->bhqk")
    d_values = product(probs_b, d_att, "bhqk,bqhd->bkhd").astype(bf16)
    d_values = d_values.reshape(micros, slot_count, width)
    d_scores = probs * (d_probs - jnp.sum(probs * d_probs, axis=-1, keepdims=True))
    d_queries = product(d_scores.astype(bf16), keys, "bhqk,bkhd->bqhd") * scale
    d_queries = d_queries.reshape(micros, picks, width).astype(bf16)
    d_low_q = (adapter_scale * product(d_queries, up_b[:rank], "btm,rm->btr")).astype(bf16)
    d_low_v = (adapter_scale * product(d_values, up_b[rank:], "btm,rm->btr")).astype(bf16)
    down_gradient = jnp.concatenate(
        [product(h1_p, d_low_q, "btd,btr->dr"), product(h1, d_low_v, "btd,btr->dr")], axis=1
    )
    up_gradient = adapter_scale * jnp.concatenate(
        [
            product(low_p[..., :rank], d_queries, "btr,btm->rm"),
            product(low[..., rank:], d_values, "btr,btm->rm"),
        ],
        axis=0,
    )
    down_gradient, up_gradient, loss, counted = lax.psum(
        (down_gradient, up_gradient, loss, jnp.sum(valid)), BOTH
    )
    norm = jnp.sqrt(jnp.sum(down_gradient * down_gradient) + jnp.sum(up_gradient * up_gradient))
    factor = clip_level / jnp.maximum(norm, clip_level)
    down_gradient = down_gradient * factor
    up_gradient = up_gradient * factor
    owned = left_statistics.shape[0]
    own_blocks = lambda a, b: lax.dynamic_slice_in_dim(
        split_into_blocks(a, b, STATS_BLOCK_ROWS), lax.axis_index("fsdp") * owned, owned, 0
    )
    new_own, left_new, right_new = shampoo_update(
        own_blocks(down_gradient, up_gradient),
        own_blocks(adapter_down_weight, adapter_up_weight),
        left_statistics,
        right_statistics,
    )
    new_blocks = lax.all_gather(new_own, "fsdp", axis=0, tiled=True)
    down_new, up_new = merge_from_blocks(new_blocks, width)
    return (
        jnp.stack([loss, counted]),
        norm,
        down_gradient,
        up_gradient,
        left_new,
        right_new,
        down_new,
        up_new,
    )


def solution(mesh):
    direct = dict(mesh.shape) == {"dp": 8, "fsdp": 4}
    rows = P(BOTH, None)
    placed = (
        P(None, BOTH, None),
        P(None, BOTH),
        P(None, BOTH, None),
        rows,
        rows,
        rows,
        rows,
        rows,
        rows,
        P(BOTH),
        P(),
        P(),
        P("fsdp", None, None),
        P("fsdp", None, None),
    )
    return jax.shard_map(
        functools.partial(on_device, direct),
        mesh=mesh,
        in_specs=placed,
        out_specs=(P(), P(), P(), P(), P("fsdp", None, None), P("fsdp", None, None), P(), P()),
        check_vma=False,
    )
```

```python
import functools
import jax
import jax.numpy as jnp
from jax import lax
from jax.experimental import pallas as pl
from jax.experimental.pallas import tpu as pltpu
from jax.sharding import PartitionSpec as P

ATTENTION_HEADS = 16
STATS_BLOCK_ROWS = 256
NEWTON = 8
CAPACITY = 80

ln_eps = 1e-05
adapter_alpha = 32.0
beta_stats = 0.95
root_eps = 1e-12
clip_level = 0.01
learn_rate = 0.05
masked_score = -1e30

BOTH = ("dp", "fsdp")
MESH = pl.DeviceIdType.MESH
VMEM = pl.BlockSpec(memory_space=pltpu.VMEM)
ANY = pl.BlockSpec(memory_space=pl.ANY)
f32 = jnp.float32
bf16 = jnp.bfloat16


def place():
    d, f = lax.axis_index("dp"), lax.axis_index("fsdp")
    return d // 2, lax.rem(d, 2), f // 2, lax.rem(f, 2)


def target(z, x, y, c):
    return (z * 2 + x, y * 2 + c)


def nth(i):
    return (i // 4, lax.rem(i, 4))


def greet_all(count):
    me = lax.axis_index("dp") * 4 + lax.axis_index("fsdp")
    sem = pltpu.get_barrier_semaphore()
    for i in range(1, count):
        pl.semaphore_signal(
            sem, inc=1, device_id=nth(lax.rem(me + i, count)), device_id_type=MESH
        )
    pl.semaphore_wait(sem, count - 1)
    return me


def remote(src, dst, send, recv, device):
    return pltpu.make_async_remote_copy(
        src_ref=src, dst_ref=dst, send_sem=send, recv_sem=recv, device_id=device, device_id_type=MESH
    )


def params(collective=None, vmem=60):
    if collective is None:
        return pltpu.CompilerParams(vmem_limit_bytes=vmem * 2**20)
    return pltpu.CompilerParams(
        vmem_limit_bytes=vmem * 2**20, collective_id=collective, has_side_effects=True
    )


def spread_kernel(count, a_ref, b_ref, a_out, b_out, send, recv):
    me = greet_all(count)
    copies = []
    for i in range(1, count):
        to = nth(lax.rem(me + i, count))
        for k, (src, dst) in enumerate(((a_ref, a_out), (b_ref, b_out))):
            copy = remote(src, dst.at[me], send.at[k, i], recv.at[k, i], to)
            copy.start()
            copies.append(copy)
    a_out[me] = a_ref[...]
    b_out[me] = b_ref[...]
    for copy in copies:
        copy.wait()


def spread(a, b, count, collective):
    return pl.pallas_call(
        functools.partial(spread_kernel, count),
        out_shape=[
            jax.ShapeDtypeStruct((count,) + a.shape, a.dtype),
            jax.ShapeDtypeStruct((count,) + b.shape, b.dtype),
        ],
        in_specs=[VMEM] * 2,
        out_specs=[VMEM] * 2,
        scratch_shapes=[pltpu.SemaphoreType.DMA((2, count))] * 2,
        compiler_params=params(collective),
        name="spread",
    )(a, b)


def iota(shape, dim):
    return lax.broadcasted_iota(jnp.int32, shape, dim)


def marks(condition):
    return jnp.where(condition, 1.0, 0.0).astype(bf16)


def dot(a, b, ca, cb):
    return lax.dot_general(a, b, (((ca,), (cb,)), ((), ())), preferred_element_type=f32)


def ranks(high, low, rows):
    width = low.shape[1]
    count = dot(marks(iota((rows, width), 0) == high), marks(iota((128, width), 0) == low), 1, 1)
    present = marks(count > 0.5)
    through = dot(present, marks(iota((128, 128), 0) <= iota((128, 128), 1)), 1, 0)
    return through - present.astype(f32), through[:, 127:128], present.astype(f32)


def select_kernel(capacity, ids_ref, table_ref, round_ref, rows_ref, most_ref, marks_ref):
    units, width = ids_ref.shape[0], ids_ref.shape[2]
    local_rows = table_ref.shape[0]
    grid_rows = -(-local_rows // 128)
    pad_rows = -(-grid_rows // 16) * 16
    me = lax.axis_index("dp") * lax.axis_size("fsdp") + lax.axis_index("fsdp")
    begin = (round_ref[0] * capacity).astype(f32)
    most = jnp.zeros((1, 1), f32)
    for unit in range(units):
        local = ids_ref[unit] - me * local_rows
        inside = (local >= 0) & (local < local_rows)
        high = jnp.where(inside, local >> 7, -1)
        low = jnp.where(inside, local & 127, -1)
        before, row_total, present = ranks(high, low, pad_rows)
        earlier = marks(iota((pad_rows, pad_rows), 1) < iota((pad_rows, pad_rows), 0))
        offset = dot(earlier, jnp.broadcast_to(row_total, (pad_rows, 128)).astype(bf16), 1, 0)
        rank = jnp.where(present > 0.5, before + offset - begin, -1.0)
        most = jnp.maximum(most, jnp.sum(row_total, axis=0, keepdims=True))
        for row in range(grid_rows):
            columns = min(128, local_rows - row * 128)
            hit = iota((capacity, 128), 0).astype(f32) == rank[row : row + 1, :]
            marks_ref[unit * capacity : (unit + 1) * capacity, row * 128 : row * 128 + columns] = (
                marks(hit)[:, :columns]
            )
    most_ref[...] = jnp.broadcast_to(most, most_ref.shape)
    for unit in range(units):
        rows_ref[unit] = dot(
            marks_ref[unit * capacity : (unit + 1) * capacity, :], table_ref[...], 1, 0
        ).astype(bf16)


def select(unit_ids, table, which_round, capacity):
    units = unit_ids.shape[0]
    return pl.pallas_call(
        functools.partial(select_kernel, capacity),
        out_shape=[
            jax.ShapeDtypeStruct((units, capacity, table.shape[1]), bf16),
            jax.ShapeDtypeStruct((8, 128), f32),
        ],
        in_specs=[VMEM, VMEM, pl.BlockSpec(memory_space=pltpu.SMEM)],
        out_specs=[VMEM] * 2,
        scratch_shapes=[pltpu.VMEM((units * capacity, table.shape[0]), bf16)],
        compiler_params=params(),
        name="select",
    )(unit_ids, table, which_round)


def slots_kernel(capacity, owners, local_rows, ids_ref, round_ref, slot_ref):
    ids = ids_ref[...]
    grid_rows = -(-local_rows // 128)
    pad_rows = -(-owners * grid_rows // 16) * 16
    begin = (round_ref[0] * capacity).astype(f32)
    owner = jnp.floor((ids.astype(f32) + 0.5) * (1.0 / local_rows)).astype(jnp.int32)
    local = ids - owner * local_rows
    high = jnp.where(ids >= 0, owner * grid_rows + (local >> 7), -1)
    low = jnp.where(ids >= 0, local & 127, -1)
    before, row_total, present = ranks(high, low, pad_rows)
    group = lambda dim: jnp.floor(
        (iota((pad_rows, pad_rows), dim).astype(f32) + 0.5) * (1.0 / grid_rows)
    )
    earlier = (iota((pad_rows, pad_rows), 1) < iota((pad_rows, pad_rows), 0)) & (
        group(0) == group(1)
    )
    offset = dot(
        marks(earlier), jnp.broadcast_to(row_total, (pad_rows, 128)).astype(bf16), 1, 0
    )
    rank = before + offset - begin
    rank = jnp.where((present > 0.5) & (rank >= 0.0) & (rank < capacity), rank, -1.0)
    width = ids.shape[1]
    of_low = dot(rank.astype(bf16), marks(iota((pad_rows, width), 0) == high), 0, 0)
    own_rank = jnp.sum(jnp.where(iota((128, width), 0) == low, of_low, 0.0), axis=0, keepdims=True)
    slot = owner * capacity + own_rank.astype(jnp.int32)
    slot_ref[...] = jnp.where((ids >= 0) & (own_rank >= 0.0), slot, -1)


def slots(ids, which_round, capacity, owners, local_rows):
    return pl.pallas_call(
        functools.partial(slots_kernel, capacity, owners, local_rows),
        out_shape=jax.ShapeDtypeStruct(ids.shape, jnp.int32),
        in_specs=[VMEM, pl.BlockSpec(memory_space=pltpu.SMEM)],
        out_specs=VMEM,
        compiler_params=params(),
        name="slots",
    )(ids, which_round)


def send_rows(rows_ref, most_ref, rows_out, most_out, sems):
    z, x, y, c = place()
    chip = (z * 2 + x) * 2 + y
    copies = []
    for i in range(1, 16):
        to = lax.rem(chip + i, 16)
        device = target(to // 4, lax.rem(to // 2, 2), lax.rem(to, 2), c)
        for k, (src, dst) in enumerate(
            ((rows_ref.at[to], rows_out.at[chip, c]), (most_ref, most_out.at[chip, c]))
        ):
            copies.append(remote(src, dst, sems.at[0, k, i], sems.at[1, k, i], device))
    return copies


def exchange_kernel(weights, with_rows, *refs):
    if with_rows:
        (rows_ref, most_ref), refs = refs[:2], refs[2:]
    w_in, refs = refs[:weights], refs[weights:]
    if with_rows:
        (rows_out, most_out), refs = refs[:2], refs[2:]
    w_out, refs = refs[:weights], refs[weights:]
    sems, mate_sems, own_sems, chain_sems, plane_sems, core_sems = refs
    greet_all(32)
    z, x, y, c = place()
    chip = (z * 2 + x) * 2 + y
    mate = target(z, x, y, 1 - c)

    def chain(a, zz, way):
        src = w_out[a].at[zz, x, y, c]
        k = (way + 1) // 2
        return remote(
            src, src, chain_sems.at[0, a, k, zz], chain_sems.at[1, a, k, zz], target(z + way, x, y, c)
        )

    def halves(a):
        rows = w_out[a].shape[4]
        return pl.ds(0, rows // 2), pl.ds(rows // 2, rows // 2)

    def plane(a, zz, step):
        upper, lower = halves(a)
        over_x, over_y = target(z, 1 - x, y, c), target(z, x, 1 - y, c)
        full = w_out[a]
        if step == 1:
            pairs = (
                (full.at[zz, x, y, c, upper], over_x),
                (full.at[zz, x, y, c, lower], over_y),
            )
        else:
            pairs = (
                (full.at[zz, :, y, c, upper], over_y),
                (full.at[zz, x, :, c, lower], over_x),
            )
        return [
            remote(
                ref, ref, plane_sems.at[0, a, zz, step - 1, k], plane_sems.at[1, a, zz, step - 1, k], to
            )
            for k, (ref, to) in enumerate(pairs)
        ]

    def landed(a, zz, step):
        upper, lower = halves(a)
        full = w_out[a]
        over_x, over_y = target(z, 1 - x, y, c), target(z, x, 1 - y, c)
        if step == 1:
            pairs = (
                (full.at[zz, 1 - x, y, c, upper], over_x),
                (full.at[zz, x, 1 - y, c, lower], over_y),
            )
        else:
            pairs = (
                (full.at[zz, :, 1 - y, c, upper], over_y),
                (full.at[zz, 1 - x, :, c, lower], over_x),
            )
        return [
            remote(
                ref, ref, plane_sems.at[0, a, zz, step - 1, k], plane_sems.at[1, a, zz, step - 1, k], to
            )
            for k, (ref, to) in enumerate(pairs)
        ]

    def to_mate(a, zz):
        ref = w_out[a].at[zz, :, :, c]
        return remote(ref, ref, core_sems.at[0, a, zz], core_sems.at[1, a, zz], mate)

    def from_mate(a, zz):
        ref = w_out[a].at[zz, :, :, 1 - c]
        return remote(ref, ref, core_sems.at[0, a, zz], core_sems.at[1, a, zz], mate)

    def chain_in(a, zz, way):
        ref = w_out[a].at[zz, x, y, c]
        k = (way + 1) // 2
        return remote(
            ref, ref, chain_sems.at[0, a, k, zz], chain_sems.at[1, a, k, zz], target(z - way, x, y, c)
        )

    arrays = range(weights)
    own = [
        pltpu.make_async_copy(w_in[a], w_out[a].at[z, x, y, c], own_sems.at[a]) for a in arrays
    ]
    for copy in own:
        copy.start()
    if with_rows:
        row_copies = send_rows(rows_ref, most_ref, rows_out, most_out, sems)
        own_rows = [
            pltpu.make_async_copy(rows_ref.at[chip], rows_out.at[chip, c], own_sems.at[weights]),
            pltpu.make_async_copy(most_ref, most_out.at[chip, c], own_sems.at[weights + 1]),
        ]
        for copy in row_copies + own_rows:
            copy.start()
    for copy in own:
        copy.wait()

    def for_each_arrival(step, act):
        for way in (1, -1):
            zz = z - way * (step + 1)

            @pl.when((zz >= 0) & (zz < 4))
            def _(zz=zz, way=way):
                act(zz, way)

    def may_go(way):
        return (z + way >= 0) & (z + way < 4)

    for way in (1, -1):

        @pl.when(may_go(way))
        def _(way=way):
            for a in arrays:
                chain(a, z, way).start()

    for a in arrays:
        for copy in plane(a, z, 1):
            copy.start()

    def second(zz):
        for a in arrays:
            for copy in landed(a, zz, 1):
                copy.wait_recv()
            for copy in plane(a, zz, 2):
                copy.start()

    def third(zz):
        for a in arrays:
            for copy in landed(a, zz, 2):
                copy.wait_recv()
            to_mate(a, zz).start()

    def arrive(zz, way):
        for a in arrays:
            chain_in(a, zz, way).wait_recv()
            for copy in plane(a, zz, 1):
                copy.start()

        @pl.when(may_go(way))
        def _():
            for a in arrays:
                chain(a, zz, way).start()

    for_each_arrival(0, arrive)
    second(z)
    for_each_arrival(1, arrive)
    for_each_arrival(0, lambda zz, way: second(zz))
    third(z)
    for_each_arrival(2, arrive)
    for_each_arrival(1, lambda zz, way: second(zz))
    for_each_arrival(0, lambda zz, way: third(zz))

    def row_mate(k, of, core):
        ref = (rows_out, most_out)[k].at[of, core]
        return remote(ref, ref, mate_sems.at[0, k, of], mate_sems.at[1, k, of], mate)

    if with_rows:
        for copy in own_rows:
            copy.wait()
        for k in range(2):
            row_mate(k, chip, c).start()
        for i in range(1, 16):
            of = lax.rem(chip + 16 - i, 16)
            for k in range(2):
                row_copies[(i - 1) * 2 + k].wait_recv()
                row_mate(k, of, c).start()

    for_each_arrival(2, lambda zz, way: second(zz))
    for_each_arrival(1, lambda zz, way: third(zz))
    for_each_arrival(2, lambda zz, way: third(zz))

    if with_rows:
        for i in range(16):
            of = lax.rem(chip + 16 - i, 16)
            for k in range(2):
                row_mate(k, of, c).wait_send()
                row_mate(k, of, 1 - c).wait_recv()
        for copy in row_copies:
            copy.wait_send()
    for a in arrays:
        for zz in range(4):
            for step in (1, 2):
                for copy in plane(a, zz, step):
                    copy.wait_send()
            to_mate(a, zz).wait_send()
            from_mate(a, zz).wait_recv()

    def sent(zz, way):
        for a in arrays:
            chain(a, zz, way).wait_send()

    for way in (1, -1):

        @pl.when(may_go(way))
        def _(way=way):
            sent(z, way)
            for step in range(2):
                zz = z - way * (step + 1)

                @pl.when((zz >= 0) & (zz < 4))
                def _(zz=zz):
                    sent(zz, way)


def exchange(rows, weights, collective):
    count = len(weights)
    rows_out = [jax.ShapeDtypeStruct((16, 2) + v.shape[-2:], v.dtype) for v in rows]
    return pl.pallas_call(
        functools.partial(exchange_kernel, count, len(rows) > 0),
        out_shape=rows_out
        + [jax.ShapeDtypeStruct((4, 2, 2, 2) + w.shape, w.dtype) for w in weights],
        in_specs=[VMEM] * len(rows) + [ANY] * count,
        out_specs=[ANY, VMEM][: len(rows)] + [ANY] * count,
        scratch_shapes=[
            pltpu.SemaphoreType.DMA((2, 2, 16)),
            pltpu.SemaphoreType.DMA((2, 2, 16)),
            pltpu.SemaphoreType.DMA((count + 2,)),
            pltpu.SemaphoreType.DMA((2, max(count, 1), 2, 4)),
            pltpu.SemaphoreType.DMA((2, max(count, 1), 4, 2, 2)),
            pltpu.SemaphoreType.DMA((2, max(count, 1), 4)),
        ],
        compiler_params=params(collective),
        name="exchange",
    )(*rows, *weights)


def vocabulary_kernel(group, rows_ref, table_ref, mean_ref, total_ref):
    logits = dot(rows_ref[...], table_ref[...], 1, 1)
    top = jnp.max(logits, axis=1, keepdims=True)
    weights = jnp.exp(logits - top)
    amount = jnp.sum(weights, axis=1, keepdims=True)
    mean = dot(weights.astype(bf16), table_ref[...], 1, 0)
    mean_ref[...] = (mean / amount).astype(bf16)
    total = top + jnp.log(amount)
    for k in range(total_ref.shape[0]):
        total_ref[k] = jnp.broadcast_to(
            jnp.pad(as_row(total[k * group : (k + 1) * group]), ((0, 0), (0, 128 - group))), (8, 128)
        )


def same(size):
    return iota((size, size), 0) == iota((size, size), 1)


def as_row(column):
    return jnp.sum(jnp.where(same(column.shape[0]), column, 0.0), axis=0, keepdims=True)


def as_column(row):
    return jnp.sum(jnp.where(same(row.shape[1]), row, 0.0), axis=1, keepdims=True)


def vocabulary(rows, table, group, tile):
    count, width = rows.shape
    return pl.pallas_call(
        functools.partial(vocabulary_kernel, group),
        grid=(count // tile,),
        out_shape=[
            jax.ShapeDtypeStruct((count, width), bf16),
            jax.ShapeDtypeStruct((count // group, 8, 128), f32),
        ],
        in_specs=[
            pl.BlockSpec((tile, width), lambda i: (i, 0)),
            pl.BlockSpec(table.shape, lambda i: (0, 0)),
        ],
        out_specs=[
            pl.BlockSpec((tile, width), lambda i: (i, 0)),
            pl.BlockSpec((tile // group, 8, 128), lambda i: (i, 0, 0)),
        ],
        compiler_params=params(),
        name="vocabulary",
    )(rows, table)


def merged(parts):
    size = parts[0][0].shape[0]
    rows = [total[:1, :size] for _, total in parts]
    top = functools.reduce(jnp.maximum, rows)
    total = top + jnp.log(sum(jnp.exp(row - top) for row in rows))
    mean = sum(
        values.astype(f32) * as_column(jnp.exp(row - total)) for (values, _), row in zip(parts, rows)
    )
    return mean, jnp.broadcast_to(jnp.pad(total, ((0, 0), (0, 128 - size))), (8, 128))


def merge_kernel(
    q_ref, t_ref, q_out, t_out,
    core_q, core_t, keep_q, keep_t, send_q, send_t, got_q, got_t,
    next_q, next_t, pass_q, pass_t, last_q, last_t, end_q, end_t, final_q, final_t,
    core_sems, one_sems, two_sems, z_sems,
):
    greet_all(32)
    z, x, y, c = place()
    mate = target(z, x, y, 1 - c)
    over = (target(z, 1 - x, y, c), target(z, x, 1 - y, c))
    half = q_ref.shape[-1] // 2
    cols = (slice(0, half), slice(half, 2 * half))
    mine = (x, y)

    def nth_plane(i):
        return lax.rem(z + 1 + i, 4)

    def core_copies(zz):
        return [
            remote(q_ref.at[zz, :, :, 1 - c], core_q.at[zz], core_sems.at[0, 0, zz], core_sems.at[1, 0, zz], mate),
            remote(t_ref.at[zz, :, :, 1 - c], core_t.at[zz], core_sems.at[0, 1, zz], core_sems.at[1, 1, zz], mate),
        ]

    def one_copies(zz, k):
        return [
            remote(send_q.at[k, zz], got_q.at[k, zz], one_sems.at[0, 0, k, zz], one_sems.at[1, 0, k, zz], over[k]),
            remote(send_t.at[k, zz], got_t.at[k, zz], one_sems.at[0, 1, k, zz], one_sems.at[1, 1, k, zz], over[k]),
        ]

    def two_copies(zz, k):
        return [
            remote(pass_q.at[k, zz], last_q.at[k, zz], two_sems.at[0, 0, k, zz], two_sems.at[1, 0, k, zz], over[1 - k]),
            remote(pass_t.at[k, zz], last_t.at[k, zz], two_sems.at[0, 1, k, zz], two_sems.at[1, 1, k, zz], over[1 - k]),
        ]

    def z_copies(zz, frm, k):
        return [
            remote(end_q.at[k, zz], final_q.at[k, frm], z_sems.at[0, 0, k, zz], z_sems.at[1, 0, k, frm], target(zz, x, y, c)),
            remote(end_t.at[k, zz], final_t.at[k, frm], z_sems.at[0, 1, k, zz], z_sems.at[1, 1, k, frm], target(zz, x, y, c)),
        ]

    def start(copies):
        for copy in copies:
            copy.start()

    def landed(copies):
        for copy in copies:
            copy.wait_recv()

    def left(copies):
        for copy in copies:
            copy.wait_send()

    @pl.loop(0, 4)
    def _(i):
        start(core_copies(nth_plane(i)))

    @pl.loop(0, 4)
    def _(i):
        zz = nth_plane(i)
        landed(core_copies(zz))
        for xx in range(2):
            for yy in range(2):
                mean, total = merged(
                    [(q_ref[zz, xx, yy, c], t_ref[zz, xx, yy, c]), (core_q[zz, xx, yy], core_t[zz, xx, yy])]
                )
                for k, (own, other) in enumerate(((xx, yy), (yy, xx))):
                    part = mean[:, cols[k]]

                    @pl.when(own == mine[k])
                    def _(k=k, other=other, part=part, total=total):
                        keep_q[k, zz, other] = part
                        keep_t[k, zz, other] = total

                    @pl.when(own != mine[k])
                    def _(k=k, other=other, part=part, total=total):
                        send_q[k, zz, other] = part.astype(bf16)
                        send_t[k, zz, other] = total
        for k in range(2):
            start(one_copies(zz, k))

    @pl.loop(0, 4)
    def _(i):
        zz = nth_plane(i)
        for k in range(2):
            landed(one_copies(zz, k))
            for other in range(2):
                mean, total = merged(
                    [(keep_q[k, zz, other], keep_t[k, zz, other]), (got_q[k, zz, other], got_t[k, zz, other])]
                )

                @pl.when(other == mine[1 - k])
                def _(k=k, mean=mean, total=total):
                    next_q[k, zz] = mean
                    next_t[k, zz] = total

                @pl.when(other != mine[1 - k])
                def _(k=k, mean=mean, total=total):
                    pass_q[k, zz] = mean.astype(bf16)
                    pass_t[k, zz] = total

            start(two_copies(zz, k))

    @pl.loop(0, 4)
    def _(i):
        zz = nth_plane(i)
        for k in range(2):
            landed(two_copies(zz, k))
            mean, total = merged([(next_q[k, zz], next_t[k, zz]), (last_q[k, zz], last_t[k, zz])])

            @pl.when(i < 3)
            def _(k=k, mean=mean, total=total):
                end_q[k, zz] = mean.astype(bf16)
                end_t[k, zz] = total
                start(z_copies(zz, z, k))

            @pl.when(i == 3)
            def _(k=k, mean=mean, total=total):
                next_q[k, z] = mean
                next_t[k, z] = total

    for k in range(2):
        parts = [(next_q[k, z], next_t[k, z])]
        for i in range(3):
            frm = nth_plane(i)
            landed(z_copies(frm, frm, k))
            parts.append((final_q[k, frm], final_t[k, frm]))
        mean, total = merged(parts)
        q_out[:, cols[k]] = mean
        if k == 0:
            t_out[...] = total

    @pl.loop(0, 4)
    def _(i):
        zz = nth_plane(i)
        left(core_copies(zz))
        for k in range(2):
            left(one_copies(zz, k))
            left(two_copies(zz, k))

    @pl.loop(0, 3)
    def _(i):
        for k in range(2):
            left(z_copies(nth_plane(i), z, k))


def merge(means, totals, collective):
    rows, width = means.shape[-2:]
    half = width // 2
    tile = (8, 128)
    vmem = pltpu.VMEM
    return pl.pallas_call(
        merge_kernel,
        out_shape=[jax.ShapeDtypeStruct((rows, width), f32), jax.ShapeDtypeStruct(tile, f32)],
        in_specs=[VMEM] * 2,
        out_specs=[VMEM] * 2,
        scratch_shapes=[
            vmem((4, 2, 2, rows, width), bf16), vmem((4, 2, 2) + tile, f32),
            vmem((2, 4, 2, rows, half), f32), vmem((2, 4, 2) + tile, f32),
            vmem((2, 4, 2, rows, half), bf16), vmem((2, 4, 2) + tile, f32),
            vmem((2, 4, 2, rows, half), bf16), vmem((2, 4, 2) + tile, f32),
            vmem((2, 4, rows, half), f32), vmem((2, 4) + tile, f32),
            vmem((2, 4, rows, half), bf16), vmem((2, 4) + tile, f32),
            vmem((2, 4, rows, half), bf16), vmem((2, 4) + tile, f32),
            vmem((2, 4, rows, half), bf16), vmem((2, 4) + tile, f32),
            vmem((2, 4, rows, half), bf16), vmem((2, 4) + tile, f32),
            pltpu.SemaphoreType.DMA((2, 2, 4)),
            pltpu.SemaphoreType.DMA((2, 2, 2, 4)),
            pltpu.SemaphoreType.DMA((2, 2, 2, 4)),
            pltpu.SemaphoreType.DMA((2, 2, 2, 4)),
        ],
        compiler_params=params(collective),
        name="merge",
    )(means, totals)


def total_kernel(g_ref, g_out, parts, summed, one_sems, two_sems):
    me = greet_all(32)

    def tile(ref, k):
        return ref.at[k // 8, :, pl.ds(pl.multiple_of(lax.rem(k, 8) * 128, 128), 128)]

    def out(i):
        to = lax.rem(me + i, 32)
        return remote(tile(g_ref, to), parts.at[me], one_sems.at[0, to], one_sems.at[1, me], nth(to))

    def into(i):
        frm = lax.rem(me + i, 32)
        return remote(tile(g_ref, me), parts.at[frm], one_sems.at[0, frm], one_sems.at[1, frm], nth(frm))

    def back(i):
        to = lax.rem(me + i, 32)
        return remote(summed, tile(g_out, me), two_sems.at[0, to], two_sems.at[1, me], nth(to))

    def into_back(i):
        frm = lax.rem(me + i, 32)
        return remote(summed, tile(g_out, frm), two_sems.at[0, frm], two_sems.at[1, frm], nth(frm))

    for i in range(1, 32):
        out(i).start()
    columns = pl.ds(pl.multiple_of(lax.rem(me, 8) * 128, 128), 128)
    running = g_ref[me // 8, :, columns]
    for i in range(1, 32):
        into(i).wait_recv()
        running = running + parts[lax.rem(me + i, 32)]
    summed[...] = running
    g_out[me // 8, :, columns] = running
    for i in range(1, 32):
        back(i).start()
    for i in range(1, 32):
        into_back(i).wait_recv()
    for i in range(1, 32):
        out(i).wait_send()
        back(i).wait_send()


def total_of(gradient, collective):
    return pl.pallas_call(
        total_kernel,
        out_shape=jax.ShapeDtypeStruct(gradient.shape, f32),
        in_specs=[VMEM],
        out_specs=VMEM,
        scratch_shapes=[
            pltpu.VMEM((32, 8, 128), f32),
            pltpu.VMEM((8, 128), f32),
            pltpu.SemaphoreType.DMA((2, 32)),
            pltpu.SemaphoreType.DMA((2, 32)),
        ],
        compiler_params=params(collective),
        name="total",
    )(gradient)


def exact(a, b, ca, cb):
    return lax.dot_general(
        a, b, (((ca,), (cb,)), ((), ())), precision=lax.Precision.HIGHEST, preferred_element_type=f32
    )


def small_product(a, b):
    return sum(a[:, k : k + 1] * b[k : k + 1, :] for k in range(a.shape[0]))


def newton(matrix, product, apply):
    size = matrix.shape[0]
    identity = jnp.where(same(size), 1.0, 0.0)
    trace = jnp.sum(matrix * identity, keepdims=True)
    current = matrix / trace
    for step in range(NEWTON):
        factor = (5.0 * identity - current) * 0.25
        apply(factor)
        if step < NEWTON - 1:
            square = product(factor, factor)
            current = product(product(square, square), current)
    return lax.rsqrt(jnp.sqrt(trace))


def update_kernel(g_ref, w_ref, left_ref, right_ref, norm_ref, g_out, left_out, right_out, new_ref):
    owned, block = left_ref.shape[0], left_ref.shape[1]
    rank = right_ref.shape[1]
    group = lax.axis_index("fsdp")
    own = lax.rem(lax.axis_index("dp"), owned)
    data = jnp.where(iota(g_ref.shape, 1) < rank, g_ref[...], 0.0)
    norm = jnp.sqrt(jnp.sum(data * data, keepdims=True).reshape(1, 1))
    norm_ref[...] = jnp.broadcast_to(norm, norm_ref.shape)
    factor = clip_level / jnp.maximum(norm, clip_level)
    g_out[...] = data * factor
    for k in range(owned):
        grad = g_out[group, :, k * block : (k + 1) * block]
        left_out[k] = beta_stats * left_ref[k] + (1.0 - beta_stats) * exact(grad, grad, 0, 0)
        right_out[k] = (
            beta_stats * right_ref[k] + (1.0 - beta_stats) * exact(grad, grad, 1, 1)[:rank, :rank]
        )
    columns = pl.ds(pl.multiple_of(own * block, block), block)
    grad = g_out[group, :, columns]
    left = left_out[own] + root_eps * jnp.where(same(block), 1.0, 0.0)
    right = right_out[own] + root_eps * jnp.where(same(rank), 1.0, 0.0)
    state = {"left": grad, "right": jnp.where(same(rank), 1.0, 0.0)}

    def apply_left(factor):
        state["left"] = exact(state["left"], factor, 1, 1)

    def apply_right(factor):
        state["right"] = small_product(state["right"], factor)

    scale = newton(right, small_product, apply_right)
    scale = scale * newton(left, lambda a, b: exact(a, b, 1, 0), apply_left)
    root = state["right"] * scale
    rows = state["left"][:rank]
    update = sum(as_column(root[k : k + 1, :]) * rows[k : k + 1, :] for k in range(rank))
    new = w_ref[group, :rank, columns] - learn_rate * update
    new_ref[...] = jnp.pad(new, ((0, 8 - rank), (0, 0)))


def update(gradient, weights, left, right):
    return pl.pallas_call(
        update_kernel,
        out_shape=[
            jax.ShapeDtypeStruct((8, 128), f32),
            jax.ShapeDtypeStruct(gradient.shape, f32),
            jax.ShapeDtypeStruct(left.shape, f32),
            jax.ShapeDtypeStruct(right.shape, f32),
            jax.ShapeDtypeStruct((8, left.shape[1]), f32),
        ],
        in_specs=[VMEM] * 4,
        out_specs=[VMEM] * 5,
        compiler_params=params(),
        name="update",
    )(gradient, weights, left, right)


def share_kernel(new_ref, all_ref, sems):
    d, f = lax.axis_index("dp"), lax.axis_index("fsdp")
    half, me = d // 4, f * 4 + lax.rem(d, 4)

    def device(k):
        return (half * 4 + lax.rem(k, 4), k // 4)

    barrier = pltpu.get_barrier_semaphore()
    for i in range(1, 16):
        pl.semaphore_signal(barrier, inc=1, device_id=device(lax.rem(me + i, 16)), device_id_type=MESH)
    pl.semaphore_wait(barrier, 15)
    for i in range(1, 16):
        to = lax.rem(me + i, 16)
        remote(new_ref, all_ref.at[me], sems.at[0, to], sems.at[1, me], device(to)).start()
    all_ref[me] = new_ref[...]
    for i in range(1, 16):
        frm = lax.rem(me + i, 16)
        copy = remote(new_ref, all_ref.at[frm], sems.at[0, frm], sems.at[1, frm], device(frm))
        copy.wait_recv()
        copy.wait_send()


def share(new, collective):
    return pl.pallas_call(
        share_kernel,
        out_shape=jax.ShapeDtypeStruct((16,) + new.shape, f32),
        in_specs=[VMEM],
        out_specs=VMEM,
        scratch_shapes=[pltpu.SemaphoreType.DMA((2, 16))],
        compiler_params=params(collective),
        name="share",
    )(new)


def layer_norm(v, gain, shift):
    centred = v - jnp.mean(v, axis=-1, keepdims=True)
    inverse = lax.rsqrt(jnp.mean(centred * centred, axis=-1, keepdims=True) + ln_eps)
    normed = centred * inverse
    return normed * gain + shift, normed, inverse


def norm_back(grad_out, gain, normed, inverse):
    scaled = grad_out * gain
    return inverse * (
        scaled
        - jnp.mean(scaled, axis=-1, keepdims=True)
        - normed * jnp.mean(scaled * normed, axis=-1, keepdims=True)
    )


def product(left, right, pattern):
    return jnp.einsum(pattern, left, right, preferred_element_type=f32)


def on_device(
    direct,
    token_identifiers,
    lengths,
    loss_positions,
    token_embedding_table,
    positions,
    query_key_value_matrix,
    output_weight,
    up_weight,
    down_weight,
    vectors,
    adapter_down_weight,
    adapter_up_weight,
    left_statistics,
    right_statistics,
):
    width = adapter_down_weight.shape[0]
    rank = adapter_down_weight.shape[1] // 2
    micros, _, slot_count = token_identifiers.shape
    picks = loss_positions.shape[2]
    ff = up_weight.shape[1]
    head = width // ATTENTION_HEADS
    scale = head ** (-0.5)
    adapter_scale = adapter_alpha / rank
    vocab_slice = token_embedding_table.shape[0]
    devices = lax.axis_size("dp") * lax.axis_size("fsdp")
    me = lax.axis_index(BOTH)
    unit = 2 if direct else 1

    lens = lengths[:, 0]
    ids = token_identifiers[:, 0]
    ids = jnp.where(iota(ids.shape, 1) < lens[:, None], ids, -1)
    packed_ids = ids.reshape(-1, 128)
    amount = vectors.shape[0]
    packed_vec = jnp.pad(vectors.astype(f32), (0, -amount % 1024)).reshape(-1, 128)
    if direct:
        all_ids, all_vec = spread(packed_ids, packed_vec, devices, 0)
    else:
        all_ids, all_vec = (lax.all_gather(v, BOTH) for v in (packed_ids, packed_vec))
    vec = all_vec.reshape(devices, -1)[:, :amount].reshape(-1)
    unit_ids = all_ids.reshape(devices // unit, 1, -1)
    own_ids = lax.dynamic_index_in_dim(unit_ids, me // unit, 0, keepdims=False)

    def own_slots(which):
        both = slots(own_ids, which, CAPACITY, devices, vocab_slice).reshape(unit, -1)
        return lax.dynamic_index_in_dim(both, me % unit, 0, keepdims=False)

    def rows_of(received, slot):
        rows = jnp.take(received.reshape(-1, width), jnp.maximum(slot, 0), axis=0)
        return jnp.where(slot[:, None] >= 0, rows, jnp.zeros((), bf16))

    first = jnp.zeros((1,), jnp.int32)
    slot = own_slots(first)
    rows, most = select(unit_ids, token_embedding_table, first, CAPACITY)
    wide = jnp.concatenate([query_key_value_matrix, up_weight, output_weight, positions], axis=1)
    if direct:
        received, all_most, wide, down_w = exchange([rows, most], [wide, down_weight], 1)
        wide = wide.reshape(-1, wide.shape[-1])
        down_w = down_w.reshape(-1, width)
    else:
        received = lax.all_to_all(rows, BOTH, 0, 0, tiled=True)
        all_most = lax.pmax(most, BOTH)
        wide = lax.all_gather(wide, BOTH, axis=0, tiled=True)
        down_w = lax.all_gather(down_weight, BOTH, axis=0, tiled=True)
    most = jnp.max(all_most)

    def further(state):
        step, rows_sum = state
        which = step.reshape(1)
        rows, most = select(unit_ids, token_embedding_table, which, CAPACITY)
        if direct:
            received = exchange([rows, most], [], 2)[0]
        else:
            received = lax.all_to_all(rows, BOTH, 0, 0, tiled=True)
        return step + 1, rows_sum + rows_of(received, own_slots(which))

    embedded = lax.while_loop(
        lambda state: (state[0] * CAPACITY).astype(f32) < most,
        further,
        (jnp.ones((), jnp.int32), rows_of(received, slot)),
    )[1].reshape(micros, slot_count, width)

    qkv_w = wide[:, : 3 * width]
    up_w = wide[:, 3 * width : 3 * width + ff]
    out_w = wide[:, 3 * width + ff : 4 * width + ff]
    pos_w = wide[:, 4 * width + ff :]
    sizes = [width] * 6 + [3 * width, width, ff, width]
    ends = [sum(sizes[: i + 1]) for i in range(len(sizes))]
    norms = [vec[end - size : end] for size, end in zip(sizes, ends)]

    down_b = adapter_down_weight.astype(bf16)
    up_b = adapter_up_weight.astype(bf16)
    picked = loss_positions[:, 0]
    take = jax.vmap(lambda v, p: jnp.take(v, p, axis=0))
    start_x = embedded.astype(f32) + pos_w.astype(f32)
    h1 = layer_norm(start_x, norms[0], norms[1])[0].astype(bf16)
    low = product(h1, down_b, "btd,dr->btr").astype(bf16)
    pair = product(h1, qkv_w[:, width:], "btd,de->bte") + norms[6][width:]
    keys = pair[..., :width].astype(bf16).reshape(micros, slot_count, -1, head)
    values = pair[..., width:] + adapter_scale * product(low[..., rank:], up_b[rank:], "btr,rm->btm")
    values = values.astype(bf16).reshape(micros, slot_count, -1, head)
    h1_p, low_p = take(h1, picked), take(low, picked)
    queries = product(h1_p, qkv_w[:, :width], "btd,de->bte") + norms[6][:width]
    queries = queries + adapter_scale * product(low_p[..., :rank], up_b[:rank], "btr,rm->btm")
    queries = queries.astype(bf16).reshape(micros, picks, -1, head)
    raw = product(queries, keys, "bqhd,bkhd->bhqk") * scale
    slot_index = jnp.arange(slot_count, dtype=jnp.int32)
    allowed = (slot_index <= picked[:, :, None]) & (slot_index < lens[:, None, None])
    probs = jax.nn.softmax(jnp.where(allowed[:, None], raw, masked_score), axis=-1)
    probs_b = probs.astype(bf16)
    attended = product(probs_b, values, "bhqk,bkhd->bqhd").reshape(-1, width).astype(bf16)
    x_p = take(start_x, picked).reshape(-1, width)
    middle = x_p + product(attended, out_w, "td,de->te") + norms[7]
    norm_two, normed_two, inverse_two = layer_norm(middle, norms[2], norms[3])
    before = product(norm_two.astype(bf16), up_w, "td,df->tf") + norms[8]
    activated, gelu_back = jax.vjp(lambda v: jax.nn.gelu(v, approximate=True), before)
    final = middle + product(activated.astype(bf16), down_w, "tf,fd->td") + norms[9]
    hidden, normed_three, inverse_three = layer_norm(final, norms[4], norms[5])
    hidden = hidden.astype(bf16)

    valid = (picked + 1 < lens[:, None]).astype(f32).reshape(-1)
    wanted = take(embedded, jnp.minimum(picked + 1, slot_count - 1)).reshape(-1, width)
    if direct:
        (every,) = exchange([], [hidden], 3)
        every = every.reshape(-1, width)
    else:
        every = lax.all_gather(hidden, BOTH, axis=0, tiled=True)
    own_rows = valid.shape[0]
    means, totals = vocabulary(every, token_embedding_table, own_rows, 4 * own_rows)
    if direct:
        mean_row, own_total = merge(
            means.reshape(4, 2, 2, 2, own_rows, width), totals.reshape(4, 2, 2, 2, 8, 128), 4
        )
        own_total = own_total[0, :own_rows]
    else:
        part = totals[:, 0, :own_rows].reshape(-1)
        top = lax.pmax(part, BOTH)
        total = top + jnp.log(lax.psum(jnp.exp(part - top), BOTH))
        mean_row = lax.psum_scatter(
            means.astype(f32) * jnp.exp(part - total)[:, None], BOTH, scatter_dimension=0, tiled=True
        )
        own_total = lax.dynamic_slice_in_dim(total, me * own_rows, own_rows, 0)
    chosen = jnp.sum(hidden.astype(f32) * wanted.astype(f32), axis=1)
    loss = jnp.sum(valid * (own_total - chosen))
    d_hidden = valid[:, None] * (mean_row - wanted.astype(f32))

    d_final = norm_back(d_hidden, norms[4], normed_three, inverse_three)
    d_act = product(d_final.astype(bf16), down_w, "td,fd->tf")
    d_before = gelu_back(d_act)[0].astype(bf16)
    d_two = product(d_before, up_w, "tf,df->td")
    d_middle = d_final + norm_back(d_two, norms[2], normed_two, inverse_two)
    d_att = product(d_middle.astype(bf16), out_w, "te,de->td").astype(bf16)
    d_att = d_att.reshape(micros, picks, -1, head)
    d_probs = product(d_att, values, "bqhd,bkhd->bhqk")
    d_values = product(probs_b, d_att, "bhqk,bqhd->bkhd").astype(bf16)
    d_values = d_values.reshape(micros, slot_count, width)
    d_scores = probs * (d_probs - jnp.sum(probs * d_probs, axis=-1, keepdims=True))
    d_queries = product(d_scores.astype(bf16), keys, "bhqk,bkhd->bqhd") * scale
    d_queries = d_queries.reshape(micros, picks, width).astype(bf16)
    d_low_q = (adapter_scale * product(d_queries, up_b[:rank], "btm,rm->btr")).astype(bf16)
    d_low_v = (adapter_scale * product(d_values, up_b[rank:], "btm,rm->btr")).astype(bf16)
    gradient = jnp.stack(
        [
            product(d_low_q, h1_p, "btr,btd->rd"),
            product(d_low_v, h1, "btr,btd->rd"),
            adapter_scale * product(low_p[..., :rank], d_queries, "btr,btm->rm"),
            adapter_scale * product(low[..., rank:], d_values, "btr,btm->rm"),
        ]
    )
    gradient = jnp.pad(gradient, ((0, 0), (0, 8 - rank), (0, 0)))
    gradient = gradient.at[0, rank, :2].set(jnp.stack([loss, jnp.sum(valid)]))
    gradient = total_of(gradient, 5) if direct else lax.psum(gradient, BOTH)
    old = jnp.concatenate([adapter_down_weight.T, adapter_up_weight]).reshape(4, rank, width)
    norm, clipped, left_new, right_new, new = update(
        gradient, jnp.pad(old, ((0, 0), (0, 8 - rank), (0, 0))), left_statistics, right_statistics
    )
    if direct:
        blocks = share(new, 6)
    else:
        blocks = lax.all_gather(new, ("fsdp", "dp"))
        blocks = blocks.reshape(lax.axis_size("fsdp"), -1, 8, new.shape[1])
        blocks = blocks[:, : left_statistics.shape[0]].reshape(-1, 8, new.shape[1])
    updated = jnp.swapaxes(blocks[:, :rank].reshape(4, -1, rank, new.shape[1]), 1, 2)
    updated = updated.reshape(2, 2 * rank, width)
    clipped = clipped[:, :rank].reshape(2, 2 * rank, width)
    return (
        gradient[0, rank, :2],
        norm[0, 0],
        clipped[0].T,
        clipped[1],
        left_new,
        right_new,
        updated[0].T,
        updated[1],
    )


def solution(mesh):
    direct = dict(mesh.shape) == {"dp": 8, "fsdp": 4}
    rows = P(BOTH, None)
    placed = (
        P(None, BOTH, None),
        P(None, BOTH),
        P(None, BOTH, None),
        rows,
        rows,
        rows,
        rows,
        rows,
        rows,
        P(BOTH),
        P(),
        P(),
        P("fsdp", None, None),
        P("fsdp", None, None),
    )
    return jax.shard_map(
        functools.partial(on_device, direct),
        mesh=mesh,
        in_specs=placed,
        out_specs=(P(), P(), P(), P(), P("fsdp", None, None), P("fsdp", None, None), P(), P()),
        check_vma=False,
    )
```

```python
import functools
import jax
import jax.numpy as jnp
from jax import lax
from jax.experimental import pallas as pl
from jax.experimental.pallas import tpu as pltpu
from jax.sharding import PartitionSpec as P

ATTENTION_HEADS = 16
STATS_BLOCK_ROWS = 256
NEWTON = 8
CAPACITY = 80

ln_eps = 1e-05
adapter_alpha = 32.0
beta_stats = 0.95
root_eps = 1e-12
clip_level = 0.01
learn_rate = 0.05
masked_score = -1e30

BOTH = ("dp", "fsdp")
MESH = pl.DeviceIdType.MESH
VMEM = pl.BlockSpec(memory_space=pltpu.VMEM)
ANY = pl.BlockSpec(memory_space=pl.ANY)
f32 = jnp.float32
bf16 = jnp.bfloat16


def place():
    d, f = lax.axis_index("dp"), lax.axis_index("fsdp")
    return d // 2, lax.rem(d, 2), f // 2, lax.rem(f, 2)


def target(z, x, y, c):
    return (z * 2 + x, y * 2 + c)


def nth(i):
    return (i // 4, lax.rem(i, 4))


def greet_all(count):
    me = lax.axis_index("dp") * 4 + lax.axis_index("fsdp")
    sem = pltpu.get_barrier_semaphore()
    for i in range(1, count):
        pl.semaphore_signal(
            sem, inc=1, device_id=nth(lax.rem(me + i, count)), device_id_type=MESH
        )
    pl.semaphore_wait(sem, count - 1)
    return me


def remote(src, dst, send, recv, device):
    return pltpu.make_async_remote_copy(
        src_ref=src, dst_ref=dst, send_sem=send, recv_sem=recv, device_id=device, device_id_type=MESH
    )


def params(collective=None, vmem=60):
    if collective is None:
        return pltpu.CompilerParams(vmem_limit_bytes=vmem * 2**20)
    return pltpu.CompilerParams(
        vmem_limit_bytes=vmem * 2**20, collective_id=collective, has_side_effects=True
    )


def iota(shape, dim):
    return lax.broadcasted_iota(jnp.int32, shape, dim)


def marks(condition):
    return jnp.where(condition, 1.0, 0.0).astype(bf16)


def dot(a, b, ca, cb):
    return lax.dot_general(a, b, (((ca,), (cb,)), ((), ())), preferred_element_type=f32)


GRID = 16


def cells(ids, local_rows):
    owner = jnp.floor((ids.astype(f32) + 0.5) * (1.0 / local_rows)).astype(jnp.int32)
    local = ids - owner * local_rows
    return owner, jnp.where(ids >= 0, owner * GRID + (local >> 7), -1), local & 127


def presence(ids, owners, local_rows):
    width = ids.shape[1]
    _, high, low = cells(ids, local_rows)
    count = dot(
        marks(iota((owners * GRID, width), 0) == high), marks(iota((128, width), 0) == low), 1, 1
    )
    return marks(count > 0.5).reshape(owners, GRID, 128)


def presence_kernel(local_rows, ids_ref, own_ref):
    own_ref[...] = presence(ids_ref[...], own_ref.shape[0], local_rows)


def ranked(present):
    rows = present.shape[0]
    through = dot(present, marks(iota((128, 128), 0) <= iota((128, 128), 1)), 1, 0)
    of = lambda dim: iota((rows, rows), dim)
    earlier = marks((of(1) < of(0)) & (of(0) // GRID == of(1) // GRID))
    row_total = jnp.broadcast_to(through[:, 127:128], (rows, 128)).astype(bf16)
    offset = dot(earlier, row_total, 1, 0)
    has = present.astype(f32)
    return jnp.where(has > 0.5, through - has + offset, -1.0), offset[:, :1] + through[:, 127:128]


def mark_rows(capacity, rank_ref, marks_ref, units, local_rows):
    @pl.loop(0, units)
    def _(unit):
        rows = pl.ds(pl.multiple_of(unit * capacity, 16), capacity)
        own = rank_ref[pl.ds(pl.multiple_of(unit * GRID, GRID), GRID), :]
        for row in range(-(-local_rows // 128)):
            columns = min(128, local_rows - row * 128)
            hit = iota((capacity, 128), 0).astype(f32) == own[row : row + 1, :]
            marks_ref[rows, row * 128 : row * 128 + columns] = marks(hit)[:, :columns]


def select_kernel(capacity, asked_ref, table_ref, round_ref, rows_ref, most_ref, marks_ref, rank_ref):
    units, members = asked_ref.shape[:2]
    local_rows, width = table_ref.shape
    begin = (round_ref[0] * capacity).astype(f32)
    most = jnp.zeros((1, 1), f32)
    for first in range(0, units, 16):
        together = asked_ref[first : first + 16, 0]
        for member in range(1, members):
            together = jnp.maximum(together, asked_ref[first : first + 16, member])
        rank, amount = ranked(together.reshape(-1, 128))
        most = jnp.maximum(most, jnp.max(amount, keepdims=True))
        rank_ref[first * GRID : first * GRID + rank.shape[0]] = rank - begin
    most_ref[...] = jnp.broadcast_to(most, most_ref.shape)
    mark_rows(capacity, rank_ref, marks_ref, units, local_rows)

    @pl.loop(0, units // 4)
    def _(four):
        rows_ref[pl.ds(four * 4, 4)] = look_up(capacity, four, marks_ref, table_ref)


def look_up(capacity, four, marks_ref, table_ref):
    part = pl.ds(pl.multiple_of(four * (4 * capacity), 4 * capacity), 4 * capacity)
    found = dot(marks_ref[part, :], table_ref[...], 1, 0)
    return found.astype(bf16).reshape(4, capacity, table_ref.shape[1])


def select(asked, table, which_round, capacity):
    units = asked.shape[0]
    return pl.pallas_call(
        functools.partial(select_kernel, capacity),
        out_shape=[
            jax.ShapeDtypeStruct((units, capacity, table.shape[1]), bf16),
            jax.ShapeDtypeStruct((8, 128), f32),
        ],
        in_specs=[VMEM, VMEM, pl.BlockSpec(memory_space=pltpu.SMEM)],
        out_specs=[VMEM] * 2,
        scratch_shapes=[
            pltpu.VMEM((units * capacity, table.shape[0]), bf16),
            pltpu.VMEM((units * GRID, 128), f32),
        ],
        compiler_params=params(),
        name="select",
    )(asked, table, which_round)


def slots_of(capacity, begin, local_rows, ids, own_ref, mate_ref):
    owner, high, low = cells(ids, local_rows)
    width = ids.shape[1]
    own_rank = jnp.zeros((1, width), f32)
    for first in range(0, own_ref.shape[0], 16):
        together = jnp.maximum(own_ref[first : first + 16], mate_ref[first : first + 16])
        rank, _ = ranked(together.reshape(-1, 128))
        rank = rank - begin
        rank = jnp.where((rank >= 0.0) & (rank < capacity), rank + 1.0, 0.0)
        rows = rank.shape[0]
        of_low = dot(rank.astype(bf16), marks(iota((rows, width), 0) + first * GRID == high), 0, 0)
        own_rank += jnp.sum(
            jnp.where(iota((128, width), 0) == low, of_low, 0.0), axis=0, keepdims=True
        )
    slot = owner * capacity + own_rank.astype(jnp.int32) - 1
    return jnp.where(own_rank > 0.5, slot, -1)


def slots_kernel(capacity, local_rows, ids_ref, own_ref, mate_ref, round_ref, slot_ref):
    begin = (round_ref[0] * capacity).astype(f32)
    slot_ref[...] = slots_of(capacity, begin, local_rows, ids_ref[...], own_ref, mate_ref)


def slots(ids, own, mate, which_round, capacity, local_rows):
    return pl.pallas_call(
        functools.partial(slots_kernel, capacity, local_rows),
        out_shape=jax.ShapeDtypeStruct(ids.shape, jnp.int32),
        in_specs=[VMEM] * 3 + [pl.BlockSpec(memory_space=pltpu.SMEM)],
        out_specs=VMEM,
        compiler_params=params(),
        name="slots",
    )(ids, own, mate, which_round)


class Piece:
    def __init__(self, src, out, rows, cols, flat, sems):
        self.src, self.out, self.rows, self.cols, self.flat = src, out, rows, cols, flat
        self.own_sem, self.chain_sems, self.plane_sems, self.core_sems = sems
        self.z, self.x, self.y, self.c = place()

    def at(self, zz, xx, yy, cc, half=None):
        begin, count = self.rows
        if half is not None:
            begin, count = begin + half * (count // 2), count // 2
        return self.out.at[zz, xx, yy, cc, pl.ds(begin, count), pl.ds(*self.cols)]

    def own(self):
        src = self.src.at[pl.ds(*self.rows), pl.ds(*self.cols)]
        return pltpu.make_async_copy(src, self.at(self.z, self.x, self.y, self.c), self.own_sem)

    def chain(self, zz, way, incoming=False):
        z, x, y, c = self.z, self.x, self.y, self.c
        every = slice(None)
        ref = self.at(zz, every, every, c) if self.flat else self.at(zz, x, y, c)
        k = (way + 1) // 2
        to = target(z - way if incoming else z + way, x, y, c)
        return remote(ref, ref, self.chain_sems.at[0, k, zz], self.chain_sems.at[1, k, zz], to)

    def plane(self, zz, step, incoming=False):
        z, x, y, c = self.z, self.x, self.y, self.c
        every = slice(None)
        over_x, over_y = target(z, 1 - x, y, c), target(z, x, 1 - y, c)
        xx, yy = (1 - x, 1 - y) if incoming else (x, y)
        if step == 0:
            pairs = ((self.at(zz, xx, y, c, 0), over_x), (self.at(zz, x, yy, c, 1), over_y))
        else:
            pairs = ((self.at(zz, every, yy, c, 0), over_y), (self.at(zz, xx, every, c, 1), over_x))
        return [
            remote(ref, ref, self.plane_sems.at[0, zz, step, k], self.plane_sems.at[1, zz, step, k], to)
            for k, (ref, to) in enumerate(pairs)
        ]

    def mate(self, zz, incoming=False):
        z, x, y, c = self.z, self.x, self.y, self.c
        ref = self.at(zz, slice(None), slice(None), 1 - c if incoming else c)
        return remote(ref, ref, self.core_sems.at[0, zz], self.core_sems.at[1, zz], target(z, x, y, 1 - c))

    def arrivals(self, step, act):
        for way in (1, -1):
            zz = self.z - way * (step + 1)

            @pl.when((zz >= 0) & (zz < 4))
            def _(zz=zz, way=way):
                act(zz, way)

    def pass_on(self, zz, way):
        @pl.when((self.z + way >= 0) & (self.z + way < 4))
        def _():
            self.chain(zz, way).start()

    def first(self, zz):
        for copy in self.plane(zz, 0):
            copy.start()

    def load(self):
        self.own().start()

    def start(self):
        self.own().wait()
        if not self.flat:
            for way in (1, -1):
                self.pass_on(self.z, way)
        self.first(self.z)

    def arrive(self, step):
        def act(zz, way):
            self.chain(zz, way, True).wait_recv()
            self.pass_on(zz, way)
            if self.flat:
                self.mate(zz).start()
            else:
                self.first(zz)

        self.arrivals(step, act)

    def second_of(self, zz, way=None):
        for copy in self.plane(zz, 0, True):
            copy.wait_recv()
        for copy in self.plane(zz, 1):
            copy.start()

    def third_of(self, zz, way=None):
        for copy in self.plane(zz, 1, True):
            copy.wait_recv()
        self.mate(zz).start()
        if self.flat:
            for way in (1, -1):
                self.pass_on(self.z, way)

    def second(self, step=None):
        if step is None:
            self.second_of(self.z)
        else:
            self.arrivals(step, self.second_of)

    def third(self, step=None):
        if step is None:
            self.third_of(self.z)
        else:
            self.arrivals(step, self.third_of)

    def finish(self, incoming=True):
        planes = (self.z,) if self.flat else range(4)
        for zz in planes:
            for step in range(2):
                for copy in self.plane(zz, step):
                    copy.wait_send()
        for zz in range(4):
            self.mate(zz).wait_send()
            if incoming:
                self.mate(zz, True).wait_recv()
        for way in (1, -1):

            @pl.when((self.z + way >= 0) & (self.z + way < 4))
            def _(way=way):
                for step in range(3):
                    zz = self.z - way * step

                    @pl.when((zz >= 0) & (zz < 4))
                    def _(zz=zz):
                        self.chain(zz, way).wait_send()


def shares(weights):
    return [jax.ShapeDtypeStruct((4, 2, 2, 2) + w.shape, w.dtype) for w in weights]


def piece_scratch(count):
    return [
        pltpu.SemaphoreType.DMA,
        pltpu.SemaphoreType.DMA((2, 2, 4)),
        pltpu.SemaphoreType.DMA((2, 4, 2, 2)),
        pltpu.SemaphoreType.DMA((2, 4)),
    ] * count


def each(pieces, name, *args):
    for piece in pieces:
        getattr(piece, name)(*args)


def chained_steps(pieces):
    do = lambda *calls: lambda: [each(pieces, *call) for call in calls]
    return [
        do(("second",), ("arrive", 0)),
        do(("third",), ("second", 0), ("arrive", 1)),
        do(("third", 0), ("second", 1), ("arrive", 2)),
        do(("third", 1), ("second", 2)),
        do(("third", 2)),
    ]


def mixed_steps(chained, flat):
    do = lambda *calls: lambda: [each(*call) for call in calls]
    return [
        do((flat, "second"), (chained, "second"), (chained, "arrive", 0)),
        do((flat, "third"), (chained, "third"), (chained, "second", 0), (chained, "arrive", 1)),
        do((flat, "arrive", 0), (chained, "third", 0), (chained, "second", 1), (chained, "arrive", 2)),
        do((flat, "arrive", 1), (chained, "third", 1), (chained, "second", 2)),
        do((flat, "arrive", 2), (chained, "third", 2)),
    ]


class Rows:
    def __init__(self, rows_ref, most_ref, rows_out, most_out, sems):
        self.own_refs, self.outs = (rows_ref, most_ref), (rows_out, most_out)
        self.sems, self.mate_sems, self.own_sems = sems
        self.z, self.x, self.y, self.c = place()
        self.chip = (self.z * 2 + self.x) * 2 + self.y

    def out(self, k, to):
        device = target(to // 4, lax.rem(to // 2, 2), lax.rem(to, 2), self.c)
        src = self.own_refs[k].at[to] if k == 0 else self.own_refs[k]
        return remote(
            src, self.outs[k].at[self.chip, self.c], self.sems.at[0, k, to], self.sems.at[1, k, self.chip], device
        )

    def into(self, k, frm):
        device = target(frm // 4, lax.rem(frm // 2, 2), lax.rem(frm, 2), self.c)
        dst = self.outs[k].at[frm, self.c]
        return remote(dst, dst, self.sems.at[0, k, frm], self.sems.at[1, k, frm], device)

    def mate(self, k, of, core):
        ref = self.outs[k].at[of, core]
        to = target(self.z, self.x, self.y, 1 - self.c)
        return remote(ref, ref, self.mate_sems.at[0, k, of], self.mate_sems.at[1, k, of], to)

    def own(self, k):
        src = self.own_refs[k].at[self.chip] if k == 0 else self.own_refs[k]
        return pltpu.make_async_copy(src, self.outs[k].at[self.chip, self.c], self.own_sems.at[k])

    def send(self, to):
        @pl.when(to == self.chip)
        def _():
            for k in range(2):
                self.own(k).start()

        @pl.when(to != self.chip)
        def _():
            for k in range(2):
                self.out(k, to).start()

    def forward(self):
        for k in range(2):
            self.own(k).wait()
            self.mate(k, self.chip, self.c).start()
        for i in range(1, 16):
            frm = lax.rem(self.chip + 16 - i, 16)
            for k in range(2):
                self.into(k, frm).wait_recv()
                self.mate(k, frm, self.c).start()

    def finish(self):
        for i in range(16):
            of = lax.rem(self.chip + i, 16)
            for k in range(2):
                self.mate(k, of, self.c).wait_send()
                self.mate(k, of, 1 - self.c).wait_recv()
                if i:
                    self.out(k, of).wait_send()

    @staticmethod
    def shapes(rows, most):
        return [
            jax.ShapeDtypeStruct((16, 2) + rows[1:], bf16),
            jax.ShapeDtypeStruct((16, 2) + most, f32),
        ]

    @staticmethod
    def scratch():
        return [
            pltpu.SemaphoreType.DMA((2, 2, 16)),
            pltpu.SemaphoreType.DMA((2, 2, 16)),
            pltpu.SemaphoreType.DMA((2,)),
        ]


def rows_kernel(rows_ref, most_ref, rows_out, most_out, *sems):
    greet_all(32)
    rows = Rows(rows_ref, most_ref, rows_out, most_out, sems)
    for to in range(16):
        rows.send(to)
    rows.forward()
    rows.finish()


def send_rows(rows, most, collective):
    return pl.pallas_call(
        rows_kernel,
        out_shape=Rows.shapes(rows.shape, most.shape),
        in_specs=[VMEM] * 2,
        out_specs=[ANY, VMEM],
        scratch_shapes=Rows.scratch(),
        compiler_params=params(collective),
        name="send_rows",
    )(rows, most)


def fetch_kernel(
    capacity, ids_ref, vec_ref, table_ref, w_ref,
    received_ref, most_ref, slot_ref, asked_ref, own_ref, mate_ref, vec_out, w_out,
    marks_ref, rank_ref, rows_ref, count_ref, mosts_ref, *sems,
):
    ask_sems, mate_sems = sems[:2]
    rows = Rows(rows_ref, count_ref, received_ref, mosts_ref, sems[2:5])
    piece = Piece(w_ref, w_out, (0, w_ref.shape[0]), (0, w_ref.shape[1]), False, sems[5:])
    piece.load()
    local_rows = table_ref.shape[0]
    own_ref[...] = presence(ids_ref[...], 32, local_rows)
    me = greet_all(32)
    z, x, y, c = place()
    to_mate = remote(own_ref, mate_ref, mate_sems.at[0], mate_sems.at[1], target(z, x, y, 1 - c))
    to_mate.start()
    copies = []
    for i in range(1, 32):
        to = lax.rem(me + i, 32)
        for k, (src, dst) in enumerate(((own_ref.at[to], asked_ref), (vec_ref, vec_out))):
            copy = remote(src, dst.at[me], ask_sems.at[0, k, i], ask_sems.at[1, k, i], nth(to))
            copy.start()
            copies.append(copy)
    piece.start()
    asked_ref[me] = own_ref[me]
    vec_out[me] = vec_ref[...]
    for copy in copies:
        copy.wait()
    together = jnp.concatenate(
        [jnp.maximum(asked_ref[2 * unit], asked_ref[2 * unit + 1]) for unit in range(16)]
    )
    rank, amount = ranked(together)
    count_ref[...] = jnp.broadcast_to(jnp.max(amount, keepdims=True), count_ref.shape)
    rank_ref[...] = rank
    mark_rows(capacity, rank_ref, marks_ref, 16, local_rows)
    piece.second()
    piece.arrive(0)

    planes = [lax.rem(z + i, 4) for i in (2, 3, 1, 0)]
    for plane in planes:
        rows_ref[pl.ds(plane * 4, 4)] = look_up(capacity, plane, marks_ref, table_ref)
    piece.second(0)
    piece.arrive(1)
    for plane in planes:
        for k in range(4):
            rows.send(plane * 4 + k)
    piece.third()
    piece.second(1)
    piece.third(0)
    to_mate.wait()
    slot_ref[...] = slots_of(capacity, 0.0, local_rows, ids_ref[...], own_ref, mate_ref)
    piece.arrive(2)
    piece.third(1)
    piece.second(2)
    piece.third(2)
    rows.forward()
    rows.finish()
    piece.finish()
    most = mosts_ref[0, 0]
    for k in range(1, 32):
        most = jnp.maximum(most, mosts_ref[k // 2, k % 2])
    most_ref[...] = most


def fetch(ids, vec, table, weights, capacity, collective):
    grids = jax.ShapeDtypeStruct((32, GRID, 128), bf16)
    width = table.shape[1]
    small = jax.ShapeDtypeStruct((8, 128), f32)
    return pl.pallas_call(
        functools.partial(fetch_kernel, capacity),
        out_shape=[
            jax.ShapeDtypeStruct((16, 2, capacity, width), bf16), small,
            jax.ShapeDtypeStruct(ids.shape, jnp.int32), grids, grids, grids,
            jax.ShapeDtypeStruct((32,) + vec.shape, vec.dtype),
        ]
        + shares([weights]),
        in_specs=[VMEM] * 3 + [ANY],
        out_specs=[ANY] + [VMEM] * 6 + [ANY],
        scratch_shapes=[
            pltpu.VMEM((16 * capacity, table.shape[0]), bf16),
            pltpu.VMEM((16 * GRID, 128), f32),
            pltpu.VMEM((16, capacity, width), bf16),
            pltpu.VMEM((8, 128), f32),
            pltpu.VMEM((16, 2, 8, 128), f32),
            pltpu.SemaphoreType.DMA((2, 2, 32)),
            pltpu.SemaphoreType.DMA((2,)),
        ]
        + Rows.scratch()
        + piece_scratch(1),
        compiler_params=params(collective),
        name="fetch",
    )(ids, vec, table, weights)


def vocabulary_kernel(group, rows_ref, table_ref, mean_ref, total_ref):
    logits = dot(rows_ref[...], table_ref[...], 1, 1)
    top = jnp.max(logits, axis=1, keepdims=True)
    weights = jnp.exp(logits - top)
    amount = jnp.sum(weights, axis=1, keepdims=True)
    mean = dot(weights.astype(bf16), table_ref[...], 1, 0)
    mean_ref[...] = (mean / amount).astype(bf16)
    total = top + jnp.log(amount)
    for k in range(total_ref.shape[0]):
        total_ref[k] = as_tile(as_row(total[k * group : (k + 1) * group]))


def as_tile(row):
    return jnp.broadcast_to(jnp.pad(row, ((0, 0), (0, 128 - row.shape[1]))), (8, 128))


def same(size):
    return iota((size, size), 0) == iota((size, size), 1)


def as_row(column):
    return jnp.sum(jnp.where(same(column.shape[0]), column, 0.0), axis=0, keepdims=True)


def as_column(row):
    return jnp.sum(jnp.where(same(row.shape[1]), row, 0.0), axis=1, keepdims=True)


def vocabulary(rows, table, group, tile):
    count, width = rows.shape
    return pl.pallas_call(
        functools.partial(vocabulary_kernel, group),
        grid=(count // tile,),
        out_shape=[
            jax.ShapeDtypeStruct((count, width), bf16),
            jax.ShapeDtypeStruct((count // group, 8, 128), f32),
        ],
        in_specs=[
            pl.BlockSpec((tile, width), lambda i: (i, 0)),
            pl.BlockSpec(table.shape, lambda i: (0, 0)),
        ],
        out_specs=[
            pl.BlockSpec((tile, width), lambda i: (i, 0)),
            pl.BlockSpec((tile // group, 8, 128), lambda i: (i, 0, 0)),
        ],
        compiler_params=params(),
        name="vocabulary",
    )(rows, table)


def merged(parts):
    size = parts[0][0].shape[0]
    rows = [total[:1, :size] for _, total in parts]
    top = functools.reduce(jnp.maximum, rows)
    total = top + jnp.log(sum(jnp.exp(row - top) for row in rows))
    mean = sum(
        values.astype(f32) * as_column(jnp.exp(row - total)) for (values, _), row in zip(parts, rows)
    )
    return mean, as_tile(total)


def head_kernel(
    hidden_ref, table_ref, q_out, t_out,
    every_ref, q_ref, t_ref, core_q, core_t, keep_q, keep_t, send_q, send_t, got_q, got_t,
    next_q, next_t, pass_q, pass_t, last_q, last_t, end_q, end_t, final_q, final_t,
    core_sems, one_sems, two_sems, z_sems, *sems,
):
    rows, width = hidden_ref.shape
    piece = Piece(hidden_ref, every_ref, (0, rows), (0, width), False, sems)
    piece.load()
    greet_all(32)
    z, x, y, c = place()
    mate = target(z, x, y, 1 - c)
    over = (target(z, 1 - x, y, c), target(z, x, 1 - y, c))
    half = width // 2
    cols = (slice(0, half), slice(half, width))
    mine = (x, y)
    is_end = (z == 0) | (z == 3)
    up = jnp.where((z == 0) | (z == 2), 1, -1)

    def nth_plane(i):
        from_end = z + up * i
        inside = jnp.where(i == 0, z, jnp.where(i == 1, z + up, jnp.where(i == 2, z - up, z - 2 * up)))
        return jnp.where(is_end, from_end, inside)

    def core_copies(zz):
        return [
            remote(q_ref.at[zz, :, :, 1 - c], core_q.at[zz], core_sems.at[0, 0, zz], core_sems.at[1, 0, zz], mate),
            remote(t_ref.at[zz, :, :, 1 - c], core_t.at[zz], core_sems.at[0, 1, zz], core_sems.at[1, 1, zz], mate),
        ]

    def one_copies(zz, k):
        return [
            remote(send_q.at[k, zz], got_q.at[k, zz], one_sems.at[0, 0, k, zz], one_sems.at[1, 0, k, zz], over[k]),
            remote(send_t.at[k, zz], got_t.at[k, zz], one_sems.at[0, 1, k, zz], one_sems.at[1, 1, k, zz], over[k]),
        ]

    def two_copies(zz, k):
        return [
            remote(pass_q.at[k, zz], last_q.at[k, zz], two_sems.at[0, 0, k, zz], two_sems.at[1, 0, k, zz], over[1 - k]),
            remote(pass_t.at[k, zz], last_t.at[k, zz], two_sems.at[0, 1, k, zz], two_sems.at[1, 1, k, zz], over[1 - k]),
        ]

    def z_copies(zz, frm, k):
        return [
            remote(end_q.at[k, zz], final_q.at[k, frm], z_sems.at[0, 0, k, zz], z_sems.at[1, 0, k, frm], target(zz, x, y, c)),
            remote(end_t.at[k, zz], final_t.at[k, frm], z_sems.at[0, 1, k, zz], z_sems.at[1, 1, k, frm], target(zz, x, y, c)),
        ]

    def start(copies):
        for copy in copies:
            copy.start()

    def landed(copies):
        for copy in copies:
            copy.wait_recv()

    def left(copies):
        for copy in copies:
            copy.wait_send()

    def arrive(i):
        zz = nth_plane(i)
        way = jnp.where(zz < z, 1, -1)
        piece.chain(zz, way, True).wait_recv()
        piece.pass_on(zz, way)
        piece.first(zz)

    def second(i):
        piece.second_of(nth_plane(i))

    def third(i):
        piece.third_of(nth_plane(i))

    def compute(i):
        zz = nth_plane(i)
        piece.mate(zz, True).wait_recv()

        @pl.loop(0, 2)
        def _(xx):
            logits = dot(every_ref[zz, xx].reshape(4 * rows, width), table_ref[...], 1, 1)
            top = jnp.max(logits, axis=1, keepdims=True)
            weights = jnp.exp(logits - top)
            amount = jnp.sum(weights, axis=1, keepdims=True)
            mean = dot(weights.astype(bf16), table_ref[...], 1, 0) / amount
            q_ref[zz, xx] = mean.astype(bf16).reshape(2, 2, rows, width)
            total = top + jnp.log(amount)
            for k in range(4):
                t_ref[zz, xx, k // 2, k % 2] = as_tile(as_row(total[k * rows : (k + 1) * rows]))

        start(core_copies(zz))

    def merge_cores(i):
        zz = nth_plane(i)
        landed(core_copies(zz))

        @pl.loop(0, 2)
        def _(xx):
            for yy in range(2):
                mean, total = merged(
                    [(q_ref[zz, xx, yy, c], t_ref[zz, xx, yy, c]), (core_q[zz, xx, yy], core_t[zz, xx, yy])]
                )
                for k, (own, other) in enumerate(((xx, yy), (yy, xx))):
                    part = mean[:, cols[k]]

                    @pl.when(own == mine[k])
                    def _(k=k, other=other, part=part, total=total):
                        keep_q[k, zz, other] = part
                        keep_t[k, zz, other] = total

                    @pl.when(own != mine[k])
                    def _(k=k, other=other, part=part, total=total):
                        send_q[k, zz, other] = part.astype(bf16)
                        send_t[k, zz, other] = total

        for k in range(2):
            start(one_copies(zz, k))

    def merge_first(i):
        zz = nth_plane(i)
        for k in range(2):
            landed(one_copies(zz, k))
            for other in range(2):
                mean, total = merged(
                    [(keep_q[k, zz, other], keep_t[k, zz, other]), (got_q[k, zz, other], got_t[k, zz, other])]
                )

                @pl.when(other == mine[1 - k])
                def _(k=k, mean=mean, total=total):
                    next_q[k, zz] = mean
                    next_t[k, zz] = total

                @pl.when(other != mine[1 - k])
                def _(k=k, mean=mean, total=total):
                    pass_q[k, zz] = mean.astype(bf16)
                    pass_t[k, zz] = total

            start(two_copies(zz, k))

    def merge_second(i):
        zz = nth_plane(i)
        for k in range(2):
            landed(two_copies(zz, k))
            mean, total = merged([(next_q[k, zz], next_t[k, zz]), (last_q[k, zz], last_t[k, zz])])

            @pl.when(i > 0)
            def _(k=k, mean=mean, total=total):
                end_q[k, zz] = mean.astype(bf16)
                end_t[k, zz] = total
                start(z_copies(zz, z, k))

            @pl.when(i == 0)
            def _(k=k, mean=mean, total=total):
                next_q[k, z] = mean
                next_t[k, z] = total

    piece.start()
    second(0)
    arrive(1)
    third(0)
    arrive(2)
    second(1)

    @pl.loop(0, 7)
    def _(i):
        for act, lag, begin in (
            (compute, 0, 0), (third, -1, 1), (second, -2, 2), (arrive, -3, 3),
            (merge_cores, 1, 0), (merge_first, 2, 0), (merge_second, 3, 0),
        ):
            @pl.when((i - lag >= begin) & (i - lag < 4))
            def _(act=act, lag=lag):
                act(i - lag)

    for k in range(2):
        parts = [(next_q[k, z], next_t[k, z])]
        for i in range(1, 4):
            frm = nth_plane(i)
            landed(z_copies(frm, frm, k))
            parts.append((final_q[k, frm], final_t[k, frm]))
        mean, total = merged(parts)
        q_out[:, cols[k]] = mean
        if k == 0:
            t_out[...] = total

    @pl.loop(0, 4)
    def _(i):
        zz = nth_plane(i)
        left(core_copies(zz))
        for k in range(2):
            left(one_copies(zz, k))
            left(two_copies(zz, k))

    @pl.loop(1, 4)
    def _(i):
        for k in range(2):
            left(z_copies(nth_plane(i), z, k))

    piece.finish(False)


def head(hidden, table, collective):
    rows, width = hidden.shape
    half = width // 2
    tile = (8, 128)
    vmem = pltpu.VMEM
    return pl.pallas_call(
        head_kernel,
        out_shape=[jax.ShapeDtypeStruct((rows, width), f32), jax.ShapeDtypeStruct(tile, f32)],
        in_specs=[VMEM] * 2,
        out_specs=[VMEM] * 2,
        scratch_shapes=[
            vmem((4, 2, 2, 2, rows, width), bf16),
            vmem((4, 2, 2, 2, rows, width), bf16), vmem((4, 2, 2, 2) + tile, f32),
            vmem((4, 2, 2, rows, width), bf16), vmem((4, 2, 2) + tile, f32),
            vmem((2, 4, 2, rows, half), f32), vmem((2, 4, 2) + tile, f32),
            vmem((2, 4, 2, rows, half), bf16), vmem((2, 4, 2) + tile, f32),
            vmem((2, 4, 2, rows, half), bf16), vmem((2, 4, 2) + tile, f32),
            vmem((2, 4, rows, half), f32), vmem((2, 4) + tile, f32),
            vmem((2, 4, rows, half), bf16), vmem((2, 4) + tile, f32),
            vmem((2, 4, rows, half), bf16), vmem((2, 4) + tile, f32),
            vmem((2, 4, rows, half), bf16), vmem((2, 4) + tile, f32),
            vmem((2, 4, rows, half), bf16), vmem((2, 4) + tile, f32),
            pltpu.SemaphoreType.DMA((2, 2, 4)),
            pltpu.SemaphoreType.DMA((2, 2, 2, 4)),
            pltpu.SemaphoreType.DMA((2, 2, 2, 4)),
            pltpu.SemaphoreType.DMA((2, 2, 2, 4)),
        ]
        + piece_scratch(1),
        compiler_params=params(collective),
        name="head",
    )(hidden, table)


def exact(a, b, ca, cb):
    return lax.dot_general(
        a, b, (((ca,), (cb,)), ((), ())), precision=lax.Precision.HIGHEST, preferred_element_type=f32
    )


def fine(a, b, cb):
    a_high, b_high = a.astype(bf16), b.astype(bf16)
    a_low, b_low = (a - a_high.astype(f32)).astype(bf16), (b - b_high.astype(f32)).astype(bf16)
    return dot(a_high, b_high, 1, cb) + (dot(a_high, b_low, 1, cb) + dot(a_low, b_high, 1, cb))


def small_product(a, b):
    return sum(a[:, k : k + 1] * b[k : k + 1, :] for k in range(a.shape[0]))


def newton(matrix, product, apply, state):
    size = matrix.shape[0]
    identity = jnp.where(same(size), 1.0, 0.0)
    trace = jnp.sum(matrix * identity, keepdims=True)

    def step(_, carry):
        current, state = carry
        factor = (5.0 * identity - current) * 0.25
        square = product(factor, factor)
        return product(product(square, square), current), apply(state, factor)

    current, state = lax.fori_loop(0, NEWTON - 1, step, (matrix / trace, state))
    state = apply(state, (5.0 * identity - current) * 0.25)
    return state * lax.rsqrt(jnp.sqrt(trace))


def renew(g_ref, w_ref, left_ref, right_ref, small_ref, a_ref, b_ref, left_out, right_out, clip_ref, new_ref):
    owned, block = left_ref.shape[0], left_ref.shape[1]
    rank = right_ref.shape[1]
    group = lax.axis_index("fsdp")
    own = lax.rem(lax.axis_index("dp"), owned)
    data = jnp.where(iota(g_ref.shape, 1) < rank, g_ref[...], 0.0)
    norm = jnp.sqrt(jnp.sum(data * data, keepdims=True).reshape(1, 1))
    lane = iota((8, 128), 1)
    small_ref[...] = jnp.where(lane == 2, norm, g_ref[0, rank : rank + 1, :128])
    factor = clip_level / jnp.maximum(norm, clip_level)
    clip_ref[...] = data * factor
    a_ref[...] = jnp.concatenate([clip_ref[0, :rank], clip_ref[1, :rank]])
    b_ref[...] = jnp.concatenate([clip_ref[2, :rank], clip_ref[3, :rank]])
    for k in range(owned):
        grad = clip_ref[group, :, k * block : (k + 1) * block]
        left_out[k] = beta_stats * left_ref[k] + (1.0 - beta_stats) * exact(grad, grad, 0, 0)
        right_out[k] = (
            beta_stats * right_ref[k] + (1.0 - beta_stats) * exact(grad, grad, 1, 1)[:rank, :rank]
        )
    columns = pl.ds(pl.multiple_of(own * block, block), block)
    grad = clip_ref[group, :, columns]
    left = left_out[own] + root_eps * jnp.where(same(block), 1.0, 0.0)
    right = right_out[own] + root_eps * jnp.where(same(rank), 1.0, 0.0)
    root = newton(right, small_product, small_product, jnp.where(same(rank), 1.0, 0.0))
    rows = newton(left, lambda a, b: fine(a, b, 0), lambda a, b: fine(a, b, 1), grad)[:rank]
    update = sum(as_column(root[k : k + 1, :]) * rows[k : k + 1, :] for k in range(rank))
    new = w_ref[group, :rank, columns] - learn_rate * update
    new_ref[...] = jnp.pad(new, ((0, 8 - rank), (0, 0)))


def renew_kernel(*refs):
    renew(*refs)


def renew_shapes(left, right, width):
    small = [(8, 128), (8, width), (8, width), left.shape, right.shape]
    return [jax.ShapeDtypeStruct(shape, f32) for shape in small]


def renewed(gradient, weights, left, right):
    width = gradient.shape[2]
    return pl.pallas_call(
        renew_kernel,
        out_shape=renew_shapes(left, right, width)
        + [jax.ShapeDtypeStruct(gradient.shape, f32), jax.ShapeDtypeStruct((8, left.shape[1]), f32)],
        in_specs=[VMEM] * 4,
        out_specs=[VMEM] * 7,
        compiler_params=params(),
        name="renewed",
    )(gradient, weights, left, right)


def finish_kernel(
    g_ref, w_ref, left_ref, right_ref,
    small_ref, a_ref, b_ref, left_out, right_out, a_new, b_new,
    parts, summed, total_ref, clip_ref, new_ref, all_ref, one_sems, two_sems, block_sems,
):
    me = greet_all(32)

    def tile(ref, k):
        return ref.at[k // 8, :, pl.ds(pl.multiple_of(lax.rem(k, 8) * 128, 128), 128)]

    def out(i):
        to = lax.rem(me + i, 32)
        return remote(tile(g_ref, to), parts.at[me], one_sems.at[0, to], one_sems.at[1, me], nth(to))

    def into(i):
        frm = lax.rem(me + i, 32)
        return remote(tile(g_ref, me), parts.at[frm], one_sems.at[0, frm], one_sems.at[1, frm], nth(frm))

    def back(i):
        to = lax.rem(me + i, 32)
        return remote(summed, tile(total_ref, me), two_sems.at[0, to], two_sems.at[1, me], nth(to))

    def into_back(i):
        frm = lax.rem(me + i, 32)
        return remote(summed, tile(total_ref, frm), two_sems.at[0, frm], two_sems.at[1, frm], nth(frm))

    for i in range(1, 32):
        out(i).start()
    columns = pl.ds(pl.multiple_of(lax.rem(me, 8) * 128, 128), 128)
    for i in range(1, 32):
        into(i).wait_recv()
    running = g_ref[me // 8, :, columns]
    for i in range(1, 32):
        running = running + parts[lax.rem(me + i, 32)]
    summed[...] = running
    total_ref[me // 8, :, columns] = running
    for i in range(1, 32):
        back(i).start()
    for i in range(1, 32):
        into_back(i).wait_recv()
    renew(
        total_ref, w_ref, left_ref, right_ref, small_ref, a_ref, b_ref, left_out, right_out, clip_ref, new_ref
    )
    d, f = lax.axis_index("dp"), lax.axis_index("fsdp")
    half, mine = d // 4, f * 4 + lax.rem(d, 4)

    def share(i, incoming=False):
        k = lax.rem(mine + i, 16)
        device = (half * 4 + lax.rem(k, 4), k // 4)
        return remote(
            new_ref, all_ref.at[k if incoming else mine],
            block_sems.at[0, k], block_sems.at[1, k if incoming else mine], device,
        )

    for i in range(1, 16):
        share(i).start()
    all_ref[mine] = new_ref[...]
    for i in range(1, 16):
        share(i, True).wait_recv()
    rank, block = right_ref.shape[1], left_ref.shape[1]
    for k in range(16):
        ref, row = (a_new, b_new)[k // 8], k // 4 % 2 * rank
        ref[row : row + rank, k % 4 * block : (k % 4 + 1) * block] = all_ref[k, :rank]
    for i in range(1, 16):
        share(i).wait_send()
    for i in range(1, 32):
        out(i).wait_send()
        back(i).wait_send()


def finished(gradient, weights, left, right, collective):
    width = gradient.shape[2]
    new = (8, left.shape[1])
    return pl.pallas_call(
        finish_kernel,
        out_shape=renew_shapes(left, right, width) + [jax.ShapeDtypeStruct((8, width), f32)] * 2,
        in_specs=[VMEM] * 4,
        out_specs=[VMEM] * 7,
        scratch_shapes=[
            pltpu.VMEM((32, 8, 128), f32),
            pltpu.VMEM((8, 128), f32),
            pltpu.VMEM(gradient.shape, f32),
            pltpu.VMEM(gradient.shape, f32),
            pltpu.VMEM(new, f32),
            pltpu.VMEM((16,) + new, f32),
            pltpu.SemaphoreType.DMA((2, 32)),
            pltpu.SemaphoreType.DMA((2, 32)),
            pltpu.SemaphoreType.DMA((2, 16)),
        ],
        compiler_params=params(collective),
        name="finished",
    )(gradient, weights, left, right)


def normal(v, gain, shift):
    centred = v - jnp.mean(v, axis=-1, keepdims=True)
    inverse = lax.rsqrt(jnp.mean(centred * centred, axis=-1, keepdims=True) + ln_eps)
    normed = centred * inverse
    return normed * gain + shift, normed, inverse


def normal_back(grad, gain, normed, inverse):
    scaled = grad * gain
    return inverse * (
        scaled
        - jnp.mean(scaled, axis=-1, keepdims=True)
        - normed * jnp.mean(scaled * normed, axis=-1, keepdims=True)
    )


GAIN, SHIFT, QKV_BIAS, OUT_BIAS, UP_BIAS = (0, 2, 4), (1, 3, 5), 6, 9, 10


def expand_chunk(slot_ref, rows_ref, begin, chunk):
    count = rows_ref.shape[0]
    part = lambda k: slot_ref[0, :, pl.ds(pl.multiple_of(begin + k, 128), 128)].astype(f32)
    column = jnp.concatenate([as_column(part(k)) for k in range(0, chunk, 128)]).astype(jnp.int32)
    return dot(marks(iota((chunk, count), 1) == column), rows_ref[...], 1, 0)


def spread_heads(v, heads, size):
    rows, width = v.shape
    tiled = jnp.concatenate([v] * heads, axis=0)
    shape = (heads * rows, width)
    return jnp.where(iota(shape, 0) // rows == iota(shape, 1) // size, tiled, jnp.zeros((), v.dtype))


def join_heads(v, heads, size):
    rows = v.shape[0] // heads
    own = jnp.where(iota(v.shape, 0) // rows == iota(v.shape, 1) // size, v, 0.0)
    return sum(own[k * rows : (k + 1) * rows] for k in range(heads))


def attend_kernel(
    heads, adapter_scale, count_w, with_more, lens_ref, slot_ref, rows_ref, pos_ref, qkv_ref, vec_ref, pick_ref,
    down_ref, up_ref, *refs,
):
    if with_more:
        more_ref, *refs = refs
    w_in, refs = refs[:count_w], refs[count_w:]
    (h1_ref, low_ref, k_ref, v_ref, p_ref, h1p_ref, lowp_ref, xp_ref, wanted_ref, att_ref), refs = refs[:10], refs[10:]
    w_out, (emb_ref, q_ref), sems = refs[:count_w], refs[count_w : count_w + 2], refs[count_w + 2 :]
    micro = pl.program_id(0)
    count, width = emb_ref.shape
    length = lens_ref[micro]
    size = width // heads
    chunk = 256
    vec = lambda k: vec_ref[k : k + 1, :]
    if count_w:
        (up_in, down_in), (up_out, down_out) = w_in, w_out
        rows, cols = down_in.shape[0], up_in.shape[1]
        layout = (
            (up_in, up_out, (0, up_in.shape[0]), (0, cols * 3 // 4), False),
            (down_in, down_out, (0, rows * 3 // 4), (0, width), False),
            (up_in, up_out, (0, up_in.shape[0]), (cols * 3 // 4, cols // 4), True),
            (down_in, down_out, (rows * 3 // 4, rows // 4), (0, width), True),
        )
        pieces = [Piece(*place, sems[4 * k : 4 * k + 4]) for k, place in enumerate(layout)]
        steps = mixed_steps(pieces[:2], pieces[2:])

        def at(when, *acts):
            @pl.when(micro == when)
            def _():
                for act in acts:
                    act()
    else:
        steps = [None] * 5
        at = lambda when, *acts: None
    if count_w:
        at(0, lambda: each(pieces, "load"), lambda: greet_all(32), lambda: each(pieces, "start"))

    @pl.loop(0, count // chunk)
    def _(k):
        rows = pl.ds(pl.multiple_of(k * chunk, chunk), chunk)
        emb = expand_chunk(slot_ref, rows_ref, k * chunk, chunk).astype(bf16)
        if with_more:
            emb = emb + more_ref[0, rows]
        emb_ref[rows] = emb
        x = emb.astype(f32) + pos_ref[rows].astype(f32)
        h1_ref[0, rows] = normal(x, vec(GAIN[0]), vec(SHIFT[0]))[0].astype(bf16)

    at(0, steps[0])
    at(1, steps[3])

    @pl.loop(0, count // chunk)
    def _(k):
        rows = pl.ds(pl.multiple_of(k * chunk, chunk), chunk)
        h1 = h1_ref[0, rows]
        low = dot(h1, down_ref[...], 1, 0).astype(bf16)
        low_ref[0, rows] = low
        keys = dot(h1, qkv_ref[:, width : 2 * width], 1, 0) + vec(QKV_BIAS + 1)
        k_ref[0, rows] = keys.astype(bf16)
        values = dot(h1, qkv_ref[:, 2 * width :], 1, 0) + vec(QKV_BIAS + 2)
        values += adapter_scale * dot(low[:, 8:16], up_ref[8:16, :], 1, 0)
        v_ref[0, rows] = values.astype(bf16)

    at(0, steps[1])
    at(1, steps[4])
    pick = pick_ref[0]
    picks = pick.shape[0]
    here = marks(iota((picks, count), 1) == pick)
    after = marks(iota((picks, count), 1) == pick + 1)
    xp_ref[0] = dot(here, emb_ref[...], 1, 0) + dot(here, pos_ref[...], 1, 0)
    wanted_ref[0] = dot(after, emb_ref[...], 1, 0).astype(bf16)
    h1p = dot(here, h1_ref[0], 1, 0).astype(bf16)
    lowp = dot(here, low_ref[0], 1, 0).astype(bf16)
    h1p_ref[0] = h1p
    lowp_ref[0] = lowp
    queries = dot(h1p, qkv_ref[:, :width], 1, 0) + vec(QKV_BIAS)
    queries += adapter_scale * dot(lowp[:, 0:8], up_ref[0:8, :], 1, 0)
    q_ref[...] = queries.astype(bf16)
    some = 256 // size
    slot = iota((picks, count), 1)
    allowed = (slot <= pick) & (slot < length)
    allowed = jnp.concatenate([jnp.where(allowed, 1.0, 0.0)] * some, axis=0) > 0.5

    @pl.loop(0, width // 256)
    def _(k):
        lanes = pl.ds(pl.multiple_of(k * 256, 256), 256)
        scores = dot(spread_heads(q_ref[:, lanes], some, size), k_ref[0, :, lanes], 1, 1)
        scores = jnp.where(allowed, scores * size**-0.5, masked_score)
        weights = jnp.exp(scores - jnp.max(scores, axis=1, keepdims=True))
        probs = weights / jnp.sum(weights, axis=1, keepdims=True)
        p_ref[0, pl.ds(pl.multiple_of(k * some * picks, some * picks), some * picks)] = probs
        attended = dot(probs.astype(bf16), v_ref[0, :, lanes], 1, 0)
        att_ref[0, :, lanes] = join_heads(attended, some, size).astype(bf16)

    at(0, steps[2])
    if count_w:
        at(1, lambda: each(pieces, "finish"))


def whole(shape):
    return pl.BlockSpec(shape, lambda *_: (0,) * len(shape))


def of_micro(shape):
    return pl.BlockSpec((1,) + shape, lambda m: (m,) + (0,) * len(shape))


def attend(heads, adapter_scale, lens, slot, rows, more, wide, vec, pick, down, up, weights, collective):
    micros, _, count = slot.shape
    width = rows.shape[1]
    picks = pick.shape[1]
    more = [] if more is None else [more]
    outs = [
        ((count, width), bf16), ((count, 128), bf16), ((count, width), bf16), ((count, width), bf16),
        ((heads * picks, count), f32), ((picks, width), bf16), ((picks, 128), bf16),
        ((picks, width), f32), ((picks, width), bf16), ((picks, width), bf16),
    ]
    return pl.pallas_call(
        functools.partial(attend_kernel, heads, adapter_scale, len(weights), len(more) > 0),
        grid=(micros,),
        out_shape=[jax.ShapeDtypeStruct((micros,) + shape, kind) for shape, kind in outs] + shares(weights),
        in_specs=[
            pl.BlockSpec(memory_space=pltpu.SMEM), of_micro((1, count)), whole(rows.shape),
            pl.BlockSpec((count, width), lambda m: (0, 3)),
            pl.BlockSpec((width, 3 * width), lambda m: (0, 0)),
            whole(vec.shape), of_micro((picks, 1)), whole(down.shape), whole(up.shape),
        ]
        + [of_micro((count, width))] * len(more)
        + [ANY] * len(weights),
        out_specs=[of_micro(shape) for shape, _ in outs] + [ANY] * len(weights),
        scratch_shapes=[pltpu.VMEM((count, width), bf16), pltpu.VMEM((picks, width), bf16)]
        + piece_scratch(2 * len(weights)),
        compiler_params=params(collective),
        name="attend",
    )(lens, slot, rows, wide, wide, vec, pick, down, up, *more, *weights)


def attend_back_kernel(
    heads, adapter_scale, rank, datt_ref, h1_ref, low_ref, k_ref, v_ref, p_ref, h1p_ref, lowp_ref, up_ref, loss_ref,
    g_ref, dv_ref, dq_ref,
):
    count, width = h1_ref.shape[1:]
    size = width // heads
    picks = datt_ref.shape[1]
    some = 256 // size

    @pl.loop(0, width // 256)
    def _(k):
        lanes = pl.ds(pl.multiple_of(k * 256, 256), 256)
        own = pl.ds(pl.multiple_of(k * some * picks, some * picks), some * picks)
        d_heads = spread_heads(datt_ref[0, :, lanes], some, size)
        probs = p_ref[0, own]
        d_probs = dot(d_heads, v_ref[0, :, lanes], 1, 1)
        dv_ref[:, lanes] = dot(probs.astype(bf16), d_heads, 0, 0).astype(bf16)
        weighted = probs * d_probs
        d_scores = weighted - probs * jnp.sum(weighted, axis=1, keepdims=True)
        d_queries = dot(d_scores.astype(bf16), k_ref[0, :, lanes], 1, 0)
        dq_ref[:, lanes] = (join_heads(d_queries, some, size) * size**-0.5).astype(bf16)

    d_low_q = (adapter_scale * dot(dq_ref[...], up_ref[0:8, :], 1, 1)).astype(bf16)
    d_low_v = (adapter_scale * dot(dv_ref[...], up_ref[8:16, :], 1, 1)).astype(bf16)
    parts = (
        dot(d_low_q, h1p_ref[0], 0, 0),
        dot(d_low_v, h1_ref[0], 0, 0),
        adapter_scale * dot(lowp_ref[0, :, 0:8], dq_ref[...], 0, 0),
        adapter_scale * dot(low_ref[0, :, 8:16], dv_ref[...], 0, 0),
    )

    @pl.when(pl.program_id(0) == 0)
    def _():
        g_ref[...] = jnp.zeros_like(g_ref)
        g_ref[0, rank : rank + 1, :128] = loss_ref[:1, :]

    for k, part in enumerate(parts):
        g_ref[k] += part


def attend_back(heads, adapter_scale, rank, datt, h1, low, keys, values, probs, h1p, lowp, up, loss):
    micros, count, width = h1.shape
    picks = datt.shape[1]
    ins = (datt, h1, low, keys, values, probs, h1p, lowp)
    return pl.pallas_call(
        functools.partial(attend_back_kernel, heads, adapter_scale, rank),
        grid=(micros,),
        out_shape=jax.ShapeDtypeStruct((4, 8, width), f32),
        in_specs=[of_micro(v.shape[1:]) for v in ins] + [whole(up.shape), whole(loss.shape)],
        out_specs=whole((4, 8, width)),
        scratch_shapes=[pltpu.VMEM((count, width), bf16), pltpu.VMEM((picks, width), bf16)],
        compiler_params=params(),
        name="attend_back",
    )(*ins, up, loss)


def gelu(v):
    inner = 0.7978845608028654 * (v + 0.044715 * v * v * v)
    return 0.5 * v * (1.0 + jnp.tanh(inner))


def gelu_slope(v):
    bend = jnp.tanh(0.7978845608028654 * (v + 0.044715 * v * v * v))
    return 0.5 * (1.0 + bend) + 0.5 * v * (1.0 - bend * bend) * 0.7978845608028654 * (
        1.0 + 3.0 * 0.044715 * v * v
    )


def forward_kernel(
    att_ref, xp_ref, out_ref, up_ref, down_ref, vec_ref, bias_ref,
    hidden_ref, before_ref, two_ref, three_ref, inverse_ref, acc_ref, h2_ref,
):
    vec = lambda k: vec_ref[k : k + 1, :]
    step = pl.program_id(0)

    @pl.when(step == 0)
    def _():
        middle = xp_ref[...] + dot(att_ref[...], out_ref[...], 1, 0) + vec(OUT_BIAS)
        h2, two, inverse = normal(middle, vec(GAIN[1]), vec(SHIFT[1]))
        h2_ref[...] = h2.astype(bf16)
        two_ref[...] = two
        inverse_ref[0] = jnp.broadcast_to(inverse, inverse_ref.shape[1:])
        acc_ref[...] = middle + vec(vec_ref.shape[0] - 1)

    before = dot(h2_ref[...], up_ref[...], 1, 0) + bias_ref[...]
    before_ref[...] = before
    acc_ref[...] += dot(gelu(before).astype(bf16), down_ref[...], 1, 0)

    @pl.when(step == pl.num_programs(0) - 1)
    def _():
        hidden, three, inverse = normal(acc_ref[...], vec(GAIN[2]), vec(SHIFT[2]))
        hidden_ref[...] = hidden.astype(bf16)
        three_ref[...] = three
        inverse_ref[1] = jnp.broadcast_to(inverse, inverse_ref.shape[1:])


def forward(att, xp, out_w, up_w, down_w, vec, bias):
    rows, width = att.shape
    ff = down_w.shape[0]
    tile = 512
    fixed = whole((rows, width))
    return pl.pallas_call(
        forward_kernel,
        grid=(ff // tile,),
        out_shape=[
            jax.ShapeDtypeStruct((rows, width), bf16),
            jax.ShapeDtypeStruct((rows, ff), f32),
            jax.ShapeDtypeStruct((rows, width), f32),
            jax.ShapeDtypeStruct((rows, width), f32),
            jax.ShapeDtypeStruct((2, rows, 128), f32),
        ],
        in_specs=[
            fixed, fixed, pl.BlockSpec((width, width), lambda i: (0, 4)), pl.BlockSpec((width, tile), lambda i: (0, i)),
            pl.BlockSpec((tile, width), lambda i: (i, 0)), whole(vec.shape), pl.BlockSpec((1, tile), lambda i: (0, i)),
        ],
        out_specs=[
            fixed, pl.BlockSpec((rows, tile), lambda i: (0, i)), fixed, fixed, whole((2, rows, 128)),
        ],
        scratch_shapes=[pltpu.VMEM((rows, width), f32), pltpu.VMEM((rows, width), bf16)],
        compiler_params=params(),
        name="forward",
    )(att, xp, out_w, up_w, down_w, vec, bias)


def backward_kernel(
    mean_ref, total_ref, hidden_ref, wanted_ref, valid_ref, before_ref, two_ref, three_ref, inverse_ref,
    out_ref, up_ref, down_ref, vec_ref, datt_ref, loss_ref, final_ref, acc_ref,
):
    vec = lambda k: vec_ref[k : k + 1, :]
    step = pl.program_id(0)
    rows = valid_ref.shape[0]

    @pl.when(step == 0)
    def _():
        valid = valid_ref[...]
        wanted = wanted_ref[...].astype(f32)
        chosen = jnp.sum(hidden_ref[...].astype(f32) * wanted, axis=1, keepdims=True)
        loss = jnp.sum(valid * (as_column(total_ref[:1, :rows]) - chosen), keepdims=True)
        counted = jnp.sum(valid, keepdims=True)
        lane = iota(loss_ref.shape, 1)
        loss_ref[...] = jnp.where(lane == 0, loss, jnp.where(lane == 1, counted, 0.0))
        d_hidden = valid * (mean_ref[...] - wanted)
        final_ref[...] = normal_back(d_hidden, vec(GAIN[2]), three_ref[...], inverse_ref[1, :, :1])
        acc_ref[...] = jnp.zeros_like(acc_ref)

    d_act = dot(final_ref[...].astype(bf16), down_ref[...], 1, 1)
    d_before = (d_act * gelu_slope(before_ref[...])).astype(bf16)
    acc_ref[...] += dot(d_before, up_ref[...], 1, 1)

    @pl.when(step == pl.num_programs(0) - 1)
    def _():
        d_middle = final_ref[...] + normal_back(
            acc_ref[...], vec(GAIN[1]), two_ref[...], inverse_ref[0, :, :1]
        )
        datt_ref[...] = dot(d_middle.astype(bf16), out_ref[...], 1, 1).astype(bf16)


def backward(mean, total, hidden, wanted, valid, before, two, three, inverse, out_w, up_w, down_w, vec):
    rows, width = mean.shape
    ff = down_w.shape[0]
    tile = 512
    fixed = whole((rows, width))
    return pl.pallas_call(
        backward_kernel,
        grid=(ff // tile,),
        out_shape=[
            jax.ShapeDtypeStruct((rows, width), bf16),
            jax.ShapeDtypeStruct((8, 128), f32),
        ],
        in_specs=[
            fixed, whole(total.shape), fixed, fixed, whole((rows, 1)), pl.BlockSpec((rows, tile), lambda i: (0, i)),
            fixed, fixed, whole(inverse.shape), pl.BlockSpec((width, width), lambda i: (0, 4)),
            pl.BlockSpec((width, tile), lambda i: (0, i)),
            pl.BlockSpec((tile, width), lambda i: (i, 0)), whole(vec.shape),
        ],
        out_specs=[fixed, whole((8, 128))],
        scratch_shapes=[pltpu.VMEM((rows, width), f32)] * 2,
        compiler_params=params(),
        name="backward",
    )(mean, total, hidden, wanted, valid, before, two, three, inverse, out_w, up_w, down_w, vec)


def on_device(
    direct,
    token_identifiers,
    lengths,
    loss_positions,
    token_embedding_table,
    positions,
    query_key_value_matrix,
    output_weight,
    up_weight,
    down_weight,
    vectors,
    adapter_down_weight,
    adapter_up_weight,
    left_statistics,
    right_statistics,
):
    width = adapter_down_weight.shape[0]
    rank = adapter_down_weight.shape[1] // 2
    micros, _, slot_count = token_identifiers.shape
    picks = loss_positions.shape[2]
    ff = up_weight.shape[1]
    adapter_scale = adapter_alpha / rank
    local_rows = token_embedding_table.shape[0]
    devices = lax.axis_size("dp") * lax.axis_size("fsdp")
    me = lax.axis_index(BOTH)

    lens = lengths[:, 0]
    ids = token_identifiers[:, 0]
    ids = jnp.where(iota(ids.shape, 1) < lens[:, None], ids, -1).reshape(1, -1)
    amount = vectors.shape[0]
    packed_vec = jnp.pad(vectors.astype(f32), (0, -amount % 1024)).reshape(-1, 128)
    first = jnp.zeros((1,), jnp.int32)
    wide = jnp.concatenate([query_key_value_matrix, positions, output_weight], axis=1)
    if direct:
        received, most, slot, asked, own, mate, all_vec, wide = fetch(
            ids, packed_vec, token_embedding_table, wide, CAPACITY, 0
        )
        asked = asked.reshape(devices // 2, 2, GRID, 128)
        wide = wide.reshape(-1, wide.shape[-1])
    else:
        own = pl.pallas_call(
            functools.partial(presence_kernel, local_rows),
            out_shape=jax.ShapeDtypeStruct((devices, GRID, 128), bf16),
            compiler_params=params(),
            name="presence",
        )(ids)
        mate = own
        asked = lax.all_to_all(own, BOTH, 0, 0, tiled=True).reshape(devices, 1, GRID, 128)
        rows, most = select(asked, token_embedding_table, first, CAPACITY)
        most = lax.pmax(most, BOTH)
        received = lax.all_to_all(rows, BOTH, 0, 0, tiled=True)
        slot = slots(ids, own, mate, first, CAPACITY, local_rows)
        all_vec = lax.all_gather(packed_vec, BOTH)
        wide = lax.all_gather(wide, BOTH, axis=0, tiled=True)
    vec = all_vec.reshape(devices, -1)[:, :amount].reshape(-1, width)
    by_micro = lambda v: v.reshape(micros, 1, slot_count)
    most = most[0, 0]
    gap = 8 - rank
    split = lambda v: jnp.pad(v.reshape(2, rank, width), ((0, 0), (0, gap), (0, 0)))
    down_b = split(adapter_down_weight.T.astype(bf16)).reshape(16, width)
    down_b = jnp.pad(down_b, ((0, 112), (0, 0))).T
    up_b = split(adapter_up_weight.astype(bf16)).reshape(16, width)
    picked = loss_positions[:, 0]
    valid = (picked + 1 < lens[:, None]).astype(f32).reshape(-1, 1)
    old = jnp.concatenate([adapter_down_weight.T, adapter_up_weight]).reshape(4, rank, width)
    old = jnp.pad(old, ((0, 0), (0, gap), (0, 0)))
    bias = vec[UP_BIAS:-1].reshape(1, ff)
    flat = lambda v: v.reshape(-1, width)

    def rest(more, collective):
        layer = attend(
            ATTENTION_HEADS, adapter_scale, lens, by_micro(slot), received.reshape(-1, width), more, wide, vec,
            picked[:, :, None], down_b, up_b, *(([up_weight, down_weight], collective) if direct else ([], None)),
        )
        *layer, up_w, down_w = layer if direct else (
            *layer, *(lax.all_gather(w, BOTH, axis=0, tiled=True) for w in (up_weight, down_weight))
        )
        up_w, down_w = up_w.reshape(width, ff), down_w.reshape(ff, width)
        h1, low, keys, values, probs, h1_p, low_p, x_p, wanted, attended = layer
        hidden, before, two, three, inverse = forward(
            flat(attended), flat(x_p), wide, up_w, down_w, vec, bias
        )
        own_rows = hidden.shape[0]
        if direct:
            mean_row, total = head(hidden, token_embedding_table, collective + 1)
        else:
            every = lax.all_gather(hidden, BOTH, axis=0, tiled=True)
            means, totals = vocabulary(every, token_embedding_table, own_rows, 4 * own_rows)
            part = totals[:, 0, :own_rows].reshape(-1)
            top = lax.pmax(part, BOTH)
            total = top + jnp.log(lax.psum(jnp.exp(part - top), BOTH))
            mean_row = lax.psum_scatter(
                means.astype(f32) * jnp.exp(part - total)[:, None], BOTH, scatter_dimension=0, tiled=True
            )
            total = lax.dynamic_slice_in_dim(total, me * own_rows, own_rows, 0)
            total = jnp.broadcast_to(jnp.pad(total, (0, 128 - own_rows)), (8, 128))
        d_attended, loss = backward(
            mean_row, total, hidden, flat(wanted), valid, before, two, three, inverse, wide, up_w, down_w, vec
        )
        gradient = attend_back(
            ATTENTION_HEADS, adapter_scale, rank, d_attended.reshape(micros, picks, width),
            h1, low, keys, values, probs, h1_p, low_p, up_b, loss,
        )
        if direct:
            small, down_g, up_g, left_new, right_new, down_new, up_new = finished(
                gradient, old, left_statistics, right_statistics, collective + 2
            )
        else:
            small, down_g, up_g, left_new, right_new, _, new = renewed(
                lax.psum(gradient, BOTH), old, left_statistics, right_statistics
            )
            blocks = lax.all_gather(new, ("fsdp", "dp"))
            blocks = blocks.reshape(lax.axis_size("fsdp"), -1, 8, new.shape[1])
            blocks = blocks[:, : left_statistics.shape[0]].reshape(-1, 8, new.shape[1])
            updated = jnp.swapaxes(blocks[:, :rank].reshape(4, -1, rank, new.shape[1]), 1, 2)
            down_new, up_new = updated.reshape(2, 2 * rank, width)
        return small[0, :2], small[0, 2], down_g.T, up_g, left_new, right_new, down_new.T, up_new

    def another(state):
        step, rows_sum = state
        which = step.reshape(1)
        rows, most = select(asked, token_embedding_table, which, CAPACITY)
        if direct:
            received = send_rows(rows, most, 1)[0]
        else:
            received = lax.all_to_all(rows, BOTH, 0, 0, tiled=True)
        slot = slots(ids, own, mate, which, CAPACITY, local_rows)
        found = jnp.take(received.reshape(-1, width), jnp.maximum(slot[0], 0), axis=0)
        found = jnp.where(slot[0][:, None] >= 0, found, jnp.zeros((), bf16))
        return step + 1, rows_sum + found.reshape(micros, slot_count, width)

    def in_rounds():
        more = lax.while_loop(
            lambda state: (state[0] * CAPACITY).astype(f32) < most,
            another,
            (jnp.ones((), jnp.int32), jnp.zeros((micros, slot_count, width), bf16)),
        )[1]
        return rest(more, 5)

    plain = rest(None, 2)
    return lax.cond(most > CAPACITY, in_rounds, lambda: plain)


def solution(mesh):
    direct = dict(mesh.shape) == {"dp": 8, "fsdp": 4}
    rows = P(BOTH, None)
    placed = (
        P(None, BOTH, None),
        P(None, BOTH),
        P(None, BOTH, None),
        rows,
        rows,
        rows,
        rows,
        rows,
        rows,
        P(BOTH),
        P(),
        P(),
        P("fsdp", None, None),
        P("fsdp", None, None),
    )
    return jax.shard_map(
        functools.partial(on_device, direct),
        mesh=mesh,
        in_specs=placed,
        out_specs=(P(), P(), P(), P(), P("fsdp", None, None), P("fsdp", None, None), P(), P()),
        check_vma=False,
    )
```

```python
import functools
import jax
import jax.numpy as jnp
from jax import lax
from jax.experimental import pallas as pl
from jax.experimental.pallas import tpu as pltpu
from jax.sharding import PartitionSpec as P

ATTENTION_HEADS = 16
STATS_BLOCK_ROWS = 256
NEWTON = 8
CAPACITY = 80

ln_eps = 1e-05
adapter_alpha = 32.0
beta_stats = 0.95
root_eps = 1e-12
clip_level = 0.01
learn_rate = 0.05
masked_score = -1e30

BOTH = ("dp", "fsdp")
MESH = pl.DeviceIdType.MESH
VMEM = pl.BlockSpec(memory_space=pltpu.VMEM)
ANY = pl.BlockSpec(memory_space=pl.ANY)
f32 = jnp.float32
bf16 = jnp.bfloat16


def place():
    d, f = lax.axis_index("dp"), lax.axis_index("fsdp")
    return d // 2, lax.rem(d, 2), f // 2, lax.rem(f, 2)


def target(z, x, y, c):
    return (z * 2 + x, y * 2 + c)


def nth(i):
    return (i // 4, lax.rem(i, 4))


def greet_all(count):
    me = lax.axis_index("dp") * 4 + lax.axis_index("fsdp")
    sem = pltpu.get_barrier_semaphore()
    for i in range(1, count):
        pl.semaphore_signal(
            sem, inc=1, device_id=nth(lax.rem(me + i, count)), device_id_type=MESH
        )
    pl.semaphore_wait(sem, count - 1)
    return me


def remote(src, dst, send, recv, device):
    return pltpu.make_async_remote_copy(
        src_ref=src, dst_ref=dst, send_sem=send, recv_sem=recv, device_id=device, device_id_type=MESH
    )


def params(collective=None, vmem=60):
    if collective is None:
        return pltpu.CompilerParams(vmem_limit_bytes=vmem * 2**20)
    return pltpu.CompilerParams(
        vmem_limit_bytes=vmem * 2**20, collective_id=collective, has_side_effects=True
    )


def iota(shape, dim):
    return lax.broadcasted_iota(jnp.int32, shape, dim)


def marks(condition):
    return jnp.where(condition, 1.0, 0.0).astype(bf16)


def dot(a, b, ca, cb):
    return lax.dot_general(a, b, (((ca,), (cb,)), ((), ())), preferred_element_type=f32)


GRID = 16


def cells(ids, local_rows):
    owner = jnp.floor((ids.astype(f32) + 0.5) * (1.0 / local_rows)).astype(jnp.int32)
    local = ids - owner * local_rows
    return owner, jnp.where(ids >= 0, owner * GRID + (local >> 7), -1), local & 127


def presence(ids, owners, local_rows):
    width = ids.shape[1]
    _, high, low = cells(ids, local_rows)
    count = dot(
        marks(iota((owners * GRID, width), 0) == high), marks(iota((128, width), 0) == low), 1, 1
    )
    return marks(count > 0.5).reshape(owners, GRID, 128)


def presence_kernel(local_rows, ids_ref, own_ref):
    own_ref[...] = presence(ids_ref[...], own_ref.shape[0], local_rows)


def ranked(present):
    rows = present.shape[0]
    through = dot(present, marks(iota((128, 128), 0) <= iota((128, 128), 1)), 1, 0)
    of = lambda dim: iota((rows, rows), dim)
    earlier = marks((of(1) < of(0)) & (of(0) // GRID == of(1) // GRID))
    row_total = jnp.broadcast_to(through[:, 127:128], (rows, 128)).astype(bf16)
    offset = dot(earlier, row_total, 1, 0)
    has = present.astype(f32)
    return jnp.where(has > 0.5, through - has + offset, -1.0), offset[:, :1] + through[:, 127:128]


def mark_rows(capacity, rank_ref, marks_ref, units, local_rows):
    @pl.loop(0, units)
    def _(unit):
        rows = pl.ds(pl.multiple_of(unit * capacity, 16), capacity)
        own = rank_ref[pl.ds(pl.multiple_of(unit * GRID, GRID), GRID), :]
        for row in range(-(-local_rows // 128)):
            columns = min(128, local_rows - row * 128)
            hit = iota((capacity, 128), 0).astype(f32) == own[row : row + 1, :]
            marks_ref[rows, row * 128 : row * 128 + columns] = marks(hit)[:, :columns]


def select_kernel(capacity, asked_ref, table_ref, round_ref, rows_ref, most_ref, marks_ref, rank_ref):
    units, members = asked_ref.shape[:2]
    local_rows, width = table_ref.shape
    begin = (round_ref[0] * capacity).astype(f32)
    most = jnp.zeros((1, 1), f32)
    for first in range(0, units, 16):
        together = asked_ref[first : first + 16, 0]
        for member in range(1, members):
            together = jnp.maximum(together, asked_ref[first : first + 16, member])
        rank, amount = ranked(together.reshape(-1, 128))
        most = jnp.maximum(most, jnp.max(amount, keepdims=True))
        rank_ref[first * GRID : first * GRID + rank.shape[0]] = rank - begin
    most_ref[...] = jnp.broadcast_to(most, most_ref.shape)
    mark_rows(capacity, rank_ref, marks_ref, units, local_rows)

    @pl.loop(0, units // 4)
    def _(four):
        rows_ref[pl.ds(four * 4, 4)] = look_up(capacity, four, marks_ref, table_ref)


def look_up(capacity, four, marks_ref, table_ref):
    part = pl.ds(pl.multiple_of(four * (4 * capacity), 4 * capacity), 4 * capacity)
    found = dot(marks_ref[part, :], table_ref[...], 1, 0)
    return found.astype(bf16).reshape(4, capacity, table_ref.shape[1])


def select(asked, table, which_round, capacity):
    units = asked.shape[0]
    return pl.pallas_call(
        functools.partial(select_kernel, capacity),
        out_shape=[
            jax.ShapeDtypeStruct((units, capacity, table.shape[1]), bf16),
            jax.ShapeDtypeStruct((8, 128), f32),
        ],
        in_specs=[VMEM, VMEM, pl.BlockSpec(memory_space=pltpu.SMEM)],
        out_specs=[VMEM] * 2,
        scratch_shapes=[
            pltpu.VMEM((units * capacity, table.shape[0]), bf16),
            pltpu.VMEM((units * GRID, 128), f32),
        ],
        compiler_params=params(),
        name="select",
    )(asked, table, which_round)


def slots_of(capacity, begin, local_rows, ids, own_ref, mate_ref):
    owner, high, low = cells(ids, local_rows)
    width = ids.shape[1]
    own_rank = jnp.zeros((1, width), f32)
    for first in range(0, own_ref.shape[0], 16):
        together = jnp.maximum(own_ref[first : first + 16], mate_ref[first : first + 16])
        rank, _ = ranked(together.reshape(-1, 128))
        rank = rank - begin
        rank = jnp.where((rank >= 0.0) & (rank < capacity), rank + 1.0, 0.0)
        rows = rank.shape[0]
        of_low = dot(rank.astype(bf16), marks(iota((rows, width), 0) + first * GRID == high), 0, 0)
        own_rank += jnp.sum(
            jnp.where(iota((128, width), 0) == low, of_low, 0.0), axis=0, keepdims=True
        )
    slot = owner * capacity + own_rank.astype(jnp.int32) - 1
    return jnp.where(own_rank > 0.5, slot, -1)


def slots_kernel(capacity, local_rows, ids_ref, own_ref, mate_ref, round_ref, slot_ref):
    begin = (round_ref[0] * capacity).astype(f32)
    slot_ref[...] = slots_of(capacity, begin, local_rows, ids_ref[...], own_ref, mate_ref)


def slots(ids, own, mate, which_round, capacity, local_rows):
    return pl.pallas_call(
        functools.partial(slots_kernel, capacity, local_rows),
        out_shape=jax.ShapeDtypeStruct(ids.shape, jnp.int32),
        in_specs=[VMEM] * 3 + [pl.BlockSpec(memory_space=pltpu.SMEM)],
        out_specs=VMEM,
        compiler_params=params(),
        name="slots",
    )(ids, own, mate, which_round)


class Piece:
    def __init__(self, sources, out, sems):
        self.sources, self.out, self.rows = sources, out, out.shape[4]
        self.own_sems, self.chain_sems, self.plane_sems, self.core_sems = sems
        self.z, self.x, self.y, self.c = place()

    def at(self, zz, xx, yy, cc, half=None):
        ref = self.out.at[zz, xx, yy, cc]
        return ref if half is None else self.out.at[zz, xx, yy, cc, pl.ds(half * (self.rows // 2), self.rows // 2)]

    def own(self):
        copies, begin = [], 0
        for k, src in enumerate(self.sources):
            dst = self.out.at[self.z, self.x, self.y, self.c, :, pl.ds(begin, src.shape[1])]
            copies.append(pltpu.make_async_copy(src, dst, self.own_sems.at[k]))
            begin += src.shape[1]
        return copies

    def chain(self, zz, way, incoming=False):
        z, x, y, c = self.z, self.x, self.y, self.c
        ref = self.at(zz, x, y, c)
        k = (way + 1) // 2
        to = target(z - way if incoming else z + way, x, y, c)
        return remote(ref, ref, self.chain_sems.at[0, k, zz], self.chain_sems.at[1, k, zz], to)

    def plane(self, zz, step, incoming=False):
        z, x, y, c = self.z, self.x, self.y, self.c
        every = slice(None)
        over_x, over_y = target(z, 1 - x, y, c), target(z, x, 1 - y, c)
        xx, yy = (1 - x, 1 - y) if incoming else (x, y)
        if step == 0:
            pairs = ((self.at(zz, xx, y, c, 0), over_x), (self.at(zz, x, yy, c, 1), over_y))
        else:
            pairs = ((self.at(zz, every, yy, c, 0), over_y), (self.at(zz, xx, every, c, 1), over_x))
        return [
            remote(ref, ref, self.plane_sems.at[0, zz, step, k], self.plane_sems.at[1, zz, step, k], to)
            for k, (ref, to) in enumerate(pairs)
        ]

    def mate(self, zz, incoming=False):
        z, x, y, c = self.z, self.x, self.y, self.c
        ref = self.at(zz, slice(None), slice(None), 1 - c if incoming else c)
        return remote(ref, ref, self.core_sems.at[0, zz], self.core_sems.at[1, zz], target(z, x, y, 1 - c))

    def arrivals(self, step, act):
        for way in (1, -1):
            zz = self.z - way * (step + 1)

            @pl.when((zz >= 0) & (zz < 4))
            def _(zz=zz, way=way):
                act(zz, way)

    def pass_on(self, zz, way):
        @pl.when((self.z + way >= 0) & (self.z + way < 4))
        def _():
            self.chain(zz, way).start()

    def first(self, zz):
        for copy in self.plane(zz, 0):
            copy.start()

    def load(self):
        for copy in self.own():
            copy.start()

    def start(self):
        for copy in self.own():
            copy.wait()
        for way in (1, -1):
            self.pass_on(self.z, way)
        self.first(self.z)

    def arrive(self, step):
        def act(zz, way):
            self.chain(zz, way, True).wait_recv()
            self.pass_on(zz, way)
            self.first(zz)

        self.arrivals(step, act)

    def second_of(self, zz, way=None):
        for copy in self.plane(zz, 0, True):
            copy.wait_recv()
        for copy in self.plane(zz, 1):
            copy.start()

    def third_of(self, zz, way=None):
        for copy in self.plane(zz, 1, True):
            copy.wait_recv()
        self.mate(zz).start()

    def second(self, step=None):
        if step is None:
            self.second_of(self.z)
        else:
            self.arrivals(step, self.second_of)

    def third(self, step=None):
        if step is None:
            self.third_of(self.z)
        else:
            self.arrivals(step, self.third_of)

    def finish(self, incoming=True):
        for zz in range(4):
            for step in range(2):
                for copy in self.plane(zz, step):
                    copy.wait_send()
        for zz in range(4):
            self.mate(zz).wait_send()
            if incoming:
                self.mate(zz, True).wait_recv()
        for way in (1, -1):

            @pl.when((self.z + way >= 0) & (self.z + way < 4))
            def _(way=way):
                for step in range(3):
                    zz = self.z - way * step

                    @pl.when((zz >= 0) & (zz < 4))
                    def _(zz=zz):
                        self.chain(zz, way).wait_send()


class Spread(Piece):
    def __init__(self, out, sems):
        super().__init__([], out, (None, None) + tuple(sems))

    def finish(self):
        for k in range(self.out.shape[0]):
            for step in range(2):
                for copy in self.plane(k, step):
                    copy.wait_send()
            self.mate(k).wait_send()
            self.mate(k, True).wait_recv()


class LayerWeights:
    def __init__(self, ins, outs, sems):
        (self.out_in, self.up_in, self.down_in), (out, self.up, self.down) = ins, outs
        self.own_sems, self.z_sems, sems = sems[0], sems[1], sems[2:]
        self.output = Piece([self.out_in], out, sems[:4])
        self.ups, self.downs = Spread(self.up, sems[4:6]), Spread(self.down, sems[6:8])
        self.z, self.x, self.y, self.c = place()
        self.side = lax.rem(self.z, 2)
        self.planes = (self.z, self.z + 1 - 2 * self.side, lax.rem(self.z + 2, 4), 3 - self.z)

    def up_block(self, side, k):
        size = self.up.shape[5] // 2
        return self.up_in.at[:, pl.ds(pl.multiple_of((2 * k + side) * size, 128), size)]

    def up_place(self, zz, k):
        size = self.up.shape[5] // 2
        return self.up.at[zz, self.x, self.y, self.c, :, pl.ds(k * size, size)]

    def owned(self):
        return [
            pltpu.make_async_copy(self.up_block(self.side, k), self.up_place(self.z, k), self.own_sems.at[k])
            for k in range(2)
        ] + [
            pltpu.make_async_copy(
                self.down_in, self.down.at[self.z // 2, self.x, self.y, self.c], self.own_sems.at[2]
            )
        ]

    def up_copies(self, i, incoming=False):
        other = self.planes[i]
        frm = other if incoming else self.z
        return [
            remote(
                self.up_block(lax.rem(other, 2), k), self.up_place(frm, k),
                self.z_sems.at[0, k, other], self.z_sems.at[1, k, frm], target(other, self.x, self.y, self.c),
            )
            for k in range(2)
        ]

    def down_copy(self, incoming=False):
        other = self.planes[2]
        frm = other if incoming else self.z
        return remote(
            self.down_in, self.down.at[frm // 2, self.x, self.y, self.c],
            self.z_sems.at[0, 2, other], self.z_sems.at[1, 2, frm], target(other, self.x, self.y, self.c),
        )

    def load(self):
        self.output.load()
        for copy in self.owned():
            copy.start()

    def send_up(self, i):
        for copy in self.up_copies(i):
            copy.start()

    def start(self):
        self.output.start()
        for copy in self.owned():
            copy.wait()
        self.downs.first(self.z // 2)
        self.ups.first(self.z)
        self.send_up(1)
        self.down_copy().start()

    def arrive_up(self, i):
        for copy in self.up_copies(i, True):
            copy.wait_recv()
        self.ups.first(self.planes[i])

    def arrive_down(self):
        self.down_copy(True).wait_recv()
        self.downs.first(self.planes[2] // 2)

    def steps(self):
        ups, downs, output, planes = self.ups, self.downs, self.output, self.planes
        here, there = self.z // 2, planes[2] // 2
        return [
            lambda: (
                output.arrive(0), downs.second_of(here), ups.second_of(planes[0]), output.second(),
                self.arrive_up(1), self.send_up(2),
            ),
            lambda: (
                output.arrive(1), downs.third_of(here), ups.third_of(planes[0]), self.arrive_down(),
                ups.second_of(planes[1]), output.second(0), output.third(), self.send_up(3),
            ),
            lambda: (
                output.arrive(2), self.arrive_up(2), downs.second_of(there), ups.third_of(planes[1]),
                output.third(0), output.second(1),
            ),
            lambda: (
                self.arrive_up(3), ups.second_of(planes[2]), downs.third_of(there), output.third(1),
                output.second(2),
            ),
            lambda: (ups.second_of(planes[3]), ups.third_of(planes[2]), output.third(2)),
            lambda: ups.third_of(planes[3]),
        ]

    def finish(self):
        for i in range(1, 4):
            for copy in self.up_copies(i):
                copy.wait_send()
        self.down_copy().wait_send()
        self.ups.finish()
        self.downs.finish()
        self.output.finish()

    @staticmethod
    def shapes(weights):
        if not weights:
            return []
        out, up, down = weights
        return shares([out]) + [
            jax.ShapeDtypeStruct((4, 2, 2, 2, up.shape[0], up.shape[1] // 2), bf16),
            jax.ShapeDtypeStruct((2, 2, 2, 2) + down.shape, bf16),
        ]

    @staticmethod
    def scratch(weights):
        if not weights:
            return []
        spread = [pltpu.SemaphoreType.DMA((2, 4, 2, 2)), pltpu.SemaphoreType.DMA((2, 4))]
        return (
            [pltpu.SemaphoreType.DMA((3,)), pltpu.SemaphoreType.DMA((2, 3, 4))] + piece_scratch(1) + spread * 2
        )


def shares(weights):
    return [jax.ShapeDtypeStruct((4, 2, 2, 2) + w.shape, w.dtype) for w in weights]


def piece_scratch(count):
    return [
        pltpu.SemaphoreType.DMA((2,)),
        pltpu.SemaphoreType.DMA((2, 2, 4)),
        pltpu.SemaphoreType.DMA((2, 4, 2, 2)),
        pltpu.SemaphoreType.DMA((2, 4)),
    ] * count


class Rows:
    def __init__(self, rows_ref, most_ref, rows_out, most_out, sems):
        self.own_refs, self.outs = (rows_ref, most_ref), (rows_out, most_out)
        self.sems, self.mate_sems, self.own_sems = sems
        self.z, self.x, self.y, self.c = place()
        self.chip = (self.z * 2 + self.x) * 2 + self.y

    def out(self, k, to):
        device = target(to // 4, lax.rem(to // 2, 2), lax.rem(to, 2), self.c)
        src = self.own_refs[k].at[to] if k == 0 else self.own_refs[k]
        return remote(
            src, self.outs[k].at[self.chip, self.c], self.sems.at[0, k, to], self.sems.at[1, k, self.chip], device
        )

    def into(self, k, frm):
        device = target(frm // 4, lax.rem(frm // 2, 2), lax.rem(frm, 2), self.c)
        dst = self.outs[k].at[frm, self.c]
        return remote(dst, dst, self.sems.at[0, k, frm], self.sems.at[1, k, frm], device)

    def mate(self, k, of, core):
        ref = self.outs[k].at[of, core]
        to = target(self.z, self.x, self.y, 1 - self.c)
        return remote(ref, ref, self.mate_sems.at[0, k, of], self.mate_sems.at[1, k, of], to)

    def own(self, k):
        src = self.own_refs[k].at[self.chip] if k == 0 else self.own_refs[k]
        return pltpu.make_async_copy(src, self.outs[k].at[self.chip, self.c], self.own_sems.at[k])

    def send(self, to):
        @pl.when(to == self.chip)
        def _():
            for k in range(2):
                self.own(k).start()

        @pl.when(to != self.chip)
        def _():
            for k in range(2):
                self.out(k, to).start()

    def forward(self):
        for k in range(2):
            self.own(k).wait()
            self.mate(k, self.chip, self.c).start()
        for i in range(1, 16):
            frm = lax.rem(self.chip + 16 - i, 16)
            for k in range(2):
                self.into(k, frm).wait_recv()
                self.mate(k, frm, self.c).start()

    def finish(self):
        for i in range(16):
            of = lax.rem(self.chip + i, 16)
            for k in range(2):
                self.mate(k, of, self.c).wait_send()
                self.mate(k, of, 1 - self.c).wait_recv()
                if i:
                    self.out(k, of).wait_send()

    @staticmethod
    def shapes(rows, most):
        return [
            jax.ShapeDtypeStruct((16, 2) + rows[1:], bf16),
            jax.ShapeDtypeStruct((16, 2) + most, f32),
        ]

    @staticmethod
    def scratch():
        return [
            pltpu.SemaphoreType.DMA((2, 2, 16)),
            pltpu.SemaphoreType.DMA((2, 2, 16)),
            pltpu.SemaphoreType.DMA((2,)),
        ]


def rows_kernel(rows_ref, most_ref, rows_out, most_out, *sems):
    greet_all(32)
    rows = Rows(rows_ref, most_ref, rows_out, most_out, sems)
    for to in range(16):
        rows.send(to)
    rows.forward()
    rows.finish()


def send_rows(rows, most, collective):
    return pl.pallas_call(
        rows_kernel,
        out_shape=Rows.shapes(rows.shape, most.shape),
        in_specs=[VMEM] * 2,
        out_specs=[ANY, VMEM],
        scratch_shapes=Rows.scratch(),
        compiler_params=params(collective),
        name="send_rows",
    )(rows, most)


def fetch_kernel(
    capacity, lens_ref, ids_ref, vec_ref, table_ref, qkv_ref, pos_ref,
    received_ref, most_ref, slot_ref, asked_ref, own_ref, mate_ref, vec_out, w_out,
    marks_ref, rank_ref, rows_ref, count_ref, mosts_ref, pack_ref, packs_ref, *sems,
):
    ask_sems, mate_sems = sems[:2]
    rows = Rows(rows_ref, count_ref, received_ref, mosts_ref, sems[2:5])
    piece = Piece([qkv_ref, pos_ref], w_out, sems[5:])
    piece.load()
    local_rows = table_ref.shape[0]
    ids = jnp.concatenate(
        [
            jnp.where(iota(ids_ref.shape[1:], 1) < lens_ref[0, m], ids_ref[m], -1)
            for m in range(ids_ref.shape[0])
        ],
        axis=1,
    )
    own_ref[...] = presence(ids, 32, local_rows)
    length = vec_ref.shape[1]
    vec = jnp.pad(vec_ref[...].astype(f32), ((0, 0), (0, 1024 - length)))
    pack_ref[...] = jnp.concatenate([vec[:, k * 128 : (k + 1) * 128] for k in range(8)])
    me = greet_all(32)
    z, x, y, c = place()
    to_mate = remote(own_ref, mate_ref, mate_sems.at[0], mate_sems.at[1], target(z, x, y, 1 - c))
    to_mate.start()
    copies = []
    for i in range(1, 32):
        to = lax.rem(me + i, 32)
        for k, (src, dst) in enumerate(((own_ref.at[to], asked_ref), (pack_ref, packs_ref))):
            copy = remote(src, dst.at[me], ask_sems.at[0, k, i], ask_sems.at[1, k, i], nth(to))
            copy.start()
            copies.append(copy)
    piece.start()
    asked_ref[me] = own_ref[me]
    packs_ref[me] = pack_ref[...]
    for copy in copies:
        copy.wait()
    together = jnp.concatenate(
        [jnp.maximum(asked_ref[2 * unit], asked_ref[2 * unit + 1]) for unit in range(16)]
    )
    rank, amount = ranked(together)
    count_ref[...] = jnp.broadcast_to(jnp.max(amount, keepdims=True), count_ref.shape)
    rank_ref[...] = rank
    mark_rows(capacity, rank_ref, marks_ref, 16, local_rows)
    piece.second()
    piece.arrive(0)
    planes = [lax.rem(z + i, 4) for i in (2, 3, 1, 0)]
    for plane in planes:
        rows_ref[pl.ds(plane * 4, 4)] = look_up(capacity, plane, marks_ref, table_ref)
    piece.second(0)
    piece.arrive(1)
    for plane in planes:
        for k in range(4):
            rows.send(plane * 4 + lax.rem(x * 2 + y + k, 4))
    piece.third()
    piece.second(1)
    piece.third(0)
    to_mate.wait()
    slot_ref[...] = slots_of(capacity, 0.0, local_rows, ids, own_ref, mate_ref)
    width = vec_out.shape[1]
    for device in range(32):
        for k in range(-(-length // 128)):
            begin, end = k * 128, min(length, k * 128 + 128)
            at = device * length + begin
            while begin < end:
                count = min(end - begin, 128 - at % 128)
                vec_out[at // width : at // width + 1, at % width : at % width + count] = packs_ref[
                    device, k : k + 1, begin - k * 128 : begin - k * 128 + count
                ]
                at, begin = at + count, begin + count
    piece.arrive(2)
    piece.third(1)
    piece.second(2)
    piece.third(2)
    rows.forward()
    rows.finish()
    piece.finish()
    most = mosts_ref[0, 0]
    for k in range(1, 32):
        most = jnp.maximum(most, mosts_ref[k // 2, k % 2])
    most_ref[...] = most


def fetch(lens, ids, vec, table, qkv, positions, capacity, collective):
    grids = jax.ShapeDtypeStruct((32, GRID, 128), bf16)
    width = table.shape[1]
    small = jax.ShapeDtypeStruct((8, 128), f32)
    w = jax.ShapeDtypeStruct((qkv.shape[0], qkv.shape[1] + positions.shape[1]), bf16)
    return pl.pallas_call(
        functools.partial(fetch_kernel, capacity),
        out_shape=[
            jax.ShapeDtypeStruct((16, 2, capacity, width), bf16), small,
            jax.ShapeDtypeStruct((1, ids.size), jnp.int32), grids, grids, grids,
            jax.ShapeDtypeStruct((32 * vec.shape[1] // width, width), f32),
        ]
        + shares([w]),
        in_specs=[pl.BlockSpec(memory_space=pltpu.SMEM)] + [VMEM] * 3 + [ANY] * 2,
        out_specs=[ANY] + [VMEM] * 6 + [ANY],
        scratch_shapes=[
            pltpu.VMEM((16 * capacity, table.shape[0]), bf16),
            pltpu.VMEM((16 * GRID, 128), f32),
            pltpu.VMEM((16, capacity, width), bf16),
            pltpu.VMEM((8, 128), f32),
            pltpu.VMEM((16, 2, 8, 128), f32),
            pltpu.VMEM((8, 128), f32),
            pltpu.VMEM((32, 8, 128), f32),
            pltpu.SemaphoreType.DMA((2, 2, 32)),
            pltpu.SemaphoreType.DMA((2,)),
        ]
        + Rows.scratch()
        + piece_scratch(1),
        compiler_params=params(collective),
        name="fetch",
    )(lens, ids, vec, table, qkv, positions)


def vocabulary_kernel(group, rows_ref, table_ref, mean_ref, total_ref):
    logits = dot(rows_ref[...], table_ref[...], 1, 1)
    top = jnp.max(logits, axis=1, keepdims=True)
    weights = jnp.exp(logits - top)
    amount = jnp.sum(weights, axis=1, keepdims=True)
    mean = dot(weights.astype(bf16), table_ref[...], 1, 0)
    mean_ref[...] = (mean / amount).astype(bf16)
    total = top + jnp.log(amount)
    for k in range(total_ref.shape[0]):
        total_ref[k] = as_tile(as_row(total[k * group : (k + 1) * group]))


def as_tile(row):
    return jnp.broadcast_to(jnp.pad(row, ((0, 0), (0, 128 - row.shape[1]))), (8, 128))


def same(size):
    return iota((size, size), 0) == iota((size, size), 1)


def as_row(column):
    return jnp.sum(jnp.where(same(column.shape[0]), column, 0.0), axis=0, keepdims=True)


def as_column(row):
    return jnp.sum(jnp.where(same(row.shape[1]), row, 0.0), axis=1, keepdims=True)


def vocabulary(rows, table, group, tile):
    count, width = rows.shape
    return pl.pallas_call(
        functools.partial(vocabulary_kernel, group),
        grid=(count // tile,),
        out_shape=[
            jax.ShapeDtypeStruct((count, width), bf16),
            jax.ShapeDtypeStruct((count // group, 8, 128), f32),
        ],
        in_specs=[
            pl.BlockSpec((tile, width), lambda i: (i, 0)),
            pl.BlockSpec(table.shape, lambda i: (0, 0)),
        ],
        out_specs=[
            pl.BlockSpec((tile, width), lambda i: (i, 0)),
            pl.BlockSpec((tile // group, 8, 128), lambda i: (i, 0, 0)),
        ],
        compiler_params=params(),
        name="vocabulary",
    )(rows, table)


def merged(parts):
    size = parts[0][0].shape[0]
    rows = [total[:1, :size] for _, total in parts]
    top = functools.reduce(jnp.maximum, rows)
    total = top + jnp.log(sum(jnp.exp(row - top) for row in rows))
    mean = sum(
        values.astype(f32) * as_column(jnp.exp(row - total)) for (values, _), row in zip(parts, rows)
    )
    return mean, as_tile(total)


def exact(a, b, ca, cb):
    return lax.dot_general(
        a, b, (((ca,), (cb,)), ((), ())), precision=lax.Precision.HIGHEST, preferred_element_type=f32
    )


def fine(a, b, cb):
    a_high, b_high = a.astype(bf16), b.astype(bf16)
    a_low, b_low = (a - a_high.astype(f32)).astype(bf16), (b - b_high.astype(f32)).astype(bf16)
    return dot(a_high, b_high, 1, cb) + (dot(a_high, b_low, 1, cb) + dot(a_low, b_high, 1, cb))


def small_product(a, b):
    return sum(a[:, k : k + 1] * b[k : k + 1, :] for k in range(a.shape[0]))


def newton(matrix, product, apply, state):
    size = matrix.shape[0]
    identity = jnp.where(same(size), 1.0, 0.0)
    trace = jnp.sum(matrix * identity, keepdims=True)

    def step(_, carry):
        current, state = carry
        factor = (5.0 * identity - current) * 0.25
        square = product(factor, factor)
        return product(product(square, square), current), apply(state, factor)

    current, state = lax.fori_loop(0, NEWTON - 1, step, (matrix / trace, state))
    state = apply(state, (5.0 * identity - current) * 0.25)
    return state * lax.rsqrt(jnp.sqrt(trace))


def clipped(g_ref, rank):
    data = jnp.where(iota(g_ref.shape, 1) < rank, g_ref[...], 0.0)
    norm = jnp.sqrt(jnp.sum(data * data, keepdims=True).reshape(1, 1))
    return data * (clip_level / jnp.maximum(norm, clip_level)), norm


def renew(g_ref, down_ref, up_ref, left_ref, right_ref, clip_ref, new_ref):
    owned, block = left_ref.shape[0], left_ref.shape[1]
    rank = right_ref.shape[1]
    group = lax.axis_index("fsdp")
    own = lax.rem(lax.axis_index("dp"), owned)
    clip_ref[...], _ = clipped(g_ref, rank)
    columns = pl.ds(pl.multiple_of(own * block, block), block)
    grad = clip_ref[group, :, columns]
    left, right = stats_of(left_ref[own], right_ref[own], grad)
    left = left + root_eps * jnp.where(same(block), 1.0, 0.0)
    right = right + root_eps * jnp.where(same(rank), 1.0, 0.0)
    root = newton(right, small_product, small_product, jnp.where(same(rank), 1.0, 0.0))
    rows = newton(left, lambda a, b: fine(a, b, 0), lambda a, b: fine(a, b, 1), grad)[:rank]
    update = sum(as_column(root[k : k + 1, :]) * rows[k : k + 1, :] for k in range(rank))
    old = [ref[k * rank : (k + 1) * rank, columns] for ref in (down_ref, up_ref) for k in range(2)]
    old = functools.reduce(lambda a, k: jnp.where(group == k, old[k], a), range(1, 4), old[0])
    new = old - learn_rate * update
    new_ref[...] = jnp.pad(new, ((0, 8 - rank), (0, 0)))


def stats_of(left, right, grad):
    rank = right.shape[0]
    return (
        beta_stats * left + (1.0 - beta_stats) * exact(grad, grad, 0, 0),
        beta_stats * right + (1.0 - beta_stats) * exact(grad, grad, 1, 1)[:rank, :rank],
    )


def settle_kernel(g_ref, all_ref, left_ref, right_ref, small_ref, a_ref, b_ref, left_out, right_out, a_new, b_new, clip_ref):
    owned, block = left_ref.shape[0], left_ref.shape[1]
    rank = right_ref.shape[1]
    clip_ref[...], norm = clipped(g_ref, rank)
    small_ref[...] = jnp.where(iota((8, 128), 1) == 2, norm, g_ref[0, rank : rank + 1, :128])
    a_ref[...] = jnp.concatenate([clip_ref[0, :rank], clip_ref[1, :rank]])
    b_ref[...] = jnp.concatenate([clip_ref[2, :rank], clip_ref[3, :rank]])
    group = lax.axis_index("fsdp")
    for k in range(owned):
        grad = clip_ref[group, :, k * block : (k + 1) * block]
        left_out[k], right_out[k] = stats_of(left_ref[k], right_ref[k], grad)
    for k in range(all_ref.shape[0]):
        ref, row = (a_new, b_new)[k // 8], k // 4 % 2 * rank
        ref[row : row + rank, k % 4 * block : (k % 4 + 1) * block] = all_ref[k, :rank]


def settled(gradient, blocks, left, right):
    width = gradient.shape[2]
    shapes = [(8, 128), (8, width), (8, width), left.shape, right.shape, (8, width), (8, width)]
    return pl.pallas_call(
        settle_kernel,
        out_shape=[jax.ShapeDtypeStruct(shape, f32) for shape in shapes],
        in_specs=[VMEM] * 4,
        out_specs=[VMEM] * 7,
        scratch_shapes=[pltpu.VMEM(gradient.shape, f32)],
        compiler_params=params(),
        name="settled",
    )(gradient, blocks, left, right)


def renew_kernel(*refs):
    renew(*refs)


def renewed(gradient, down, up, left, right):
    return pl.pallas_call(
        renew_kernel,
        out_shape=[
            jax.ShapeDtypeStruct(gradient.shape, f32), jax.ShapeDtypeStruct((8, left.shape[1]), f32),
        ],
        in_specs=[VMEM] * 5,
        out_specs=[VMEM] * 2,
        compiler_params=params(),
        name="renewed",
    )(gradient, down, up, left, right)


def finish_kernel(
    g_ref, down_ref, up_ref, left_ref, right_ref, total_ref, all_ref,
    parts, summed, clip_ref, new_ref, one_sems, two_sems, block_sems,
):
    me = greet_all(32)

    def tile(ref, k):
        return ref.at[k // 8, :, pl.ds(pl.multiple_of(lax.rem(k, 8) * 128, 128), 128)]

    def out(i):
        to = lax.rem(me + i, 32)
        return remote(tile(g_ref, to), parts.at[me], one_sems.at[0, to], one_sems.at[1, me], nth(to))

    def into(i):
        frm = lax.rem(me + i, 32)
        return remote(tile(g_ref, me), parts.at[frm], one_sems.at[0, frm], one_sems.at[1, frm], nth(frm))

    def back(i):
        to = lax.rem(me + i, 32)
        return remote(summed, tile(total_ref, me), two_sems.at[0, to], two_sems.at[1, me], nth(to))

    def into_back(i):
        frm = lax.rem(me + i, 32)
        return remote(summed, tile(total_ref, frm), two_sems.at[0, frm], two_sems.at[1, frm], nth(frm))

    for i in range(1, 32):
        out(i).start()
    columns = pl.ds(pl.multiple_of(lax.rem(me, 8) * 128, 128), 128)
    for i in range(1, 32):
        into(i).wait_recv()
    running = g_ref[me // 8, :, columns]
    for i in range(1, 32):
        running = running + parts[lax.rem(me + i, 32)]
    summed[...] = running
    total_ref[me // 8, :, columns] = running
    for i in range(1, 32):
        back(i).start()
    for i in range(1, 32):
        into_back(i).wait_recv()
    renew(total_ref, down_ref, up_ref, left_ref, right_ref, clip_ref, new_ref)
    d, f = lax.axis_index("dp"), lax.axis_index("fsdp")
    half, mine = d // 4, f * 4 + lax.rem(d, 4)

    def share(i, incoming=False):
        k = lax.rem(mine + i, 16)
        device = (half * 4 + lax.rem(k, 4), k // 4)
        return remote(
            new_ref, all_ref.at[k if incoming else mine],
            block_sems.at[0, k], block_sems.at[1, k if incoming else mine], device,
        )

    for i in range(1, 16):
        share(i).start()
    all_ref[mine] = new_ref[...]
    for i in range(1, 16):
        share(i, True).wait_recv()
    for i in range(1, 16):
        share(i).wait_send()
    for i in range(1, 32):
        out(i).wait_send()
        back(i).wait_send()


def finished(gradient, down, up, left, right, collective):
    new = (8, left.shape[1])
    return pl.pallas_call(
        finish_kernel,
        out_shape=[
            jax.ShapeDtypeStruct(gradient.shape, f32), jax.ShapeDtypeStruct((16,) + new, f32),
        ],
        in_specs=[VMEM] * 5,
        out_specs=[VMEM] * 2,
        scratch_shapes=[
            pltpu.VMEM((32, 8, 128), f32),
            pltpu.VMEM((8, 128), f32),
            pltpu.VMEM(gradient.shape, f32),
            pltpu.VMEM(new, f32),
            pltpu.SemaphoreType.DMA((2, 32)),
            pltpu.SemaphoreType.DMA((2, 32)),
            pltpu.SemaphoreType.DMA((2, 16)),
        ],
        compiler_params=params(collective),
        name="finished",
    )(gradient, down, up, left, right)


def normal(v, gain, shift):
    centred = v - jnp.mean(v, axis=-1, keepdims=True)
    inverse = lax.rsqrt(jnp.mean(centred * centred, axis=-1, keepdims=True) + ln_eps)
    normed = centred * inverse
    return normed * gain + shift, normed, inverse


def normal_back(grad, gain, normed, inverse):
    scaled = grad * gain
    return inverse * (
        scaled
        - jnp.mean(scaled, axis=-1, keepdims=True)
        - normed * jnp.mean(scaled * normed, axis=-1, keepdims=True)
    )


GAIN, SHIFT, QKV_BIAS, OUT_BIAS, UP_BIAS = (0, 2, 4), (1, 3, 5), 6, 9, 10


def expand_chunk(slot_ref, rows_ref, begin, chunk):
    count = rows_ref.shape[0]
    part = lambda k: slot_ref[0, :, pl.ds(pl.multiple_of(begin + k, 128), 128)].astype(f32)
    column = jnp.concatenate([as_column(part(k)) for k in range(0, chunk, 128)]).astype(jnp.int32)
    return dot(marks(iota((chunk, count), 1) == column), rows_ref[...], 1, 0)


def spread_heads(v, heads, size):
    rows, width = v.shape
    tiled = jnp.concatenate([v] * heads, axis=0)
    shape = (heads * rows, width)
    return jnp.where(iota(shape, 0) // rows == iota(shape, 1) // size, tiled, jnp.zeros((), v.dtype))


def join_heads(v, heads, size):
    rows = v.shape[0] // heads
    own = jnp.where(iota(v.shape, 0) // rows == iota(v.shape, 1) // size, v, 0.0)
    return sum(own[k * rows : (k + 1) * rows] for k in range(heads))


def two_sets(v, rows):
    rank, width = v.shape[0] // 2, v.shape[1]
    v = v.astype(bf16)
    zeros = lambda count: jnp.zeros((count, width), bf16)
    return jnp.concatenate([v[:rank], zeros(8 - rank), v[rank:], zeros(rows - 8 - rank)])


def attend_kernel(
    heads, adapter_scale, count_w, with_more, lens_ref, slot_ref, rows_ref, pos_ref, qkv_ref, vec_ref, pick_ref,
    down_ref, up_ref, *refs,
):
    if with_more:
        more_ref, *refs = refs
    w_in, refs = refs[:count_w], refs[count_w:]
    (h1_ref, low_ref, k_ref, v_ref, p_ref, h1p_ref, lowp_ref, xp_ref, wanted_ref, att_ref), refs = refs[:10], refs[10:]
    w_out, refs = refs[:count_w], refs[count_w:]
    if count_w:
        (xp_pair, att_pair), refs = refs[:2], refs[2:]
    (emb_ref, q_ref), sems = refs[:2], refs[2:]
    if count_w:
        (xp_own, att_own, pair_sems), sems = sems[:3], sems[3:]
    micro = pl.program_id(0)
    count, width = emb_ref.shape
    length = lens_ref[0, micro]
    down, up = two_sets(down_ref[...], 128), two_sets(up_ref[...], 16)
    size = width // heads
    chunk = 256
    vec = lambda k: vec_ref[k : k + 1, :]
    if count_w:
        gather = LayerWeights(w_in, w_out, sems)
        steps = gather.steps()

        def to_pair(m):
            device = target(gather.planes[1], gather.x, gather.y, gather.c)
            return [
                remote(src.at[m], dst.at[m], pair_sems.at[0, k, m], pair_sems.at[1, k, m], device)
                for k, (src, dst) in enumerate(((xp_own, xp_pair), (att_own, att_pair)))
            ]

    def beside(loop):
        for number, step in enumerate(steps if count_w else []):
            if number % 3 == loop:

                @pl.when(micro == number // 3)
                def _(step=step):
                    step()

    if count_w:

        @pl.when(micro == 0)
        def _():
            gather.load()
            greet_all(32)
            gather.start()

    @pl.loop(0, count // chunk)
    def _(k):
        rows = pl.ds(pl.multiple_of(k * chunk, chunk), chunk)
        emb = expand_chunk(slot_ref, rows_ref, k * chunk, chunk).astype(bf16)
        if with_more:
            emb = emb + more_ref[0, rows]
        emb_ref[rows] = emb
        x = emb.astype(f32) + pos_ref[rows].astype(f32)
        h1_ref[0, rows] = normal(x, vec(GAIN[0]), vec(SHIFT[0]))[0].astype(bf16)

    beside(0)

    @pl.loop(0, count // chunk)
    def _(k):
        rows = pl.ds(pl.multiple_of(k * chunk, chunk), chunk)
        h1 = h1_ref[0, rows]
        low = dot(h1, down, 1, 1).astype(bf16)
        low_ref[0, rows] = low
        keys = dot(h1, qkv_ref[:, width : 2 * width], 1, 0) + vec(QKV_BIAS + 1)
        k_ref[0, rows] = keys.astype(bf16)
        values = dot(h1, qkv_ref[:, 2 * width :], 1, 0) + vec(QKV_BIAS + 2)
        values += adapter_scale * dot(low[:, 8:16], up[8:16], 1, 0)
        v_ref[0, rows] = values.astype(bf16)

    beside(1)

    pick = as_column(pick_ref[0].astype(f32)).astype(jnp.int32)
    picks = pick.shape[0]
    here = marks(iota((picks, count), 1) == pick)
    after = marks(iota((picks, count), 1) == pick + 1)
    xp_ref[0] = dot(here, emb_ref[...], 1, 0) + dot(here, pos_ref[...], 1, 0)
    wanted_ref[0] = dot(after, emb_ref[...], 1, 0).astype(bf16)
    h1p = dot(here, h1_ref[0], 1, 0).astype(bf16)
    lowp = dot(here, low_ref[0], 1, 0).astype(bf16)
    h1p_ref[0] = h1p
    lowp_ref[0] = lowp
    queries = dot(h1p, qkv_ref[:, :width], 1, 0) + vec(QKV_BIAS)
    queries += adapter_scale * dot(lowp[:, 0:8], up[0:8], 1, 0)
    q_ref[...] = queries.astype(bf16)
    some = 256 // size
    slot = iota((picks, count), 1)
    allowed = (slot <= pick) & (slot < length)
    allowed = jnp.concatenate([jnp.where(allowed, 1.0, 0.0)] * some, axis=0) > 0.5

    @pl.loop(0, width // 256)
    def _(k):
        lanes = pl.ds(pl.multiple_of(k * 256, 256), 256)
        scores = dot(spread_heads(q_ref[:, lanes], some, size), k_ref[0, :, lanes], 1, 1)
        scores = jnp.where(allowed, scores * size**-0.5, masked_score)
        weights = jnp.exp(scores - jnp.max(scores, axis=1, keepdims=True))
        probs = weights / jnp.sum(weights, axis=1, keepdims=True)
        p_ref[0, pl.ds(pl.multiple_of(k * some * picks, some * picks), some * picks)] = probs
        attended = dot(probs.astype(bf16), v_ref[0, :, lanes], 1, 0)
        att_ref[0, :, lanes] = join_heads(attended, some, size).astype(bf16)

    beside(2)

    if count_w:
        xp_own[micro] = xp_ref[0]
        att_own[micro] = att_ref[0]
        for copy in to_pair(micro):
            copy.start()

        @pl.when(micro == pl.num_programs(0) - 1)
        def _():
            gather.finish()
            for m in range(xp_own.shape[0]):
                for copy in to_pair(m):
                    copy.wait()


def whole(shape):
    return pl.BlockSpec(shape, lambda *_: (0,) * len(shape))


def of_micro(shape):
    return pl.BlockSpec((1,) + shape, lambda m: (m,) + (0,) * len(shape))


def attend(heads, adapter_scale, lens, slot, rows, more, wide, vec, pick, down, up, weights, collective):
    micros, _, count = slot.shape
    width = rows.shape[1]
    picks = pick.shape[2]
    more = [] if more is None else [more]
    outs = [
        ((count, width), bf16), ((count, 128), bf16), ((count, width), bf16), ((count, width), bf16),
        ((heads * picks, count), f32), ((picks, width), bf16), ((picks, 128), bf16),
        ((picks, width), f32), ((picks, width), bf16), ((picks, width), bf16),
    ]
    return pl.pallas_call(
        functools.partial(attend_kernel, heads, adapter_scale, len(weights), len(more) > 0),
        grid=(micros,),
        out_shape=[jax.ShapeDtypeStruct((micros,) + shape, kind) for shape, kind in outs]
        + LayerWeights.shapes(weights)
        + [jax.ShapeDtypeStruct((micros, picks, width), kind) for kind in (f32, bf16) if weights],
        in_specs=[
            pl.BlockSpec(memory_space=pltpu.SMEM), of_micro((1, count)), whole(rows.shape),
            pl.BlockSpec((count, width), lambda m: (0, 3)),
            pl.BlockSpec((width, 3 * width), lambda m: (0, 0)),
            whole(vec.shape), of_micro((1, picks)), whole(down.shape), whole(up.shape),
        ]
        + [of_micro((count, width))] * len(more)
        + [ANY] * len(weights),
        out_specs=[of_micro(shape) for shape, _ in outs] + [ANY] * (len(weights) + 2 if weights else 0),
        scratch_shapes=[pltpu.VMEM((count, width), bf16), pltpu.VMEM((picks, width), bf16)]
        + [pltpu.VMEM((micros, picks, width), kind) for kind in (f32, bf16) if weights]
        + [pltpu.SemaphoreType.DMA((2, 2, micros)) for _ in weights[:1]]
        + LayerWeights.scratch(weights),
        compiler_params=params(collective),
        name="attend",
    )(lens, slot, rows, wide, wide, vec, pick, down, up, *more, *weights)


def attend_back_kernel(
    heads, adapter_scale, rank, datt_ref, h1_ref, low_ref, k_ref, v_ref, p_ref, h1p_ref, lowp_ref, up_ref, loss_ref,
    g_ref, dq_ref, dlow_ref,
):
    count, width = h1_ref.shape[1:]
    size = width // heads
    picks = datt_ref.shape[1]
    some = 256 // size
    up = two_sets(up_ref[...], 16)

    @pl.when(pl.program_id(0) == 0)
    def _():
        g_ref[...] = jnp.zeros_like(g_ref)
        g_ref[0, rank : rank + 1, :128] = loss_ref[:1, :]

    dlow_ref[...] = jnp.zeros_like(dlow_ref)

    @pl.loop(0, width // 256)
    def _(k):
        lanes = pl.ds(pl.multiple_of(k * 256, 256), 256)
        own = pl.ds(pl.multiple_of(k * some * picks, some * picks), some * picks)
        d_heads = spread_heads(datt_ref[0, :, lanes], some, size)
        probs = p_ref[0, own]
        d_probs = dot(d_heads, v_ref[0, :, lanes], 1, 1)
        probs_b = probs.astype(bf16)
        v_up = two_sets_of_values(up_ref, lanes)
        dlow_ref[...] += dot(dot(d_heads, v_up, 1, 1).astype(bf16), probs_b, 0, 0)
        taken = dot(probs_b, low_ref[0, :, 8:16], 1, 0)
        g_ref[3, :, lanes] += adapter_scale * dot(taken.astype(bf16), d_heads, 0, 0)
        weighted = probs * d_probs
        d_scores = weighted - probs * jnp.sum(weighted, axis=1, keepdims=True)
        d_queries = dot(d_scores.astype(bf16), k_ref[0, :, lanes], 1, 0)
        dq_ref[:, lanes] = (join_heads(d_queries, some, size) * size**-0.5).astype(bf16)

    d_low_q = (adapter_scale * dot(dq_ref[...], up[0:8], 1, 1)).astype(bf16)
    d_low_v = (adapter_scale * dlow_ref[...]).astype(bf16)
    g_ref[0] += dot(d_low_q, h1p_ref[0], 0, 0)
    g_ref[1] += dot(d_low_v, h1_ref[0], 1, 0)
    g_ref[2] += adapter_scale * dot(lowp_ref[0, :, 0:8], dq_ref[...], 0, 0)


def two_sets_of_values(up_ref, lanes):
    rank = up_ref.shape[0] // 2
    v = up_ref[:, lanes].astype(bf16)[rank:]
    return jnp.concatenate([v, jnp.zeros((8 - rank, v.shape[1]), bf16)])


def attend_back(heads, adapter_scale, rank, datt, h1, low, keys, values, probs, h1p, lowp, up, loss):
    micros, count, width = h1.shape
    picks = datt.shape[1]
    ins = (datt, h1, low, keys, values, probs, h1p, lowp)
    return pl.pallas_call(
        functools.partial(attend_back_kernel, heads, adapter_scale, rank),
        grid=(micros,),
        out_shape=jax.ShapeDtypeStruct((4, 8, width), f32),
        in_specs=[of_micro(v.shape[1:]) for v in ins] + [whole(up.shape), whole(loss.shape)],
        out_specs=whole((4, 8, width)),
        scratch_shapes=[pltpu.VMEM((picks, width), bf16), pltpu.VMEM((8, count), f32)],
        compiler_params=params(),
        name="attend_back",
    )(*ins, up, loss)


def gelu(v):
    inner = 0.7978845608028654 * (v + 0.044715 * v * v * v)
    return 0.5 * v * (1.0 + jnp.tanh(inner))


def gelu_slope(v):
    bend = jnp.tanh(0.7978845608028654 * (v + 0.044715 * v * v * v))
    return 0.5 * (1.0 + bend) + 0.5 * v * (1.0 - bend * bend) * 0.7978845608028654 * (
        1.0 + 3.0 * 0.044715 * v * v
    )


def middle_kernel(
    lens_ref, pick_ref, att_ref, xp_ref, att_pair, xp_pair, wanted_ref, vec_ref, out_hbm, up_hbm, down_hbm, table_ref, datt_ref, loss_ref,
    out_ref, up_ref, down_ref, middle_ref, two_ref, three_ref, hidden_ref, before_ref, final_ref,
    rows_ref, part_ref, got_ref, load_sems, pair_sems, every_ref, q_ref, t_ref, core_q, core_t, keep_q, keep_t, send_q, send_t, got_q, got_t,
    next_q, next_t, pass_q, pass_t, last_q, last_t, end_q, end_t, final_q, final_t,
    core_sems, one_sems, two_sems, z_sems, *sems,
):
    rows, width = hidden_ref.shape
    piece = Piece([hidden_ref], every_ref, sems)
    vec = lambda k: vec_ref[k : k + 1, :]
    loads = [
        pltpu.make_async_copy(src, dst, load_sems.at[k])
        for k, (src, dst) in enumerate(((out_hbm, out_ref), (up_hbm, up_ref), (down_hbm, down_ref)))
    ]
    for load in loads:
        load.start()
    greet_all(32)
    z, x, y, c = place()
    side = lax.rem(z, 2)
    pair = target(z + 1 - 2 * side, x, y, c)

    def to_pair(number, values):
        rows_ref[0] = values
        copy = remote(
            rows_ref.at[0], rows_ref.at[1], pair_sems.at[0, number], pair_sems.at[1, number], pair
        )
        copy.start()
        copy.wait()
        return rows_ref[...].reshape(2 * rows, width)

    def of_pair(number, values):
        part_ref[...] = values[rows:].astype(bf16)
        copy = remote(part_ref, got_ref, pair_sems.at[0, number], pair_sems.at[1, number], pair)
        copy.start()
        copy.wait()
        return values[:rows] + got_ref[...].astype(f32)

    loads[0].wait()
    both = lambda own, other: jnp.concatenate([own[...], other[...]])
    middle = both(xp_ref, xp_pair) + dot(both(att_ref, att_pair), out_ref[...], 1, 0) + vec(OUT_BIAS)
    middle_ref[...] = middle[:rows]
    every_h2, two, inverse_two = normal(middle, vec(GAIN[1]), vec(SHIFT[1]))
    two_ref[...], inverse_two = two[:rows], inverse_two[:rows]
    bias = jnp.concatenate(
        [jnp.where(side == 0, vec(UP_BIAS + 2 * k), vec(UP_BIAS + 2 * k + 1)) for k in range(2)], axis=1
    )
    loads[1].wait()
    before = dot(every_h2.astype(bf16), up_ref[...], 1, 0) + bias
    before_ref[...] = before
    loads[2].wait()
    added = of_pair(0, dot(gelu(before).astype(bf16), down_ref[...], 1, 0))
    final = middle_ref[...] + added + vec(vec_ref.shape[0] - 1)
    hidden, three, inverse_three = normal(final, vec(GAIN[2]), vec(SHIFT[2]))
    hidden_ref[...] = hidden.astype(bf16)
    three_ref[...] = three

    piece.load()
    mate = target(z, x, y, 1 - c)
    over = (target(z, 1 - x, y, c), target(z, x, 1 - y, c))
    half = width // 2
    cols = (slice(0, half), slice(half, width))
    mine = (x, y)
    is_end = (z == 0) | (z == 3)
    up = jnp.where((z == 0) | (z == 2), 1, -1)

    def nth_plane(i):
        from_end = z + up * i
        inside = jnp.where(i == 0, z, jnp.where(i == 1, z + up, jnp.where(i == 2, z - up, z - 2 * up)))
        return jnp.where(is_end, from_end, inside)

    def core_copies(zz):
        return [
            remote(q_ref.at[zz, :, :, 1 - c], core_q.at[zz], core_sems.at[0, 0, zz], core_sems.at[1, 0, zz], mate),
            remote(t_ref.at[zz, :, :, 1 - c], core_t.at[zz], core_sems.at[0, 1, zz], core_sems.at[1, 1, zz], mate),
        ]

    def one_copies(zz, k):
        return [
            remote(send_q.at[k, zz], got_q.at[k, zz], one_sems.at[0, 0, k, zz], one_sems.at[1, 0, k, zz], over[k]),
            remote(send_t.at[k, zz], got_t.at[k, zz], one_sems.at[0, 1, k, zz], one_sems.at[1, 1, k, zz], over[k]),
        ]

    def two_copies(zz, k):
        return [
            remote(pass_q.at[k, zz], last_q.at[k, zz], two_sems.at[0, 0, k, zz], two_sems.at[1, 0, k, zz], over[1 - k]),
            remote(pass_t.at[k, zz], last_t.at[k, zz], two_sems.at[0, 1, k, zz], two_sems.at[1, 1, k, zz], over[1 - k]),
        ]

    def z_copies(zz, frm, k):
        return [
            remote(end_q.at[k, zz], final_q.at[k, frm], z_sems.at[0, 0, k, zz], z_sems.at[1, 0, k, frm], target(zz, x, y, c)),
            remote(end_t.at[k, zz], final_t.at[k, frm], z_sems.at[0, 1, k, zz], z_sems.at[1, 1, k, frm], target(zz, x, y, c)),
        ]

    def start(copies):
        for copy in copies:
            copy.start()

    def landed(copies):
        for copy in copies:
            copy.wait_recv()

    def left(copies):
        for copy in copies:
            copy.wait_send()

    def arrive(i):
        zz = nth_plane(i)
        way = jnp.where(zz < z, 1, -1)
        piece.chain(zz, way, True).wait_recv()
        piece.pass_on(zz, way)
        piece.first(zz)

    def second(i):
        piece.second_of(nth_plane(i))

    def third(i):
        piece.third_of(nth_plane(i))

    def compute(i):
        zz = nth_plane(i)
        piece.mate(zz, True).wait_recv()

        @pl.loop(0, 2)
        def _(xx):
            logits = dot(every_ref[zz, xx].reshape(4 * rows, width), table_ref[...], 1, 1)
            top = jnp.max(logits, axis=1, keepdims=True)
            weights = jnp.exp(logits - top)
            amount = jnp.sum(weights, axis=1, keepdims=True)
            mean = dot(weights.astype(bf16), table_ref[...], 1, 0) / amount
            q_ref[zz, xx] = mean.astype(bf16).reshape(2, 2, rows, width)
            total = top + jnp.log(amount)
            for k in range(4):
                t_ref[zz, xx, k // 2, k % 2] = as_tile(as_row(total[k * rows : (k + 1) * rows]))

        start(core_copies(zz))

    def merge_cores(i):
        zz = nth_plane(i)
        landed(core_copies(zz))

        @pl.loop(0, 2)
        def _(xx):
            for yy in range(2):
                mean, total = merged(
                    [(q_ref[zz, xx, yy, c], t_ref[zz, xx, yy, c]), (core_q[zz, xx, yy], core_t[zz, xx, yy])]
                )
                for k, (own, other) in enumerate(((xx, yy), (yy, xx))):
                    part = mean[:, cols[k]]

                    @pl.when(own == mine[k])
                    def _(k=k, other=other, part=part, total=total):
                        keep_q[k, zz, other] = part
                        keep_t[k, zz, other] = total

                    @pl.when(own != mine[k])
                    def _(k=k, other=other, part=part, total=total):
                        send_q[k, zz, other] = part.astype(bf16)
                        send_t[k, zz, other] = total

        for k in range(2):
            start(one_copies(zz, k))

    def merge_first(i):
        zz = nth_plane(i)
        for k in range(2):
            landed(one_copies(zz, k))
            for other in range(2):
                mean, total = merged(
                    [(keep_q[k, zz, other], keep_t[k, zz, other]), (got_q[k, zz, other], got_t[k, zz, other])]
                )

                @pl.when(other == mine[1 - k])
                def _(k=k, mean=mean, total=total):
                    next_q[k, zz] = mean
                    next_t[k, zz] = total

                @pl.when(other != mine[1 - k])
                def _(k=k, mean=mean, total=total):
                    pass_q[k, zz] = mean.astype(bf16)
                    pass_t[k, zz] = total

            start(two_copies(zz, k))

    def merge_second(i):
        zz = nth_plane(i)
        for k in range(2):
            landed(two_copies(zz, k))
            mean, total = merged([(next_q[k, zz], next_t[k, zz]), (last_q[k, zz], last_t[k, zz])])

            @pl.when(i > 0)
            def _(k=k, mean=mean, total=total):
                end_q[k, zz] = mean.astype(bf16)
                end_t[k, zz] = total
                start(z_copies(zz, z, k))

            @pl.when(i == 0)
            def _(k=k, mean=mean, total=total):
                next_q[k, z] = mean
                next_t[k, z] = total

    piece.start()
    second(0)
    arrive(1)
    third(0)
    arrive(2)
    second(1)

    @pl.loop(0, 7)
    def _(i):
        for act, lag, begin in (
            (compute, 0, 0), (third, -1, 1), (second, -2, 2), (arrive, -3, 3),
            (merge_cores, 1, 0), (merge_first, 2, 0), (merge_second, 3, 0),
        ):
            @pl.when((i - lag >= begin) & (i - lag < 4))
            def _(act=act, lag=lag):
                act(i - lag)

    for k in range(2):
        parts = [(next_q[k, z], next_t[k, z])]
        for i in range(1, 4):
            frm = nth_plane(i)
            landed(z_copies(frm, frm, k))
            parts.append((final_q[k, frm], final_t[k, frm]))
        mean, total = merged(parts)
        final_ref[:, cols[k]] = mean

    valid = jnp.concatenate(
        [
            jnp.where(as_column(pick_ref[m].astype(f32)) + 1.0 < lens_ref[0, m].astype(f32), 1.0, 0.0)
            for m in range(pick_ref.shape[0])
        ]
    )
    wanted = wanted_ref[...].astype(f32)
    chosen = jnp.sum(hidden_ref[...].astype(f32) * wanted, axis=1, keepdims=True)
    loss = jnp.sum(valid * (as_column(total[:1, :rows]) - chosen), keepdims=True)
    counted = jnp.sum(valid, keepdims=True)
    lane = iota(loss_ref.shape, 1)
    loss_ref[...] = jnp.where(lane == 0, loss, jnp.where(lane == 1, counted, 0.0))
    d_hidden = valid * (final_ref[...] - wanted)
    d_final = normal_back(d_hidden, vec(GAIN[2]), three_ref[...], inverse_three)
    middle_ref[...] = d_final
    d_act = dot(to_pair(1, d_final.astype(bf16)), down_ref[...], 1, 1)
    d_before = (d_act * gelu_slope(before_ref[...])).astype(bf16)
    d_two = of_pair(2, dot(d_before, up_ref[...], 1, 1))
    d_middle = middle_ref[...] + normal_back(d_two, vec(GAIN[1]), two_ref[...], inverse_two)
    datt_ref[...] = dot(d_middle.astype(bf16), out_ref[...], 1, 1).astype(bf16)

    @pl.loop(0, 4)
    def _(i):
        zz = nth_plane(i)
        left(core_copies(zz))
        for k in range(2):
            left(one_copies(zz, k))
            left(two_copies(zz, k))

    @pl.loop(1, 4)
    def _(i):
        for k in range(2):
            left(z_copies(nth_plane(i), z, k))

    piece.finish(False)


def middle(lens, pick, att, xp, att_pair, xp_pair, wanted, vec, out_w, up_w, down_w, table, collective):
    rows, width = att.shape
    half = width // 2
    tile = (8, 128)
    vmem = pltpu.VMEM
    own = (rows, width)
    return pl.pallas_call(
        middle_kernel,
        out_shape=[jax.ShapeDtypeStruct(own, bf16), jax.ShapeDtypeStruct(tile, f32)],
        in_specs=[pl.BlockSpec(memory_space=pltpu.SMEM)] + [VMEM] * 7 + [ANY] * 3 + [VMEM],
        out_specs=[VMEM] * 2,
        scratch_shapes=[
            vmem(out_w.shape, bf16), vmem(up_w.shape, bf16), vmem(down_w.shape, bf16),
            vmem(own, f32), vmem(own, f32), vmem(own, f32), vmem(own, bf16),
            vmem((2 * rows, up_w.shape[1]), f32), vmem(own, f32),
            vmem((2,) + own, bf16), vmem(own, bf16), vmem(own, bf16),
            pltpu.SemaphoreType.DMA((3,)),
            pltpu.SemaphoreType.DMA((2, 4)),
            vmem((4, 2, 2, 2, rows, width), bf16),
            vmem((4, 2, 2, 2, rows, width), bf16), vmem((4, 2, 2, 2) + tile, f32),
            vmem((4, 2, 2, rows, width), bf16), vmem((4, 2, 2) + tile, f32),
            vmem((2, 4, 2, rows, half), f32), vmem((2, 4, 2) + tile, f32),
            vmem((2, 4, 2, rows, half), bf16), vmem((2, 4, 2) + tile, f32),
            vmem((2, 4, 2, rows, half), bf16), vmem((2, 4, 2) + tile, f32),
            vmem((2, 4, rows, half), f32), vmem((2, 4) + tile, f32),
            vmem((2, 4, rows, half), bf16), vmem((2, 4) + tile, f32),
            vmem((2, 4, rows, half), bf16), vmem((2, 4) + tile, f32),
            vmem((2, 4, rows, half), bf16), vmem((2, 4) + tile, f32),
            vmem((2, 4, rows, half), bf16), vmem((2, 4) + tile, f32),
            pltpu.SemaphoreType.DMA((2, 2, 4)),
            pltpu.SemaphoreType.DMA((2, 2, 2, 4)),
            pltpu.SemaphoreType.DMA((2, 2, 2, 4)),
            pltpu.SemaphoreType.DMA((2, 2, 2, 4)),
        ]
        + piece_scratch(1),
        compiler_params=params(collective),
        name="middle",
    )(lens, pick, att, xp, att_pair, xp_pair, wanted, vec, out_w, up_w, down_w, table)


def forward_kernel(
    att_ref, xp_ref, out_ref, up_ref, down_ref, vec_ref, bias_ref,
    hidden_ref, before_ref, two_ref, three_ref, inverse_ref, acc_ref, h2_ref,
):
    vec = lambda k: vec_ref[k : k + 1, :]
    step = pl.program_id(0)

    @pl.when(step == 0)
    def _():
        middle = xp_ref[...] + dot(att_ref[...], out_ref[...], 1, 0) + vec(OUT_BIAS)
        h2, two, inverse = normal(middle, vec(GAIN[1]), vec(SHIFT[1]))
        h2_ref[...] = h2.astype(bf16)
        two_ref[...] = two
        inverse_ref[0] = jnp.broadcast_to(inverse, inverse_ref.shape[1:])
        acc_ref[...] = middle + vec(vec_ref.shape[0] - 1)

    before = dot(h2_ref[...], up_ref[...], 1, 0) + bias_ref[...]
    before_ref[...] = before
    acc_ref[...] += dot(gelu(before).astype(bf16), down_ref[...], 1, 0)

    @pl.when(step == pl.num_programs(0) - 1)
    def _():
        hidden, three, inverse = normal(acc_ref[...], vec(GAIN[2]), vec(SHIFT[2]))
        hidden_ref[...] = hidden.astype(bf16)
        three_ref[...] = three
        inverse_ref[1] = jnp.broadcast_to(inverse, inverse_ref.shape[1:])


def forward(att, xp, out_w, up_w, down_w, vec, bias):
    rows, width = att.shape
    ff = down_w.shape[0]
    tile = 512
    fixed = whole((rows, width))
    return pl.pallas_call(
        forward_kernel,
        grid=(ff // tile,),
        out_shape=[
            jax.ShapeDtypeStruct((rows, width), bf16),
            jax.ShapeDtypeStruct((rows, ff), f32),
            jax.ShapeDtypeStruct((rows, width), f32),
            jax.ShapeDtypeStruct((rows, width), f32),
            jax.ShapeDtypeStruct((2, rows, 128), f32),
        ],
        in_specs=[
            fixed, fixed, whole(out_w.shape), pl.BlockSpec((width, tile), lambda i: (0, i)),
            pl.BlockSpec((tile, width), lambda i: (i, 0)), whole(vec.shape), pl.BlockSpec((1, tile), lambda i: (0, i)),
        ],
        out_specs=[
            fixed, pl.BlockSpec((rows, tile), lambda i: (0, i)), fixed, fixed, whole((2, rows, 128)),
        ],
        scratch_shapes=[pltpu.VMEM((rows, width), f32), pltpu.VMEM((rows, width), bf16)],
        compiler_params=params(),
        name="forward",
    )(att, xp, out_w, up_w, down_w, vec, bias)


def backward_kernel(
    mean_ref, total_ref, hidden_ref, wanted_ref, valid_ref, before_ref, two_ref, three_ref, inverse_ref,
    out_ref, up_ref, down_ref, vec_ref, datt_ref, loss_ref, final_ref, acc_ref,
):
    vec = lambda k: vec_ref[k : k + 1, :]
    step = pl.program_id(0)
    rows = valid_ref.shape[0]

    @pl.when(step == 0)
    def _():
        valid = valid_ref[...]
        wanted = wanted_ref[...].astype(f32)
        chosen = jnp.sum(hidden_ref[...].astype(f32) * wanted, axis=1, keepdims=True)
        loss = jnp.sum(valid * (as_column(total_ref[:1, :rows]) - chosen), keepdims=True)
        counted = jnp.sum(valid, keepdims=True)
        lane = iota(loss_ref.shape, 1)
        loss_ref[...] = jnp.where(lane == 0, loss, jnp.where(lane == 1, counted, 0.0))
        d_hidden = valid * (mean_ref[...] - wanted)
        final_ref[...] = normal_back(d_hidden, vec(GAIN[2]), three_ref[...], inverse_ref[1, :, :1])
        acc_ref[...] = jnp.zeros_like(acc_ref)

    d_act = dot(final_ref[...].astype(bf16), down_ref[...], 1, 1)
    d_before = (d_act * gelu_slope(before_ref[...])).astype(bf16)
    acc_ref[...] += dot(d_before, up_ref[...], 1, 1)

    @pl.when(step == pl.num_programs(0) - 1)
    def _():
        d_middle = final_ref[...] + normal_back(
            acc_ref[...], vec(GAIN[1]), two_ref[...], inverse_ref[0, :, :1]
        )
        datt_ref[...] = dot(d_middle.astype(bf16), out_ref[...], 1, 1).astype(bf16)


def backward(mean, total, hidden, wanted, valid, before, two, three, inverse, out_w, up_w, down_w, vec):
    rows, width = mean.shape
    ff = down_w.shape[0]
    tile = 512
    fixed = whole((rows, width))
    return pl.pallas_call(
        backward_kernel,
        grid=(ff // tile,),
        out_shape=[
            jax.ShapeDtypeStruct((rows, width), bf16),
            jax.ShapeDtypeStruct((8, 128), f32),
        ],
        in_specs=[
            fixed, whole(total.shape), fixed, fixed, whole((rows, 1)), pl.BlockSpec((rows, tile), lambda i: (0, i)),
            fixed, fixed, whole(inverse.shape), whole(out_w.shape),
            pl.BlockSpec((width, tile), lambda i: (0, i)),
            pl.BlockSpec((tile, width), lambda i: (i, 0)), whole(vec.shape),
        ],
        out_specs=[fixed, whole((8, 128))],
        scratch_shapes=[pltpu.VMEM((rows, width), f32)] * 2,
        compiler_params=params(),
        name="backward",
    )(mean, total, hidden, wanted, valid, before, two, three, inverse, out_w, up_w, down_w, vec)


def on_device(
    direct,
    token_identifiers,
    lengths,
    loss_positions,
    token_embedding_table,
    positions,
    query_key_value_matrix,
    output_weight,
    up_weight,
    down_weight,
    vectors,
    adapter_down_weight,
    adapter_up_weight,
    left_statistics,
    right_statistics,
):
    width = adapter_down_weight.shape[0]
    rank = adapter_down_weight.shape[1] // 2
    micros, _, slot_count = token_identifiers.shape
    picks = loss_positions.shape[2]
    ff = up_weight.shape[1]
    adapter_scale = adapter_alpha / rank
    local_rows = token_embedding_table.shape[0]
    devices = lax.axis_size("dp") * lax.axis_size("fsdp")
    me = lax.axis_index(BOTH)

    first = jnp.zeros((1,), jnp.int32)

    def masked_ids():
        ids = token_identifiers[:, 0]
        return jnp.where(iota(ids.shape, 1) < lengths, ids, -1).reshape(1, -1)

    if direct:
        received, most, slot, asked, own, mate, vec, wide = fetch(
            lengths.T, token_identifiers, vectors.reshape(1, -1), token_embedding_table, query_key_value_matrix,
            positions, CAPACITY, 0,
        )
        asked = asked.reshape(devices // 2, 2, GRID, 128)
        wide = wide.reshape(-1, wide.shape[-1])
    else:
        ids = masked_ids()
        own = pl.pallas_call(
            functools.partial(presence_kernel, local_rows),
            out_shape=jax.ShapeDtypeStruct((devices, GRID, 128), bf16),
            compiler_params=params(),
            name="presence",
        )(ids)
        mate = own
        asked = lax.all_to_all(own, BOTH, 0, 0, tiled=True).reshape(devices, 1, GRID, 128)
        rows, most = select(asked, token_embedding_table, first, CAPACITY)
        most = lax.pmax(most, BOTH)
        received = lax.all_to_all(rows, BOTH, 0, 0, tiled=True)
        slot = slots(ids, own, mate, first, CAPACITY, local_rows)
        vec = lax.all_gather(vectors.astype(f32), BOTH, axis=0, tiled=True).reshape(-1, width)
        wide = jnp.concatenate([query_key_value_matrix, positions], axis=1)
        wide = lax.all_gather(wide, BOTH, axis=0, tiled=True)
    by_micro = lambda v: v.reshape(micros, 1, slot_count)
    most = most[0, 0]
    flat = lambda v: v.reshape(-1, width)

    def rest(more, collective):
        layer = attend(
            ATTENTION_HEADS, adapter_scale, lengths.T, by_micro(slot), received.reshape(-1, width), more, wide, vec,
            loss_positions, adapter_down_weight.T, adapter_up_weight,
            *(([output_weight, up_weight, down_weight], collective) if direct else ([], None)),
        )
        layer, layer_w = layer[:10], layer[10:]
        h1, low, keys, values, probs, h1_p, low_p, x_p, wanted, attended = layer
        if direct:
            out_w, up_w, down_w, x_pair, attended_pair = (w.reshape(-1, w.shape[-1]) for w in layer_w)
            d_attended, loss = middle(
                lengths.T, loss_positions, flat(attended), flat(x_p), attended_pair, x_pair, flat(wanted), vec,
                out_w, up_w, down_w, token_embedding_table, collective + 1,
            )
        else:
            out_w, up_w, down_w = (
                lax.all_gather(w, BOTH, axis=0, tiled=True) for w in (output_weight, up_weight, down_weight)
            )
            bias = vec[UP_BIAS:-1].reshape(1, ff)
            valid = (loss_positions[:, 0] + 1 < lengths).astype(f32).reshape(-1, 1)
            hidden, before, two, three, inverse = forward(
                flat(attended), flat(x_p), out_w, up_w, down_w, vec, bias
            )
            own_rows = hidden.shape[0]
            every = lax.all_gather(hidden, BOTH, axis=0, tiled=True)
            means, totals = vocabulary(every, token_embedding_table, own_rows, 4 * own_rows)
            part = totals[:, 0, :own_rows].reshape(-1)
            top = lax.pmax(part, BOTH)
            total = top + jnp.log(lax.psum(jnp.exp(part - top), BOTH))
            mean_row = lax.psum_scatter(
                means.astype(f32) * jnp.exp(part - total)[:, None], BOTH, scatter_dimension=0, tiled=True
            )
            total = lax.dynamic_slice_in_dim(total, me * own_rows, own_rows, 0)
            total = jnp.broadcast_to(jnp.pad(total, (0, 128 - own_rows)), (8, 128))
            d_attended, loss = backward(
                mean_row, total, hidden, flat(wanted), valid, before, two, three, inverse, out_w, up_w, down_w, vec
            )
        gradient = attend_back(
            ATTENTION_HEADS, adapter_scale, rank, d_attended.reshape(micros, picks, width),
            h1, low, keys, values, probs, h1_p, low_p, adapter_up_weight, loss,
        )
        if direct:
            return finished(
                gradient, adapter_down_weight.T, adapter_up_weight, left_statistics, right_statistics, collective + 2
            )
        gradient = lax.psum(gradient, BOTH)
        _, new = renewed(gradient, adapter_down_weight.T, adapter_up_weight, left_statistics, right_statistics)
        blocks = lax.all_gather(new, ("fsdp", "dp"))
        blocks = blocks.reshape(lax.axis_size("fsdp"), -1, 8, new.shape[1])
        return [gradient, blocks[:, : left_statistics.shape[0]].reshape(-1, 8, new.shape[1])]

    def another(state):
        step, rows_sum = state
        ids = masked_ids()
        which = step.reshape(1)
        rows, most = select(asked, token_embedding_table, which, CAPACITY)
        if direct:
            received = send_rows(rows, most, 1)[0]
        else:
            received = lax.all_to_all(rows, BOTH, 0, 0, tiled=True)
        slot = slots(ids, own, mate, which, CAPACITY, local_rows)
        found = jnp.take(received.reshape(-1, width), jnp.maximum(slot[0], 0), axis=0)
        found = jnp.where(slot[0][:, None] >= 0, found, jnp.zeros((), bf16))
        return step + 1, rows_sum + found.reshape(micros, slot_count, width)

    def in_rounds():
        more = lax.while_loop(
            lambda state: (state[0] * CAPACITY).astype(f32) < most,
            another,
            (jnp.ones((), jnp.int32), jnp.zeros((micros, slot_count, width), bf16)),
        )[1]
        return rest(more, 5)

    plain = rest(None, 2)
    gradient, blocks = lax.cond(most > CAPACITY, in_rounds, lambda: plain)
    small, down_g, up_g, left_new, right_new, down_new, up_new = settled(
        gradient, blocks, left_statistics, right_statistics
    )
    return small[0, :2], small[0, 2], down_g.T, up_g, left_new, right_new, down_new.T, up_new


def solution(mesh):
    direct = dict(mesh.shape) == {"dp": 8, "fsdp": 4}
    rows = P(BOTH, None)
    placed = (
        P(None, BOTH, None),
        P(None, BOTH),
        P(None, BOTH, None),
        rows,
        rows,
        rows,
        rows,
        rows,
        rows,
        P(BOTH),
        P(),
        P(),
        P("fsdp", None, None),
        P("fsdp", None, None),
    )
    return jax.shard_map(
        functools.partial(on_device, direct),
        mesh=mesh,
        in_specs=placed,
        out_specs=(P(), P(), P(), P(), P("fsdp", None, None), P("fsdp", None, None), P(), P()),
        check_vma=False,
    )
```

```python
import functools
import jax
import jax.numpy as jnp
from jax import lax
from jax.experimental import pallas as pl
from jax.experimental.pallas import tpu as pltpu
from jax.sharding import PartitionSpec as P

ATTENTION_HEADS = 16
STATS_BLOCK_ROWS = 256
NEWTON = 8
CAPACITY = 80

ln_eps = 1e-05
adapter_alpha = 32.0
beta_stats = 0.95
root_eps = 1e-12
clip_level = 0.01
learn_rate = 0.05
masked_score = -1e30

BOTH = ("dp", "fsdp")
MESH = pl.DeviceIdType.MESH
VMEM = pl.BlockSpec(memory_space=pltpu.VMEM)
ANY = pl.BlockSpec(memory_space=pl.ANY)
f32 = jnp.float32
bf16 = jnp.bfloat16


def place():
    d, f = lax.axis_index("dp"), lax.axis_index("fsdp")
    return d // 2, lax.rem(d, 2), f // 2, lax.rem(f, 2)


def target(z, x, y, c):
    return (z * 2 + x, y * 2 + c)


def nth(i):
    return (i // 4, lax.rem(i, 4))


class Greeting:
    def __init__(self, devices):
        self.sem, self.count = pltpu.get_barrier_semaphore(), len(devices)
        for device in devices:
            pl.semaphore_signal(self.sem, inc=1, device_id=device, device_id_type=MESH)

    def wait(self):
        pl.semaphore_wait(self.sem, self.count)


def own_number():
    return lax.axis_index("dp") * 4 + lax.axis_index("fsdp")


def greet_all(count):
    me = own_number()
    return Greeting([nth(lax.rem(me + i, count)) for i in range(1, count)])


def greet_near():
    z, x, y, c = place()
    near = [target(lax.rem(z + i, 4), x, y, c) for i in range(1, 4)]
    near += [target(z, 1 - x, y, c), target(z, x, 1 - y, c), target(z, x, y, 1 - c)]
    return Greeting(near)


def remote(src, dst, send, recv, device):
    return pltpu.make_async_remote_copy(
        src_ref=src, dst_ref=dst, send_sem=send, recv_sem=recv, device_id=device, device_id_type=MESH
    )


def params(collective=None, vmem=60):
    if collective is None:
        return pltpu.CompilerParams(vmem_limit_bytes=vmem * 2**20)
    return pltpu.CompilerParams(
        vmem_limit_bytes=vmem * 2**20, collective_id=collective, has_side_effects=True
    )


def iota(shape, dim):
    return lax.broadcasted_iota(jnp.int32, shape, dim)


def marks(condition):
    return jnp.where(condition, 1.0, 0.0).astype(bf16)


def dot(a, b, ca, cb):
    return lax.dot_general(a, b, (((ca,), (cb,)), ((), ())), preferred_element_type=f32)


GRID = 16


def cells(ids, local_rows):
    owner = jnp.floor((ids.astype(f32) + 0.5) * (1.0 / local_rows)).astype(jnp.int32)
    local = ids - owner * local_rows
    return owner, jnp.where(ids >= 0, owner * GRID + (local >> 7), -1), local & 127


def presence(ids, owners, local_rows):
    width = ids.shape[1]
    _, high, low = cells(ids, local_rows)
    count = dot(
        marks(iota((owners * GRID, width), 0) == high), marks(iota((128, width), 0) == low), 1, 1
    )
    return marks(count > 0.5).reshape(owners, GRID, 128)


def presence_kernel(local_rows, ids_ref, own_ref):
    own_ref[...] = presence(ids_ref[...], own_ref.shape[0], local_rows)


def ranked(present):
    rows = present.shape[0]
    through = dot(present, marks(iota((128, 128), 0) <= iota((128, 128), 1)), 1, 0)
    of = lambda dim: iota((rows, rows), dim)
    earlier = marks((of(1) < of(0)) & (of(0) // GRID == of(1) // GRID))
    row_total = jnp.broadcast_to(through[:, 127:128], (rows, 128)).astype(bf16)
    offset = dot(earlier, row_total, 1, 0)
    has = present.astype(f32)
    return jnp.where(has > 0.5, through - has + offset, -1.0), offset[:, :1] + through[:, 127:128]


def mark_rows(capacity, rank_ref, marks_ref, units, local_rows):
    @pl.loop(0, units)
    def _(unit):
        rows = pl.ds(pl.multiple_of(unit * capacity, 16), capacity)
        own = rank_ref[pl.ds(pl.multiple_of(unit * GRID, GRID), GRID), :]
        for row in range(-(-local_rows // 128)):
            columns = min(128, local_rows - row * 128)
            hit = iota((capacity, 128), 0).astype(f32) == own[row : row + 1, :]
            marks_ref[rows, row * 128 : row * 128 + columns] = marks(hit)[:, :columns]


def select_kernel(capacity, asked_ref, table_ref, round_ref, rows_ref, most_ref, marks_ref, rank_ref):
    units, members = asked_ref.shape[:2]
    local_rows, width = table_ref.shape
    begin = (round_ref[0] * capacity).astype(f32)
    most = jnp.zeros((1, 1), f32)
    for first in range(0, units, 16):
        together = asked_ref[first : first + 16, 0]
        for member in range(1, members):
            together = jnp.maximum(together, asked_ref[first : first + 16, member])
        rank, amount = ranked(together.reshape(-1, 128))
        most = jnp.maximum(most, jnp.max(amount, keepdims=True))
        rank_ref[first * GRID : first * GRID + rank.shape[0]] = rank - begin
    most_ref[...] = jnp.broadcast_to(most, most_ref.shape)
    mark_rows(capacity, rank_ref, marks_ref, units, local_rows)

    @pl.loop(0, units // 4)
    def _(four):
        rows_ref[pl.ds(four * 4, 4)] = look_up(capacity, four, marks_ref, table_ref)


def look_up(capacity, four, marks_ref, table_ref):
    part = pl.ds(pl.multiple_of(four * (4 * capacity), 4 * capacity), 4 * capacity)
    found = dot(marks_ref[part, :], table_ref[...], 1, 0)
    return found.astype(bf16).reshape(4, capacity, table_ref.shape[1])


def select(asked, table, which_round, capacity):
    units = asked.shape[0]
    return pl.pallas_call(
        functools.partial(select_kernel, capacity),
        out_shape=[
            jax.ShapeDtypeStruct((units, capacity, table.shape[1]), bf16),
            jax.ShapeDtypeStruct((8, 128), f32),
        ],
        in_specs=[VMEM, VMEM, pl.BlockSpec(memory_space=pltpu.SMEM)],
        out_specs=[VMEM] * 2,
        scratch_shapes=[
            pltpu.VMEM((units * capacity, table.shape[0]), bf16),
            pltpu.VMEM((units * GRID, 128), f32),
        ],
        compiler_params=params(),
        name="select",
    )(asked, table, which_round)


def slots_of(capacity, begin, local_rows, ids, own_ref, mate_ref):
    owner, high, low = cells(ids, local_rows)
    width = ids.shape[1]
    own_rank = jnp.zeros((1, width), f32)
    for first in range(0, own_ref.shape[0], 16):
        together = jnp.maximum(own_ref[first : first + 16], mate_ref[first : first + 16])
        rank, _ = ranked(together.reshape(-1, 128))
        rank = rank - begin
        rank = jnp.where((rank >= 0.0) & (rank < capacity), rank + 1.0, 0.0)
        rows = rank.shape[0]
        of_low = dot(rank.astype(bf16), marks(iota((rows, width), 0) + first * GRID == high), 0, 0)
        own_rank += jnp.sum(
            jnp.where(iota((128, width), 0) == low, of_low, 0.0), axis=0, keepdims=True
        )
    slot = owner * capacity + own_rank.astype(jnp.int32) - 1
    return jnp.where(own_rank > 0.5, slot, -1)


def slots_kernel(capacity, local_rows, ids_ref, own_ref, mate_ref, round_ref, slot_ref):
    begin = (round_ref[0] * capacity).astype(f32)
    slot_ref[...] = slots_of(capacity, begin, local_rows, ids_ref[...], own_ref, mate_ref)


def slots(ids, own, mate, which_round, capacity, local_rows):
    return pl.pallas_call(
        functools.partial(slots_kernel, capacity, local_rows),
        out_shape=jax.ShapeDtypeStruct(ids.shape, jnp.int32),
        in_specs=[VMEM] * 3 + [pl.BlockSpec(memory_space=pltpu.SMEM)],
        out_specs=VMEM,
        compiler_params=params(),
        name="slots",
    )(ids, own, mate, which_round)


class Piece:
    def __init__(self, sources, out, sems):
        self.sources, self.out, self.rows = sources, out, out.shape[4]
        self.own_sems, self.chain_sems, self.plane_sems, self.core_sems = sems
        self.z, self.x, self.y, self.c = place()

    def at(self, zz, xx, yy, cc, half=None):
        ref = self.out.at[zz, xx, yy, cc]
        return ref if half is None else self.out.at[zz, xx, yy, cc, pl.ds(half * (self.rows // 2), self.rows // 2)]

    def own(self):
        copies, begin = [], 0
        for k, src in enumerate(self.sources):
            dst = self.out.at[self.z, self.x, self.y, self.c, :, pl.ds(begin, src.shape[1])]
            copies.append(pltpu.make_async_copy(src, dst, self.own_sems.at[k]))
            begin += src.shape[1]
        return copies

    def chain(self, zz, way, incoming=False):
        z, x, y, c = self.z, self.x, self.y, self.c
        ref = self.at(zz, x, y, c)
        k = (way + 1) // 2
        to = target(z - way if incoming else z + way, x, y, c)
        return remote(ref, ref, self.chain_sems.at[0, k, zz], self.chain_sems.at[1, k, zz], to)

    def plane(self, zz, step, incoming=False):
        z, x, y, c = self.z, self.x, self.y, self.c
        every = slice(None)
        over_x, over_y = target(z, 1 - x, y, c), target(z, x, 1 - y, c)
        xx, yy = (1 - x, 1 - y) if incoming else (x, y)
        if step == 0:
            pairs = ((self.at(zz, xx, y, c, 0), over_x), (self.at(zz, x, yy, c, 1), over_y))
        else:
            pairs = ((self.at(zz, every, yy, c, 0), over_y), (self.at(zz, xx, every, c, 1), over_x))
        return [
            remote(ref, ref, self.plane_sems.at[0, zz, step, k], self.plane_sems.at[1, zz, step, k], to)
            for k, (ref, to) in enumerate(pairs)
        ]

    def mate(self, zz, incoming=False):
        z, x, y, c = self.z, self.x, self.y, self.c
        ref = self.at(zz, slice(None), slice(None), 1 - c if incoming else c)
        return remote(ref, ref, self.core_sems.at[0, zz], self.core_sems.at[1, zz], target(z, x, y, 1 - c))

    def arrivals(self, step, act):
        for way in (1, -1):
            zz = self.z - way * (step + 1)

            @pl.when((zz >= 0) & (zz < 4))
            def _(zz=zz, way=way):
                act(zz, way)

    def pass_on(self, zz, way):
        @pl.when((self.z + way >= 0) & (self.z + way < 4))
        def _():
            self.chain(zz, way).start()

    def first(self, zz):
        for copy in self.plane(zz, 0):
            copy.start()

    def load(self):
        for copy in self.own():
            copy.start()

    def start(self):
        for copy in self.own():
            copy.wait()
        for way in (1, -1):
            self.pass_on(self.z, way)
        self.first(self.z)

    def arrive(self, step):
        def act(zz, way):
            self.chain(zz, way, True).wait_recv()
            self.pass_on(zz, way)
            self.first(zz)

        self.arrivals(step, act)

    def second_of(self, zz, way=None):
        for copy in self.plane(zz, 0, True):
            copy.wait_recv()
        for copy in self.plane(zz, 1):
            copy.start()

    def third_of(self, zz, way=None):
        for copy in self.plane(zz, 1, True):
            copy.wait_recv()
        self.mate(zz).start()

    def second(self, step=None):
        if step is None:
            self.second_of(self.z)
        else:
            self.arrivals(step, self.second_of)

    def third(self, step=None):
        if step is None:
            self.third_of(self.z)
        else:
            self.arrivals(step, self.third_of)

    def finish(self, incoming=True):
        for zz in range(4):
            for step in range(2):
                for copy in self.plane(zz, step):
                    copy.wait_send()
        for zz in range(4):
            self.mate(zz).wait_send()
            if incoming:
                self.mate(zz, True).wait_recv()
        for way in (1, -1):

            @pl.when((self.z + way >= 0) & (self.z + way < 4))
            def _(way=way):
                for step in range(3):
                    zz = self.z - way * step

                    @pl.when((zz >= 0) & (zz < 4))
                    def _(zz=zz):
                        self.chain(zz, way).wait_send()


class Spread(Piece):
    def __init__(self, out, sems):
        super().__init__([], out, (None, None) + tuple(sems))

    def finish(self):
        for k in range(self.out.shape[0]):
            for step in range(2):
                for copy in self.plane(k, step):
                    copy.wait_send()
            self.mate(k).wait_send()
            self.mate(k, True).wait_recv()


class LayerWeights:
    def __init__(self, ins, outs, sems):
        (self.out_in, self.up_in, self.down_in), (out, self.up, self.down) = ins, outs
        self.own_sems, self.z_sems, sems = sems[0], sems[1], sems[2:]
        self.output = Piece([self.out_in], out, sems[:4])
        self.ups, self.downs = Spread(self.up, sems[4:6]), Spread(self.down, sems[6:8])
        self.z, self.x, self.y, self.c = place()
        self.side = lax.rem(self.z, 2)
        self.planes = (self.z, self.z + 1 - 2 * self.side, lax.rem(self.z + 2, 4), 3 - self.z)

    def up_block(self, side, k):
        size = self.up.shape[5] // 2
        return self.up_in.at[:, pl.ds(pl.multiple_of((2 * k + side) * size, 128), size)]

    def up_place(self, zz, k):
        size = self.up.shape[5] // 2
        return self.up.at[zz, self.x, self.y, self.c, :, pl.ds(k * size, size)]

    def owned(self):
        return [
            pltpu.make_async_copy(self.up_block(self.side, k), self.up_place(self.z, k), self.own_sems.at[k])
            for k in range(2)
        ] + [
            pltpu.make_async_copy(
                self.down_in, self.down.at[self.z // 2, self.x, self.y, self.c], self.own_sems.at[2]
            )
        ]

    def up_copies(self, i, incoming=False):
        other = self.planes[i]
        frm = other if incoming else self.z
        return [
            remote(
                self.up_block(lax.rem(other, 2), k), self.up_place(frm, k),
                self.z_sems.at[0, k, other], self.z_sems.at[1, k, frm], target(other, self.x, self.y, self.c),
            )
            for k in range(2)
        ]

    def down_copy(self, incoming=False):
        other = self.planes[2]
        frm = other if incoming else self.z
        return remote(
            self.down_in, self.down.at[frm // 2, self.x, self.y, self.c],
            self.z_sems.at[0, 2, other], self.z_sems.at[1, 2, frm], target(other, self.x, self.y, self.c),
        )

    def load(self):
        self.output.load()
        for copy in self.owned():
            copy.start()

    def send_up(self, i):
        for copy in self.up_copies(i):
            copy.start()

    def start(self):
        self.output.start()
        for copy in self.owned():
            copy.wait()
        self.downs.first(self.z // 2)
        self.ups.first(self.z)
        self.send_up(1)
        self.down_copy().start()

    def arrive_up(self, i):
        for copy in self.up_copies(i, True):
            copy.wait_recv()
        self.ups.first(self.planes[i])

    def arrive_down(self):
        self.down_copy(True).wait_recv()
        self.downs.first(self.planes[2] // 2)

    def steps(self):
        ups, downs, output, planes = self.ups, self.downs, self.output, self.planes
        here, there = self.z // 2, planes[2] // 2
        return [
            lambda: (
                output.arrive(0), downs.second_of(here), ups.second_of(planes[0]), output.second(),
                self.arrive_up(1), self.send_up(2),
            ),
            lambda: (
                output.arrive(1), downs.third_of(here), ups.third_of(planes[0]), self.arrive_down(),
                ups.second_of(planes[1]), output.second(0), output.third(), self.send_up(3),
            ),
            lambda: (
                output.arrive(2), self.arrive_up(2), downs.second_of(there), ups.third_of(planes[1]),
                output.third(0), output.second(1),
            ),
            lambda: (
                self.arrive_up(3), ups.second_of(planes[2]), downs.third_of(there), output.third(1),
                output.second(2),
            ),
            lambda: (ups.second_of(planes[3]), ups.third_of(planes[2]), output.third(2)),
            lambda: ups.third_of(planes[3]),
        ]

    def finish(self):
        for i in range(1, 4):
            for copy in self.up_copies(i):
                copy.wait_send()
        self.down_copy().wait_send()
        self.ups.finish()
        self.downs.finish()
        self.output.finish()

    @staticmethod
    def shapes(weights):
        if not weights:
            return []
        out, up, down = weights
        return shares([out]) + [
            jax.ShapeDtypeStruct((4, 2, 2, 2, up.shape[0], up.shape[1] // 2), bf16),
            jax.ShapeDtypeStruct((2, 2, 2, 2) + down.shape, bf16),
        ]

    @staticmethod
    def scratch(weights):
        if not weights:
            return []
        spread = [pltpu.SemaphoreType.DMA((2, 4, 2, 2)), pltpu.SemaphoreType.DMA((2, 4))]
        return (
            [pltpu.SemaphoreType.DMA((3,)), pltpu.SemaphoreType.DMA((2, 3, 4))] + piece_scratch(1) + spread * 2
        )


def shares(weights):
    return [jax.ShapeDtypeStruct((4, 2, 2, 2) + w.shape, w.dtype) for w in weights]


def piece_scratch(count):
    return [
        pltpu.SemaphoreType.DMA((2,)),
        pltpu.SemaphoreType.DMA((2, 2, 4)),
        pltpu.SemaphoreType.DMA((2, 4, 2, 2)),
        pltpu.SemaphoreType.DMA((2, 4)),
    ] * count


class Rows:
    def __init__(self, rows_ref, most_ref, rows_out, most_out, sems):
        self.own_refs, self.outs = (rows_ref, most_ref), (rows_out, most_out)
        self.sems, self.mate_sems, self.own_sems = sems
        self.z, self.x, self.y, self.c = place()
        self.chip = (self.z * 2 + self.x) * 2 + self.y

    def out(self, k, to):
        device = target(to // 4, lax.rem(to // 2, 2), lax.rem(to, 2), self.c)
        src = self.own_refs[k].at[to] if k == 0 else self.own_refs[k]
        return remote(
            src, self.outs[k].at[self.chip, self.c], self.sems.at[0, k, to], self.sems.at[1, k, self.chip], device
        )

    def into(self, k, frm):
        device = target(frm // 4, lax.rem(frm // 2, 2), lax.rem(frm, 2), self.c)
        dst = self.outs[k].at[frm, self.c]
        return remote(dst, dst, self.sems.at[0, k, frm], self.sems.at[1, k, frm], device)

    def mate(self, k, of, core):
        ref = self.outs[k].at[of, core]
        to = target(self.z, self.x, self.y, 1 - self.c)
        return remote(ref, ref, self.mate_sems.at[0, k, of], self.mate_sems.at[1, k, of], to)

    def own(self, k):
        src = self.own_refs[k].at[self.chip] if k == 0 else self.own_refs[k]
        return pltpu.make_async_copy(src, self.outs[k].at[self.chip, self.c], self.own_sems.at[k])

    def send(self, to):
        @pl.when(to == self.chip)
        def _():
            for k in range(2):
                self.own(k).start()

        @pl.when(to != self.chip)
        def _():
            for k in range(2):
                self.out(k, to).start()

    def forward(self):
        for k in range(2):
            self.own(k).wait()
            self.mate(k, self.chip, self.c).start()
        for i in range(1, 16):
            frm = lax.rem(self.chip + 16 - i, 16)
            for k in range(2):
                self.into(k, frm).wait_recv()
                self.mate(k, frm, self.c).start()

    def finish(self):
        for i in range(16):
            of = lax.rem(self.chip + i, 16)
            for k in range(2):
                self.mate(k, of, self.c).wait_send()
                self.mate(k, of, 1 - self.c).wait_recv()
                if i:
                    self.out(k, of).wait_send()

    @staticmethod
    def shapes(rows, most):
        return [
            jax.ShapeDtypeStruct((16, 2) + rows[1:], bf16),
            jax.ShapeDtypeStruct((16, 2) + most, f32),
        ]

    @staticmethod
    def scratch():
        return [
            pltpu.SemaphoreType.DMA((2, 2, 16)),
            pltpu.SemaphoreType.DMA((2, 2, 16)),
            pltpu.SemaphoreType.DMA((2,)),
        ]


def rows_kernel(rows_ref, most_ref, rows_out, most_out, *sems):
    greet_all(32).wait()
    rows = Rows(rows_ref, most_ref, rows_out, most_out, sems)
    for to in range(16):
        rows.send(to)
    rows.forward()
    rows.finish()


def send_rows(rows, most, collective):
    return pl.pallas_call(
        rows_kernel,
        out_shape=Rows.shapes(rows.shape, most.shape),
        in_specs=[VMEM] * 2,
        out_specs=[ANY, VMEM],
        scratch_shapes=Rows.scratch(),
        compiler_params=params(collective),
        name="send_rows",
    )(rows, most)


def fetch_kernel(
    capacity, lens_ref, ids_ref, vec_ref, table_ref, qkv_ref, pos_ref,
    received_ref, most_ref, slot_ref, asked_ref, own_ref, mate_ref, vec_out, w_out,
    marks_ref, rank_ref, rows_ref, count_ref, mosts_ref, pack_ref, packs_ref, *sems,
):
    ask_sems, mate_sems = sems[:2]
    rows = Rows(rows_ref, count_ref, received_ref, mosts_ref, sems[2:5])
    piece = Piece([qkv_ref, pos_ref], w_out, sems[5:])
    greeting = greet_all(32)
    piece.load()
    local_rows = table_ref.shape[0]
    ids = jnp.concatenate(
        [
            jnp.where(iota(ids_ref.shape[1:], 1) < lens_ref[0, m], ids_ref[m], -1)
            for m in range(ids_ref.shape[0])
        ],
        axis=1,
    )
    own_ref[...] = presence(ids, 32, local_rows)
    length = vec_ref.shape[0]
    vec = jnp.pad(vec_ref[...].astype(f32).reshape(1, length), ((0, 0), (0, 1024 - length)))
    pack_ref[...] = jnp.concatenate([vec[:, k * 128 : (k + 1) * 128] for k in range(8)])
    me = own_number()
    z, x, y, c = place()
    to_mate = remote(own_ref, mate_ref, mate_sems.at[0], mate_sems.at[1], target(z, x, y, 1 - c))
    greeting.wait()

    def to_all(k, src, dst):
        copies = []
        for i in range(1, 32):
            to = lax.rem(me + i, 32)
            own = src.at[to] if k == 0 else src
            copies.append(remote(own, dst.at[me], ask_sems.at[0, k, i], ask_sems.at[1, k, i], nth(to)))
            copies[-1].start()
        return copies

    copies = to_all(0, own_ref, asked_ref)
    piece.start()
    to_mate.start()
    packs = to_all(1, pack_ref, packs_ref)
    asked_ref[me] = own_ref[me]
    packs_ref[me] = pack_ref[...]
    for copy in copies:
        copy.wait()
    together = jnp.concatenate(
        [jnp.maximum(asked_ref[2 * unit], asked_ref[2 * unit + 1]) for unit in range(16)]
    )
    rank, amount = ranked(together)
    count_ref[...] = jnp.broadcast_to(jnp.max(amount, keepdims=True), count_ref.shape)
    rank_ref[...] = rank
    mark_rows(capacity, rank_ref, marks_ref, 16, local_rows)
    piece.second()
    piece.arrive(0)
    planes = [lax.rem(z + i, 4) for i in (2, 3, 1, 0)]
    for plane in planes:
        rows_ref[pl.ds(plane * 4, 4)] = look_up(capacity, plane, marks_ref, table_ref)
    piece.second(0)
    piece.arrive(1)
    for plane in planes:
        for k in range(4):
            rows.send(plane * 4 + lax.rem(x * 2 + y + k, 4))
    piece.third()
    piece.second(1)
    piece.third(0)
    to_mate.wait()
    slot_ref[...] = slots_of(capacity, 0.0, local_rows, ids, own_ref, mate_ref)
    for copy in packs:
        copy.wait()
    width = vec_out.shape[1]
    for device in range(32):
        for k in range(-(-length // 128)):
            begin, end = k * 128, min(length, k * 128 + 128)
            at = device * length + begin
            while begin < end:
                count = min(end - begin, 128 - at % 128)
                vec_out[at // width : at // width + 1, at % width : at % width + count] = packs_ref[
                    device, k : k + 1, begin - k * 128 : begin - k * 128 + count
                ]
                at, begin = at + count, begin + count
    piece.arrive(2)
    piece.third(1)
    piece.second(2)
    piece.third(2)
    rows.forward()
    rows.finish()
    piece.finish()
    most_ref[0] = jnp.max(mosts_ref[...])


def fetch(lens, ids, vec, table, qkv, positions, capacity, collective):
    grids = jax.ShapeDtypeStruct((32, GRID, 128), bf16)
    width = table.shape[1]
    w = jax.ShapeDtypeStruct((qkv.shape[0], qkv.shape[1] + positions.shape[1]), bf16)
    return pl.pallas_call(
        functools.partial(fetch_kernel, capacity),
        out_shape=[
            jax.ShapeDtypeStruct((16, 2, capacity, width), bf16), jax.ShapeDtypeStruct((1,), f32),
            jax.ShapeDtypeStruct((1, ids.size), jnp.int32), grids, grids, grids,
            jax.ShapeDtypeStruct((32 * vec.shape[0] // width, width), f32),
        ]
        + shares([w]),
        in_specs=[pl.BlockSpec(memory_space=pltpu.SMEM)] + [VMEM] * 3 + [ANY] * 2,
        out_specs=[ANY, pl.BlockSpec(memory_space=pltpu.SMEM)] + [VMEM] * 5 + [ANY],
        scratch_shapes=[
            pltpu.VMEM((16 * capacity, table.shape[0]), bf16),
            pltpu.VMEM((16 * GRID, 128), f32),
            pltpu.VMEM((16, capacity, width), bf16),
            pltpu.VMEM((8, 128), f32),
            pltpu.VMEM((16, 2, 8, 128), f32),
            pltpu.VMEM((8, 128), f32),
            pltpu.VMEM((32, 8, 128), f32),
            pltpu.SemaphoreType.DMA((2, 2, 32)),
            pltpu.SemaphoreType.DMA((2,)),
        ]
        + Rows.scratch()
        + piece_scratch(1),
        compiler_params=params(collective),
        name="fetch",
    )(lens, ids, vec, table, qkv, positions)


def vocabulary_kernel(group, rows_ref, table_ref, mean_ref, total_ref):
    logits = dot(rows_ref[...], table_ref[...], 1, 1)
    top = jnp.max(logits, axis=1, keepdims=True)
    weights = jnp.exp(logits - top)
    amount = jnp.sum(weights, axis=1, keepdims=True)
    mean = dot(weights.astype(bf16), table_ref[...], 1, 0)
    mean_ref[...] = (mean / amount).astype(bf16)
    total = top + jnp.log(amount)
    for k in range(total_ref.shape[0]):
        total_ref[k] = as_tile(as_row(total[k * group : (k + 1) * group]))


def as_tile(row):
    return jnp.broadcast_to(jnp.pad(row, ((0, 0), (0, 128 - row.shape[1]))), (8, 128))


def same(size):
    return iota((size, size), 0) == iota((size, size), 1)


def as_row(column):
    return jnp.sum(jnp.where(same(column.shape[0]), column, 0.0), axis=0, keepdims=True)


def as_column(row):
    return jnp.sum(jnp.where(same(row.shape[1]), row, 0.0), axis=1, keepdims=True)


def vocabulary(rows, table, group, tile):
    count, width = rows.shape
    return pl.pallas_call(
        functools.partial(vocabulary_kernel, group),
        grid=(count // tile,),
        out_shape=[
            jax.ShapeDtypeStruct((count, width), bf16),
            jax.ShapeDtypeStruct((count // group, 8, 128), f32),
        ],
        in_specs=[
            pl.BlockSpec((tile, width), lambda i: (i, 0)),
            pl.BlockSpec(table.shape, lambda i: (0, 0)),
        ],
        out_specs=[
            pl.BlockSpec((tile, width), lambda i: (i, 0)),
            pl.BlockSpec((tile // group, 8, 128), lambda i: (i, 0, 0)),
        ],
        compiler_params=params(),
        name="vocabulary",
    )(rows, table)


def merged(parts):
    size = parts[0][0].shape[0]
    rows = [total[:1, :size] for _, total in parts]
    top = functools.reduce(jnp.maximum, rows)
    total = top + jnp.log(sum(jnp.exp(row - top) for row in rows))
    mean = sum(
        values.astype(f32) * as_column(jnp.exp(row - total)) for (values, _), row in zip(parts, rows)
    )
    return mean, as_tile(total)


def exact(a, b, ca, cb):
    return lax.dot_general(
        a, b, (((ca,), (cb,)), ((), ())), precision=lax.Precision.HIGHEST, preferred_element_type=f32
    )


def fine(a, b, cb):
    a_high, b_high = a.astype(bf16), b.astype(bf16)
    a_low, b_low = (a - a_high.astype(f32)).astype(bf16), (b - b_high.astype(f32)).astype(bf16)
    return dot(a_high, b_high, 1, cb) + (dot(a_high, b_low, 1, cb) + dot(a_low, b_high, 1, cb))


def small_product(a, b):
    return sum(a[:, k : k + 1] * b[k : k + 1, :] for k in range(a.shape[0]))


def newton(matrix, product, apply, state):
    size = matrix.shape[0]
    identity = jnp.where(same(size), 1.0, 0.0)
    trace = jnp.sum(matrix * identity, keepdims=True)

    def step(_, carry):
        current, state = carry
        factor = (5.0 * identity - current) * 0.25
        square = product(factor, factor)
        return product(product(square, square), current), apply(state, factor)

    current, state = lax.fori_loop(0, NEWTON - 1, step, (matrix / trace, state))
    state = apply(state, (5.0 * identity - current) * 0.25)
    return state * lax.rsqrt(jnp.sqrt(trace))


def clipped(g_ref, rank):
    data = jnp.where(iota(g_ref.shape, 1) < rank, g_ref[...], 0.0)
    norm = jnp.sqrt(jnp.sum(data * data, keepdims=True).reshape(1, 1))
    return data * (clip_level / jnp.maximum(norm, clip_level)), norm


def renew(g_ref, down_ref, up_ref, left_ref, right_ref, clip_ref, new_ref):
    owned, block = left_ref.shape[0], left_ref.shape[1]
    rank = right_ref.shape[1]
    group = lax.axis_index("fsdp")
    own = lax.rem(lax.axis_index("dp"), owned)
    clip_ref[...], _ = clipped(g_ref, rank)
    columns = pl.ds(pl.multiple_of(own * block, block), block)
    grad = clip_ref[group, :, columns]
    left, right = stats_of(left_ref[own], right_ref[own], grad)
    left = left + root_eps * jnp.where(same(block), 1.0, 0.0)
    right = right + root_eps * jnp.where(same(rank), 1.0, 0.0)
    root = newton(right, small_product, small_product, jnp.where(same(rank), 1.0, 0.0))
    rows = newton(left, lambda a, b: fine(a, b, 0), lambda a, b: fine(a, b, 1), grad)[:rank]
    update = sum(as_column(root[k : k + 1, :]) * rows[k : k + 1, :] for k in range(rank))
    old = [ref[k * rank : (k + 1) * rank, columns] for ref in (down_ref, up_ref) for k in range(2)]
    old = functools.reduce(lambda a, k: jnp.where(group == k, old[k], a), range(1, 4), old[0])
    new = old - learn_rate * update
    new_ref[...] = jnp.pad(new, ((0, 8 - rank), (0, 0)))


def stats_of(left, right, grad):
    rank = right.shape[0]
    return (
        beta_stats * left + (1.0 - beta_stats) * exact(grad, grad, 0, 0),
        beta_stats * right + (1.0 - beta_stats) * exact(grad, grad, 1, 1)[:rank, :rank],
    )


def settle_kernel(g_ref, all_ref, left_ref, right_ref, loss_ref, norm_ref, a_ref, b_ref, left_out, right_out, a_new, b_new, clip_ref):
    owned, block = left_ref.shape[0], left_ref.shape[1]
    rank = right_ref.shape[1]
    clip_ref[...], norm = clipped(g_ref, rank)
    norm_ref[0] = jnp.sum(norm)
    for k in range(2):
        loss_ref[k] = jnp.sum(g_ref[0, rank : rank + 1, k : k + 1])
    a_ref[...] = jnp.concatenate([clip_ref[0, :rank], clip_ref[1, :rank]])
    b_ref[...] = jnp.concatenate([clip_ref[2, :rank], clip_ref[3, :rank]])
    group = lax.axis_index("fsdp")
    for k in range(owned):
        grad = clip_ref[group, :, k * block : (k + 1) * block]
        left_out[k], right_out[k] = stats_of(left_ref[k], right_ref[k], grad)
    for k in range(all_ref.shape[0]):
        ref, row = (a_new, b_new)[k // 8], k // 4 % 2 * rank
        ref[row : row + rank, k % 4 * block : (k % 4 + 1) * block] = all_ref[k, :rank]


def settled(gradient, blocks, left, right):
    width = gradient.shape[2]
    shapes = [(2,), (1,), (8, width), (8, width), left.shape, right.shape, (8, width), (8, width)]
    return pl.pallas_call(
        settle_kernel,
        out_shape=[jax.ShapeDtypeStruct(shape, f32) for shape in shapes],
        in_specs=[VMEM] * 4,
        out_specs=[pl.BlockSpec(memory_space=pltpu.SMEM)] * 2 + [VMEM] * 6,
        scratch_shapes=[pltpu.VMEM(gradient.shape, f32)],
        compiler_params=params(),
        name="settled",
    )(gradient, blocks, left, right)


def renew_kernel(*refs):
    renew(*refs)


def renewed(gradient, down, up, left, right):
    return pl.pallas_call(
        renew_kernel,
        out_shape=[
            jax.ShapeDtypeStruct(gradient.shape, f32), jax.ShapeDtypeStruct((8, left.shape[1]), f32),
        ],
        in_specs=[VMEM] * 5,
        out_specs=[VMEM] * 2,
        compiler_params=params(),
        name="renewed",
    )(gradient, down, up, left, right)


def finish_kernel(
    back, count, *refs,
):
    back_in, refs = refs[:count], refs[count:]
    (down_ref, up_ref, left_ref, right_ref, total_out, all_out), refs = refs[:6], refs[6:]
    (total_ref, all_ref, g_ref, dq_ref, dlow_ref), refs = refs[:5], refs[5:]

    @pl.when(pl.program_id(0) == 0)
    def _():
        greet_all(32)

    back(*back_in, g_ref, dq_ref, dlow_ref)

    @pl.when(pl.program_id(0) == pl.num_programs(0) - 1)
    def _():
        pl.semaphore_wait(pltpu.get_barrier_semaphore(), 31)
        finish(g_ref, down_ref, up_ref, left_ref, right_ref, total_ref, all_ref, *refs)
        total_out[...] = total_ref[...]
        all_out[...] = all_ref[...]


def finish(
    g_ref, down_ref, up_ref, left_ref, right_ref, total_ref, all_ref,
    parts, summed, clip_ref, new_ref, one_sems, two_sems, block_sems,
):
    me = own_number()

    def tile(ref, k):
        return ref.at[k // 8, :, pl.ds(pl.multiple_of(lax.rem(k, 8) * 128, 128), 128)]

    def out(i):
        to = lax.rem(me + i, 32)
        return remote(tile(g_ref, to), parts.at[me], one_sems.at[0, to], one_sems.at[1, me], nth(to))

    def into(i):
        frm = lax.rem(me + i, 32)
        return remote(tile(g_ref, me), parts.at[frm], one_sems.at[0, frm], one_sems.at[1, frm], nth(frm))

    def back(i):
        to = lax.rem(me + i, 32)
        return remote(summed, tile(total_ref, me), two_sems.at[0, to], two_sems.at[1, me], nth(to))

    def into_back(i):
        frm = lax.rem(me + i, 32)
        return remote(summed, tile(total_ref, frm), two_sems.at[0, frm], two_sems.at[1, frm], nth(frm))

    for i in range(1, 32):
        out(i).start()
    columns = pl.ds(pl.multiple_of(lax.rem(me, 8) * 128, 128), 128)
    for i in range(1, 32):
        into(i).wait_recv()
    running = g_ref[me // 8, :, columns]
    for i in range(1, 32):
        running = running + parts[lax.rem(me + i, 32)]
    summed[...] = running
    total_ref[me // 8, :, columns] = running
    for i in range(1, 32):
        back(i).start()
    for i in range(1, 32):
        into_back(i).wait_recv()
    renew(total_ref, down_ref, up_ref, left_ref, right_ref, clip_ref, new_ref)
    d, f = lax.axis_index("dp"), lax.axis_index("fsdp")
    half, mine = d // 4, f * 4 + lax.rem(d, 4)

    def share(i, incoming=False):
        k = lax.rem(mine + i, 16)
        device = (half * 4 + lax.rem(k, 4), k // 4)
        return remote(
            new_ref, all_ref.at[k if incoming else mine],
            block_sems.at[0, k], block_sems.at[1, k if incoming else mine], device,
        )

    for i in range(1, 16):
        share(i).start()
    all_ref[mine] = new_ref[...]
    for i in range(1, 16):
        share(i, True).wait_recv()
    for i in range(1, 16):
        share(i).wait_send()
    for i in range(1, 32):
        out(i).wait_send()
        back(i).wait_send()


def finished(back, down, up, left, right, collective):
    new = (8, left.shape[1])
    shape = back["shape"]
    return pl.pallas_call(
        functools.partial(finish_kernel, back["kernel"], len(back["args"])),
        grid=back["grid"],
        out_shape=[jax.ShapeDtypeStruct(shape, f32), jax.ShapeDtypeStruct((16,) + new, f32)],
        in_specs=back["in_specs"] + [whole(v.shape) for v in (down, up, left, right)],
        out_specs=[whole(shape), whole((16,) + new)],
        scratch_shapes=[pltpu.VMEM(shape, f32), pltpu.VMEM((16,) + new, f32), pltpu.VMEM(shape, f32)]
        + back["scratch_shapes"]
        + [
            pltpu.VMEM((32, 8, 128), f32),
            pltpu.VMEM((8, 128), f32),
            pltpu.VMEM(shape, f32),
            pltpu.VMEM(new, f32),
            pltpu.SemaphoreType.DMA((2, 32)),
            pltpu.SemaphoreType.DMA((2, 32)),
            pltpu.SemaphoreType.DMA((2, 16)),
        ],
        compiler_params=params(collective),
        name="finished",
    )(*back["args"], down, up, left, right)


def normal(v, gain, shift):
    centred = v - jnp.mean(v, axis=-1, keepdims=True)
    inverse = lax.rsqrt(jnp.mean(centred * centred, axis=-1, keepdims=True) + ln_eps)
    normed = centred * inverse
    return normed * gain + shift, normed, inverse


def normal_back(grad, gain, normed, inverse):
    scaled = grad * gain
    return inverse * (
        scaled
        - jnp.mean(scaled, axis=-1, keepdims=True)
        - normed * jnp.mean(scaled * normed, axis=-1, keepdims=True)
    )


GAIN, SHIFT, QKV_BIAS, OUT_BIAS, UP_BIAS = (0, 2, 4), (1, 3, 5), 6, 9, 10


def expand_chunk(slot_ref, rows_ref, begin, chunk):
    count = rows_ref.shape[0]
    part = lambda k: slot_ref[0, :, pl.ds(pl.multiple_of(begin + k, 128), 128)].astype(f32)
    column = jnp.concatenate([as_column(part(k)) for k in range(0, chunk, 128)]).astype(jnp.int32)
    return dot(marks(iota((chunk, count), 1) == column), rows_ref[...], 1, 0)


def spread_heads(v, heads, size):
    rows, width = v.shape
    tiled = jnp.concatenate([v] * heads, axis=0)
    shape = (heads * rows, width)
    return jnp.where(iota(shape, 0) // rows == iota(shape, 1) // size, tiled, jnp.zeros((), v.dtype))


def join_heads(v, heads, size):
    rows = v.shape[0] // heads
    own = jnp.where(iota(v.shape, 0) // rows == iota(v.shape, 1) // size, v, 0.0)
    return sum(own[k * rows : (k + 1) * rows] for k in range(heads))


def two_sets(v, rows):
    rank, width = v.shape[0] // 2, v.shape[1]
    v = v.astype(bf16)
    zeros = lambda count: jnp.zeros((count, width), bf16)
    return jnp.concatenate([v[:rank], zeros(8 - rank), v[rank:], zeros(rows - 8 - rank)])


def attend_kernel(
    heads, adapter_scale, count_w, with_more, lens_ref, slot_ref, rows_hbm, wide_hbm, vec_ref, pick_ref,
    down_ref, up_ref, *refs,
):
    if with_more:
        more_ref, *refs = refs
    w_in, refs = refs[:count_w], refs[count_w:]
    (h1_ref, low_ref, k_ref, v_ref, p_ref, h1p_ref, lowp_ref, xp_ref, wanted_ref, att_ref), refs = refs[:10], refs[10:]
    w_out, refs = refs[:count_w], refs[count_w:]
    if count_w:
        (xp_pair, att_pair), refs = refs[:2], refs[2:]
    (emb_ref, q_ref, rows_ref, pos_ref, qkv_ref, load_sems), sems = refs[:6], refs[6:]
    if count_w:
        (xp_own, att_own, pair_sems), sems = sems[:3], sems[3:]
    micro = pl.program_id(0)
    count, width = emb_ref.shape
    length = lens_ref[0, micro]
    down, up = two_sets(down_ref[...], 128), two_sets(up_ref[...], 16)
    size = width // heads
    chunk = 256
    vec = lambda k: vec_ref[k : k + 1, :]
    if count_w:
        gather = LayerWeights(w_in, w_out, sems)
        steps = gather.steps()

        def to_pair(m):
            device = target(gather.planes[1], gather.x, gather.y, gather.c)
            return [
                remote(src.at[m], dst.at[m], pair_sems.at[0, k, m], pair_sems.at[1, k, m], device)
                for k, (src, dst) in enumerate(((xp_own, xp_pair), (att_own, att_pair)))
            ]

    def beside(loop):
        for number, step in enumerate(steps if count_w else []):
            if number % 3 == loop:

                @pl.when(micro == number // 3)
                def _(step=step):
                    step()

    parts = ((rows_hbm, rows_ref), (wide_hbm.at[:, 3 * width :], pos_ref), (wide_hbm.at[:, : 3 * width], qkv_ref))
    loads = [pltpu.make_async_copy(src, dst, load_sems.at[k]) for k, (src, dst) in enumerate(parts)]

    @pl.when(micro == 0)
    def _():
        if count_w:
            greeting = greet_near()
        for load in loads:
            load.start()
        if count_w:
            gather.load()
            greeting.wait()
            gather.start()
        for load in loads[:2]:
            load.wait()

    @pl.loop(0, count // chunk)
    def _(k):
        rows = pl.ds(pl.multiple_of(k * chunk, chunk), chunk)
        emb = expand_chunk(slot_ref, rows_ref, k * chunk, chunk).astype(bf16)
        if with_more:
            emb = emb + more_ref[0, rows]
        emb_ref[rows] = emb
        x = emb.astype(f32) + pos_ref[rows].astype(f32)
        h1_ref[0, rows] = normal(x, vec(GAIN[0]), vec(SHIFT[0]))[0].astype(bf16)

    @pl.when(micro == 0)
    def _():
        loads[2].wait()

    beside(0)

    @pl.loop(0, count // chunk)
    def _(k):
        rows = pl.ds(pl.multiple_of(k * chunk, chunk), chunk)
        h1 = h1_ref[0, rows]
        low = dot(h1, down, 1, 1).astype(bf16)
        low_ref[0, rows] = low
        keys = dot(h1, qkv_ref[:, width : 2 * width], 1, 0) + vec(QKV_BIAS + 1)
        k_ref[0, rows] = keys.astype(bf16)
        values = dot(h1, qkv_ref[:, 2 * width :], 1, 0) + vec(QKV_BIAS + 2)
        values += adapter_scale * dot(low[:, 8:16], up[8:16], 1, 0)
        v_ref[0, rows] = values.astype(bf16)

    beside(1)

    pick = as_column(pick_ref[0].astype(f32)).astype(jnp.int32)
    picks = pick.shape[0]
    here = marks(iota((picks, count), 1) == pick)
    after = marks(iota((picks, count), 1) == pick + 1)
    xp_ref[0] = dot(here, emb_ref[...], 1, 0) + dot(here, pos_ref[...], 1, 0)
    wanted_ref[0] = dot(after, emb_ref[...], 1, 0).astype(bf16)
    h1p = dot(here, h1_ref[0], 1, 0).astype(bf16)
    lowp = dot(here, low_ref[0], 1, 0).astype(bf16)
    h1p_ref[0] = h1p
    lowp_ref[0] = lowp
    queries = dot(h1p, qkv_ref[:, :width], 1, 0) + vec(QKV_BIAS)
    queries += adapter_scale * dot(lowp[:, 0:8], up[0:8], 1, 0)
    q_ref[...] = queries.astype(bf16)
    some = 256 // size
    slot = iota((picks, count), 1)
    allowed = (slot <= pick) & (slot < length)
    allowed = jnp.concatenate([jnp.where(allowed, 1.0, 0.0)] * some, axis=0) > 0.5

    @pl.loop(0, width // 256)
    def _(k):
        lanes = pl.ds(pl.multiple_of(k * 256, 256), 256)
        scores = dot(spread_heads(q_ref[:, lanes], some, size), k_ref[0, :, lanes], 1, 1)
        scores = jnp.where(allowed, scores * size**-0.5, masked_score)
        weights = jnp.exp(scores - jnp.max(scores, axis=1, keepdims=True))
        probs = (weights / jnp.sum(weights, axis=1, keepdims=True)).astype(bf16)
        p_ref[0, pl.ds(pl.multiple_of(k * some * picks, some * picks), some * picks)] = probs
        attended = dot(probs, v_ref[0, :, lanes], 1, 0)
        att_ref[0, :, lanes] = join_heads(attended, some, size).astype(bf16)

    beside(2)

    if count_w:
        xp_own[micro] = xp_ref[0]
        att_own[micro] = att_ref[0]
        for copy in to_pair(micro):
            copy.start()

        @pl.when(micro == pl.num_programs(0) - 1)
        def _():
            gather.finish()
            for m in range(xp_own.shape[0]):
                for copy in to_pair(m):
                    copy.wait()


def whole(shape):
    return pl.BlockSpec(shape, lambda *_: (0,) * len(shape))


def of_micro(shape):
    return pl.BlockSpec((1,) + shape, lambda m: (m,) + (0,) * len(shape))


def attend(heads, adapter_scale, lens, slot, rows, more, wide, vec, pick, down, up, weights, collective):
    micros, _, count = slot.shape
    width = rows.shape[1]
    picks = pick.shape[2]
    more = [] if more is None else [more]
    outs = [
        ((count, width), bf16), ((count, 128), bf16), ((count, width), bf16), ((count, width), bf16),
        ((heads * picks, count), bf16), ((picks, width), bf16), ((picks, 128), bf16),
        ((picks, width), f32), ((picks, width), bf16), ((picks, width), bf16),
    ]
    return pl.pallas_call(
        functools.partial(attend_kernel, heads, adapter_scale, len(weights), len(more) > 0),
        grid=(micros,),
        out_shape=[jax.ShapeDtypeStruct((micros,) + shape, kind) for shape, kind in outs]
        + LayerWeights.shapes(weights)
        + [jax.ShapeDtypeStruct((micros, picks, width), kind) for kind in (f32, bf16) if weights],
        in_specs=[
            pl.BlockSpec(memory_space=pltpu.SMEM), of_micro((1, count)), ANY, ANY, whole(vec.shape), of_micro((1, picks)), whole(down.shape), whole(up.shape),
        ]
        + [of_micro((count, width))] * len(more)
        + [ANY] * len(weights),
        out_specs=[of_micro(shape) for shape, _ in outs] + [ANY] * (len(weights) + 2 if weights else 0),
        scratch_shapes=[
            pltpu.VMEM((count, width), bf16), pltpu.VMEM((picks, width), bf16), pltpu.VMEM(rows.shape, bf16),
            pltpu.VMEM((count, width), bf16), pltpu.VMEM((width, 3 * width), bf16), pltpu.SemaphoreType.DMA((3,)),
        ]
        + [pltpu.VMEM((micros, picks, width), kind) for kind in (f32, bf16) if weights]
        + [pltpu.SemaphoreType.DMA((2, 2, micros)) for _ in weights[:1]]
        + LayerWeights.scratch(weights),
        compiler_params=params(collective),
        name="attend",
    )(lens, slot, rows, wide, vec, pick, down, up, *more, *weights)


def attend_back_kernel(
    heads, adapter_scale, rank, datt_ref, h1_ref, low_ref, k_ref, v_ref, p_ref, h1p_ref, lowp_ref, up_ref, loss_ref,
    g_ref, dq_ref, dlow_ref,
):
    count, width = h1_ref.shape[1:]
    size = width // heads
    picks = datt_ref.shape[1]
    some = 256 // size
    up = two_sets(up_ref[...], 16)

    @pl.when(pl.program_id(0) == 0)
    def _():
        g_ref[...] = jnp.zeros_like(g_ref)
        g_ref[0, rank : rank + 1, :128] = loss_ref[:1, :]

    dlow_ref[...] = jnp.zeros_like(dlow_ref)

    @pl.loop(0, width // 256)
    def _(k):
        lanes = pl.ds(pl.multiple_of(k * 256, 256), 256)
        own = pl.ds(pl.multiple_of(k * some * picks, some * picks), some * picks)
        d_heads = spread_heads(datt_ref[0, :, lanes], some, size)
        probs_b = p_ref[0, own]
        probs = probs_b.astype(f32)
        d_probs = dot(d_heads, v_ref[0, :, lanes], 1, 1)
        v_up = two_sets_of_values(up_ref, lanes)
        dlow_ref[...] += dot(dot(d_heads, v_up, 1, 1).astype(bf16), probs_b, 0, 0)
        taken = dot(probs_b, low_ref[0, :, 8:16], 1, 0)
        g_ref[3, :, lanes] += adapter_scale * dot(taken.astype(bf16), d_heads, 0, 0)
        weighted = probs * d_probs
        d_scores = weighted - probs * jnp.sum(weighted, axis=1, keepdims=True)
        d_queries = dot(d_scores.astype(bf16), k_ref[0, :, lanes], 1, 0)
        dq_ref[:, lanes] = (join_heads(d_queries, some, size) * size**-0.5).astype(bf16)

    d_low_q = (adapter_scale * dot(dq_ref[...], up[0:8], 1, 1)).astype(bf16)
    d_low_v = (adapter_scale * dlow_ref[...]).astype(bf16)
    g_ref[0] += dot(d_low_q, h1p_ref[0], 0, 0)
    g_ref[1] += dot(d_low_v, h1_ref[0], 1, 0)
    g_ref[2] += adapter_scale * dot(lowp_ref[0, :, 0:8], dq_ref[...], 0, 0)


def two_sets_of_values(up_ref, lanes):
    rank = up_ref.shape[0] // 2
    v = up_ref[:, lanes].astype(bf16)[rank:]
    return jnp.concatenate([v, jnp.zeros((8 - rank, v.shape[1]), bf16)])


def back_parts(heads, adapter_scale, rank, datt, h1, low, keys, values, probs, h1p, lowp, up, loss):
    micros, count, width = h1.shape
    picks = datt.shape[1]
    ins = (datt, h1, low, keys, values, probs, h1p, lowp)
    return dict(
        kernel=functools.partial(attend_back_kernel, heads, adapter_scale, rank),
        grid=(micros,),
        in_specs=[of_micro(v.shape[1:]) for v in ins] + [whole(up.shape), whole(loss.shape)],
        args=(*ins, up, loss),
        shape=(4, 8, width),
        scratch_shapes=[pltpu.VMEM((picks, width), bf16), pltpu.VMEM((8, count), f32)],
    )


def attend_back(parts):
    return pl.pallas_call(
        parts["kernel"],
        grid=parts["grid"],
        out_shape=jax.ShapeDtypeStruct(parts["shape"], f32),
        in_specs=parts["in_specs"],
        out_specs=whole(parts["shape"]),
        scratch_shapes=parts["scratch_shapes"],
        compiler_params=params(),
        name="attend_back",
    )(*parts["args"])


def gelu(v):
    inner = 0.7978845608028654 * (v + 0.044715 * v * v * v)
    return 0.5 * v * (1.0 + jnp.tanh(inner))


def gelu_slope(v):
    bend = jnp.tanh(0.7978845608028654 * (v + 0.044715 * v * v * v))
    return 0.5 * (1.0 + bend) + 0.5 * v * (1.0 - bend * bend) * 0.7978845608028654 * (
        1.0 + 3.0 * 0.044715 * v * v
    )


def middle_kernel(
    lens_ref, pick_ref, att_ref, xp_ref, att_pair, xp_pair, wanted_ref, vec_ref, out_hbm, up_hbm, down_hbm, table_ref, datt_ref, loss_ref,
    out_ref, up_ref, down_ref, middle_ref, two_ref, three_ref, hidden_ref, before_ref, final_ref,
    rows_ref, part_ref, got_ref, load_sems, pair_sems, every_ref, q_ref, t_ref, core_q, core_t, keep_q, keep_t, send_q, send_t, got_q, got_t,
    next_q, next_t, pass_q, pass_t, last_q, last_t, end_q, end_t, final_q, final_t,
    core_sems, one_sems, two_sems, z_sems, *sems,
):
    rows, width = hidden_ref.shape
    piece = Piece([hidden_ref], every_ref, sems)
    greeting = greet_near()
    vec = lambda k: vec_ref[k : k + 1, :]
    loads = [
        pltpu.make_async_copy(src, dst, load_sems.at[k])
        for k, (src, dst) in enumerate(((out_hbm, out_ref), (up_hbm, up_ref), (down_hbm, down_ref)))
    ]
    for load in loads:
        load.start()
    z, x, y, c = place()
    side = lax.rem(z, 2)
    pair = target(z + 1 - 2 * side, x, y, c)

    def to_pair(number, values):
        rows_ref[0] = values
        copy = remote(
            rows_ref.at[0], rows_ref.at[1], pair_sems.at[0, 4 + number], pair_sems.at[1, 4 + number], pair
        )
        copy.start()
        copy.wait()
        return rows_ref[...].reshape(2 * rows, width)

    half = width // 2
    cols = (slice(0, half), slice(half, width))

    def of_pair(number, product):
        own, copies = [], []
        for k in range(2):
            part = product(cols[k])
            part_ref[k] = part[rows:].astype(bf16)
            spot = 2 * number + k
            copy = remote(part_ref.at[k], got_ref.at[k], pair_sems.at[0, spot], pair_sems.at[1, spot], pair)
            copy.start()
            own.append(part[:rows])
            copies.append(copy)
        for copy in copies:
            copy.wait()
        return jnp.concatenate([own[k] + got_ref[k].astype(f32) for k in range(2)], axis=1)

    loads[0].wait()
    both = lambda own, other: jnp.concatenate([own[...], other[...]])
    middle = both(xp_ref, xp_pair) + dot(both(att_ref, att_pair), out_ref[...], 1, 0) + vec(OUT_BIAS)
    middle_ref[...] = middle[:rows]
    every_h2, two, inverse_two = normal(middle, vec(GAIN[1]), vec(SHIFT[1]))
    two_ref[...], inverse_two = two[:rows], inverse_two[:rows]
    bias = jnp.concatenate(
        [jnp.where(side == 0, vec(UP_BIAS + 2 * k), vec(UP_BIAS + 2 * k + 1)) for k in range(2)], axis=1
    )
    loads[1].wait()
    before = dot(every_h2.astype(bf16), up_ref[...], 1, 0) + bias
    before_ref[...] = before
    loads[2].wait()
    activated = gelu(before).astype(bf16)
    greeting.wait()
    added = of_pair(0, lambda some: dot(activated, down_ref[:, some], 1, 0))
    final = middle_ref[...] + added + vec(vec_ref.shape[0] - 1)
    hidden, three, inverse_three = normal(final, vec(GAIN[2]), vec(SHIFT[2]))
    hidden_ref[...] = hidden.astype(bf16)
    three_ref[...] = three

    piece.load()
    mate = target(z, x, y, 1 - c)
    over = (target(z, 1 - x, y, c), target(z, x, 1 - y, c))
    mine = (x, y)
    is_end = (z == 0) | (z == 3)
    up = jnp.where((z == 0) | (z == 2), 1, -1)

    def nth_plane(i):
        from_end = z + up * i
        inside = jnp.where(i == 0, z, jnp.where(i == 1, z + up, jnp.where(i == 2, z - up, z - 2 * up)))
        return jnp.where(is_end, from_end, inside)

    def core_copies(zz):
        return [
            remote(q_ref.at[zz, :, :, 1 - c], core_q.at[zz], core_sems.at[0, 0, zz], core_sems.at[1, 0, zz], mate),
            remote(t_ref.at[zz, :, :, 1 - c], core_t.at[zz], core_sems.at[0, 1, zz], core_sems.at[1, 1, zz], mate),
        ]

    def one_copies(zz, k):
        return [
            remote(send_q.at[k, zz], got_q.at[k, zz], one_sems.at[0, 0, k, zz], one_sems.at[1, 0, k, zz], over[k]),
            remote(send_t.at[k, zz], got_t.at[k, zz], one_sems.at[0, 1, k, zz], one_sems.at[1, 1, k, zz], over[k]),
        ]

    def two_copies(zz, k):
        return [
            remote(pass_q.at[k, zz], last_q.at[k, zz], two_sems.at[0, 0, k, zz], two_sems.at[1, 0, k, zz], over[1 - k]),
            remote(pass_t.at[k, zz], last_t.at[k, zz], two_sems.at[0, 1, k, zz], two_sems.at[1, 1, k, zz], over[1 - k]),
        ]

    def z_copies(zz, frm, k):
        return [
            remote(end_q.at[k, zz], final_q.at[k, frm], z_sems.at[0, 0, k, zz], z_sems.at[1, 0, k, frm], target(zz, x, y, c)),
            remote(end_t.at[k, zz], final_t.at[k, frm], z_sems.at[0, 1, k, zz], z_sems.at[1, 1, k, frm], target(zz, x, y, c)),
        ]

    def start(copies):
        for copy in copies:
            copy.start()

    def landed(copies):
        for copy in copies:
            copy.wait_recv()

    def left(copies):
        for copy in copies:
            copy.wait_send()

    def arrive(i):
        zz = nth_plane(i)
        way = jnp.where(zz < z, 1, -1)
        piece.chain(zz, way, True).wait_recv()
        piece.pass_on(zz, way)
        piece.first(zz)

    def second(i):
        piece.second_of(nth_plane(i))

    def third(i):
        piece.third_of(nth_plane(i))

    def compute(i):
        zz = nth_plane(i)
        piece.mate(zz, True).wait_recv()

        @pl.loop(0, 2)
        def _(xx):
            logits = dot(every_ref[zz, xx].reshape(4 * rows, width), table_ref[...], 1, 1)
            top = jnp.max(logits, axis=1, keepdims=True)
            weights = jnp.exp(logits - top)
            amount = jnp.sum(weights, axis=1, keepdims=True)
            mean = dot(weights.astype(bf16), table_ref[...], 1, 0) / amount
            q_ref[zz, xx] = mean.astype(bf16).reshape(2, 2, rows, width)
            total = top + jnp.log(amount)
            for k in range(4):
                t_ref[zz, xx, k // 2, k % 2] = as_tile(as_row(total[k * rows : (k + 1) * rows]))

        start(core_copies(zz))

    def merge_cores(i):
        zz = nth_plane(i)
        landed(core_copies(zz))

        @pl.loop(0, 2)
        def _(xx):
            for yy in range(2):
                mean, total = merged(
                    [(q_ref[zz, xx, yy, c], t_ref[zz, xx, yy, c]), (core_q[zz, xx, yy], core_t[zz, xx, yy])]
                )
                for k, (own, other) in enumerate(((xx, yy), (yy, xx))):
                    part = mean[:, cols[k]]

                    @pl.when(own == mine[k])
                    def _(k=k, other=other, part=part, total=total):
                        keep_q[k, zz, other] = part
                        keep_t[k, zz, other] = total

                    @pl.when(own != mine[k])
                    def _(k=k, other=other, part=part, total=total):
                        send_q[k, zz, other] = part.astype(bf16)
                        send_t[k, zz, other] = total

        for k in range(2):
            start(one_copies(zz, k))

    def merge_first(i):
        zz = nth_plane(i)
        for k in range(2):
            landed(one_copies(zz, k))
            for other in range(2):
                mean, total = merged(
                    [(keep_q[k, zz, other], keep_t[k, zz, other]), (got_q[k, zz, other], got_t[k, zz, other])]
                )

                @pl.when(other == mine[1 - k])
                def _(k=k, mean=mean, total=total):
                    next_q[k, zz] = mean
                    next_t[k, zz] = total

                @pl.when(other != mine[1 - k])
                def _(k=k, mean=mean, total=total):
                    pass_q[k, zz] = mean.astype(bf16)
                    pass_t[k, zz] = total

            start(two_copies(zz, k))

    def merge_second(i):
        zz = nth_plane(i)
        for k in range(2):
            landed(two_copies(zz, k))
            mean, total = merged([(next_q[k, zz], next_t[k, zz]), (last_q[k, zz], last_t[k, zz])])

            @pl.when(i > 0)
            def _(k=k, mean=mean, total=total):
                end_q[k, zz] = mean.astype(bf16)
                end_t[k, zz] = total
                start(z_copies(zz, z, k))

            @pl.when(i == 0)
            def _(k=k, mean=mean, total=total):
                next_q[k, z] = mean
                next_t[k, z] = total

    piece.start()
    second(0)
    arrive(1)
    third(0)
    second(1)
    arrive(2)

    @pl.loop(0, 7)
    def _(i):
        for act, lag, begin in (
            (merge_second, 3, 0), (merge_first, 2, 0), (merge_cores, 1, 0), (compute, 0, 0),
            (third, -1, 1), (second, -2, 2), (arrive, -3, 3),
        ):
            @pl.when((i - lag >= begin) & (i - lag < 4))
            def _(act=act, lag=lag):
                act(i - lag)

    for k in range(2):
        parts = [(next_q[k, z], next_t[k, z])]
        for i in range(1, 4):
            frm = nth_plane(i)
            landed(z_copies(frm, frm, k))
            parts.append((final_q[k, frm], final_t[k, frm]))
        mean, total = merged(parts)
        final_ref[:, cols[k]] = mean

    valid = jnp.concatenate(
        [
            jnp.where(as_column(pick_ref[m].astype(f32)) + 1.0 < lens_ref[0, m].astype(f32), 1.0, 0.0)
            for m in range(pick_ref.shape[0])
        ]
    )
    wanted = wanted_ref[...].astype(f32)
    chosen = jnp.sum(hidden_ref[...].astype(f32) * wanted, axis=1, keepdims=True)
    loss = jnp.sum(valid * (as_column(total[:1, :rows]) - chosen), keepdims=True)
    counted = jnp.sum(valid, keepdims=True)
    lane = iota(loss_ref.shape, 1)
    loss_ref[...] = jnp.where(lane == 0, loss, jnp.where(lane == 1, counted, 0.0))
    d_hidden = valid * (final_ref[...] - wanted)
    d_final = normal_back(d_hidden, vec(GAIN[2]), three_ref[...], inverse_three)
    middle_ref[...] = d_final
    d_act = dot(to_pair(0, d_final.astype(bf16)), down_ref[...], 1, 1)
    d_before = (d_act * gelu_slope(before_ref[...])).astype(bf16)
    d_two = of_pair(1, lambda some: dot(d_before, up_ref[some, :], 1, 1))
    d_middle = middle_ref[...] + normal_back(d_two, vec(GAIN[1]), two_ref[...], inverse_two)
    datt_ref[...] = dot(d_middle.astype(bf16), out_ref[...], 1, 1).astype(bf16)

    @pl.loop(0, 4)
    def _(i):
        zz = nth_plane(i)
        left(core_copies(zz))
        for k in range(2):
            left(one_copies(zz, k))
            left(two_copies(zz, k))

    @pl.loop(1, 4)
    def _(i):
        for k in range(2):
            left(z_copies(nth_plane(i), z, k))

    piece.finish(False)


def middle(lens, pick, att, xp, att_pair, xp_pair, wanted, vec, out_w, up_w, down_w, table, collective):
    rows, width = att.shape
    half = width // 2
    tile = (8, 128)
    vmem = pltpu.VMEM
    own = (rows, width)
    return pl.pallas_call(
        middle_kernel,
        out_shape=[jax.ShapeDtypeStruct(own, bf16), jax.ShapeDtypeStruct(tile, f32)],
        in_specs=[pl.BlockSpec(memory_space=pltpu.SMEM)] + [VMEM] * 7 + [ANY] * 3 + [VMEM],
        out_specs=[VMEM] * 2,
        scratch_shapes=[
            vmem(out_w.shape, bf16), vmem(up_w.shape, bf16), vmem(down_w.shape, bf16),
            vmem(own, f32), vmem(own, f32), vmem(own, f32), vmem(own, bf16),
            vmem((2 * rows, up_w.shape[1]), f32), vmem(own, f32),
            vmem((2,) + own, bf16), vmem((2, rows, half), bf16), vmem((2, rows, half), bf16),
            pltpu.SemaphoreType.DMA((3,)),
            pltpu.SemaphoreType.DMA((2, 5)),
            vmem((4, 2, 2, 2, rows, width), bf16),
            vmem((4, 2, 2, 2, rows, width), bf16), vmem((4, 2, 2, 2) + tile, f32),
            vmem((4, 2, 2, rows, width), bf16), vmem((4, 2, 2) + tile, f32),
            vmem((2, 4, 2, rows, half), f32), vmem((2, 4, 2) + tile, f32),
            vmem((2, 4, 2, rows, half), bf16), vmem((2, 4, 2) + tile, f32),
            vmem((2, 4, 2, rows, half), bf16), vmem((2, 4, 2) + tile, f32),
            vmem((2, 4, rows, half), f32), vmem((2, 4) + tile, f32),
            vmem((2, 4, rows, half), bf16), vmem((2, 4) + tile, f32),
            vmem((2, 4, rows, half), bf16), vmem((2, 4) + tile, f32),
            vmem((2, 4, rows, half), bf16), vmem((2, 4) + tile, f32),
            vmem((2, 4, rows, half), bf16), vmem((2, 4) + tile, f32),
            pltpu.SemaphoreType.DMA((2, 2, 4)),
            pltpu.SemaphoreType.DMA((2, 2, 2, 4)),
            pltpu.SemaphoreType.DMA((2, 2, 2, 4)),
            pltpu.SemaphoreType.DMA((2, 2, 2, 4)),
        ]
        + piece_scratch(1),
        compiler_params=params(collective),
        name="middle",
    )(lens, pick, att, xp, att_pair, xp_pair, wanted, vec, out_w, up_w, down_w, table)


def forward_kernel(
    att_ref, xp_ref, out_ref, up_ref, down_ref, vec_ref, bias_ref,
    hidden_ref, before_ref, two_ref, three_ref, inverse_ref, acc_ref, h2_ref,
):
    vec = lambda k: vec_ref[k : k + 1, :]
    step = pl.program_id(0)

    @pl.when(step == 0)
    def _():
        middle = xp_ref[...] + dot(att_ref[...], out_ref[...], 1, 0) + vec(OUT_BIAS)
        h2, two, inverse = normal(middle, vec(GAIN[1]), vec(SHIFT[1]))
        h2_ref[...] = h2.astype(bf16)
        two_ref[...] = two
        inverse_ref[0] = jnp.broadcast_to(inverse, inverse_ref.shape[1:])
        acc_ref[...] = middle + vec(vec_ref.shape[0] - 1)

    before = dot(h2_ref[...], up_ref[...], 1, 0) + bias_ref[...]
    before_ref[...] = before
    acc_ref[...] += dot(gelu(before).astype(bf16), down_ref[...], 1, 0)

    @pl.when(step == pl.num_programs(0) - 1)
    def _():
        hidden, three, inverse = normal(acc_ref[...], vec(GAIN[2]), vec(SHIFT[2]))
        hidden_ref[...] = hidden.astype(bf16)
        three_ref[...] = three
        inverse_ref[1] = jnp.broadcast_to(inverse, inverse_ref.shape[1:])


def forward(att, xp, out_w, up_w, down_w, vec, bias):
    rows, width = att.shape
    ff = down_w.shape[0]
    tile = 512
    fixed = whole((rows, width))
    return pl.pallas_call(
        forward_kernel,
        grid=(ff // tile,),
        out_shape=[
            jax.ShapeDtypeStruct((rows, width), bf16),
            jax.ShapeDtypeStruct((rows, ff), f32),
            jax.ShapeDtypeStruct((rows, width), f32),
            jax.ShapeDtypeStruct((rows, width), f32),
            jax.ShapeDtypeStruct((2, rows, 128), f32),
        ],
        in_specs=[
            fixed, fixed, whole(out_w.shape), pl.BlockSpec((width, tile), lambda i: (0, i)),
            pl.BlockSpec((tile, width), lambda i: (i, 0)), whole(vec.shape), pl.BlockSpec((1, tile), lambda i: (0, i)),
        ],
        out_specs=[
            fixed, pl.BlockSpec((rows, tile), lambda i: (0, i)), fixed, fixed, whole((2, rows, 128)),
        ],
        scratch_shapes=[pltpu.VMEM((rows, width), f32), pltpu.VMEM((rows, width), bf16)],
        compiler_params=params(),
        name="forward",
    )(att, xp, out_w, up_w, down_w, vec, bias)


def backward_kernel(
    mean_ref, total_ref, hidden_ref, wanted_ref, valid_ref, before_ref, two_ref, three_ref, inverse_ref,
    out_ref, up_ref, down_ref, vec_ref, datt_ref, loss_ref, final_ref, acc_ref,
):
    vec = lambda k: vec_ref[k : k + 1, :]
    step = pl.program_id(0)
    rows = valid_ref.shape[0]

    @pl.when(step == 0)
    def _():
        valid = valid_ref[...]
        wanted = wanted_ref[...].astype(f32)
        chosen = jnp.sum(hidden_ref[...].astype(f32) * wanted, axis=1, keepdims=True)
        loss = jnp.sum(valid * (as_column(total_ref[:1, :rows]) - chosen), keepdims=True)
        counted = jnp.sum(valid, keepdims=True)
        lane = iota(loss_ref.shape, 1)
        loss_ref[...] = jnp.where(lane == 0, loss, jnp.where(lane == 1, counted, 0.0))
        d_hidden = valid * (mean_ref[...] - wanted)
        final_ref[...] = normal_back(d_hidden, vec(GAIN[2]), three_ref[...], inverse_ref[1, :, :1])
        acc_ref[...] = jnp.zeros_like(acc_ref)

    d_act = dot(final_ref[...].astype(bf16), down_ref[...], 1, 1)
    d_before = (d_act * gelu_slope(before_ref[...])).astype(bf16)
    acc_ref[...] += dot(d_before, up_ref[...], 1, 1)

    @pl.when(step == pl.num_programs(0) - 1)
    def _():
        d_middle = final_ref[...] + normal_back(
            acc_ref[...], vec(GAIN[1]), two_ref[...], inverse_ref[0, :, :1]
        )
        datt_ref[...] = dot(d_middle.astype(bf16), out_ref[...], 1, 1).astype(bf16)


def backward(mean, total, hidden, wanted, valid, before, two, three, inverse, out_w, up_w, down_w, vec):
    rows, width = mean.shape
    ff = down_w.shape[0]
    tile = 512
    fixed = whole((rows, width))
    return pl.pallas_call(
        backward_kernel,
        grid=(ff // tile,),
        out_shape=[
            jax.ShapeDtypeStruct((rows, width), bf16),
            jax.ShapeDtypeStruct((8, 128), f32),
        ],
        in_specs=[
            fixed, whole(total.shape), fixed, fixed, whole((rows, 1)), pl.BlockSpec((rows, tile), lambda i: (0, i)),
            fixed, fixed, whole(inverse.shape), whole(out_w.shape),
            pl.BlockSpec((width, tile), lambda i: (0, i)),
            pl.BlockSpec((tile, width), lambda i: (i, 0)), whole(vec.shape),
        ],
        out_specs=[fixed, whole((8, 128))],
        scratch_shapes=[pltpu.VMEM((rows, width), f32)] * 2,
        compiler_params=params(),
        name="backward",
    )(mean, total, hidden, wanted, valid, before, two, three, inverse, out_w, up_w, down_w, vec)


def on_device(
    direct,
    token_identifiers,
    lengths,
    loss_positions,
    token_embedding_table,
    positions,
    query_key_value_matrix,
    output_weight,
    up_weight,
    down_weight,
    vectors,
    adapter_down_weight,
    adapter_up_weight,
    left_statistics,
    right_statistics,
):
    width = adapter_down_weight.shape[0]
    rank = adapter_down_weight.shape[1] // 2
    micros, _, slot_count = token_identifiers.shape
    picks = loss_positions.shape[2]
    ff = up_weight.shape[1]
    adapter_scale = adapter_alpha / rank
    local_rows = token_embedding_table.shape[0]
    devices = lax.axis_size("dp") * lax.axis_size("fsdp")
    me = lax.axis_index(BOTH)

    first = jnp.zeros((1,), jnp.int32)

    def masked_ids():
        ids = token_identifiers[:, 0]
        return jnp.where(iota(ids.shape, 1) < lengths, ids, -1).reshape(1, -1)

    if direct:
        received, most, slot, asked, own, mate, vec, wide = fetch(
            lengths.T, token_identifiers, vectors, token_embedding_table, query_key_value_matrix,
            positions, CAPACITY, 0,
        )
        asked = asked.reshape(devices // 2, 2, GRID, 128)
        wide = wide.reshape(-1, wide.shape[-1])
    else:
        ids = masked_ids()
        own = pl.pallas_call(
            functools.partial(presence_kernel, local_rows),
            out_shape=jax.ShapeDtypeStruct((devices, GRID, 128), bf16),
            compiler_params=params(),
            name="presence",
        )(ids)
        mate = own
        asked = lax.all_to_all(own, BOTH, 0, 0, tiled=True).reshape(devices, 1, GRID, 128)
        rows, most = select(asked, token_embedding_table, first, CAPACITY)
        most = lax.pmax(most, BOTH)
        received = lax.all_to_all(rows, BOTH, 0, 0, tiled=True)
        slot = slots(ids, own, mate, first, CAPACITY, local_rows)
        vec = lax.all_gather(vectors.astype(f32), BOTH, axis=0, tiled=True).reshape(-1, width)
        wide = jnp.concatenate([query_key_value_matrix, positions], axis=1)
        wide = lax.all_gather(wide, BOTH, axis=0, tiled=True)
    by_micro = lambda v: v.reshape(micros, 1, slot_count)
    most = most.reshape(-1)[0]
    flat = lambda v: v.reshape(-1, width)

    def rest(more, collective):
        layer = attend(
            ATTENTION_HEADS, adapter_scale, lengths.T, by_micro(slot), received.reshape(-1, width), more, wide, vec,
            loss_positions, adapter_down_weight.T, adapter_up_weight,
            *(([output_weight, up_weight, down_weight], collective) if direct else ([], None)),
        )
        layer, layer_w = layer[:10], layer[10:]
        h1, low, keys, values, probs, h1_p, low_p, x_p, wanted, attended = layer
        if direct:
            out_w, up_w, down_w, x_pair, attended_pair = (w.reshape(-1, w.shape[-1]) for w in layer_w)
            d_attended, loss = middle(
                lengths.T, loss_positions, flat(attended), flat(x_p), attended_pair, x_pair, flat(wanted), vec,
                out_w, up_w, down_w, token_embedding_table, collective + 1,
            )
        else:
            out_w, up_w, down_w = (
                lax.all_gather(w, BOTH, axis=0, tiled=True) for w in (output_weight, up_weight, down_weight)
            )
            bias = vec[UP_BIAS:-1].reshape(1, ff)
            valid = (loss_positions[:, 0] + 1 < lengths).astype(f32).reshape(-1, 1)
            hidden, before, two, three, inverse = forward(
                flat(attended), flat(x_p), out_w, up_w, down_w, vec, bias
            )
            own_rows = hidden.shape[0]
            every = lax.all_gather(hidden, BOTH, axis=0, tiled=True)
            means, totals = vocabulary(every, token_embedding_table, own_rows, 4 * own_rows)
            part = totals[:, 0, :own_rows].reshape(-1)
            top = lax.pmax(part, BOTH)
            total = top + jnp.log(lax.psum(jnp.exp(part - top), BOTH))
            mean_row = lax.psum_scatter(
                means.astype(f32) * jnp.exp(part - total)[:, None], BOTH, scatter_dimension=0, tiled=True
            )
            total = lax.dynamic_slice_in_dim(total, me * own_rows, own_rows, 0)
            total = jnp.broadcast_to(jnp.pad(total, (0, 128 - own_rows)), (8, 128))
            d_attended, loss = backward(
                mean_row, total, hidden, flat(wanted), valid, before, two, three, inverse, out_w, up_w, down_w, vec
            )
        back = back_parts(
            ATTENTION_HEADS, adapter_scale, rank, d_attended.reshape(micros, picks, width),
            h1, low, keys, values, probs, h1_p, low_p, adapter_up_weight, loss,
        )
        if direct:
            return finished(
                back, adapter_down_weight.T, adapter_up_weight, left_statistics, right_statistics, collective + 2
            )
        gradient = lax.psum(attend_back(back), BOTH)
        _, new = renewed(gradient, adapter_down_weight.T, adapter_up_weight, left_statistics, right_statistics)
        blocks = lax.all_gather(new, ("fsdp", "dp"))
        blocks = blocks.reshape(lax.axis_size("fsdp"), -1, 8, new.shape[1])
        return [gradient, blocks[:, : left_statistics.shape[0]].reshape(-1, 8, new.shape[1])]

    def another(state):
        step, rows_sum = state
        ids = masked_ids()
        which = step.reshape(1)
        rows, most = select(asked, token_embedding_table, which, CAPACITY)
        if direct:
            received = send_rows(rows, most, 1)[0]
        else:
            received = lax.all_to_all(rows, BOTH, 0, 0, tiled=True)
        slot = slots(ids, own, mate, which, CAPACITY, local_rows)
        found = jnp.take(received.reshape(-1, width), jnp.maximum(slot[0], 0), axis=0)
        found = jnp.where(slot[0][:, None] >= 0, found, jnp.zeros((), bf16))
        return step + 1, rows_sum + found.reshape(micros, slot_count, width)

    def in_rounds():
        more = lax.while_loop(
            lambda state: (state[0] * CAPACITY).astype(f32) < most,
            another,
            (jnp.ones((), jnp.int32), jnp.zeros((micros, slot_count, width), bf16)),
        )[1]
        return rest(more, 5)

    plain = rest(None, 2)
    gradient, blocks = lax.cond(most > CAPACITY, in_rounds, lambda: plain)
    losses, norm, down_g, up_g, left_new, right_new, down_new, up_new = settled(
        gradient, blocks, left_statistics, right_statistics
    )
    return losses, norm[0], down_g.T, up_g, left_new, right_new, down_new.T, up_new


def solution(mesh):
    direct = dict(mesh.shape) == {"dp": 8, "fsdp": 4}
    rows = P(BOTH, None)
    placed = (
        P(None, BOTH, None),
        P(None, BOTH),
        P(None, BOTH, None),
        rows,
        rows,
        rows,
        rows,
        rows,
        rows,
        P(BOTH),
        P(),
        P(),
        P("fsdp", None, None),
        P("fsdp", None, None),
    )
    return jax.shard_map(
        functools.partial(on_device, direct),
        mesh=mesh,
        in_specs=placed,
        out_specs=(P(), P(), P(), P(), P("fsdp", None, None), P("fsdp", None, None), P(), P()),
        check_vma=False,
    )
```

```python
import functools
import jax
import jax.numpy as jnp
from jax import lax
from jax.experimental import pallas as pl
from jax.experimental.pallas import tpu as pltpu
from jax.sharding import PartitionSpec as P

ATTENTION_HEADS = 16
STATS_BLOCK_ROWS = 256
NEWTON = 8
CAPACITY = 80

ln_eps = 1e-05
adapter_alpha = 32.0
beta_stats = 0.95
root_eps = 1e-12
clip_level = 0.01
learn_rate = 0.05
masked_score = -1e30

BOTH = ("dp", "fsdp")
MESH = pl.DeviceIdType.MESH
VMEM = pl.BlockSpec(memory_space=pltpu.VMEM)
ANY = pl.BlockSpec(memory_space=pl.ANY)
f32 = jnp.float32
bf16 = jnp.bfloat16


def place():
    d, f = lax.axis_index("dp"), lax.axis_index("fsdp")
    return d // 2, lax.rem(d, 2), f // 2, lax.rem(f, 2)


def target(z, x, y, c):
    return (z * 2 + x, y * 2 + c)


def nth(i):
    return (i // 4, lax.rem(i, 4))


class Greeting:
    def __init__(self, devices):
        self.sem, self.count = pltpu.get_barrier_semaphore(), len(devices)
        for device in devices:
            pl.semaphore_signal(self.sem, inc=1, device_id=device, device_id_type=MESH)

    def wait(self):
        pl.semaphore_wait(self.sem, self.count)


def own_number():
    return lax.axis_index("dp") * 4 + lax.axis_index("fsdp")


def greet_all(count):
    me = own_number()
    return Greeting([nth(lax.rem(me + i, count)) for i in range(1, count)])


def greet_near():
    z, x, y, c = place()
    near = [target(lax.rem(z + i, 4), x, y, c) for i in range(1, 4)]
    near += [target(z, 1 - x, y, c), target(z, x, 1 - y, c), target(z, x, y, 1 - c)]
    return Greeting(near)


def remote(src, dst, send, recv, device):
    return pltpu.make_async_remote_copy(
        src_ref=src, dst_ref=dst, send_sem=send, recv_sem=recv, device_id=device, device_id_type=MESH
    )


def params(collective=None, vmem=60):
    if collective is None:
        return pltpu.CompilerParams(vmem_limit_bytes=vmem * 2**20)
    return pltpu.CompilerParams(
        vmem_limit_bytes=vmem * 2**20, collective_id=collective, has_side_effects=True
    )


def iota(shape, dim):
    return lax.broadcasted_iota(jnp.int32, shape, dim)


def marks(condition):
    return jnp.where(condition, 1.0, 0.0).astype(bf16)


def dot(a, b, ca, cb):
    return lax.dot_general(a, b, (((ca,), (cb,)), ((), ())), preferred_element_type=f32)


GRID = 16


def cells(ids, local_rows):
    owner = jnp.floor((ids.astype(f32) + 0.5) * (1.0 / local_rows)).astype(jnp.int32)
    local = ids - owner * local_rows
    return owner, jnp.where(ids >= 0, owner * GRID + (local >> 7), -1), local & 127


def presence(ids, owners, local_rows):
    width = ids.shape[1]
    _, high, low = cells(ids, local_rows)
    count = dot(
        marks(iota((owners * GRID, width), 0) == high), marks(iota((128, width), 0) == low), 1, 1
    )
    return marks(count > 0.5).reshape(owners, GRID, 128)


def presence_kernel(local_rows, ids_ref, own_ref):
    own_ref[...] = presence(ids_ref[...], own_ref.shape[0], local_rows)


def ranked(present):
    rows = present.shape[0]
    through = dot(present, marks(iota((128, 128), 0) <= iota((128, 128), 1)), 1, 0)
    of = lambda dim: iota((rows, rows), dim)
    earlier = marks((of(1) < of(0)) & (of(0) // GRID == of(1) // GRID))
    row_total = jnp.broadcast_to(through[:, 127:128], (rows, 128)).astype(bf16)
    offset = dot(earlier, row_total, 1, 0)
    has = present.astype(f32)
    return jnp.where(has > 0.5, through - has + offset, -1.0), offset[:, :1] + through[:, 127:128]


def mark_rows(capacity, rank_ref, marks_ref, units, local_rows):
    @pl.loop(0, units)
    def _(unit):
        rows = pl.ds(pl.multiple_of(unit * capacity, 16), capacity)
        own = rank_ref[pl.ds(pl.multiple_of(unit * GRID, GRID), GRID), :]
        for row in range(-(-local_rows // 128)):
            columns = min(128, local_rows - row * 128)
            hit = iota((capacity, 128), 0).astype(f32) == own[row : row + 1, :]
            marks_ref[rows, row * 128 : row * 128 + columns] = marks(hit)[:, :columns]


def select_kernel(capacity, asked_ref, table_ref, round_ref, rows_ref, most_ref, marks_ref, rank_ref):
    units, members = asked_ref.shape[:2]
    local_rows, width = table_ref.shape
    begin = (round_ref[0] * capacity).astype(f32)
    most = jnp.zeros((1, 1), f32)
    for first in range(0, units, 16):
        together = asked_ref[first : first + 16, 0]
        for member in range(1, members):
            together = jnp.maximum(together, asked_ref[first : first + 16, member])
        rank, amount = ranked(together.reshape(-1, 128))
        most = jnp.maximum(most, jnp.max(amount, keepdims=True))
        rank_ref[first * GRID : first * GRID + rank.shape[0]] = rank - begin
    most_ref[...] = jnp.broadcast_to(most, most_ref.shape)
    mark_rows(capacity, rank_ref, marks_ref, units, local_rows)

    @pl.loop(0, units // 4)
    def _(four):
        rows_ref[pl.ds(four * 4, 4)] = look_up(capacity, four, marks_ref, table_ref)


def look_up(capacity, four, marks_ref, table_ref):
    part = pl.ds(pl.multiple_of(four * (4 * capacity), 4 * capacity), 4 * capacity)
    found = dot(marks_ref[part, :], table_ref[...], 1, 0)
    return found.astype(bf16).reshape(4, capacity, table_ref.shape[1])


def select(asked, table, which_round, capacity):
    units = asked.shape[0]
    return pl.pallas_call(
        functools.partial(select_kernel, capacity),
        out_shape=[
            jax.ShapeDtypeStruct((units, capacity, table.shape[1]), bf16),
            jax.ShapeDtypeStruct((8, 128), f32),
        ],
        in_specs=[VMEM, VMEM, pl.BlockSpec(memory_space=pltpu.SMEM)],
        out_specs=[VMEM] * 2,
        scratch_shapes=[
            pltpu.VMEM((units * capacity, table.shape[0]), bf16),
            pltpu.VMEM((units * GRID, 128), f32),
        ],
        compiler_params=params(),
        name="select",
    )(asked, table, which_round)


def slots_of(capacity, begin, local_rows, ids, own_ref, mate_ref):
    owner, high, low = cells(ids, local_rows)
    width = ids.shape[1]
    own_rank = jnp.zeros((1, width), f32)
    for first in range(0, own_ref.shape[0], 16):
        together = jnp.maximum(own_ref[first : first + 16], mate_ref[first : first + 16])
        rank, _ = ranked(together.reshape(-1, 128))
        rank = rank - begin
        rank = jnp.where((rank >= 0.0) & (rank < capacity), rank + 1.0, 0.0)
        rows = rank.shape[0]
        of_low = dot(rank.astype(bf16), marks(iota((rows, width), 0) + first * GRID == high), 0, 0)
        own_rank += jnp.sum(
            jnp.where(iota((128, width), 0) == low, of_low, 0.0), axis=0, keepdims=True
        )
    slot = owner * capacity + own_rank.astype(jnp.int32) - 1
    return jnp.where(own_rank > 0.5, slot, -1)


def slots_kernel(capacity, local_rows, ids_ref, own_ref, mate_ref, round_ref, slot_ref):
    begin = (round_ref[0] * capacity).astype(f32)
    slot_ref[...] = slots_of(capacity, begin, local_rows, ids_ref[...], own_ref, mate_ref)


def slots(ids, own, mate, which_round, capacity, local_rows):
    return pl.pallas_call(
        functools.partial(slots_kernel, capacity, local_rows),
        out_shape=jax.ShapeDtypeStruct(ids.shape, jnp.int32),
        in_specs=[VMEM] * 3 + [pl.BlockSpec(memory_space=pltpu.SMEM)],
        out_specs=VMEM,
        compiler_params=params(),
        name="slots",
    )(ids, own, mate, which_round)


class Piece:
    def __init__(self, sources, out, sems):
        self.sources, self.out, self.rows = sources, out, out.shape[4]
        self.own_sems, self.chain_sems, self.plane_sems, self.core_sems = sems
        self.z, self.x, self.y, self.c = place()

    def at(self, zz, xx, yy, cc, half=None):
        ref = self.out.at[zz, xx, yy, cc]
        return ref if half is None else self.out.at[zz, xx, yy, cc, pl.ds(half * (self.rows // 2), self.rows // 2)]

    def own(self):
        copies, begin = [], 0
        for k, src in enumerate(self.sources):
            dst = self.out.at[self.z, self.x, self.y, self.c, :, pl.ds(begin, src.shape[1])]
            copies.append(pltpu.make_async_copy(src, dst, self.own_sems.at[k]))
            begin += src.shape[1]
        return copies

    def chain(self, zz, way, incoming=False):
        z, x, y, c = self.z, self.x, self.y, self.c
        ref = self.at(zz, x, y, c)
        k = (way + 1) // 2
        to = target(z - way if incoming else z + way, x, y, c)
        return remote(ref, ref, self.chain_sems.at[0, k, zz], self.chain_sems.at[1, k, zz], to)

    def plane(self, zz, step, incoming=False):
        z, x, y, c = self.z, self.x, self.y, self.c
        every = slice(None)
        over_x, over_y = target(z, 1 - x, y, c), target(z, x, 1 - y, c)
        xx, yy = (1 - x, 1 - y) if incoming else (x, y)
        if step == 0:
            pairs = ((self.at(zz, xx, y, c, 0), over_x), (self.at(zz, x, yy, c, 1), over_y))
        else:
            pairs = ((self.at(zz, every, yy, c, 0), over_y), (self.at(zz, xx, every, c, 1), over_x))
        return [
            remote(ref, ref, self.plane_sems.at[0, zz, step, k], self.plane_sems.at[1, zz, step, k], to)
            for k, (ref, to) in enumerate(pairs)
        ]

    def mate(self, zz, incoming=False):
        z, x, y, c = self.z, self.x, self.y, self.c
        ref = self.at(zz, slice(None), slice(None), 1 - c if incoming else c)
        return remote(ref, ref, self.core_sems.at[0, zz], self.core_sems.at[1, zz], target(z, x, y, 1 - c))

    def arrivals(self, step, act):
        for way in (1, -1):
            zz = self.z - way * (step + 1)

            @pl.when((zz >= 0) & (zz < 4))
            def _(zz=zz, way=way):
                act(zz, way)

    def pass_on(self, zz, way):
        @pl.when((self.z + way >= 0) & (self.z + way < 4))
        def _():
            self.chain(zz, way).start()

    def first(self, zz):
        for copy in self.plane(zz, 0):
            copy.start()

    def load(self):
        for copy in self.own():
            copy.start()

    def start(self):
        for copy in self.own():
            copy.wait()
        for way in (1, -1):
            self.pass_on(self.z, way)
        self.first(self.z)

    def arrive(self, step):
        def act(zz, way):
            self.chain(zz, way, True).wait_recv()
            self.pass_on(zz, way)
            self.first(zz)

        self.arrivals(step, act)

    def second_of(self, zz, way=None):
        for copy in self.plane(zz, 0, True):
            copy.wait_recv()
        for copy in self.plane(zz, 1):
            copy.start()

    def third_of(self, zz, way=None):
        for copy in self.plane(zz, 1, True):
            copy.wait_recv()
        self.mate(zz).start()

    def second(self, step=None):
        if step is None:
            self.second_of(self.z)
        else:
            self.arrivals(step, self.second_of)

    def third(self, step=None):
        if step is None:
            self.third_of(self.z)
        else:
            self.arrivals(step, self.third_of)

    def finish(self, incoming=True):
        for zz in range(4):
            for step in range(2):
                for copy in self.plane(zz, step):
                    copy.wait_send()
        for zz in range(4):
            self.mate(zz).wait_send()
            if incoming:
                self.mate(zz, True).wait_recv()
        for way in (1, -1):

            @pl.when((self.z + way >= 0) & (self.z + way < 4))
            def _(way=way):
                for step in range(3):
                    zz = self.z - way * step

                    @pl.when((zz >= 0) & (zz < 4))
                    def _(zz=zz):
                        self.chain(zz, way).wait_send()


class Spread(Piece):
    def __init__(self, out, sems):
        super().__init__([], out, (None, None) + tuple(sems))

    def finish(self):
        for k in range(self.out.shape[0]):
            for step in range(2):
                for copy in self.plane(k, step):
                    copy.wait_send()
            self.mate(k).wait_send()
            self.mate(k, True).wait_recv()


class LayerWeights:
    def __init__(self, ins, outs, sems):
        (self.out_in, self.up_in, self.down_in), (out, self.up, self.down) = ins, outs
        self.own_sems, self.z_sems, sems = sems[0], sems[1], sems[2:]
        self.output = Piece([self.out_in], out, sems[:4])
        self.ups, self.downs = Spread(self.up, sems[4:6]), Spread(self.down, sems[6:8])
        self.z, self.x, self.y, self.c = place()
        self.side = lax.rem(self.z, 2)
        self.planes = (self.z, self.z + 1 - 2 * self.side, lax.rem(self.z + 2, 4), 3 - self.z)

    def up_block(self, side, k):
        size = self.up.shape[5] // 2
        return self.up_in.at[:, pl.ds(pl.multiple_of((2 * k + side) * size, 128), size)]

    def up_place(self, zz, k):
        size = self.up.shape[5] // 2
        return self.up.at[zz, self.x, self.y, self.c, :, pl.ds(k * size, size)]

    def owned(self):
        return [
            pltpu.make_async_copy(self.up_block(self.side, k), self.up_place(self.z, k), self.own_sems.at[k])
            for k in range(2)
        ] + [
            pltpu.make_async_copy(
                self.down_in, self.down.at[self.z // 2, self.x, self.y, self.c], self.own_sems.at[2]
            )
        ]

    def up_copies(self, i, incoming=False):
        other = self.planes[i]
        frm = other if incoming else self.z
        return [
            remote(
                self.up_block(lax.rem(other, 2), k), self.up_place(frm, k),
                self.z_sems.at[0, k, other], self.z_sems.at[1, k, frm], target(other, self.x, self.y, self.c),
            )
            for k in range(2)
        ]

    def down_copy(self, incoming=False):
        other = self.planes[2]
        frm = other if incoming else self.z
        return remote(
            self.down_in, self.down.at[frm // 2, self.x, self.y, self.c],
            self.z_sems.at[0, 2, other], self.z_sems.at[1, 2, frm], target(other, self.x, self.y, self.c),
        )

    def load(self):
        self.output.load()
        for copy in self.owned():
            copy.start()

    def send_up(self, i):
        for copy in self.up_copies(i):
            copy.start()

    def start(self):
        self.output.start()
        for copy in self.owned():
            copy.wait()
        self.downs.first(self.z // 2)
        self.ups.first(self.z)
        self.send_up(1)
        self.down_copy().start()

    def arrive_up(self, i):
        for copy in self.up_copies(i, True):
            copy.wait_recv()
        self.ups.first(self.planes[i])

    def arrive_down(self):
        self.down_copy(True).wait_recv()
        self.downs.first(self.planes[2] // 2)

    def steps(self):
        ups, downs, output, planes = self.ups, self.downs, self.output, self.planes
        here, there = self.z // 2, planes[2] // 2
        return [
            lambda: (
                output.arrive(0), self.arrive_up(1), self.send_up(2), ups.second_of(planes[0]), output.second(),
                downs.second_of(here),
            ),
            lambda: (
                output.arrive(1), self.send_up(3), output.second(0), ups.second_of(planes[1]), self.arrive_down(),
            ),
            lambda: (output.arrive(2), self.arrive_up(2), ups.third_of(planes[0]), output.third()),
            lambda: (
                self.arrive_up(3), downs.third_of(here), output.second(1), downs.second_of(there),
            ),
            lambda: (ups.third_of(planes[1]), output.third(0), output.second(2), ups.second_of(planes[2])),
            lambda: (output.third(1), ups.second_of(planes[3])),
            lambda: (
                downs.third_of(there), ups.third_of(planes[2]), output.third(2), ups.third_of(planes[3]),
            ),
        ]

    def finish(self):
        for i in range(1, 4):
            for copy in self.up_copies(i):
                copy.wait_send()
        self.down_copy().wait_send()
        self.ups.finish()
        self.downs.finish()
        self.output.finish()

    @staticmethod
    def shapes(weights):
        if not weights:
            return []
        out, up, down = weights
        return shares([out]) + [
            jax.ShapeDtypeStruct((4, 2, 2, 2, up.shape[0], up.shape[1] // 2), bf16),
            jax.ShapeDtypeStruct((2, 2, 2, 2) + down.shape, bf16),
        ]

    @staticmethod
    def scratch(weights):
        if not weights:
            return []
        spread = [pltpu.SemaphoreType.DMA((2, 4, 2, 2)), pltpu.SemaphoreType.DMA((2, 4))]
        return (
            [pltpu.SemaphoreType.DMA((3,)), pltpu.SemaphoreType.DMA((2, 3, 4))] + piece_scratch(1) + spread * 2
        )


def shares(weights):
    return [jax.ShapeDtypeStruct((4, 2, 2, 2) + w.shape, w.dtype) for w in weights]


def piece_scratch(count):
    return [
        pltpu.SemaphoreType.DMA((2,)),
        pltpu.SemaphoreType.DMA((2, 2, 4)),
        pltpu.SemaphoreType.DMA((2, 4, 2, 2)),
        pltpu.SemaphoreType.DMA((2, 4)),
    ] * count


class Rows:
    def __init__(self, rows_ref, most_ref, rows_out, most_out, sems):
        self.own_refs, self.outs = (rows_ref, most_ref), (rows_out, most_out)
        self.sems, self.mate_sems, self.own_sems = sems
        self.z, self.x, self.y, self.c = place()
        self.chip = (self.z * 2 + self.x) * 2 + self.y

    def out(self, k, to):
        device = target(to // 4, lax.rem(to // 2, 2), lax.rem(to, 2), self.c)
        src = self.own_refs[k].at[to] if k == 0 else self.own_refs[k]
        return remote(
            src, self.outs[k].at[self.chip, self.c], self.sems.at[0, k, to], self.sems.at[1, k, self.chip], device
        )

    def into(self, k, frm):
        device = target(frm // 4, lax.rem(frm // 2, 2), lax.rem(frm, 2), self.c)
        dst = self.outs[k].at[frm, self.c]
        return remote(dst, dst, self.sems.at[0, k, frm], self.sems.at[1, k, frm], device)

    def mate(self, k, of, core):
        ref = self.outs[k].at[of, core]
        to = target(self.z, self.x, self.y, 1 - self.c)
        return remote(ref, ref, self.mate_sems.at[0, k, of], self.mate_sems.at[1, k, of], to)

    def own(self, k):
        src = self.own_refs[k].at[self.chip] if k == 0 else self.own_refs[k]
        return pltpu.make_async_copy(src, self.outs[k].at[self.chip, self.c], self.own_sems.at[k])

    def send(self, to):
        @pl.when(to == self.chip)
        def _():
            for k in range(2):
                self.own(k).start()

        @pl.when(to != self.chip)
        def _():
            for k in range(2):
                self.out(k, to).start()

    def forward(self):
        for k in range(2):
            self.own(k).wait()
            self.mate(k, self.chip, self.c).start()
        for i in range(1, 16):
            frm = lax.rem(self.chip + 16 - i, 16)
            for k in range(2):
                self.into(k, frm).wait_recv()
                self.mate(k, frm, self.c).start()

    def finish(self):
        for i in range(16):
            of = lax.rem(self.chip + i, 16)
            for k in range(2):
                self.mate(k, of, self.c).wait_send()
                self.mate(k, of, 1 - self.c).wait_recv()
                if i:
                    self.out(k, of).wait_send()

    @staticmethod
    def shapes(rows, most):
        return [
            jax.ShapeDtypeStruct((16, 2) + rows[1:], bf16),
            jax.ShapeDtypeStruct((16, 2) + most, f32),
        ]

    @staticmethod
    def scratch():
        return [
            pltpu.SemaphoreType.DMA((2, 2, 16)),
            pltpu.SemaphoreType.DMA((2, 2, 16)),
            pltpu.SemaphoreType.DMA((2,)),
        ]


def rows_kernel(rows_ref, most_ref, rows_out, most_out, *sems):
    greet_all(32).wait()
    rows = Rows(rows_ref, most_ref, rows_out, most_out, sems)
    for to in range(16):
        rows.send(to)
    rows.forward()
    rows.finish()


def send_rows(rows, most, collective):
    return pl.pallas_call(
        rows_kernel,
        out_shape=Rows.shapes(rows.shape, most.shape),
        in_specs=[VMEM] * 2,
        out_specs=[ANY, VMEM],
        scratch_shapes=Rows.scratch(),
        compiler_params=params(collective),
        name="send_rows",
    )(rows, most)


def fetch_kernel(
    capacity, lens_ref, ids_ref, vec_ref, table_ref, qkv_ref, pos_ref,
    received_ref, most_ref, slot_ref, asked_ref, own_ref, mate_ref, vec_out, w_out,
    marks_ref, rank_ref, rows_ref, count_ref, mosts_ref, pack_ref, packs_ref, *sems,
):
    ask_sems, mate_sems = sems[:2]
    rows = Rows(rows_ref, count_ref, received_ref, mosts_ref, sems[2:5])
    piece = Piece([qkv_ref, pos_ref], w_out, sems[5:])
    greeting = greet_all(32)
    piece.load()
    local_rows = table_ref.shape[0]
    ids = jnp.concatenate(
        [
            jnp.where(iota(ids_ref.shape[1:], 1) < lens_ref[0, m], ids_ref[m], -1)
            for m in range(ids_ref.shape[0])
        ],
        axis=1,
    )
    own_ref[...] = presence(ids, 32, local_rows)
    length = vec_ref.shape[0]
    vec = jnp.pad(vec_ref[...].astype(f32).reshape(1, length), ((0, 0), (0, 1024 - length)))
    pack_ref[...] = jnp.concatenate([vec[:, k * 128 : (k + 1) * 128] for k in range(8)])
    me = own_number()
    z, x, y, c = place()
    to_mate = remote(own_ref, mate_ref, mate_sems.at[0], mate_sems.at[1], target(z, x, y, 1 - c))
    greeting.wait()

    def to_all(k, src, dst):
        copies = []
        for i in range(1, 32):
            to = lax.rem(me + i, 32)
            own = src.at[to] if k == 0 else src
            copies.append(remote(own, dst.at[me], ask_sems.at[0, k, i], ask_sems.at[1, k, i], nth(to)))
            copies[-1].start()
        return copies

    copies = to_all(0, own_ref, asked_ref)
    piece.start()
    to_mate.start()
    packs = to_all(1, pack_ref, packs_ref)
    asked_ref[me] = own_ref[me]
    packs_ref[me] = pack_ref[...]
    for copy in copies:
        copy.wait()
    together = jnp.concatenate(
        [jnp.maximum(asked_ref[2 * unit], asked_ref[2 * unit + 1]) for unit in range(16)]
    )
    rank, amount = ranked(together)
    count_ref[...] = jnp.broadcast_to(jnp.max(amount, keepdims=True), count_ref.shape)
    rank_ref[...] = rank
    mark_rows(capacity, rank_ref, marks_ref, 16, local_rows)
    piece.second()
    piece.arrive(0)
    planes = [lax.rem(z + i, 4) for i in (2, 3, 1, 0)]
    for plane in planes:
        rows_ref[pl.ds(plane * 4, 4)] = look_up(capacity, plane, marks_ref, table_ref)
    piece.second(0)
    piece.arrive(1)
    for plane in planes:
        for k in range(4):
            rows.send(plane * 4 + lax.rem(x * 2 + y + k, 4))
    piece.third()
    piece.second(1)
    piece.third(0)
    to_mate.wait()
    slot_ref[...] = slots_of(capacity, 0.0, local_rows, ids, own_ref, mate_ref)
    for copy in packs:
        copy.wait()
    width = vec_out.shape[1]
    for device in range(32):
        for k in range(-(-length // 128)):
            begin, end = k * 128, min(length, k * 128 + 128)
            at = device * length + begin
            while begin < end:
                count = min(end - begin, 128 - at % 128)
                vec_out[at // width : at // width + 1, at % width : at % width + count] = packs_ref[
                    device, k : k + 1, begin - k * 128 : begin - k * 128 + count
                ]
                at, begin = at + count, begin + count
    piece.arrive(2)
    piece.third(1)
    piece.second(2)
    piece.third(2)
    rows.forward()
    rows.finish()
    piece.finish()
    most_ref[0] = jnp.max(mosts_ref[...])


def fetch(lens, ids, vec, table, qkv, positions, capacity, collective):
    grids = jax.ShapeDtypeStruct((32, GRID, 128), bf16)
    width = table.shape[1]
    w = jax.ShapeDtypeStruct((qkv.shape[0], qkv.shape[1] + positions.shape[1]), bf16)
    return pl.pallas_call(
        functools.partial(fetch_kernel, capacity),
        out_shape=[
            jax.ShapeDtypeStruct((16, 2, capacity, width), bf16), jax.ShapeDtypeStruct((1,), f32),
            jax.ShapeDtypeStruct((1, ids.size), jnp.int32), grids, grids, grids,
            jax.ShapeDtypeStruct((32 * vec.shape[0] // width, width), f32),
        ]
        + shares([w]),
        in_specs=[pl.BlockSpec(memory_space=pltpu.SMEM)] + [VMEM] * 3 + [ANY] * 2,
        out_specs=[ANY, pl.BlockSpec(memory_space=pltpu.SMEM)] + [VMEM] * 5 + [ANY],
        scratch_shapes=[
            pltpu.VMEM((16 * capacity, table.shape[0]), bf16),
            pltpu.VMEM((16 * GRID, 128), f32),
            pltpu.VMEM((16, capacity, width), bf16),
            pltpu.VMEM((8, 128), f32),
            pltpu.VMEM((16, 2, 8, 128), f32),
            pltpu.VMEM((8, 128), f32),
            pltpu.VMEM((32, 8, 128), f32),
            pltpu.SemaphoreType.DMA((2, 2, 32)),
            pltpu.SemaphoreType.DMA((2,)),
        ]
        + Rows.scratch()
        + piece_scratch(1),
        compiler_params=params(collective),
        name="fetch",
    )(lens, ids, vec, table, qkv, positions)


def vocabulary_kernel(group, rows_ref, table_ref, mean_ref, total_ref):
    logits = dot(rows_ref[...], table_ref[...], 1, 1)
    top = jnp.max(logits, axis=1, keepdims=True)
    weights = jnp.exp(logits - top)
    amount = jnp.sum(weights, axis=1, keepdims=True)
    mean = dot(weights.astype(bf16), table_ref[...], 1, 0)
    mean_ref[...] = (mean / amount).astype(bf16)
    total = top + jnp.log(amount)
    for k in range(total_ref.shape[0]):
        total_ref[k] = as_tile(as_row(total[k * group : (k + 1) * group]))


def as_tile(row):
    return jnp.broadcast_to(jnp.pad(row, ((0, 0), (0, 128 - row.shape[1]))), (8, 128))


def same(size):
    return iota((size, size), 0) == iota((size, size), 1)


def as_row(column):
    return jnp.sum(jnp.where(same(column.shape[0]), column, 0.0), axis=0, keepdims=True)


def as_column(row):
    return jnp.sum(jnp.where(same(row.shape[1]), row, 0.0), axis=1, keepdims=True)


def vocabulary(rows, table, group, tile):
    count, width = rows.shape
    return pl.pallas_call(
        functools.partial(vocabulary_kernel, group),
        grid=(count // tile,),
        out_shape=[
            jax.ShapeDtypeStruct((count, width), bf16),
            jax.ShapeDtypeStruct((count // group, 8, 128), f32),
        ],
        in_specs=[
            pl.BlockSpec((tile, width), lambda i: (i, 0)),
            pl.BlockSpec(table.shape, lambda i: (0, 0)),
        ],
        out_specs=[
            pl.BlockSpec((tile, width), lambda i: (i, 0)),
            pl.BlockSpec((tile // group, 8, 128), lambda i: (i, 0, 0)),
        ],
        compiler_params=params(),
        name="vocabulary",
    )(rows, table)


def merged(parts):
    size = parts[0][0].shape[0]
    rows = [total[:1, :size] for _, total in parts]
    top = functools.reduce(jnp.maximum, rows)
    total = top + jnp.log(sum(jnp.exp(row - top) for row in rows))
    mean = sum(
        values.astype(f32) * as_column(jnp.exp(row - total)) for (values, _), row in zip(parts, rows)
    )
    return mean, as_tile(total)


def exact(a, b, ca, cb):
    return lax.dot_general(
        a, b, (((ca,), (cb,)), ((), ())), precision=lax.Precision.HIGHEST, preferred_element_type=f32
    )


def fine(a, b, cb):
    a_high, b_high = a.astype(bf16), b.astype(bf16)
    a_low, b_low = (a - a_high.astype(f32)).astype(bf16), (b - b_high.astype(f32)).astype(bf16)
    return dot(a_high, b_high, 1, cb) + (dot(a_high, b_low, 1, cb) + dot(a_low, b_high, 1, cb))


def small_product(a, b):
    return sum(a[:, k : k + 1] * b[k : k + 1, :] for k in range(a.shape[0]))


def newton(matrix, product, apply, state):
    size = matrix.shape[0]
    identity = jnp.where(same(size), 1.0, 0.0)
    trace = jnp.sum(matrix * identity, keepdims=True)

    def step(_, carry):
        current, state = carry
        factor = (5.0 * identity - current) * 0.25
        square = product(factor, factor)
        return product(product(square, square), current), apply(state, factor)

    current, state = lax.fori_loop(0, NEWTON - 1, step, (matrix / trace, state))
    state = apply(state, (5.0 * identity - current) * 0.25)
    return state * lax.rsqrt(jnp.sqrt(trace))


def clipped(g_ref, rank):
    data = jnp.where(iota(g_ref.shape, 1) < rank, g_ref[...], 0.0)
    norm = jnp.sqrt(jnp.sum(data * data, keepdims=True).reshape(1, 1))
    return data * (clip_level / jnp.maximum(norm, clip_level)), norm


def renew(g_ref, down_ref, up_ref, left_ref, right_ref, clip_ref, new_ref):
    owned, block = left_ref.shape[0], left_ref.shape[1]
    rank = right_ref.shape[1]
    group = lax.axis_index("fsdp")
    own = lax.rem(lax.axis_index("dp"), owned)
    clip_ref[...], _ = clipped(g_ref, rank)
    columns = pl.ds(pl.multiple_of(own * block, block), block)
    grad = clip_ref[group, :, columns]
    left, right = stats_of(left_ref[own], right_ref[own], grad)
    left = left + root_eps * jnp.where(same(block), 1.0, 0.0)
    right = right + root_eps * jnp.where(same(rank), 1.0, 0.0)
    root = newton(right, small_product, small_product, jnp.where(same(rank), 1.0, 0.0))
    rows = newton(left, lambda a, b: fine(a, b, 0), lambda a, b: fine(a, b, 1), grad)[:rank]
    update = sum(as_column(root[k : k + 1, :]) * rows[k : k + 1, :] for k in range(rank))
    old = [ref[k * rank : (k + 1) * rank, columns] for ref in (down_ref, up_ref) for k in range(2)]
    old = functools.reduce(lambda a, k: jnp.where(group == k, old[k], a), range(1, 4), old[0])
    new = old - learn_rate * update
    new_ref[...] = jnp.pad(new, ((0, 8 - rank), (0, 0)))


def stats_of(left, right, grad):
    rank = right.shape[0]
    return (
        beta_stats * left + (1.0 - beta_stats) * exact(grad, grad, 0, 0),
        beta_stats * right + (1.0 - beta_stats) * exact(grad, grad, 1, 1)[:rank, :rank],
    )


def settle_kernel(g_ref, all_ref, left_ref, right_ref, loss_ref, norm_ref, a_ref, b_ref, left_out, right_out, a_new, b_new, clip_ref):
    owned, block = left_ref.shape[0], left_ref.shape[1]
    rank = right_ref.shape[1]
    clip_ref[...], norm = clipped(g_ref, rank)
    norm_ref[0] = jnp.sum(norm)
    for k in range(2):
        loss_ref[k] = jnp.sum(g_ref[0, rank : rank + 1, k : k + 1])
    a_ref[...] = jnp.concatenate([clip_ref[0, :rank], clip_ref[1, :rank]])
    b_ref[...] = jnp.concatenate([clip_ref[2, :rank], clip_ref[3, :rank]])
    group = lax.axis_index("fsdp")
    for k in range(owned):
        grad = clip_ref[group, :, k * block : (k + 1) * block]
        left_out[k], right_out[k] = stats_of(left_ref[k], right_ref[k], grad)
    for k in range(all_ref.shape[0]):
        ref, row = (a_new, b_new)[k // 8], k // 4 % 2 * rank
        ref[row : row + rank, k % 4 * block : (k % 4 + 1) * block] = all_ref[k, :rank]


def settled(gradient, blocks, left, right):
    width = gradient.shape[2]
    shapes = [(2,), (1,), (8, width), (8, width), left.shape, right.shape, (8, width), (8, width)]
    return pl.pallas_call(
        settle_kernel,
        out_shape=[jax.ShapeDtypeStruct(shape, f32) for shape in shapes],
        in_specs=[VMEM] * 4,
        out_specs=[pl.BlockSpec(memory_space=pltpu.SMEM)] * 2 + [VMEM] * 6,
        scratch_shapes=[pltpu.VMEM(gradient.shape, f32)],
        compiler_params=params(),
        name="settled",
    )(gradient, blocks, left, right)


def renew_kernel(*refs):
    renew(*refs)


def renewed(gradient, down, up, left, right):
    return pl.pallas_call(
        renew_kernel,
        out_shape=[
            jax.ShapeDtypeStruct(gradient.shape, f32), jax.ShapeDtypeStruct((8, left.shape[1]), f32),
        ],
        in_specs=[VMEM] * 5,
        out_specs=[VMEM] * 2,
        compiler_params=params(),
        name="renewed",
    )(gradient, down, up, left, right)


def finish_kernel(
    back, count, *refs,
):
    back_in, refs = refs[:count], refs[count:]
    (down_ref, up_ref, left_ref, right_ref, total_out, all_out), refs = refs[:6], refs[6:]
    (total_ref, all_ref, g_ref, dq_ref, dlow_ref), refs = refs[:5], refs[5:]

    @pl.when(pl.program_id(0) == 0)
    def _():
        greet_all(32)

    back(*back_in, g_ref, dq_ref, dlow_ref)

    @pl.when(pl.program_id(0) == pl.num_programs(0) - 1)
    def _():
        pl.semaphore_wait(pltpu.get_barrier_semaphore(), 31)
        finish(g_ref, down_ref, up_ref, left_ref, right_ref, total_ref, all_ref, *refs)
        total_out[...] = total_ref[...]
        all_out[...] = all_ref[...]


def finish(
    g_ref, down_ref, up_ref, left_ref, right_ref, total_ref, all_ref,
    parts, summed, clip_ref, new_ref, one_sems, two_sems, block_sems,
):
    me = own_number()

    def tile(ref, k):
        return ref.at[k // 8, :, pl.ds(pl.multiple_of(lax.rem(k, 8) * 128, 128), 128)]

    def out(i):
        to = lax.rem(me + i, 32)
        return remote(tile(g_ref, to), parts.at[me], one_sems.at[0, to], one_sems.at[1, me], nth(to))

    def into(i):
        frm = lax.rem(me + i, 32)
        return remote(tile(g_ref, me), parts.at[frm], one_sems.at[0, frm], one_sems.at[1, frm], nth(frm))

    def back(i):
        to = lax.rem(me + i, 32)
        return remote(summed, tile(total_ref, me), two_sems.at[0, to], two_sems.at[1, me], nth(to))

    def into_back(i):
        frm = lax.rem(me + i, 32)
        return remote(summed, tile(total_ref, frm), two_sems.at[0, frm], two_sems.at[1, frm], nth(frm))

    for i in range(1, 32):
        out(i).start()
    columns = pl.ds(pl.multiple_of(lax.rem(me, 8) * 128, 128), 128)
    for i in range(1, 32):
        into(i).wait_recv()
    running = g_ref[me // 8, :, columns]
    for i in range(1, 32):
        running = running + parts[lax.rem(me + i, 32)]
    summed[...] = running
    total_ref[me // 8, :, columns] = running
    for i in range(1, 32):
        back(i).start()
    for i in range(1, 32):
        into_back(i).wait_recv()
    renew(total_ref, down_ref, up_ref, left_ref, right_ref, clip_ref, new_ref)
    d, f = lax.axis_index("dp"), lax.axis_index("fsdp")
    half, mine = d // 4, f * 4 + lax.rem(d, 4)

    def share(i, incoming=False):
        k = lax.rem(mine + i, 16)
        device = (half * 4 + lax.rem(k, 4), k // 4)
        return remote(
            new_ref, all_ref.at[k if incoming else mine],
            block_sems.at[0, k], block_sems.at[1, k if incoming else mine], device,
        )

    for i in range(1, 16):
        share(i).start()
    all_ref[mine] = new_ref[...]
    for i in range(1, 16):
        share(i, True).wait_recv()
    for i in range(1, 16):
        share(i).wait_send()
    for i in range(1, 32):
        out(i).wait_send()
        back(i).wait_send()


def finished(back, down, up, left, right, collective):
    new = (8, left.shape[1])
    shape = back["shape"]
    return pl.pallas_call(
        functools.partial(finish_kernel, back["kernel"], len(back["args"])),
        grid=back["grid"],
        out_shape=[jax.ShapeDtypeStruct(shape, f32), jax.ShapeDtypeStruct((16,) + new, f32)],
        in_specs=back["in_specs"] + [whole(v.shape) for v in (down, up, left, right)],
        out_specs=[whole(shape), whole((16,) + new)],
        scratch_shapes=[pltpu.VMEM(shape, f32), pltpu.VMEM((16,) + new, f32), pltpu.VMEM(shape, f32)]
        + back["scratch_shapes"]
        + [
            pltpu.VMEM((32, 8, 128), f32),
            pltpu.VMEM((8, 128), f32),
            pltpu.VMEM(shape, f32),
            pltpu.VMEM(new, f32),
            pltpu.SemaphoreType.DMA((2, 32)),
            pltpu.SemaphoreType.DMA((2, 32)),
            pltpu.SemaphoreType.DMA((2, 16)),
        ],
        compiler_params=params(collective),
        name="finished",
    )(*back["args"], down, up, left, right)


def normal(v, gain, shift):
    centred = v - jnp.mean(v, axis=-1, keepdims=True)
    inverse = lax.rsqrt(jnp.mean(centred * centred, axis=-1, keepdims=True) + ln_eps)
    normed = centred * inverse
    return normed * gain + shift, normed, inverse


def normal_back(grad, gain, normed, inverse):
    scaled = grad * gain
    return inverse * (
        scaled
        - jnp.mean(scaled, axis=-1, keepdims=True)
        - normed * jnp.mean(scaled * normed, axis=-1, keepdims=True)
    )


GAIN, SHIFT, QKV_BIAS, OUT_BIAS, UP_BIAS = (0, 2, 4), (1, 3, 5), 6, 9, 10


def expand_chunk(slot_ref, rows_ref, begin, chunk):
    count = rows_ref.shape[0]
    part = lambda k: slot_ref[0, :, pl.ds(pl.multiple_of(begin + k, 128), 128)].astype(f32)
    column = jnp.concatenate([as_column(part(k)) for k in range(0, chunk, 128)]).astype(jnp.int32)
    return dot(marks(iota((chunk, count), 1) == column), rows_ref[...], 1, 0)


def spread_heads(v, heads, size):
    rows, width = v.shape
    tiled = jnp.concatenate([v] * heads, axis=0)
    shape = (heads * rows, width)
    return jnp.where(iota(shape, 0) // rows == iota(shape, 1) // size, tiled, jnp.zeros((), v.dtype))


def join_heads(v, heads, size):
    rows = v.shape[0] // heads
    own = jnp.where(iota(v.shape, 0) // rows == iota(v.shape, 1) // size, v, 0.0)
    return sum(own[k * rows : (k + 1) * rows] for k in range(heads))


def two_sets(v, rows):
    rank, width = v.shape[0] // 2, v.shape[1]
    v = v.astype(bf16)
    zeros = lambda count: jnp.zeros((count, width), bf16)
    return jnp.concatenate([v[:rank], zeros(8 - rank), v[rank:], zeros(rows - 8 - rank)])


def attend_kernel(
    heads, adapter_scale, count_w, with_more, lens_ref, slot_ref, rows_hbm, wide_hbm, vec_ref, pick_ref,
    down_ref, up_ref, *refs,
):
    if with_more:
        more_ref, *refs = refs
    w_in, refs = refs[:count_w], refs[count_w:]
    (h1_ref, low_ref, k_ref, v_ref, p_ref, h1p_ref, lowp_ref, xp_ref, wanted_ref, att_ref), refs = refs[:10], refs[10:]
    w_out, refs = refs[:count_w], refs[count_w:]
    if count_w:
        (xp_pair, att_pair), refs = refs[:2], refs[2:]
    (emb_ref, q_ref, rows_ref, pos_ref, qkv_ref, load_sems), sems = refs[:6], refs[6:]
    if count_w:
        (xp_own, att_own, pair_sems), sems = sems[:3], sems[3:]
    micro = pl.program_id(0)
    count, width = emb_ref.shape
    length = lens_ref[0, micro]
    down, up = two_sets(down_ref[...], 128), two_sets(up_ref[...], 16)
    size = width // heads
    chunk = 256
    vec = lambda k: vec_ref[k : k + 1, :]
    if count_w:
        gather = LayerWeights(w_in, w_out, sems)
        steps = gather.steps()

        def to_pair(m):
            device = target(gather.planes[1], gather.x, gather.y, gather.c)
            return [
                remote(src.at[m], dst.at[m], pair_sems.at[0, k, m], pair_sems.at[1, k, m], device)
                for k, (src, dst) in enumerate(((xp_own, xp_pair), (att_own, att_pair)))
            ]

    def beside(loop):
        for number, step in enumerate(steps[:6] if count_w else []):
            if number % 3 == loop:

                @pl.when(micro == number // 3)
                def _(step=step):
                    step()

    parts = ((rows_hbm, rows_ref), (wide_hbm.at[:, 3 * width :], pos_ref), (wide_hbm.at[:, : 3 * width], qkv_ref))
    loads = [pltpu.make_async_copy(src, dst, load_sems.at[k]) for k, (src, dst) in enumerate(parts)]

    @pl.when(micro == 0)
    def _():
        if count_w:
            greeting = greet_near()
        for load in loads:
            load.start()
        if count_w:
            gather.load()
            greeting.wait()
            gather.start()
        for load in loads[:2]:
            load.wait()

    @pl.loop(0, count // chunk)
    def _(k):
        rows = pl.ds(pl.multiple_of(k * chunk, chunk), chunk)
        emb = expand_chunk(slot_ref, rows_ref, k * chunk, chunk).astype(bf16)
        if with_more:
            emb = emb + more_ref[0, rows]
        emb_ref[rows] = emb
        x = emb.astype(f32) + pos_ref[rows].astype(f32)
        h1_ref[0, rows] = normal(x, vec(GAIN[0]), vec(SHIFT[0]))[0].astype(bf16)

    @pl.when(micro == 0)
    def _():
        loads[2].wait()

    beside(0)

    @pl.loop(0, count // chunk)
    def _(k):
        rows = pl.ds(pl.multiple_of(k * chunk, chunk), chunk)
        h1 = h1_ref[0, rows]
        low = dot(h1, down, 1, 1).astype(bf16)
        low_ref[0, rows] = low
        keys = dot(h1, qkv_ref[:, width : 2 * width], 1, 0) + vec(QKV_BIAS + 1)
        k_ref[0, rows] = keys.astype(bf16)
        values = dot(h1, qkv_ref[:, 2 * width :], 1, 0) + vec(QKV_BIAS + 2)
        values += adapter_scale * dot(low[:, 8:16], up[8:16], 1, 0)
        v_ref[0, rows] = values.astype(bf16)

    beside(1)

    pick = as_column(pick_ref[0].astype(f32)).astype(jnp.int32)
    picks = pick.shape[0]
    here = marks(iota((picks, count), 1) == pick)
    after = marks(iota((picks, count), 1) == pick + 1)
    taken = dot(jnp.concatenate([here, after]), emb_ref[...], 1, 0)
    xp_ref[0] = taken[:picks] + dot(here, pos_ref[...], 1, 0)
    wanted_ref[0] = taken[picks:].astype(bf16)
    h1p = dot(here, h1_ref[0], 1, 0).astype(bf16)
    lowp = dot(here, low_ref[0], 1, 0).astype(bf16)
    h1p_ref[0] = h1p
    lowp_ref[0] = lowp
    queries = dot(h1p, qkv_ref[:, :width], 1, 0) + vec(QKV_BIAS)
    queries += adapter_scale * dot(lowp[:, 0:8], up[0:8], 1, 0)
    q_ref[...] = queries.astype(bf16)
    some = 256 // size
    slot = iota((picks, count), 1)
    allowed = (slot <= pick) & (slot < length)
    allowed = jnp.concatenate([jnp.where(allowed, 1.0, 0.0)] * some, axis=0) > 0.5

    @pl.loop(0, width // 256)
    def _(k):
        lanes = pl.ds(pl.multiple_of(k * 256, 256), 256)
        scores = dot(spread_heads(q_ref[:, lanes], some, size), k_ref[0, :, lanes], 1, 1)
        scores = jnp.where(allowed, scores * size**-0.5, masked_score)
        weights = jnp.exp(scores - jnp.max(scores, axis=1, keepdims=True))
        probs = (weights / jnp.sum(weights, axis=1, keepdims=True)).astype(bf16)
        p_ref[0, pl.ds(pl.multiple_of(k * some * picks, some * picks), some * picks)] = probs
        attended = dot(probs, v_ref[0, :, lanes], 1, 0)
        att_ref[0, :, lanes] = join_heads(attended, some, size).astype(bf16)

    beside(2)

    if count_w:
        xp_own[micro] = xp_ref[0]
        att_own[micro] = att_ref[0]
        for copy in to_pair(micro):
            copy.start()

        @pl.when(micro == pl.num_programs(0) - 1)
        def _():
            steps[6]()
            gather.finish()
            for m in range(xp_own.shape[0]):
                for copy in to_pair(m):
                    copy.wait()


def whole(shape):
    return pl.BlockSpec(shape, lambda *_: (0,) * len(shape))


def of_micro(shape):
    return pl.BlockSpec((1,) + shape, lambda m: (m,) + (0,) * len(shape))


def attend(heads, adapter_scale, lens, slot, rows, more, wide, vec, pick, down, up, weights, collective):
    micros, _, count = slot.shape
    width = rows.shape[1]
    picks = pick.shape[2]
    more = [] if more is None else [more]
    outs = [
        ((count, width), bf16), ((count, 128), bf16), ((count, width), bf16), ((count, width), bf16),
        ((heads * picks, count), bf16), ((picks, width), bf16), ((picks, 128), bf16),
        ((picks, width), f32), ((picks, width), bf16), ((picks, width), bf16),
    ]
    return pl.pallas_call(
        functools.partial(attend_kernel, heads, adapter_scale, len(weights), len(more) > 0),
        grid=(micros,),
        out_shape=[jax.ShapeDtypeStruct((micros,) + shape, kind) for shape, kind in outs]
        + LayerWeights.shapes(weights)
        + [jax.ShapeDtypeStruct((micros, picks, width), kind) for kind in (f32, bf16) if weights],
        in_specs=[
            pl.BlockSpec(memory_space=pltpu.SMEM), of_micro((1, count)), ANY, ANY, whole(vec.shape), of_micro((1, picks)), whole(down.shape), whole(up.shape),
        ]
        + [of_micro((count, width))] * len(more)
        + [ANY] * len(weights),
        out_specs=[of_micro(shape) for shape, _ in outs] + [ANY] * (len(weights) + 2 if weights else 0),
        scratch_shapes=[
            pltpu.VMEM((count, width), bf16), pltpu.VMEM((picks, width), bf16), pltpu.VMEM(rows.shape, bf16),
            pltpu.VMEM((count, width), bf16), pltpu.VMEM((width, 3 * width), bf16), pltpu.SemaphoreType.DMA((3,)),
        ]
        + [pltpu.VMEM((micros, picks, width), kind) for kind in (f32, bf16) if weights]
        + [pltpu.SemaphoreType.DMA((2, 2, micros)) for _ in weights[:1]]
        + LayerWeights.scratch(weights),
        compiler_params=params(collective),
        name="attend",
    )(lens, slot, rows, wide, vec, pick, down, up, *more, *weights)


def attend_back_kernel(
    heads, adapter_scale, rank, datt_ref, h1_ref, low_ref, k_ref, v_ref, p_ref, h1p_ref, lowp_ref, up_ref, loss_ref,
    g_ref, dq_ref, dlow_ref,
):
    count, width = h1_ref.shape[1:]
    size = width // heads
    picks = datt_ref.shape[1]
    some = 256 // size
    up = two_sets(up_ref[...], 16)

    @pl.when(pl.program_id(0) == 0)
    def _():
        g_ref[...] = jnp.zeros_like(g_ref)
        g_ref[0, rank : rank + 1, :128] = loss_ref[:1, :]

    dlow_ref[...] = jnp.zeros_like(dlow_ref)

    @pl.loop(0, width // 256)
    def _(k):
        lanes = pl.ds(pl.multiple_of(k * 256, 256), 256)
        own = pl.ds(pl.multiple_of(k * some * picks, some * picks), some * picks)
        d_heads = spread_heads(datt_ref[0, :, lanes], some, size)
        probs_b = p_ref[0, own]
        probs = probs_b.astype(f32)
        d_probs = dot(d_heads, v_ref[0, :, lanes], 1, 1)
        v_up = two_sets_of_values(up_ref, lanes)
        dlow_ref[...] += dot(dot(d_heads, v_up, 1, 1).astype(bf16), probs_b, 0, 0)
        taken = dot(probs_b, low_ref[0, :, 8:16], 1, 0)
        g_ref[3, :, lanes] += adapter_scale * dot(taken.astype(bf16), d_heads, 0, 0)
        weighted = probs * d_probs
        d_scores = weighted - probs * jnp.sum(weighted, axis=1, keepdims=True)
        d_queries = dot(d_scores.astype(bf16), k_ref[0, :, lanes], 1, 0)
        dq_ref[:, lanes] = (join_heads(d_queries, some, size) * size**-0.5).astype(bf16)

    d_low_q = (adapter_scale * dot(dq_ref[...], up[0:8], 1, 1)).astype(bf16)
    d_low_v = (adapter_scale * dlow_ref[...]).astype(bf16)
    g_ref[0] += dot(d_low_q, h1p_ref[0], 0, 0)
    g_ref[1] += dot(d_low_v, h1_ref[0], 1, 0)
    g_ref[2] += adapter_scale * dot(lowp_ref[0, :, 0:8], dq_ref[...], 0, 0)


def two_sets_of_values(up_ref, lanes):
    rank = up_ref.shape[0] // 2
    v = up_ref[:, lanes].astype(bf16)[rank:]
    return jnp.concatenate([v, jnp.zeros((8 - rank, v.shape[1]), bf16)])


def back_parts(heads, adapter_scale, rank, datt, h1, low, keys, values, probs, h1p, lowp, up, loss):
    micros, count, width = h1.shape
    picks = datt.shape[1]
    ins = (datt, h1, low, keys, values, probs, h1p, lowp)
    return dict(
        kernel=functools.partial(attend_back_kernel, heads, adapter_scale, rank),
        grid=(micros,),
        in_specs=[of_micro(v.shape[1:]) for v in ins] + [whole(up.shape), whole(loss.shape)],
        args=(*ins, up, loss),
        shape=(4, 8, width),
        scratch_shapes=[pltpu.VMEM((picks, width), bf16), pltpu.VMEM((8, count), f32)],
    )


def attend_back(parts):
    return pl.pallas_call(
        parts["kernel"],
        grid=parts["grid"],
        out_shape=jax.ShapeDtypeStruct(parts["shape"], f32),
        in_specs=parts["in_specs"],
        out_specs=whole(parts["shape"]),
        scratch_shapes=parts["scratch_shapes"],
        compiler_params=params(),
        name="attend_back",
    )(*parts["args"])


def gelu(v):
    inner = 0.7978845608028654 * (v + 0.044715 * v * v * v)
    return 0.5 * v * (1.0 + jnp.tanh(inner))


def gelu_slope(v):
    bend = jnp.tanh(0.7978845608028654 * (v + 0.044715 * v * v * v))
    return 0.5 * (1.0 + bend) + 0.5 * v * (1.0 - bend * bend) * 0.7978845608028654 * (
        1.0 + 3.0 * 0.044715 * v * v
    )


def middle_kernel(
    lens_ref, pick_ref, att_ref, xp_ref, att_pair, xp_pair, wanted_ref, vec_ref, out_hbm, up_hbm, down_hbm, table_ref, datt_ref, loss_ref,
    out_ref, up_ref, down_ref, middle_ref, two_ref, three_ref, hidden_ref, before_ref, final_ref,
    rows_ref, part_ref, got_ref, load_sems, pair_sems, every_ref, q_ref, t_ref, core_q, core_t, keep_q, keep_t, send_q, send_t, got_q, got_t,
    next_q, next_t, pass_q, pass_t, last_q, last_t, end_q, end_t, final_q, final_t,
    core_sems, one_sems, two_sems, z_sems, *sems,
):
    rows, width = hidden_ref.shape
    piece = Piece([hidden_ref], every_ref, sems)
    greeting = greet_near()
    vec = lambda k: vec_ref[k : k + 1, :]
    loads = [
        pltpu.make_async_copy(src, dst, load_sems.at[k])
        for k, (src, dst) in enumerate(((out_hbm, out_ref), (up_hbm, up_ref), (down_hbm, down_ref)))
    ]
    for load in loads:
        load.start()
    z, x, y, c = place()
    side = lax.rem(z, 2)
    pair = target(z + 1 - 2 * side, x, y, c)

    def to_pair(number, values):
        rows_ref[0] = values
        copy = remote(
            rows_ref.at[0], rows_ref.at[1], pair_sems.at[0, 4 + number], pair_sems.at[1, 4 + number], pair
        )
        copy.start()
        copy.wait()
        return rows_ref[...].reshape(2 * rows, width)

    half = width // 2
    cols = (slice(0, half), slice(half, width))

    def of_pair(number, product):
        own, copies = [], []
        for k in range(2):
            part = product(cols[k])
            part_ref[k] = part[rows:].astype(bf16)
            spot = 2 * number + k
            copy = remote(part_ref.at[k], got_ref.at[k], pair_sems.at[0, spot], pair_sems.at[1, spot], pair)
            copy.start()
            own.append(part[:rows])
            copies.append(copy)
        for copy in copies:
            copy.wait()
        return jnp.concatenate([own[k] + got_ref[k].astype(f32) for k in range(2)], axis=1)

    loads[0].wait()
    both = lambda own, other: jnp.concatenate([own[...], other[...]])
    middle = both(xp_ref, xp_pair) + dot(both(att_ref, att_pair), out_ref[...], 1, 0) + vec(OUT_BIAS)
    middle_ref[...] = middle[:rows]
    every_h2, two, inverse_two = normal(middle, vec(GAIN[1]), vec(SHIFT[1]))
    two_ref[...], inverse_two = two[:rows], inverse_two[:rows]
    bias = jnp.concatenate(
        [jnp.where(side == 0, vec(UP_BIAS + 2 * k), vec(UP_BIAS + 2 * k + 1)) for k in range(2)], axis=1
    )
    loads[1].wait()
    before = dot(every_h2.astype(bf16), up_ref[...], 1, 0) + bias
    before_ref[...] = before
    loads[2].wait()
    activated = gelu(before).astype(bf16)
    greeting.wait()
    added = of_pair(0, lambda some: dot(activated, down_ref[:, some], 1, 0))
    final = middle_ref[...] + added + vec(vec_ref.shape[0] - 1)
    hidden, three, inverse_three = normal(final, vec(GAIN[2]), vec(SHIFT[2]))
    hidden_ref[...] = hidden.astype(bf16)
    three_ref[...] = three

    piece.load()
    mate = target(z, x, y, 1 - c)
    over = (target(z, 1 - x, y, c), target(z, x, 1 - y, c))
    mine = (x, y)
    is_end = (z == 0) | (z == 3)
    up = jnp.where((z == 0) | (z == 2), 1, -1)

    def nth_plane(i):
        from_end = z + up * i
        inside = jnp.where(i == 0, z, jnp.where(i == 1, z + up, jnp.where(i == 2, z - up, z - 2 * up)))
        return jnp.where(is_end, from_end, inside)

    def core_copies(zz):
        return [
            remote(q_ref.at[zz, :, :, 1 - c], core_q.at[zz], core_sems.at[0, 0, zz], core_sems.at[1, 0, zz], mate),
            remote(t_ref.at[zz, :, :, 1 - c], core_t.at[zz], core_sems.at[0, 1, zz], core_sems.at[1, 1, zz], mate),
        ]

    def one_copies(zz, k):
        return [
            remote(send_q.at[k, zz], got_q.at[k, zz], one_sems.at[0, 0, k, zz], one_sems.at[1, 0, k, zz], over[k]),
            remote(send_t.at[k, zz], got_t.at[k, zz], one_sems.at[0, 1, k, zz], one_sems.at[1, 1, k, zz], over[k]),
        ]

    def two_copies(zz, k):
        return [
            remote(pass_q.at[k, zz], last_q.at[k, zz], two_sems.at[0, 0, k, zz], two_sems.at[1, 0, k, zz], over[1 - k]),
            remote(pass_t.at[k, zz], last_t.at[k, zz], two_sems.at[0, 1, k, zz], two_sems.at[1, 1, k, zz], over[1 - k]),
        ]

    def z_copies(zz, frm, k):
        return [
            remote(end_q.at[k, zz], final_q.at[k, frm], z_sems.at[0, 0, k, zz], z_sems.at[1, 0, k, frm], target(zz, x, y, c)),
            remote(end_t.at[k, zz], final_t.at[k, frm], z_sems.at[0, 1, k, zz], z_sems.at[1, 1, k, frm], target(zz, x, y, c)),
        ]

    def start(copies):
        for copy in copies:
            copy.start()

    def landed(copies):
        for copy in copies:
            copy.wait_recv()

    def left(copies):
        for copy in copies:
            copy.wait_send()

    def arrive(i):
        zz = nth_plane(i)
        way = jnp.where(zz < z, 1, -1)
        piece.chain(zz, way, True).wait_recv()
        piece.pass_on(zz, way)
        piece.first(zz)

    def second(i):
        piece.second_of(nth_plane(i))

    def third(i):
        piece.third_of(nth_plane(i))

    def compute(i):
        zz = nth_plane(i)
        piece.mate(zz, True).wait_recv()

        @pl.loop(0, 2)
        def _(xx):
            logits = dot(every_ref[zz, xx].reshape(4 * rows, width), table_ref[...], 1, 1)
            top = jnp.max(logits, axis=1, keepdims=True)
            weights = jnp.exp(logits - top)
            amount = jnp.sum(weights, axis=1, keepdims=True)
            mean = dot(weights.astype(bf16), table_ref[...], 1, 0) / amount
            q_ref[zz, xx] = mean.astype(bf16).reshape(2, 2, rows, width)
            total = top + jnp.log(amount)
            for k in range(4):
                t_ref[zz, xx, k // 2, k % 2] = as_tile(as_row(total[k * rows : (k + 1) * rows]))

        start(core_copies(zz))

    def merge_cores(i):
        zz = nth_plane(i)
        landed(core_copies(zz))

        @pl.loop(0, 2)
        def _(xx):
            for yy in range(2):
                mean, total = merged(
                    [(q_ref[zz, xx, yy, c], t_ref[zz, xx, yy, c]), (core_q[zz, xx, yy], core_t[zz, xx, yy])]
                )
                for k, (own, other) in enumerate(((xx, yy), (yy, xx))):
                    part = mean[:, cols[k]]

                    @pl.when(own == mine[k])
                    def _(k=k, other=other, part=part, total=total):
                        keep_q[k, zz, other] = part
                        keep_t[k, zz, other] = total

                    @pl.when(own != mine[k])
                    def _(k=k, other=other, part=part, total=total):
                        send_q[k, zz, other] = part.astype(bf16)
                        send_t[k, zz, other] = total

        for k in range(2):
            start(one_copies(zz, k))

    def merge_first(i):
        zz = nth_plane(i)
        for k in range(2):
            landed(one_copies(zz, k))
            for other in range(2):
                mean, total = merged(
                    [(keep_q[k, zz, other], keep_t[k, zz, other]), (got_q[k, zz, other], got_t[k, zz, other])]
                )

                @pl.when(other == mine[1 - k])
                def _(k=k, mean=mean, total=total):
                    next_q[k, zz] = mean
                    next_t[k, zz] = total

                @pl.when(other != mine[1 - k])
                def _(k=k, mean=mean, total=total):
                    pass_q[k, zz] = mean.astype(bf16)
                    pass_t[k, zz] = total

            start(two_copies(zz, k))

    def merge_second(i):
        zz = nth_plane(i)
        for k in range(2):
            landed(two_copies(zz, k))
            mean, total = merged([(next_q[k, zz], next_t[k, zz]), (last_q[k, zz], last_t[k, zz])])

            @pl.when(i > 0)
            def _(k=k, mean=mean, total=total):
                end_q[k, zz] = mean.astype(bf16)
                end_t[k, zz] = total
                start(z_copies(zz, z, k))

            @pl.when(i == 0)
            def _(k=k, mean=mean, total=total):
                next_q[k, z] = mean
                next_t[k, z] = total

    piece.start()
    second(0)
    arrive(1)
    third(0)
    second(1)
    arrive(2)

    @pl.loop(0, 7)
    def _(i):
        for act, lag, begin in (
            (merge_second, 3, 0), (merge_first, 2, 0), (merge_cores, 1, 0), (compute, 0, 0),
            (third, -1, 1), (second, -2, 2), (arrive, -3, 3),
        ):
            @pl.when((i - lag >= begin) & (i - lag < 4))
            def _(act=act, lag=lag):
                act(i - lag)

    for k in range(2):
        parts = [(next_q[k, z], next_t[k, z])]
        for i in range(1, 4):
            frm = nth_plane(i)
            landed(z_copies(frm, frm, k))
            parts.append((final_q[k, frm], final_t[k, frm]))
        mean, total = merged(parts)
        final_ref[:, cols[k]] = mean

    valid = jnp.concatenate(
        [
            jnp.where(as_column(pick_ref[m].astype(f32)) + 1.0 < lens_ref[0, m].astype(f32), 1.0, 0.0)
            for m in range(pick_ref.shape[0])
        ]
    )
    wanted = wanted_ref[...].astype(f32)
    chosen = jnp.sum(hidden_ref[...].astype(f32) * wanted, axis=1, keepdims=True)
    loss = jnp.sum(valid * (as_column(total[:1, :rows]) - chosen), keepdims=True)
    counted = jnp.sum(valid, keepdims=True)
    lane = iota(loss_ref.shape, 1)
    loss_ref[...] = jnp.where(lane == 0, loss, jnp.where(lane == 1, counted, 0.0))
    d_hidden = valid * (final_ref[...] - wanted)
    d_final = normal_back(d_hidden, vec(GAIN[2]), three_ref[...], inverse_three)
    middle_ref[...] = d_final
    d_act = dot(to_pair(0, d_final.astype(bf16)), down_ref[...], 1, 1)
    d_before = (d_act * gelu_slope(before_ref[...])).astype(bf16)
    d_two = of_pair(1, lambda some: dot(d_before, up_ref[some, :], 1, 1))
    d_middle = middle_ref[...] + normal_back(d_two, vec(GAIN[1]), two_ref[...], inverse_two)
    datt_ref[...] = dot(d_middle.astype(bf16), out_ref[...], 1, 1).astype(bf16)

    @pl.loop(0, 4)
    def _(i):
        zz = nth_plane(i)
        left(core_copies(zz))
        for k in range(2):
            left(one_copies(zz, k))
            left(two_copies(zz, k))

    @pl.loop(1, 4)
    def _(i):
        for k in range(2):
            left(z_copies(nth_plane(i), z, k))

    piece.finish(False)


def middle(lens, pick, att, xp, att_pair, xp_pair, wanted, vec, out_w, up_w, down_w, table, collective):
    rows, width = att.shape
    half = width // 2
    tile = (8, 128)
    vmem = pltpu.VMEM
    own = (rows, width)
    return pl.pallas_call(
        middle_kernel,
        out_shape=[jax.ShapeDtypeStruct(own, bf16), jax.ShapeDtypeStruct(tile, f32)],
        in_specs=[pl.BlockSpec(memory_space=pltpu.SMEM)] + [VMEM] * 7 + [ANY] * 3 + [VMEM],
        out_specs=[VMEM] * 2,
        scratch_shapes=[
            vmem(out_w.shape, bf16), vmem(up_w.shape, bf16), vmem(down_w.shape, bf16),
            vmem(own, f32), vmem(own, f32), vmem(own, f32), vmem(own, bf16),
            vmem((2 * rows, up_w.shape[1]), f32), vmem(own, f32),
            vmem((2,) + own, bf16), vmem((2, rows, half), bf16), vmem((2, rows, half), bf16),
            pltpu.SemaphoreType.DMA((3,)),
            pltpu.SemaphoreType.DMA((2, 5)),
            vmem((4, 2, 2, 2, rows, width), bf16),
            vmem((4, 2, 2, 2, rows, width), bf16), vmem((4, 2, 2, 2) + tile, f32),
            vmem((4, 2, 2, rows, width), bf16), vmem((4, 2, 2) + tile, f32),
            vmem((2, 4, 2, rows, half), f32), vmem((2, 4, 2) + tile, f32),
            vmem((2, 4, 2, rows, half), bf16), vmem((2, 4, 2) + tile, f32),
            vmem((2, 4, 2, rows, half), bf16), vmem((2, 4, 2) + tile, f32),
            vmem((2, 4, rows, half), f32), vmem((2, 4) + tile, f32),
            vmem((2, 4, rows, half), bf16), vmem((2, 4) + tile, f32),
            vmem((2, 4, rows, half), bf16), vmem((2, 4) + tile, f32),
            vmem((2, 4, rows, half), bf16), vmem((2, 4) + tile, f32),
            vmem((2, 4, rows, half), bf16), vmem((2, 4) + tile, f32),
            pltpu.SemaphoreType.DMA((2, 2, 4)),
            pltpu.SemaphoreType.DMA((2, 2, 2, 4)),
            pltpu.SemaphoreType.DMA((2, 2, 2, 4)),
            pltpu.SemaphoreType.DMA((2, 2, 2, 4)),
        ]
        + piece_scratch(1),
        compiler_params=params(collective),
        name="middle",
    )(lens, pick, att, xp, att_pair, xp_pair, wanted, vec, out_w, up_w, down_w, table)


def forward_kernel(
    att_ref, xp_ref, out_ref, up_ref, down_ref, vec_ref, bias_ref,
    hidden_ref, before_ref, two_ref, three_ref, inverse_ref, acc_ref, h2_ref,
):
    vec = lambda k: vec_ref[k : k + 1, :]
    step = pl.program_id(0)

    @pl.when(step == 0)
    def _():
        middle = xp_ref[...] + dot(att_ref[...], out_ref[...], 1, 0) + vec(OUT_BIAS)
        h2, two, inverse = normal(middle, vec(GAIN[1]), vec(SHIFT[1]))
        h2_ref[...] = h2.astype(bf16)
        two_ref[...] = two
        inverse_ref[0] = jnp.broadcast_to(inverse, inverse_ref.shape[1:])
        acc_ref[...] = middle + vec(vec_ref.shape[0] - 1)

    before = dot(h2_ref[...], up_ref[...], 1, 0) + bias_ref[...]
    before_ref[...] = before
    acc_ref[...] += dot(gelu(before).astype(bf16), down_ref[...], 1, 0)

    @pl.when(step == pl.num_programs(0) - 1)
    def _():
        hidden, three, inverse = normal(acc_ref[...], vec(GAIN[2]), vec(SHIFT[2]))
        hidden_ref[...] = hidden.astype(bf16)
        three_ref[...] = three
        inverse_ref[1] = jnp.broadcast_to(inverse, inverse_ref.shape[1:])


def forward(att, xp, out_w, up_w, down_w, vec, bias):
    rows, width = att.shape
    ff = down_w.shape[0]
    tile = 512
    fixed = whole((rows, width))
    return pl.pallas_call(
        forward_kernel,
        grid=(ff // tile,),
        out_shape=[
            jax.ShapeDtypeStruct((rows, width), bf16),
            jax.ShapeDtypeStruct((rows, ff), f32),
            jax.ShapeDtypeStruct((rows, width), f32),
            jax.ShapeDtypeStruct((rows, width), f32),
            jax.ShapeDtypeStruct((2, rows, 128), f32),
        ],
        in_specs=[
            fixed, fixed, whole(out_w.shape), pl.BlockSpec((width, tile), lambda i: (0, i)),
            pl.BlockSpec((tile, width), lambda i: (i, 0)), whole(vec.shape), pl.BlockSpec((1, tile), lambda i: (0, i)),
        ],
        out_specs=[
            fixed, pl.BlockSpec((rows, tile), lambda i: (0, i)), fixed, fixed, whole((2, rows, 128)),
        ],
        scratch_shapes=[pltpu.VMEM((rows, width), f32), pltpu.VMEM((rows, width), bf16)],
        compiler_params=params(),
        name="forward",
    )(att, xp, out_w, up_w, down_w, vec, bias)


def backward_kernel(
    mean_ref, total_ref, hidden_ref, wanted_ref, valid_ref, before_ref, two_ref, three_ref, inverse_ref,
    out_ref, up_ref, down_ref, vec_ref, datt_ref, loss_ref, final_ref, acc_ref,
):
    vec = lambda k: vec_ref[k : k + 1, :]
    step = pl.program_id(0)
    rows = valid_ref.shape[0]

    @pl.when(step == 0)
    def _():
        valid = valid_ref[...]
        wanted = wanted_ref[...].astype(f32)
        chosen = jnp.sum(hidden_ref[...].astype(f32) * wanted, axis=1, keepdims=True)
        loss = jnp.sum(valid * (as_column(total_ref[:1, :rows]) - chosen), keepdims=True)
        counted = jnp.sum(valid, keepdims=True)
        lane = iota(loss_ref.shape, 1)
        loss_ref[...] = jnp.where(lane == 0, loss, jnp.where(lane == 1, counted, 0.0))
        d_hidden = valid * (mean_ref[...] - wanted)
        final_ref[...] = normal_back(d_hidden, vec(GAIN[2]), three_ref[...], inverse_ref[1, :, :1])
        acc_ref[...] = jnp.zeros_like(acc_ref)

    d_act = dot(final_ref[...].astype(bf16), down_ref[...], 1, 1)
    d_before = (d_act * gelu_slope(before_ref[...])).astype(bf16)
    acc_ref[...] += dot(d_before, up_ref[...], 1, 1)

    @pl.when(step == pl.num_programs(0) - 1)
    def _():
        d_middle = final_ref[...] + normal_back(
            acc_ref[...], vec(GAIN[1]), two_ref[...], inverse_ref[0, :, :1]
        )
        datt_ref[...] = dot(d_middle.astype(bf16), out_ref[...], 1, 1).astype(bf16)


def backward(mean, total, hidden, wanted, valid, before, two, three, inverse, out_w, up_w, down_w, vec):
    rows, width = mean.shape
    ff = down_w.shape[0]
    tile = 512
    fixed = whole((rows, width))
    return pl.pallas_call(
        backward_kernel,
        grid=(ff // tile,),
        out_shape=[
            jax.ShapeDtypeStruct((rows, width), bf16),
            jax.ShapeDtypeStruct((8, 128), f32),
        ],
        in_specs=[
            fixed, whole(total.shape), fixed, fixed, whole((rows, 1)), pl.BlockSpec((rows, tile), lambda i: (0, i)),
            fixed, fixed, whole(inverse.shape), whole(out_w.shape),
            pl.BlockSpec((width, tile), lambda i: (0, i)),
            pl.BlockSpec((tile, width), lambda i: (i, 0)), whole(vec.shape),
        ],
        out_specs=[fixed, whole((8, 128))],
        scratch_shapes=[pltpu.VMEM((rows, width), f32)] * 2,
        compiler_params=params(),
        name="backward",
    )(mean, total, hidden, wanted, valid, before, two, three, inverse, out_w, up_w, down_w, vec)


def on_device(
    direct,
    token_identifiers,
    lengths,
    loss_positions,
    token_embedding_table,
    positions,
    query_key_value_matrix,
    output_weight,
    up_weight,
    down_weight,
    vectors,
    adapter_down_weight,
    adapter_up_weight,
    left_statistics,
    right_statistics,
):
    width = adapter_down_weight.shape[0]
    rank = adapter_down_weight.shape[1] // 2
    micros, _, slot_count = token_identifiers.shape
    picks = loss_positions.shape[2]
    ff = up_weight.shape[1]
    adapter_scale = adapter_alpha / rank
    local_rows = token_embedding_table.shape[0]
    devices = lax.axis_size("dp") * lax.axis_size("fsdp")
    me = lax.axis_index(BOTH)

    first = jnp.zeros((1,), jnp.int32)

    def masked_ids():
        ids = token_identifiers[:, 0]
        return jnp.where(iota(ids.shape, 1) < lengths, ids, -1).reshape(1, -1)

    if direct:
        received, most, slot, asked, own, mate, vec, wide = fetch(
            lengths.T, token_identifiers, vectors, token_embedding_table, query_key_value_matrix,
            positions, CAPACITY, 0,
        )
        asked = asked.reshape(devices // 2, 2, GRID, 128)
        wide = wide.reshape(-1, wide.shape[-1])
    else:
        ids = masked_ids()
        own = pl.pallas_call(
            functools.partial(presence_kernel, local_rows),
            out_shape=jax.ShapeDtypeStruct((devices, GRID, 128), bf16),
            compiler_params=params(),
            name="presence",
        )(ids)
        mate = own
        asked = lax.all_to_all(own, BOTH, 0, 0, tiled=True).reshape(devices, 1, GRID, 128)
        rows, most = select(asked, token_embedding_table, first, CAPACITY)
        most = lax.pmax(most, BOTH)
        received = lax.all_to_all(rows, BOTH, 0, 0, tiled=True)
        slot = slots(ids, own, mate, first, CAPACITY, local_rows)
        vec = lax.all_gather(vectors.astype(f32), BOTH, axis=0, tiled=True).reshape(-1, width)
        wide = jnp.concatenate([query_key_value_matrix, positions], axis=1)
        wide = lax.all_gather(wide, BOTH, axis=0, tiled=True)
    by_micro = lambda v: v.reshape(micros, 1, slot_count)
    most = most.reshape(-1)[0]
    flat = lambda v: v.reshape(-1, width)

    def rest(more, collective):
        layer = attend(
            ATTENTION_HEADS, adapter_scale, lengths.T, by_micro(slot), received.reshape(-1, width), more, wide, vec,
            loss_positions, adapter_down_weight.T, adapter_up_weight,
            *(([output_weight, up_weight, down_weight], collective) if direct else ([], None)),
        )
        layer, layer_w = layer[:10], layer[10:]
        h1, low, keys, values, probs, h1_p, low_p, x_p, wanted, attended = layer
        if direct:
            out_w, up_w, down_w, x_pair, attended_pair = (w.reshape(-1, w.shape[-1]) for w in layer_w)
            d_attended, loss = middle(
                lengths.T, loss_positions, flat(attended), flat(x_p), attended_pair, x_pair, flat(wanted), vec,
                out_w, up_w, down_w, token_embedding_table, collective + 1,
            )
        else:
            out_w, up_w, down_w = (
                lax.all_gather(w, BOTH, axis=0, tiled=True) for w in (output_weight, up_weight, down_weight)
            )
            bias = vec[UP_BIAS:-1].reshape(1, ff)
            valid = (loss_positions[:, 0] + 1 < lengths).astype(f32).reshape(-1, 1)
            hidden, before, two, three, inverse = forward(
                flat(attended), flat(x_p), out_w, up_w, down_w, vec, bias
            )
            own_rows = hidden.shape[0]
            every = lax.all_gather(hidden, BOTH, axis=0, tiled=True)
            means, totals = vocabulary(every, token_embedding_table, own_rows, 4 * own_rows)
            part = totals[:, 0, :own_rows].reshape(-1)
            top = lax.pmax(part, BOTH)
            total = top + jnp.log(lax.psum(jnp.exp(part - top), BOTH))
            mean_row = lax.psum_scatter(
                means.astype(f32) * jnp.exp(part - total)[:, None], BOTH, scatter_dimension=0, tiled=True
            )
            total = lax.dynamic_slice_in_dim(total, me * own_rows, own_rows, 0)
            total = jnp.broadcast_to(jnp.pad(total, (0, 128 - own_rows)), (8, 128))
            d_attended, loss = backward(
                mean_row, total, hidden, flat(wanted), valid, before, two, three, inverse, out_w, up_w, down_w, vec
            )
        back = back_parts(
            ATTENTION_HEADS, adapter_scale, rank, d_attended.reshape(micros, picks, width),
            h1, low, keys, values, probs, h1_p, low_p, adapter_up_weight, loss,
        )
        if direct:
            return finished(
                back, adapter_down_weight.T, adapter_up_weight, left_statistics, right_statistics, collective + 2
            )
        gradient = lax.psum(attend_back(back), BOTH)
        _, new = renewed(gradient, adapter_down_weight.T, adapter_up_weight, left_statistics, right_statistics)
        blocks = lax.all_gather(new, ("fsdp", "dp"))
        blocks = blocks.reshape(lax.axis_size("fsdp"), -1, 8, new.shape[1])
        return [gradient, blocks[:, : left_statistics.shape[0]].reshape(-1, 8, new.shape[1])]

    def another(state):
        step, rows_sum = state
        ids = masked_ids()
        which = step.reshape(1)
        rows, most = select(asked, token_embedding_table, which, CAPACITY)
        if direct:
            received = send_rows(rows, most, 1)[0]
        else:
            received = lax.all_to_all(rows, BOTH, 0, 0, tiled=True)
        slot = slots(ids, own, mate, which, CAPACITY, local_rows)
        found = jnp.take(received.reshape(-1, width), jnp.maximum(slot[0], 0), axis=0)
        found = jnp.where(slot[0][:, None] >= 0, found, jnp.zeros((), bf16))
        return step + 1, rows_sum + found.reshape(micros, slot_count, width)

    def in_rounds():
        more = lax.while_loop(
            lambda state: (state[0] * CAPACITY).astype(f32) < most,
            another,
            (jnp.ones((), jnp.int32), jnp.zeros((micros, slot_count, width), bf16)),
        )[1]
        return rest(more, 5)

    plain = rest(None, 2)
    gradient, blocks = lax.cond(most > CAPACITY, in_rounds, lambda: plain)
    losses, norm, down_g, up_g, left_new, right_new, down_new, up_new = settled(
        gradient, blocks, left_statistics, right_statistics
    )
    return losses, norm[0], down_g.T, up_g, left_new, right_new, down_new.T, up_new


def solution(mesh):
    direct = dict(mesh.shape) == {"dp": 8, "fsdp": 4}
    rows = P(BOTH, None)
    placed = (
        P(None, BOTH, None),
        P(None, BOTH),
        P(None, BOTH, None),
        rows,
        rows,
        rows,
        rows,
        rows,
        rows,
        P(BOTH),
        P(),
        P(),
        P("fsdp", None, None),
        P("fsdp", None, None),
    )
    return jax.shard_map(
        functools.partial(on_device, direct),
        mesh=mesh,
        in_specs=placed,
        out_specs=(P(), P(), P(), P(), P("fsdp", None, None), P("fsdp", None, None), P(), P()),
        check_vma=False,
    )
```

```python
import functools
import jax
import jax.numpy as jnp
from jax import lax
from jax.experimental import pallas as pl
from jax.experimental.pallas import tpu as pltpu
from jax.sharding import PartitionSpec as P

ATTENTION_HEADS = 16
STATS_BLOCK_ROWS = 256
NEWTON = 8
CAPACITY = 80

ln_eps = 1e-05
adapter_alpha = 32.0
beta_stats = 0.95
root_eps = 1e-12
clip_level = 0.01
learn_rate = 0.05
masked_score = -1e30

BOTH = ("dp", "fsdp")
MESH = pl.DeviceIdType.MESH
VMEM = pl.BlockSpec(memory_space=pltpu.VMEM)
ANY = pl.BlockSpec(memory_space=pl.ANY)
f32 = jnp.float32
bf16 = jnp.bfloat16


def place():
    d, f = lax.axis_index("dp"), lax.axis_index("fsdp")
    return d // 2, lax.rem(d, 2), f // 2, lax.rem(f, 2)


def target(z, x, y, c):
    return (z * 2 + x, y * 2 + c)


def nth(i):
    return (i // 4, lax.rem(i, 4))


class Greeting:
    def __init__(self, devices):
        self.sem, self.count = pltpu.get_barrier_semaphore(), len(devices)
        for device in devices:
            pl.semaphore_signal(self.sem, inc=1, device_id=device, device_id_type=MESH)

    def wait(self):
        pl.semaphore_wait(self.sem, self.count)


def own_number():
    return lax.axis_index("dp") * 4 + lax.axis_index("fsdp")


def greet_all(count):
    me = own_number()
    return Greeting([nth(lax.rem(me + i, count)) for i in range(1, count)])


def greet_near():
    z, x, y, c = place()
    near = [target(lax.rem(z + i, 4), x, y, c) for i in range(1, 4)]
    near += [target(z, 1 - x, y, c), target(z, x, 1 - y, c), target(z, x, y, 1 - c)]
    return Greeting(near)


def remote(src, dst, send, recv, device):
    return pltpu.make_async_remote_copy(
        src_ref=src, dst_ref=dst, send_sem=send, recv_sem=recv, device_id=device, device_id_type=MESH
    )


def params(collective=None, vmem=60):
    if collective is None:
        return pltpu.CompilerParams(vmem_limit_bytes=vmem * 2**20)
    return pltpu.CompilerParams(
        vmem_limit_bytes=vmem * 2**20, collective_id=collective, has_side_effects=True
    )


def iota(shape, dim):
    return lax.broadcasted_iota(jnp.int32, shape, dim)


def marks(condition):
    return jnp.where(condition, 1.0, 0.0).astype(bf16)


def dot(a, b, ca, cb):
    return lax.dot_general(a, b, (((ca,), (cb,)), ((), ())), preferred_element_type=f32)


GRID = 16


def cells(ids, local_rows):
    owner = jnp.floor((ids.astype(f32) + 0.5) * (1.0 / local_rows)).astype(jnp.int32)
    local = ids - owner * local_rows
    return owner, jnp.where(ids >= 0, owner * GRID + (local >> 7), -1), local & 127


def presence(ids, owners, local_rows):
    width = ids.shape[1]
    _, high, low = cells(ids, local_rows)
    count = dot(
        marks(iota((owners * GRID, width), 0) == high), marks(iota((128, width), 0) == low), 1, 1
    )
    return marks(count > 0.5).reshape(owners, GRID, 128)


def presence_kernel(local_rows, ids_ref, own_ref):
    own_ref[...] = presence(ids_ref[...], own_ref.shape[0], local_rows)


def ranked(present):
    rows = present.shape[0]
    through = dot(present, marks(iota((128, 128), 0) <= iota((128, 128), 1)), 1, 0)
    of = lambda dim: iota((rows, rows), dim)
    earlier = marks((of(1) < of(0)) & (of(0) // GRID == of(1) // GRID))
    row_total = jnp.broadcast_to(through[:, 127:128], (rows, 128)).astype(bf16)
    offset = dot(earlier, row_total, 1, 0)
    has = present.astype(f32)
    return jnp.where(has > 0.5, through - has + offset, -1.0), offset[:, :1] + through[:, 127:128]


def mark_rows(capacity, rank_ref, marks_ref, units, local_rows):
    @pl.loop(0, units)
    def _(unit):
        rows = pl.ds(pl.multiple_of(unit * capacity, 16), capacity)
        own = rank_ref[pl.ds(pl.multiple_of(unit * GRID, GRID), GRID), :]
        for row in range(-(-local_rows // 128)):
            columns = min(128, local_rows - row * 128)
            hit = iota((capacity, 128), 0).astype(f32) == own[row : row + 1, :]
            marks_ref[rows, row * 128 : row * 128 + columns] = marks(hit)[:, :columns]


def select_kernel(capacity, asked_ref, table_ref, round_ref, rows_ref, most_ref, marks_ref, rank_ref):
    units, members = asked_ref.shape[:2]
    local_rows, width = table_ref.shape
    begin = (round_ref[0] * capacity).astype(f32)
    most = jnp.zeros((1, 1), f32)
    for first in range(0, units, 16):
        together = asked_ref[first : first + 16, 0]
        for member in range(1, members):
            together = jnp.maximum(together, asked_ref[first : first + 16, member])
        rank, amount = ranked(together.reshape(-1, 128))
        most = jnp.maximum(most, jnp.max(amount, keepdims=True))
        rank_ref[first * GRID : first * GRID + rank.shape[0]] = rank - begin
    most_ref[...] = jnp.broadcast_to(most, most_ref.shape)
    mark_rows(capacity, rank_ref, marks_ref, units, local_rows)

    @pl.loop(0, units // 4)
    def _(four):
        rows_ref[pl.ds(four * 4, 4)] = look_up(capacity, four, marks_ref, table_ref)


def look_up(capacity, four, marks_ref, table_ref):
    part = pl.ds(pl.multiple_of(four * (4 * capacity), 4 * capacity), 4 * capacity)
    found = dot(marks_ref[part, :], table_ref[...], 1, 0)
    return found.astype(bf16).reshape(4, capacity, table_ref.shape[1])


def select(asked, table, which_round, capacity):
    units = asked.shape[0]
    return pl.pallas_call(
        functools.partial(select_kernel, capacity),
        out_shape=[
            jax.ShapeDtypeStruct((units, capacity, table.shape[1]), bf16),
            jax.ShapeDtypeStruct((8, 128), f32),
        ],
        in_specs=[VMEM, VMEM, pl.BlockSpec(memory_space=pltpu.SMEM)],
        out_specs=[VMEM] * 2,
        scratch_shapes=[
            pltpu.VMEM((units * capacity, table.shape[0]), bf16),
            pltpu.VMEM((units * GRID, 128), f32),
        ],
        compiler_params=params(),
        name="select",
    )(asked, table, which_round)


def slots_of(capacity, begin, local_rows, ids, own_ref, mate_ref):
    owner, high, low = cells(ids, local_rows)
    width = ids.shape[1]
    own_rank = jnp.zeros((1, width), f32)
    for first in range(0, own_ref.shape[0], 16):
        together = jnp.maximum(own_ref[first : first + 16], mate_ref[first : first + 16])
        rank, _ = ranked(together.reshape(-1, 128))
        rank = rank - begin
        rank = jnp.where((rank >= 0.0) & (rank < capacity), rank + 1.0, 0.0)
        rows = rank.shape[0]
        of_low = dot(rank.astype(bf16), marks(iota((rows, width), 0) + first * GRID == high), 0, 0)
        own_rank += jnp.sum(
            jnp.where(iota((128, width), 0) == low, of_low, 0.0), axis=0, keepdims=True
        )
    slot = owner * capacity + own_rank.astype(jnp.int32) - 1
    return jnp.where(own_rank > 0.5, slot, -1)


def slots_kernel(capacity, local_rows, ids_ref, own_ref, mate_ref, round_ref, slot_ref):
    begin = (round_ref[0] * capacity).astype(f32)
    slot_ref[...] = slots_of(capacity, begin, local_rows, ids_ref[...], own_ref, mate_ref)


def slots(ids, own, mate, which_round, capacity, local_rows):
    return pl.pallas_call(
        functools.partial(slots_kernel, capacity, local_rows),
        out_shape=jax.ShapeDtypeStruct(ids.shape, jnp.int32),
        in_specs=[VMEM] * 3 + [pl.BlockSpec(memory_space=pltpu.SMEM)],
        out_specs=VMEM,
        compiler_params=params(),
        name="slots",
    )(ids, own, mate, which_round)


class Piece:
    def __init__(self, sources, out, sems):
        self.sources, self.out, self.rows = sources, out, out.shape[4]
        self.own_sems, self.chain_sems, self.plane_sems, self.core_sems = sems
        self.z, self.x, self.y, self.c = place()

    def at(self, zz, xx, yy, cc, half=None):
        ref = self.out.at[zz, xx, yy, cc]
        return ref if half is None else self.out.at[zz, xx, yy, cc, pl.ds(half * (self.rows // 2), self.rows // 2)]

    def own(self):
        copies, begin = [], 0
        for k, src in enumerate(self.sources):
            dst = self.out.at[self.z, self.x, self.y, self.c, :, pl.ds(begin, src.shape[1])]
            copies.append(pltpu.make_async_copy(src, dst, self.own_sems.at[k]))
            begin += src.shape[1]
        return copies

    def chain(self, zz, way, incoming=False):
        z, x, y, c = self.z, self.x, self.y, self.c
        ref = self.at(zz, x, y, c)
        k = (way + 1) // 2
        to = target(z - way if incoming else z + way, x, y, c)
        return remote(ref, ref, self.chain_sems.at[0, k, zz], self.chain_sems.at[1, k, zz], to)

    def plane(self, zz, step, incoming=False):
        z, x, y, c = self.z, self.x, self.y, self.c
        every = slice(None)
        over_x, over_y = target(z, 1 - x, y, c), target(z, x, 1 - y, c)
        xx, yy = (1 - x, 1 - y) if incoming else (x, y)
        if step == 0:
            pairs = ((self.at(zz, xx, y, c, 0), over_x), (self.at(zz, x, yy, c, 1), over_y))
        else:
            pairs = ((self.at(zz, every, yy, c, 0), over_y), (self.at(zz, xx, every, c, 1), over_x))
        return [
            remote(ref, ref, self.plane_sems.at[0, zz, step, k], self.plane_sems.at[1, zz, step, k], to)
            for k, (ref, to) in enumerate(pairs)
        ]

    def mate(self, zz, incoming=False):
        z, x, y, c = self.z, self.x, self.y, self.c
        ref = self.at(zz, slice(None), slice(None), 1 - c if incoming else c)
        return remote(ref, ref, self.core_sems.at[0, zz], self.core_sems.at[1, zz], target(z, x, y, 1 - c))

    def arrivals(self, step, act):
        for way in (1, -1):
            zz = self.z - way * (step + 1)

            @pl.when((zz >= 0) & (zz < 4))
            def _(zz=zz, way=way):
                act(zz, way)

    def pass_on(self, zz, way):
        @pl.when((self.z + way >= 0) & (self.z + way < 4))
        def _():
            self.chain(zz, way).start()

    def first(self, zz):
        for copy in self.plane(zz, 0):
            copy.start()

    def load(self):
        for copy in self.own():
            copy.start()

    def start(self):
        for copy in self.own():
            copy.wait()
        for way in (1, -1):
            self.pass_on(self.z, way)
        self.first(self.z)

    def arrive(self, step):
        def act(zz, way):
            self.chain(zz, way, True).wait_recv()
            self.pass_on(zz, way)
            self.first(zz)

        self.arrivals(step, act)

    def second_of(self, zz, way=None):
        for copy in self.plane(zz, 0, True):
            copy.wait_recv()
        for copy in self.plane(zz, 1):
            copy.start()

    def third_of(self, zz, way=None):
        for copy in self.plane(zz, 1, True):
            copy.wait_recv()
        self.mate(zz).start()

    def second(self, step=None):
        if step is None:
            self.second_of(self.z)
        else:
            self.arrivals(step, self.second_of)

    def third(self, step=None):
        if step is None:
            self.third_of(self.z)
        else:
            self.arrivals(step, self.third_of)

    def finish(self, incoming=True):
        for zz in range(4):
            for step in range(2):
                for copy in self.plane(zz, step):
                    copy.wait_send()
        for zz in range(4):
            self.mate(zz).wait_send()
            if incoming:
                self.mate(zz, True).wait_recv()
        for way in (1, -1):

            @pl.when((self.z + way >= 0) & (self.z + way < 4))
            def _(way=way):
                for step in range(3):
                    zz = self.z - way * step

                    @pl.when((zz >= 0) & (zz < 4))
                    def _(zz=zz):
                        self.chain(zz, way).wait_send()


class Spread(Piece):
    def __init__(self, out, sems):
        super().__init__([], out, (None, None) + tuple(sems))

    def finish(self):
        for k in range(self.out.shape[0]):
            for step in range(2):
                for copy in self.plane(k, step):
                    copy.wait_send()
            self.mate(k).wait_send()
            self.mate(k, True).wait_recv()


class LayerWeights:
    def __init__(self, ins, outs, sems):
        (self.out_in, self.up_in, self.down_in), (out, self.up, self.down) = ins, outs
        self.own_sems, self.z_sems, sems = sems[0], sems[1], sems[2:]
        self.output = Piece([self.out_in], out, sems[:4])
        self.ups, self.downs = Spread(self.up, sems[4:6]), Spread(self.down, sems[6:8])
        self.z, self.x, self.y, self.c = place()
        self.side = lax.rem(self.z, 2)
        self.planes = (self.z, self.z + 1 - 2 * self.side, lax.rem(self.z + 2, 4), 3 - self.z)

    def up_block(self, side, k):
        size = self.up.shape[5] // 2
        return self.up_in.at[:, pl.ds(pl.multiple_of((2 * k + side) * size, 128), size)]

    def up_place(self, zz, k):
        size = self.up.shape[5] // 2
        return self.up.at[zz, self.x, self.y, self.c, :, pl.ds(k * size, size)]

    def owned(self):
        return [
            pltpu.make_async_copy(self.up_block(self.side, k), self.up_place(self.z, k), self.own_sems.at[k])
            for k in range(2)
        ] + [
            pltpu.make_async_copy(
                self.down_in, self.down.at[self.z // 2, self.x, self.y, self.c], self.own_sems.at[2]
            )
        ]

    def up_copies(self, i, incoming=False):
        other = self.planes[i]
        frm = other if incoming else self.z
        return [
            remote(
                self.up_block(lax.rem(other, 2), k), self.up_place(frm, k),
                self.z_sems.at[0, k, other], self.z_sems.at[1, k, frm], target(other, self.x, self.y, self.c),
            )
            for k in range(2)
        ]

    def down_copy(self, incoming=False):
        other = self.planes[2]
        frm = other if incoming else self.z
        return remote(
            self.down_in, self.down.at[frm // 2, self.x, self.y, self.c],
            self.z_sems.at[0, 2, other], self.z_sems.at[1, 2, frm], target(other, self.x, self.y, self.c),
        )

    def load(self):
        self.output.load()
        for copy in self.owned():
            copy.start()

    def send_up(self, i):
        for copy in self.up_copies(i):
            copy.start()

    def start(self):
        self.output.start()
        for copy in self.owned():
            copy.wait()
        self.downs.first(self.z // 2)
        self.ups.first(self.z)
        self.send_up(1)
        self.down_copy().start()

    def arrive_up(self, i):
        for copy in self.up_copies(i, True):
            copy.wait_recv()
        self.ups.first(self.planes[i])

    def arrive_down(self):
        self.down_copy(True).wait_recv()
        self.downs.first(self.planes[2] // 2)

    def steps(self):
        ups, downs, output, planes = self.ups, self.downs, self.output, self.planes
        here, there = self.z // 2, planes[2] // 2
        return [
            lambda: (
                output.arrive(0), self.arrive_up(1), self.send_up(2), ups.second_of(planes[0]), output.second(),
                downs.second_of(here),
            ),
            lambda: (
                output.arrive(1), self.send_up(3), output.second(0), ups.second_of(planes[1]), self.arrive_down(),
            ),
            lambda: (output.arrive(2), self.arrive_up(2), ups.third_of(planes[0]), output.third()),
            lambda: (
                self.arrive_up(3), downs.third_of(here), output.second(1), downs.second_of(there),
            ),
            lambda: (ups.third_of(planes[1]), output.third(0), output.second(2), ups.second_of(planes[2])),
            lambda: (output.third(1), ups.second_of(planes[3])),
            lambda: (
                downs.third_of(there), ups.third_of(planes[2]), output.third(2), ups.third_of(planes[3]),
            ),
        ]

    def finish(self):
        for i in range(1, 4):
            for copy in self.up_copies(i):
                copy.wait_send()
        self.down_copy().wait_send()
        self.ups.finish()
        self.downs.finish()
        self.output.finish()

    @staticmethod
    def shapes(weights):
        if not weights:
            return []
        out, up, down = weights
        return shares([out]) + [
            jax.ShapeDtypeStruct((4, 2, 2, 2, up.shape[0], up.shape[1] // 2), bf16),
            jax.ShapeDtypeStruct((2, 2, 2, 2) + down.shape, bf16),
        ]

    @staticmethod
    def scratch(weights):
        if not weights:
            return []
        spread = [pltpu.SemaphoreType.DMA((2, 4, 2, 2)), pltpu.SemaphoreType.DMA((2, 4))]
        return (
            [pltpu.SemaphoreType.DMA((3,)), pltpu.SemaphoreType.DMA((2, 3, 4))] + piece_scratch(1) + spread * 2
        )


def shares(weights):
    return [jax.ShapeDtypeStruct((4, 2, 2, 2) + w.shape, w.dtype) for w in weights]


def piece_scratch(count):
    return [
        pltpu.SemaphoreType.DMA((2,)),
        pltpu.SemaphoreType.DMA((2, 2, 4)),
        pltpu.SemaphoreType.DMA((2, 4, 2, 2)),
        pltpu.SemaphoreType.DMA((2, 4)),
    ] * count


def plane_by_distance(z, i):
    is_end = (z == 0) | (z == 3)
    up = jnp.where((z == 0) | (z == 2), 1, -1)
    inside = jnp.where(i == 0, z, jnp.where(i == 1, z + up, jnp.where(i == 2, z - up, z - 2 * up)))
    return jnp.where(is_end, z + up * i, inside)


class Rows:
    def __init__(self, rows_ref, most_ref, rows_out, most_out, sems):
        self.own_refs, self.outs = (rows_ref, most_ref), (rows_out, most_out)
        self.sems, self.mate_sems, self.own_sems = sems
        self.z, self.x, self.y, self.c = place()
        self.chip = (self.z * 2 + self.x) * 2 + self.y

    def out(self, k, to):
        device = target(to // 4, lax.rem(to // 2, 2), lax.rem(to, 2), self.c)
        src = self.own_refs[k].at[to] if k == 0 else self.own_refs[k]
        return remote(
            src, self.outs[k].at[self.chip, self.c], self.sems.at[0, k, to], self.sems.at[1, k, self.chip], device
        )

    def into(self, k, frm):
        device = target(frm // 4, lax.rem(frm // 2, 2), lax.rem(frm, 2), self.c)
        dst = self.outs[k].at[frm, self.c]
        return remote(dst, dst, self.sems.at[0, k, frm], self.sems.at[1, k, frm], device)

    def mate(self, k, of, core):
        ref = self.outs[k].at[of, core]
        to = target(self.z, self.x, self.y, 1 - self.c)
        return remote(ref, ref, self.mate_sems.at[0, k, of], self.mate_sems.at[1, k, of], to)

    def own(self, k):
        src = self.own_refs[k].at[self.chip] if k == 0 else self.own_refs[k]
        return pltpu.make_async_copy(src, self.outs[k].at[self.chip, self.c], self.own_sems.at[k])

    def send(self, to):
        @pl.when(to == self.chip)
        def _():
            for k in range(2):
                self.own(k).start()

        @pl.when(to != self.chip)
        def _():
            for k in range(2):
                self.out(k, to).start()

    def forward(self):
        for k in range(2):
            self.own(k).wait()
            self.mate(k, self.chip, self.c).start()
        for i in range(4):
            plane = plane_by_distance(self.z, i)
            for j in range(0 if i else 1, 4):
                frm = plane * 4 + lax.rem(self.x * 2 + self.y + j, 4)
                for k in range(2):
                    self.into(k, frm).wait_recv()
                    self.mate(k, frm, self.c).start()

    def finish(self):
        for i in range(16):
            of = lax.rem(self.chip + i, 16)
            for k in range(2):
                self.mate(k, of, self.c).wait_send()
                self.mate(k, of, 1 - self.c).wait_recv()
                if i:
                    self.out(k, of).wait_send()

    @staticmethod
    def shapes(rows, most):
        return [
            jax.ShapeDtypeStruct((16, 2) + rows[1:], bf16),
            jax.ShapeDtypeStruct((16, 2) + most, f32),
        ]

    @staticmethod
    def scratch():
        return [
            pltpu.SemaphoreType.DMA((2, 2, 16)),
            pltpu.SemaphoreType.DMA((2, 2, 16)),
            pltpu.SemaphoreType.DMA((2,)),
        ]


def rows_kernel(rows_ref, most_ref, rows_out, most_out, *sems):
    greet_all(32).wait()
    rows = Rows(rows_ref, most_ref, rows_out, most_out, sems)
    for to in range(16):
        rows.send(to)
    rows.forward()
    rows.finish()


def send_rows(rows, most, collective):
    return pl.pallas_call(
        rows_kernel,
        out_shape=Rows.shapes(rows.shape, most.shape),
        in_specs=[VMEM] * 2,
        out_specs=[ANY, VMEM],
        scratch_shapes=Rows.scratch(),
        compiler_params=params(collective),
        name="send_rows",
    )(rows, most)


def fetch_kernel(
    capacity, lens_ref, ids_ref, vec_ref, table_ref, qkv_ref, pos_ref,
    received_ref, most_ref, slot_ref, asked_ref, own_ref, mate_ref, vec_out, w_out,
    marks_ref, rank_ref, rows_ref, count_ref, mosts_ref, pack_ref, packs_ref, *sems,
):
    ask_sems, mate_sems = sems[:2]
    rows = Rows(rows_ref, count_ref, received_ref, mosts_ref, sems[2:5])
    piece = Piece([qkv_ref, pos_ref], w_out, sems[5:])
    greeting = greet_all(32)
    piece.load()
    local_rows = table_ref.shape[0]
    ids = jnp.concatenate(
        [
            jnp.where(iota(ids_ref.shape[1:], 1) < lens_ref[0, m], ids_ref[m], -1)
            for m in range(ids_ref.shape[0])
        ],
        axis=1,
    )
    own_ref[...] = presence(ids, 32, local_rows)
    length = vec_ref.shape[0]
    vec = jnp.pad(vec_ref[...].astype(f32).reshape(1, length), ((0, 0), (0, 1024 - length)))
    pack_ref[...] = jnp.concatenate([vec[:, k * 128 : (k + 1) * 128] for k in range(8)])
    me = own_number()
    z, x, y, c = place()
    to_mate = remote(own_ref, mate_ref, mate_sems.at[0], mate_sems.at[1], target(z, x, y, 1 - c))
    greeting.wait()

    def to_all(k, src, dst):
        copies = []
        for i in range(1, 32):
            to = lax.rem(me + i, 32)
            own = src.at[to] if k == 0 else src
            copies.append(remote(own, dst.at[me], ask_sems.at[0, k, i], ask_sems.at[1, k, i], nth(to)))
            copies[-1].start()
        return copies

    copies = to_all(0, own_ref, asked_ref)
    piece.start()
    to_mate.start()
    packs = to_all(1, pack_ref, packs_ref)
    asked_ref[me] = own_ref[me]
    packs_ref[me] = pack_ref[...]
    for copy in copies:
        copy.wait()
    together = jnp.concatenate(
        [jnp.maximum(asked_ref[2 * unit], asked_ref[2 * unit + 1]) for unit in range(16)]
    )
    rank, amount = ranked(together)
    count_ref[...] = jnp.broadcast_to(jnp.max(amount, keepdims=True), count_ref.shape)
    rank_ref[...] = rank
    mark_rows(capacity, rank_ref, marks_ref, 16, local_rows)
    piece.arrive(0)
    piece.second()
    planes = [lax.rem(z + i, 4) for i in (2, 3, 1, 0)]
    for plane in planes:
        rows_ref[pl.ds(plane * 4, 4)] = look_up(capacity, plane, marks_ref, table_ref)
    piece.arrive(1)
    piece.second(0)
    for plane in planes:
        for k in range(4):
            rows.send(plane * 4 + lax.rem(x * 2 + y + k, 4))
    to_mate.wait()
    slot_ref[...] = slots_of(capacity, 0.0, local_rows, ids, own_ref, mate_ref)
    piece.arrive(2)
    piece.third()
    piece.second(1)
    piece.third(0)
    piece.second(2)
    for copy in packs:
        copy.wait()
    width = vec_out.shape[1]
    for device in range(32):
        for k in range(-(-length // 128)):
            begin, end = k * 128, min(length, k * 128 + 128)
            at = device * length + begin
            while begin < end:
                count = min(end - begin, 128 - at % 128)
                vec_out[at // width : at // width + 1, at % width : at % width + count] = packs_ref[
                    device, k : k + 1, begin - k * 128 : begin - k * 128 + count
                ]
                at, begin = at + count, begin + count
    piece.third(1)
    piece.third(2)
    rows.forward()
    rows.finish()
    piece.finish()
    most_ref[0] = jnp.max(mosts_ref[...])


def fetch(lens, ids, vec, table, qkv, positions, capacity, collective):
    grids = jax.ShapeDtypeStruct((32, GRID, 128), bf16)
    width = table.shape[1]
    w = jax.ShapeDtypeStruct((qkv.shape[0], qkv.shape[1] + positions.shape[1]), bf16)
    return pl.pallas_call(
        functools.partial(fetch_kernel, capacity),
        out_shape=[
            jax.ShapeDtypeStruct((16, 2, capacity, width), bf16), jax.ShapeDtypeStruct((1,), f32),
            jax.ShapeDtypeStruct((1, ids.size), jnp.int32), grids, grids, grids,
            jax.ShapeDtypeStruct((32 * vec.shape[0] // width, width), f32),
        ]
        + shares([w]),
        in_specs=[pl.BlockSpec(memory_space=pltpu.SMEM)] + [VMEM] * 3 + [ANY] * 2,
        out_specs=[ANY, pl.BlockSpec(memory_space=pltpu.SMEM)] + [VMEM] * 5 + [ANY],
        scratch_shapes=[
            pltpu.VMEM((16 * capacity, table.shape[0]), bf16),
            pltpu.VMEM((16 * GRID, 128), f32),
            pltpu.VMEM((16, capacity, width), bf16),
            pltpu.VMEM((8, 128), f32),
            pltpu.VMEM((16, 2, 8, 128), f32),
            pltpu.VMEM((8, 128), f32),
            pltpu.VMEM((32, 8, 128), f32),
            pltpu.SemaphoreType.DMA((2, 2, 32)),
            pltpu.SemaphoreType.DMA((2,)),
        ]
        + Rows.scratch()
        + piece_scratch(1),
        compiler_params=params(collective),
        name="fetch",
    )(lens, ids, vec, table, qkv, positions)


def vocabulary_kernel(group, rows_ref, table_ref, mean_ref, total_ref):
    logits = dot(rows_ref[...], table_ref[...], 1, 1)
    top = jnp.max(logits, axis=1, keepdims=True)
    weights = jnp.exp(logits - top)
    amount = jnp.sum(weights, axis=1, keepdims=True)
    mean = dot(weights.astype(bf16), table_ref[...], 1, 0)
    mean_ref[...] = (mean / amount).astype(bf16)
    total = top + jnp.log(amount)
    for k in range(total_ref.shape[0]):
        total_ref[k] = as_tile(as_row(total[k * group : (k + 1) * group]))


def as_tile(row):
    return jnp.broadcast_to(jnp.pad(row, ((0, 0), (0, 128 - row.shape[1]))), (8, 128))


def same(size):
    return iota((size, size), 0) == iota((size, size), 1)


def as_row(column):
    return jnp.sum(jnp.where(same(column.shape[0]), column, 0.0), axis=0, keepdims=True)


def as_column(row):
    return jnp.sum(jnp.where(same(row.shape[1]), row, 0.0), axis=1, keepdims=True)


def vocabulary(rows, table, group, tile):
    count, width = rows.shape
    return pl.pallas_call(
        functools.partial(vocabulary_kernel, group),
        grid=(count // tile,),
        out_shape=[
            jax.ShapeDtypeStruct((count, width), bf16),
            jax.ShapeDtypeStruct((count // group, 8, 128), f32),
        ],
        in_specs=[
            pl.BlockSpec((tile, width), lambda i: (i, 0)),
            pl.BlockSpec(table.shape, lambda i: (0, 0)),
        ],
        out_specs=[
            pl.BlockSpec((tile, width), lambda i: (i, 0)),
            pl.BlockSpec((tile // group, 8, 128), lambda i: (i, 0, 0)),
        ],
        compiler_params=params(),
        name="vocabulary",
    )(rows, table)


def merged(parts):
    size = parts[0][0].shape[0]
    rows = [total[:1, :size] for _, total in parts]
    top = functools.reduce(jnp.maximum, rows)
    total = top + jnp.log(sum(jnp.exp(row - top) for row in rows))
    mean = sum(
        values.astype(f32) * as_column(jnp.exp(row - total)) for (values, _), row in zip(parts, rows)
    )
    return mean, as_tile(total)


def exact(a, b, ca, cb):
    return lax.dot_general(
        a, b, (((ca,), (cb,)), ((), ())), precision=lax.Precision.HIGHEST, preferred_element_type=f32
    )


def fine(a, b, cb):
    a_high, b_high = a.astype(bf16), b.astype(bf16)
    a_low, b_low = (a - a_high.astype(f32)).astype(bf16), (b - b_high.astype(f32)).astype(bf16)
    return dot(a_high, b_high, 1, cb) + (dot(a_high, b_low, 1, cb) + dot(a_low, b_high, 1, cb))


def small_product(a, b):
    return sum(a[:, k : k + 1] * b[k : k + 1, :] for k in range(a.shape[0]))


def newton(matrix, product, apply, state):
    size = matrix.shape[0]
    identity = jnp.where(same(size), 1.0, 0.0)
    trace = jnp.sum(matrix * identity, keepdims=True)

    def step(_, carry):
        current, state = carry
        factor = (5.0 * identity - current) * 0.25
        square = product(factor, factor)
        return product(product(square, square), current), apply(state, factor)

    current, state = lax.fori_loop(0, NEWTON - 1, step, (matrix / trace, state))
    state = apply(state, (5.0 * identity - current) * 0.25)
    return state * lax.rsqrt(jnp.sqrt(trace))


def clipped(g_ref, rank):
    data = jnp.where(iota(g_ref.shape, 1) < rank, g_ref[...], 0.0)
    norm = jnp.sqrt(jnp.sum(data * data, keepdims=True).reshape(1, 1))
    return data * (clip_level / jnp.maximum(norm, clip_level)), norm


def renew(g_ref, down_ref, up_ref, left_ref, right_ref, clip_ref, new_ref):
    owned, block = left_ref.shape[0], left_ref.shape[1]
    rank = right_ref.shape[1]
    group = lax.axis_index("fsdp")
    own = lax.rem(lax.axis_index("dp"), owned)
    clip_ref[...], _ = clipped(g_ref, rank)
    columns = pl.ds(pl.multiple_of(own * block, block), block)
    grad = clip_ref[group, :, columns]
    left, right = stats_of(left_ref[own], right_ref[own], grad)
    left = left + root_eps * jnp.where(same(block), 1.0, 0.0)
    right = right + root_eps * jnp.where(same(rank), 1.0, 0.0)
    root = newton(right, small_product, small_product, jnp.where(same(rank), 1.0, 0.0))
    rows = newton(left, lambda a, b: fine(a, b, 0), lambda a, b: fine(a, b, 1), grad)[:rank]
    update = sum(as_column(root[k : k + 1, :]) * rows[k : k + 1, :] for k in range(rank))
    old = [ref[k * rank : (k + 1) * rank, columns] for ref in (down_ref, up_ref) for k in range(2)]
    old = functools.reduce(lambda a, k: jnp.where(group == k, old[k], a), range(1, 4), old[0])
    new = old - learn_rate * update
    new_ref[...] = jnp.pad(new, ((0, 8 - rank), (0, 0)))


def stats_of(left, right, grad):
    rank = right.shape[0]
    columns = jnp.transpose(grad)
    outer = sum(columns[:, k : k + 1] * grad[k : k + 1, :] for k in range(rank))
    return (
        beta_stats * left + (1.0 - beta_stats) * outer,
        beta_stats * right + (1.0 - beta_stats) * exact(grad, grad, 1, 1)[:rank, :rank],
    )


def settle_kernel(g_ref, all_ref, left_ref, right_ref, loss_ref, norm_ref, a_ref, b_ref, left_out, right_out, a_new, b_new, clip_ref):
    owned, block = left_ref.shape[0], left_ref.shape[1]
    rank = right_ref.shape[1]
    clip_ref[...], norm = clipped(g_ref, rank)
    norm_ref[0] = jnp.sum(norm)
    for k in range(2):
        loss_ref[k] = jnp.sum(g_ref[0, rank : rank + 1, k : k + 1])
    a_ref[...] = jnp.concatenate([clip_ref[0, :rank], clip_ref[1, :rank]])
    b_ref[...] = jnp.concatenate([clip_ref[2, :rank], clip_ref[3, :rank]])
    group = lax.axis_index("fsdp")
    for k in range(owned):
        grad = clip_ref[group, :, k * block : (k + 1) * block]
        left_out[k], right_out[k] = stats_of(left_ref[k], right_ref[k], grad)
    for k in range(all_ref.shape[0]):
        ref, row = (a_new, b_new)[k // 8], k // 4 % 2 * rank
        ref[row : row + rank, k % 4 * block : (k % 4 + 1) * block] = all_ref[k, :rank]


def settled(gradient, blocks, left, right):
    width = gradient.shape[2]
    shapes = [(2,), (1,), (8, width), (8, width), left.shape, right.shape, (8, width), (8, width)]
    return pl.pallas_call(
        settle_kernel,
        out_shape=[jax.ShapeDtypeStruct(shape, f32) for shape in shapes],
        in_specs=[VMEM] * 4,
        out_specs=[pl.BlockSpec(memory_space=pltpu.SMEM)] * 2 + [VMEM] * 6,
        scratch_shapes=[pltpu.VMEM(gradient.shape, f32)],
        compiler_params=params(),
        name="settled",
    )(gradient, blocks, left, right)


def renew_kernel(*refs):
    renew(*refs)


def renewed(gradient, down, up, left, right):
    return pl.pallas_call(
        renew_kernel,
        out_shape=[
            jax.ShapeDtypeStruct(gradient.shape, f32), jax.ShapeDtypeStruct((8, left.shape[1]), f32),
        ],
        in_specs=[VMEM] * 5,
        out_specs=[VMEM] * 2,
        compiler_params=params(),
        name="renewed",
    )(gradient, down, up, left, right)


def finish_kernel(
    back, count, *refs,
):
    back_in, refs = refs[:count], refs[count:]
    (down_ref, up_ref, left_ref, right_ref, total_out, all_out), refs = refs[:6], refs[6:]
    (total_ref, all_ref, g_ref, dq_ref, dlow_ref), refs = refs[:5], refs[5:]

    @pl.when(pl.program_id(0) == 0)
    def _():
        greet_all(32)

    back(*back_in, g_ref, dq_ref, dlow_ref)

    @pl.when(pl.program_id(0) == pl.num_programs(0) - 1)
    def _():
        pl.semaphore_wait(pltpu.get_barrier_semaphore(), 31)
        finish(g_ref, down_ref, up_ref, left_ref, right_ref, total_ref, all_ref, *refs)
        total_out[...] = total_ref[...]
        all_out[...] = all_ref[...]


def finish(
    g_ref, down_ref, up_ref, left_ref, right_ref, total_ref, all_ref,
    parts, summed, clip_ref, new_ref, one_sems, two_sems, block_sems,
):
    me = own_number()

    def tile(ref, k):
        return ref.at[k // 8, :, pl.ds(pl.multiple_of(lax.rem(k, 8) * 128, 128), 128)]

    def out(i):
        to = lax.rem(me + i, 32)
        return remote(tile(g_ref, to), parts.at[me], one_sems.at[0, to], one_sems.at[1, me], nth(to))

    def into(i):
        frm = lax.rem(me + i, 32)
        return remote(tile(g_ref, me), parts.at[frm], one_sems.at[0, frm], one_sems.at[1, frm], nth(frm))

    def back(i):
        to = lax.rem(me + i, 32)
        return remote(summed, tile(total_ref, me), two_sems.at[0, to], two_sems.at[1, me], nth(to))

    def into_back(i):
        frm = lax.rem(me + i, 32)
        return remote(summed, tile(total_ref, frm), two_sems.at[0, frm], two_sems.at[1, frm], nth(frm))

    for i in range(1, 32):
        out(i).start()
    columns = pl.ds(pl.multiple_of(lax.rem(me, 8) * 128, 128), 128)
    for i in range(1, 32):
        into(i).wait_recv()
    running = g_ref[me // 8, :, columns]
    for i in range(1, 32):
        running = running + parts[lax.rem(me + i, 32)]
    summed[...] = running
    total_ref[me // 8, :, columns] = running
    for i in range(1, 32):
        back(i).start()
    for i in range(1, 32):
        into_back(i).wait_recv()
    renew(total_ref, down_ref, up_ref, left_ref, right_ref, clip_ref, new_ref)
    d, f = lax.axis_index("dp"), lax.axis_index("fsdp")
    half, mine = d // 4, f * 4 + lax.rem(d, 4)

    def share(i, incoming=False):
        k = lax.rem(mine + i, 16)
        device = (half * 4 + lax.rem(k, 4), k // 4)
        return remote(
            new_ref, all_ref.at[k if incoming else mine],
            block_sems.at[0, k], block_sems.at[1, k if incoming else mine], device,
        )

    for i in range(1, 16):
        share(i).start()
    all_ref[mine] = new_ref[...]
    for i in range(1, 16):
        share(i, True).wait_recv()
    for i in range(1, 16):
        share(i).wait_send()
    for i in range(1, 32):
        out(i).wait_send()
        back(i).wait_send()


def finished(back, down, up, left, right, collective):
    new = (8, left.shape[1])
    shape = back["shape"]
    return pl.pallas_call(
        functools.partial(finish_kernel, back["kernel"], len(back["args"])),
        grid=back["grid"],
        out_shape=[jax.ShapeDtypeStruct(shape, f32), jax.ShapeDtypeStruct((16,) + new, f32)],
        in_specs=back["in_specs"] + [whole(v.shape) for v in (down, up, left, right)],
        out_specs=[whole(shape), whole((16,) + new)],
        scratch_shapes=[pltpu.VMEM(shape, f32), pltpu.VMEM((16,) + new, f32), pltpu.VMEM(shape, f32)]
        + back["scratch_shapes"]
        + [
            pltpu.VMEM((32, 8, 128), f32),
            pltpu.VMEM((8, 128), f32),
            pltpu.VMEM(shape, f32),
            pltpu.VMEM(new, f32),
            pltpu.SemaphoreType.DMA((2, 32)),
            pltpu.SemaphoreType.DMA((2, 32)),
            pltpu.SemaphoreType.DMA((2, 16)),
        ],
        compiler_params=params(collective),
        name="finished",
    )(*back["args"], down, up, left, right)


def normal(v, gain, shift):
    centred = v - jnp.mean(v, axis=-1, keepdims=True)
    inverse = lax.rsqrt(jnp.mean(centred * centred, axis=-1, keepdims=True) + ln_eps)
    normed = centred * inverse
    return normed * gain + shift, normed, inverse


def normal_back(grad, gain, normed, inverse):
    scaled = grad * gain
    return inverse * (
        scaled
        - jnp.mean(scaled, axis=-1, keepdims=True)
        - normed * jnp.mean(scaled * normed, axis=-1, keepdims=True)
    )


GAIN, SHIFT, QKV_BIAS, OUT_BIAS, UP_BIAS = (0, 2, 4), (1, 3, 5), 6, 9, 10


def expand_chunk(slot_ref, rows_ref, begin, chunk):
    count = rows_ref.shape[0]
    part = lambda k: slot_ref[0, :, pl.ds(pl.multiple_of(begin + k, 128), 128)].astype(f32)
    column = jnp.concatenate([as_column(part(k)) for k in range(0, chunk, 128)]).astype(jnp.int32)
    return dot(marks(iota((chunk, count), 1) == column), rows_ref[...], 1, 0)


def spread_heads(v, heads, size):
    rows, width = v.shape
    tiled = jnp.concatenate([v] * heads, axis=0)
    shape = (heads * rows, width)
    return jnp.where(iota(shape, 0) // rows == iota(shape, 1) // size, tiled, jnp.zeros((), v.dtype))


def join_heads(v, heads, size):
    rows = v.shape[0] // heads
    own = jnp.where(iota(v.shape, 0) // rows == iota(v.shape, 1) // size, v, 0.0)
    return sum(own[k * rows : (k + 1) * rows] for k in range(heads))


def two_sets(v, rows):
    rank, width = v.shape[0] // 2, v.shape[1]
    v = v.astype(bf16)
    zeros = lambda count: jnp.zeros((count, width), bf16)
    return jnp.concatenate([v[:rank], zeros(8 - rank), v[rank:], zeros(rows - 8 - rank)])


def attend_kernel(
    heads, adapter_scale, count_w, with_more, lens_ref, slot_ref, rows_hbm, wide_hbm, vec_ref, pick_ref,
    down_ref, up_ref, *refs,
):
    if with_more:
        more_ref, *refs = refs
    w_in, refs = refs[:count_w], refs[count_w:]
    (h1_ref, low_ref, k_ref, v_ref, p_ref, h1p_ref, lowp_ref, xp_ref, wanted_ref, att_ref), refs = refs[:10], refs[10:]
    w_out, refs = refs[:count_w], refs[count_w:]
    if count_w:
        (xp_pair, att_pair), refs = refs[:2], refs[2:]
    (emb_ref, q_ref, rows_ref, pos_ref, qkv_ref, load_sems), sems = refs[:6], refs[6:]
    if count_w:
        (xp_own, att_own, pair_sems), sems = sems[:3], sems[3:]
    micro = pl.program_id(0)
    count, width = emb_ref.shape
    length = lens_ref[0, micro]
    down, up = two_sets(down_ref[...], 128), two_sets(up_ref[...], 16)
    size = width // heads
    chunk = 512
    vec = lambda k: vec_ref[k : k + 1, :]
    if count_w:
        gather = LayerWeights(w_in, w_out, sems)
        steps = gather.steps()

        def to_pair(m):
            device = target(gather.planes[1], gather.x, gather.y, gather.c)
            return [
                remote(src.at[m], dst.at[m], pair_sems.at[0, k, m], pair_sems.at[1, k, m], device)
                for k, (src, dst) in enumerate(((xp_own, xp_pair), (att_own, att_pair)))
            ]

    def beside(loop):
        for number, step in enumerate(steps[:6] if count_w else []):
            if number % 3 == loop:

                @pl.when(micro == number // 3)
                def _(step=step):
                    step()

    parts = ((rows_hbm, rows_ref), (wide_hbm.at[:, 3 * width :], pos_ref), (wide_hbm.at[:, : 3 * width], qkv_ref))
    loads = [pltpu.make_async_copy(src, dst, load_sems.at[k]) for k, (src, dst) in enumerate(parts)]

    @pl.when(micro == 0)
    def _():
        if count_w:
            greeting = greet_near()
        for load in loads:
            load.start()
        if count_w:
            gather.load()
            greeting.wait()
            gather.start()
        for load in loads[:2]:
            load.wait()

    @pl.loop(0, count // chunk)
    def _(k):
        rows = pl.ds(pl.multiple_of(k * chunk, chunk), chunk)
        emb = expand_chunk(slot_ref, rows_ref, k * chunk, chunk).astype(bf16)
        if with_more:
            emb = emb + more_ref[0, rows]
        emb_ref[rows] = emb
        x = emb.astype(f32) + pos_ref[rows].astype(f32)
        h1_ref[0, rows] = normal(x, vec(GAIN[0]), vec(SHIFT[0]))[0].astype(bf16)

    @pl.when(micro == 0)
    def _():
        loads[2].wait()

    beside(0)

    @pl.loop(0, count // chunk)
    def _(k):
        rows = pl.ds(pl.multiple_of(k * chunk, chunk), chunk)
        h1 = h1_ref[0, rows]
        low = dot(h1, down, 1, 1).astype(bf16)
        low_ref[0, rows] = low
        keys = dot(h1, qkv_ref[:, width : 2 * width], 1, 0) + vec(QKV_BIAS + 1)
        k_ref[0, rows] = keys.astype(bf16)
        values = dot(h1, qkv_ref[:, 2 * width :], 1, 0) + vec(QKV_BIAS + 2)
        values += adapter_scale * dot(low[:, 8:16], up[8:16], 1, 0)
        v_ref[0, rows] = values.astype(bf16)

    beside(1)

    pick = as_column(pick_ref[0].astype(f32)).astype(jnp.int32)
    picks = pick.shape[0]
    here = marks(iota((picks, count), 1) == pick)
    after = marks(iota((picks, count), 1) == pick + 1)
    taken = dot(jnp.concatenate([here, after]), emb_ref[...], 1, 0)
    xp_ref[0] = taken[:picks] + dot(here, pos_ref[...], 1, 0)
    wanted_ref[0] = taken[picks:].astype(bf16)
    h1p = dot(here, h1_ref[0], 1, 0).astype(bf16)
    lowp = dot(here, low_ref[0], 1, 0).astype(bf16)
    h1p_ref[0] = h1p
    lowp_ref[0] = lowp
    queries = dot(h1p, qkv_ref[:, :width], 1, 0) + vec(QKV_BIAS)
    queries += adapter_scale * dot(lowp[:, 0:8], up[0:8], 1, 0)
    q_ref[...] = queries.astype(bf16)
    some = 256 // size
    slot = iota((picks, count), 1)
    allowed = (slot <= pick) & (slot < length)
    allowed = jnp.concatenate([jnp.where(allowed, 1.0, 0.0)] * some, axis=0) > 0.5

    @pl.loop(0, width // 256)
    def _(k):
        lanes = pl.ds(pl.multiple_of(k * 256, 256), 256)
        scores = dot(spread_heads(q_ref[:, lanes], some, size), k_ref[0, :, lanes], 1, 1)
        scores = jnp.where(allowed, scores * size**-0.5, masked_score)
        weights = jnp.exp(scores - jnp.max(scores, axis=1, keepdims=True))
        probs = (weights / jnp.sum(weights, axis=1, keepdims=True)).astype(bf16)
        p_ref[0, pl.ds(pl.multiple_of(k * some * picks, some * picks), some * picks)] = probs
        attended = dot(probs, v_ref[0, :, lanes], 1, 0)
        att_ref[0, :, lanes] = join_heads(attended, some, size).astype(bf16)

    beside(2)

    if count_w:
        xp_own[micro] = xp_ref[0]
        att_own[micro] = att_ref[0]
        for copy in to_pair(micro):
            copy.start()

        @pl.when(micro == pl.num_programs(0) - 1)
        def _():
            steps[6]()
            gather.finish()
            for m in range(xp_own.shape[0]):
                for copy in to_pair(m):
                    copy.wait()


def whole(shape):
    return pl.BlockSpec(shape, lambda *_: (0,) * len(shape))


def of_micro(shape):
    return pl.BlockSpec((1,) + shape, lambda m: (m,) + (0,) * len(shape))


def attend(heads, adapter_scale, lens, slot, rows, more, wide, vec, pick, down, up, weights, collective):
    micros, _, count = slot.shape
    width = rows.shape[1]
    picks = pick.shape[2]
    more = [] if more is None else [more]
    outs = [
        ((count, width), bf16), ((count, 128), bf16), ((count, width), bf16), ((count, width), bf16),
        ((heads * picks, count), bf16), ((picks, width), bf16), ((picks, 128), bf16),
        ((picks, width), f32), ((picks, width), bf16), ((picks, width), bf16),
    ]
    return pl.pallas_call(
        functools.partial(attend_kernel, heads, adapter_scale, len(weights), len(more) > 0),
        grid=(micros,),
        out_shape=[jax.ShapeDtypeStruct((micros,) + shape, kind) for shape, kind in outs]
        + LayerWeights.shapes(weights)
        + [jax.ShapeDtypeStruct((micros, picks, width), kind) for kind in (f32, bf16) if weights],
        in_specs=[
            pl.BlockSpec(memory_space=pltpu.SMEM), of_micro((1, count)), ANY, ANY, whole(vec.shape), of_micro((1, picks)), whole(down.shape), whole(up.shape),
        ]
        + [of_micro((count, width))] * len(more)
        + [ANY] * len(weights),
        out_specs=[of_micro(shape) for shape, _ in outs] + [ANY] * (len(weights) + 2 if weights else 0),
        scratch_shapes=[
            pltpu.VMEM((count, width), bf16), pltpu.VMEM((picks, width), bf16), pltpu.VMEM(rows.shape, bf16),
            pltpu.VMEM((count, width), bf16), pltpu.VMEM((width, 3 * width), bf16), pltpu.SemaphoreType.DMA((3,)),
        ]
        + [pltpu.VMEM((micros, picks, width), kind) for kind in (f32, bf16) if weights]
        + [pltpu.SemaphoreType.DMA((2, 2, micros)) for _ in weights[:1]]
        + LayerWeights.scratch(weights),
        compiler_params=params(collective),
        name="attend",
    )(lens, slot, rows, wide, vec, pick, down, up, *more, *weights)


def attend_back_kernel(
    heads, adapter_scale, rank, datt_ref, h1_ref, low_ref, k_ref, v_ref, p_ref, h1p_ref, lowp_ref, up_ref, loss_ref,
    g_ref, dq_ref, dlow_ref,
):
    count, width = h1_ref.shape[1:]
    size = width // heads
    picks = datt_ref.shape[1]
    some = 256 // size
    up = two_sets(up_ref[...], 16)

    @pl.when(pl.program_id(0) == 0)
    def _():
        g_ref[...] = jnp.zeros_like(g_ref)
        g_ref[0, rank : rank + 1, :128] = loss_ref[:1, :]

    dlow_ref[...] = jnp.zeros_like(dlow_ref)

    @pl.loop(0, width // 256)
    def _(k):
        lanes = pl.ds(pl.multiple_of(k * 256, 256), 256)
        own = pl.ds(pl.multiple_of(k * some * picks, some * picks), some * picks)
        d_heads = spread_heads(datt_ref[0, :, lanes], some, size)
        probs_b = p_ref[0, own]
        probs = probs_b.astype(f32)
        d_probs = dot(d_heads, v_ref[0, :, lanes], 1, 1)
        v_up = two_sets_of_values(up_ref, lanes)
        dlow_ref[...] += dot(dot(d_heads, v_up, 1, 1).astype(bf16), probs_b, 0, 0)
        taken = dot(probs_b, low_ref[0, :, 8:16], 1, 0)
        g_ref[3, :, lanes] += adapter_scale * dot(taken.astype(bf16), d_heads, 0, 0)
        weighted = probs * d_probs
        d_scores = weighted - probs * jnp.sum(weighted, axis=1, keepdims=True)
        d_queries = dot(d_scores.astype(bf16), k_ref[0, :, lanes], 1, 0)
        dq_ref[:, lanes] = (join_heads(d_queries, some, size) * size**-0.5).astype(bf16)

    d_low_q = (adapter_scale * dot(dq_ref[...], up[0:8], 1, 1)).astype(bf16)
    d_low_v = (adapter_scale * dlow_ref[...]).astype(bf16)
    g_ref[0] += dot(d_low_q, h1p_ref[0], 0, 0)
    g_ref[1] += dot(d_low_v, h1_ref[0], 1, 0)
    g_ref[2] += adapter_scale * dot(lowp_ref[0, :, 0:8], dq_ref[...], 0, 0)


def two_sets_of_values(up_ref, lanes):
    rank = up_ref.shape[0] // 2
    v = up_ref[:, lanes].astype(bf16)[rank:]
    return jnp.concatenate([v, jnp.zeros((8 - rank, v.shape[1]), bf16)])


def back_parts(heads, adapter_scale, rank, datt, h1, low, keys, values, probs, h1p, lowp, up, loss):
    micros, count, width = h1.shape
    picks = datt.shape[1]
    ins = (datt, h1, low, keys, values, probs, h1p, lowp)
    return dict(
        kernel=functools.partial(attend_back_kernel, heads, adapter_scale, rank),
        grid=(micros,),
        in_specs=[of_micro(v.shape[1:]) for v in ins] + [whole(up.shape), whole(loss.shape)],
        args=(*ins, up, loss),
        shape=(4, 8, width),
        scratch_shapes=[pltpu.VMEM((picks, width), bf16), pltpu.VMEM((8, count), f32)],
    )


def attend_back(parts):
    return pl.pallas_call(
        parts["kernel"],
        grid=parts["grid"],
        out_shape=jax.ShapeDtypeStruct(parts["shape"], f32),
        in_specs=parts["in_specs"],
        out_specs=whole(parts["shape"]),
        scratch_shapes=parts["scratch_shapes"],
        compiler_params=params(),
        name="attend_back",
    )(*parts["args"])


def gelu(v):
    inner = 0.7978845608028654 * (v + 0.044715 * v * v * v)
    return 0.5 * v * (1.0 + jnp.tanh(inner))


def gelu_slope(v):
    bend = jnp.tanh(0.7978845608028654 * (v + 0.044715 * v * v * v))
    return 0.5 * (1.0 + bend) + 0.5 * v * (1.0 - bend * bend) * 0.7978845608028654 * (
        1.0 + 3.0 * 0.044715 * v * v
    )


def middle_kernel(
    lens_ref, pick_ref, att_ref, xp_ref, att_pair, xp_pair, wanted_ref, vec_ref, out_hbm, up_hbm, down_hbm, table_ref, datt_ref, loss_ref,
    out_ref, up_ref, down_ref, middle_ref, two_ref, three_ref, hidden_ref, before_ref, final_ref,
    rows_ref, part_ref, got_ref, load_sems, pair_sems, every_ref, q_ref, t_ref, core_q, core_t, keep_q, keep_t, send_q, send_t, got_q, got_t,
    next_q, next_t, pass_q, pass_t, last_q, last_t, end_q, end_t, final_q, final_t,
    core_sems, one_sems, two_sems, z_sems, *sems,
):
    rows, width = hidden_ref.shape
    piece = Piece([hidden_ref], every_ref, sems)
    greeting = greet_near()
    vec = lambda k: vec_ref[k : k + 1, :]
    loads = [
        pltpu.make_async_copy(src, dst, load_sems.at[k])
        for k, (src, dst) in enumerate(((out_hbm, out_ref), (up_hbm, up_ref), (down_hbm, down_ref)))
    ]
    for load in loads:
        load.start()
    z, x, y, c = place()
    side = lax.rem(z, 2)
    pair = target(z + 1 - 2 * side, x, y, c)

    def to_pair(number, values):
        rows_ref[0] = values
        copy = remote(
            rows_ref.at[0], rows_ref.at[1], pair_sems.at[0, 4 + number], pair_sems.at[1, 4 + number], pair
        )
        copy.start()
        copy.wait()
        return rows_ref[...].reshape(2 * rows, width)

    half = width // 2
    cols = (slice(0, half), slice(half, width))

    def of_pair(number, product):
        own, copies = [], []
        for k in range(2):
            part = product(cols[k])
            part_ref[k] = part[rows:].astype(bf16)
            spot = 2 * number + k
            copy = remote(part_ref.at[k], got_ref.at[k], pair_sems.at[0, spot], pair_sems.at[1, spot], pair)
            copy.start()
            own.append(part[:rows])
            copies.append(copy)
        for copy in copies:
            copy.wait()
        return jnp.concatenate([own[k] + got_ref[k].astype(f32) for k in range(2)], axis=1)

    loads[0].wait()
    both = lambda own, other: jnp.concatenate([own[...], other[...]])
    middle = both(xp_ref, xp_pair) + dot(both(att_ref, att_pair), out_ref[...], 1, 0) + vec(OUT_BIAS)
    middle_ref[...] = middle[:rows]
    every_h2, two, inverse_two = normal(middle, vec(GAIN[1]), vec(SHIFT[1]))
    two_ref[...], inverse_two = two[:rows], inverse_two[:rows]
    bias = jnp.concatenate(
        [jnp.where(side == 0, vec(UP_BIAS + 2 * k), vec(UP_BIAS + 2 * k + 1)) for k in range(2)], axis=1
    )
    loads[1].wait()
    before = dot(every_h2.astype(bf16), up_ref[...], 1, 0) + bias
    before_ref[...] = before
    loads[2].wait()
    activated = gelu(before).astype(bf16)
    greeting.wait()
    added = of_pair(0, lambda some: dot(activated, down_ref[:, some], 1, 0))
    final = middle_ref[...] + added + vec(vec_ref.shape[0] - 1)
    hidden, three, inverse_three = normal(final, vec(GAIN[2]), vec(SHIFT[2]))
    hidden_ref[...] = hidden.astype(bf16)
    three_ref[...] = three

    piece.load()
    mate = target(z, x, y, 1 - c)
    over = (target(z, 1 - x, y, c), target(z, x, 1 - y, c))
    mine = (x, y)
    nth_plane = lambda i: plane_by_distance(z, i)

    def core_copies(zz):
        return [
            remote(q_ref.at[zz, :, :, 1 - c], core_q.at[zz], core_sems.at[0, 0, zz], core_sems.at[1, 0, zz], mate),
            remote(t_ref.at[zz, :, :, 1 - c], core_t.at[zz], core_sems.at[0, 1, zz], core_sems.at[1, 1, zz], mate),
        ]

    def one_copies(zz, k):
        return [
            remote(send_q.at[k, zz], got_q.at[k, zz], one_sems.at[0, 0, k, zz], one_sems.at[1, 0, k, zz], over[k]),
            remote(send_t.at[k, zz], got_t.at[k, zz], one_sems.at[0, 1, k, zz], one_sems.at[1, 1, k, zz], over[k]),
        ]

    def two_copies(zz, k):
        return [
            remote(pass_q.at[k, zz], last_q.at[k, zz], two_sems.at[0, 0, k, zz], two_sems.at[1, 0, k, zz], over[1 - k]),
            remote(pass_t.at[k, zz], last_t.at[k, zz], two_sems.at[0, 1, k, zz], two_sems.at[1, 1, k, zz], over[1 - k]),
        ]

    def z_copies(zz, frm, k):
        return [
            remote(end_q.at[k, zz], final_q.at[k, frm], z_sems.at[0, 0, k, zz], z_sems.at[1, 0, k, frm], target(zz, x, y, c)),
            remote(end_t.at[k, zz], final_t.at[k, frm], z_sems.at[0, 1, k, zz], z_sems.at[1, 1, k, frm], target(zz, x, y, c)),
        ]

    def start(copies):
        for copy in copies:
            copy.start()

    def landed(copies):
        for copy in copies:
            copy.wait_recv()

    def left(copies):
        for copy in copies:
            copy.wait_send()

    def arrive(i):
        zz = nth_plane(i)
        way = jnp.where(zz < z, 1, -1)
        piece.chain(zz, way, True).wait_recv()
        piece.pass_on(zz, way)
        piece.first(zz)

    def second(i):
        piece.second_of(nth_plane(i))

    def third(i):
        piece.third_of(nth_plane(i))

    def compute(i):
        zz = nth_plane(i)
        piece.mate(zz, True).wait_recv()

        logits = dot(every_ref[zz].reshape(8 * rows, width), table_ref[...], 1, 1)
        top = jnp.max(logits, axis=1, keepdims=True)
        weights = jnp.exp(logits - top)
        amount = jnp.sum(weights, axis=1, keepdims=True)
        mean = dot(weights.astype(bf16), table_ref[...], 1, 0) * (1.0 / amount)
        q_ref[zz] = mean.astype(bf16).reshape(2, 2, 2, rows, width)
        total = top + jnp.log(amount)
        for k in range(8):
            t_ref[zz, k // 4, k // 2 % 2, k % 2] = as_tile(as_row(total[k * rows : (k + 1) * rows]))

        start(core_copies(zz))

    def merge_cores(i):
        zz = nth_plane(i)
        landed(core_copies(zz))

        @pl.loop(0, 2)
        def _(xx):
            for yy in range(2):
                mean, total = merged(
                    [(q_ref[zz, xx, yy, c], t_ref[zz, xx, yy, c]), (core_q[zz, xx, yy], core_t[zz, xx, yy])]
                )
                for k, (own, other) in enumerate(((xx, yy), (yy, xx))):
                    part = mean[:, cols[k]]

                    @pl.when(own == mine[k])
                    def _(k=k, other=other, part=part, total=total):
                        keep_q[k, zz, other] = part
                        keep_t[k, zz, other] = total

                    @pl.when(own != mine[k])
                    def _(k=k, other=other, part=part, total=total):
                        send_q[k, zz, other] = part.astype(bf16)
                        send_t[k, zz, other] = total

        for k in range(2):
            start(one_copies(zz, k))

    def merge_first(i):
        zz = nth_plane(i)
        for k in range(2):
            landed(one_copies(zz, k))
            for other in range(2):
                mean, total = merged(
                    [(keep_q[k, zz, other], keep_t[k, zz, other]), (got_q[k, zz, other], got_t[k, zz, other])]
                )

                @pl.when(other == mine[1 - k])
                def _(k=k, mean=mean, total=total):
                    next_q[k, zz] = mean
                    next_t[k, zz] = total

                @pl.when(other != mine[1 - k])
                def _(k=k, mean=mean, total=total):
                    pass_q[k, zz] = mean.astype(bf16)
                    pass_t[k, zz] = total

            start(two_copies(zz, k))

    def merge_second(i):
        zz = nth_plane(i)
        for k in range(2):
            landed(two_copies(zz, k))
            mean, total = merged([(next_q[k, zz], next_t[k, zz]), (last_q[k, zz], last_t[k, zz])])

            @pl.when(i > 0)
            def _(k=k, mean=mean, total=total):
                end_q[k, zz] = mean.astype(bf16)
                end_t[k, zz] = total
                start(z_copies(zz, z, k))

            @pl.when(i == 0)
            def _(k=k, mean=mean, total=total):
                next_q[k, z] = mean
                next_t[k, z] = total

    piece.start()
    second(0)
    arrive(1)
    third(0)
    second(1)
    arrive(2)

    @pl.loop(0, 7)
    def _(i):
        for act, lag, begin in (
            (merge_second, 3, 0), (merge_first, 2, 0), (merge_cores, 1, 0), (compute, 0, 0),
            (third, -1, 1), (second, -2, 2), (arrive, -3, 3),
        ):
            @pl.when((i - lag >= begin) & (i - lag < 4))
            def _(act=act, lag=lag):
                act(i - lag)

    for k in range(2):
        parts = [(next_q[k, z], next_t[k, z])]
        for i in range(1, 4):
            frm = nth_plane(i)
            landed(z_copies(frm, frm, k))
            parts.append((final_q[k, frm], final_t[k, frm]))
        mean, total = merged(parts)
        final_ref[:, cols[k]] = mean

    valid = jnp.concatenate(
        [
            jnp.where(as_column(pick_ref[m].astype(f32)) + 1.0 < lens_ref[0, m].astype(f32), 1.0, 0.0)
            for m in range(pick_ref.shape[0])
        ]
    )
    wanted = wanted_ref[...].astype(f32)
    chosen = jnp.sum(hidden_ref[...].astype(f32) * wanted, axis=1, keepdims=True)
    loss = jnp.sum(valid * (as_column(total[:1, :rows]) - chosen), keepdims=True)
    counted = jnp.sum(valid, keepdims=True)
    lane = iota(loss_ref.shape, 1)
    loss_ref[...] = jnp.where(lane == 0, loss, jnp.where(lane == 1, counted, 0.0))
    d_hidden = valid * (final_ref[...] - wanted)
    d_final = normal_back(d_hidden, vec(GAIN[2]), three_ref[...], inverse_three)
    middle_ref[...] = d_final
    d_act = dot(to_pair(0, d_final.astype(bf16)), down_ref[...], 1, 1)
    d_before = (d_act * gelu_slope(before_ref[...])).astype(bf16)
    d_two = of_pair(1, lambda some: dot(d_before, up_ref[some, :], 1, 1))
    d_middle = middle_ref[...] + normal_back(d_two, vec(GAIN[1]), two_ref[...], inverse_two)
    datt_ref[...] = dot(d_middle.astype(bf16), out_ref[...], 1, 1).astype(bf16)

    @pl.loop(0, 4)
    def _(i):
        zz = nth_plane(i)
        left(core_copies(zz))
        for k in range(2):
            left(one_copies(zz, k))
            left(two_copies(zz, k))

    @pl.loop(1, 4)
    def _(i):
        for k in range(2):
            left(z_copies(nth_plane(i), z, k))

    piece.finish(False)


def middle(lens, pick, att, xp, att_pair, xp_pair, wanted, vec, out_w, up_w, down_w, table, collective):
    rows, width = att.shape
    half = width // 2
    tile = (8, 128)
    vmem = pltpu.VMEM
    own = (rows, width)
    return pl.pallas_call(
        middle_kernel,
        out_shape=[jax.ShapeDtypeStruct(own, bf16), jax.ShapeDtypeStruct(tile, f32)],
        in_specs=[pl.BlockSpec(memory_space=pltpu.SMEM)] + [VMEM] * 7 + [ANY] * 3 + [VMEM],
        out_specs=[VMEM] * 2,
        scratch_shapes=[
            vmem(out_w.shape, bf16), vmem(up_w.shape, bf16), vmem(down_w.shape, bf16),
            vmem(own, f32), vmem(own, f32), vmem(own, f32), vmem(own, bf16),
            vmem((2 * rows, up_w.shape[1]), f32), vmem(own, f32),
            vmem((2,) + own, bf16), vmem((2, rows, half), bf16), vmem((2, rows, half), bf16),
            pltpu.SemaphoreType.DMA((3,)),
            pltpu.SemaphoreType.DMA((2, 5)),
            vmem((4, 2, 2, 2, rows, width), bf16),
            vmem((4, 2, 2, 2, rows, width), bf16), vmem((4, 2, 2, 2) + tile, f32),
            vmem((4, 2, 2, rows, width), bf16), vmem((4, 2, 2) + tile, f32),
            vmem((2, 4, 2, rows, half), f32), vmem((2, 4, 2) + tile, f32),
            vmem((2, 4, 2, rows, half), bf16), vmem((2, 4, 2) + tile, f32),
            vmem((2, 4, 2, rows, half), bf16), vmem((2, 4, 2) + tile, f32),
            vmem((2, 4, rows, half), f32), vmem((2, 4) + tile, f32),
            vmem((2, 4, rows, half), bf16), vmem((2, 4) + tile, f32),
            vmem((2, 4, rows, half), bf16), vmem((2, 4) + tile, f32),
            vmem((2, 4, rows, half), bf16), vmem((2, 4) + tile, f32),
            vmem((2, 4, rows, half), bf16), vmem((2, 4) + tile, f32),
            pltpu.SemaphoreType.DMA((2, 2, 4)),
            pltpu.SemaphoreType.DMA((2, 2, 2, 4)),
            pltpu.SemaphoreType.DMA((2, 2, 2, 4)),
            pltpu.SemaphoreType.DMA((2, 2, 2, 4)),
        ]
        + piece_scratch(1),
        compiler_params=params(collective),
        name="middle",
    )(lens, pick, att, xp, att_pair, xp_pair, wanted, vec, out_w, up_w, down_w, table)


def forward_kernel(
    att_ref, xp_ref, out_ref, up_ref, down_ref, vec_ref, bias_ref,
    hidden_ref, before_ref, two_ref, three_ref, inverse_ref, acc_ref, h2_ref,
):
    vec = lambda k: vec_ref[k : k + 1, :]
    step = pl.program_id(0)

    @pl.when(step == 0)
    def _():
        middle = xp_ref[...] + dot(att_ref[...], out_ref[...], 1, 0) + vec(OUT_BIAS)
        h2, two, inverse = normal(middle, vec(GAIN[1]), vec(SHIFT[1]))
        h2_ref[...] = h2.astype(bf16)
        two_ref[...] = two
        inverse_ref[0] = jnp.broadcast_to(inverse, inverse_ref.shape[1:])
        acc_ref[...] = middle + vec(vec_ref.shape[0] - 1)

    before = dot(h2_ref[...], up_ref[...], 1, 0) + bias_ref[...]
    before_ref[...] = before
    acc_ref[...] += dot(gelu(before).astype(bf16), down_ref[...], 1, 0)

    @pl.when(step == pl.num_programs(0) - 1)
    def _():
        hidden, three, inverse = normal(acc_ref[...], vec(GAIN[2]), vec(SHIFT[2]))
        hidden_ref[...] = hidden.astype(bf16)
        three_ref[...] = three
        inverse_ref[1] = jnp.broadcast_to(inverse, inverse_ref.shape[1:])


def forward(att, xp, out_w, up_w, down_w, vec, bias):
    rows, width = att.shape
    ff = down_w.shape[0]
    tile = 512
    fixed = whole((rows, width))
    return pl.pallas_call(
        forward_kernel,
        grid=(ff // tile,),
        out_shape=[
            jax.ShapeDtypeStruct((rows, width), bf16),
            jax.ShapeDtypeStruct((rows, ff), f32),
            jax.ShapeDtypeStruct((rows, width), f32),
            jax.ShapeDtypeStruct((rows, width), f32),
            jax.ShapeDtypeStruct((2, rows, 128), f32),
        ],
        in_specs=[
            fixed, fixed, whole(out_w.shape), pl.BlockSpec((width, tile), lambda i: (0, i)),
            pl.BlockSpec((tile, width), lambda i: (i, 0)), whole(vec.shape), pl.BlockSpec((1, tile), lambda i: (0, i)),
        ],
        out_specs=[
            fixed, pl.BlockSpec((rows, tile), lambda i: (0, i)), fixed, fixed, whole((2, rows, 128)),
        ],
        scratch_shapes=[pltpu.VMEM((rows, width), f32), pltpu.VMEM((rows, width), bf16)],
        compiler_params=params(),
        name="forward",
    )(att, xp, out_w, up_w, down_w, vec, bias)


def backward_kernel(
    mean_ref, total_ref, hidden_ref, wanted_ref, valid_ref, before_ref, two_ref, three_ref, inverse_ref,
    out_ref, up_ref, down_ref, vec_ref, datt_ref, loss_ref, final_ref, acc_ref,
):
    vec = lambda k: vec_ref[k : k + 1, :]
    step = pl.program_id(0)
    rows = valid_ref.shape[0]

    @pl.when(step == 0)
    def _():
        valid = valid_ref[...]
        wanted = wanted_ref[...].astype(f32)
        chosen = jnp.sum(hidden_ref[...].astype(f32) * wanted, axis=1, keepdims=True)
        loss = jnp.sum(valid * (as_column(total_ref[:1, :rows]) - chosen), keepdims=True)
        counted = jnp.sum(valid, keepdims=True)
        lane = iota(loss_ref.shape, 1)
        loss_ref[...] = jnp.where(lane == 0, loss, jnp.where(lane == 1, counted, 0.0))
        d_hidden = valid * (mean_ref[...] - wanted)
        final_ref[...] = normal_back(d_hidden, vec(GAIN[2]), three_ref[...], inverse_ref[1, :, :1])
        acc_ref[...] = jnp.zeros_like(acc_ref)

    d_act = dot(final_ref[...].astype(bf16), down_ref[...], 1, 1)
    d_before = (d_act * gelu_slope(before_ref[...])).astype(bf16)
    acc_ref[...] += dot(d_before, up_ref[...], 1, 1)

    @pl.when(step == pl.num_programs(0) - 1)
    def _():
        d_middle = final_ref[...] + normal_back(
            acc_ref[...], vec(GAIN[1]), two_ref[...], inverse_ref[0, :, :1]
        )
        datt_ref[...] = dot(d_middle.astype(bf16), out_ref[...], 1, 1).astype(bf16)


def backward(mean, total, hidden, wanted, valid, before, two, three, inverse, out_w, up_w, down_w, vec):
    rows, width = mean.shape
    ff = down_w.shape[0]
    tile = 512
    fixed = whole((rows, width))
    return pl.pallas_call(
        backward_kernel,
        grid=(ff // tile,),
        out_shape=[
            jax.ShapeDtypeStruct((rows, width), bf16),
            jax.ShapeDtypeStruct((8, 128), f32),
        ],
        in_specs=[
            fixed, whole(total.shape), fixed, fixed, whole((rows, 1)), pl.BlockSpec((rows, tile), lambda i: (0, i)),
            fixed, fixed, whole(inverse.shape), whole(out_w.shape),
            pl.BlockSpec((width, tile), lambda i: (0, i)),
            pl.BlockSpec((tile, width), lambda i: (i, 0)), whole(vec.shape),
        ],
        out_specs=[fixed, whole((8, 128))],
        scratch_shapes=[pltpu.VMEM((rows, width), f32)] * 2,
        compiler_params=params(),
        name="backward",
    )(mean, total, hidden, wanted, valid, before, two, three, inverse, out_w, up_w, down_w, vec)


def on_device(
    direct,
    token_identifiers,
    lengths,
    loss_positions,
    token_embedding_table,
    positions,
    query_key_value_matrix,
    output_weight,
    up_weight,
    down_weight,
    vectors,
    adapter_down_weight,
    adapter_up_weight,
    left_statistics,
    right_statistics,
):
    width = adapter_down_weight.shape[0]
    rank = adapter_down_weight.shape[1] // 2
    micros, _, slot_count = token_identifiers.shape
    picks = loss_positions.shape[2]
    ff = up_weight.shape[1]
    adapter_scale = adapter_alpha / rank
    local_rows = token_embedding_table.shape[0]
    devices = lax.axis_size("dp") * lax.axis_size("fsdp")
    me = lax.axis_index(BOTH)

    first = jnp.zeros((1,), jnp.int32)

    def masked_ids():
        ids = token_identifiers[:, 0]
        return jnp.where(iota(ids.shape, 1) < lengths, ids, -1).reshape(1, -1)

    if direct:
        received, most, slot, asked, own, mate, vec, wide = fetch(
            lengths.T, token_identifiers, vectors, token_embedding_table, query_key_value_matrix,
            positions, CAPACITY, 0,
        )
        asked = asked.reshape(devices // 2, 2, GRID, 128)
        wide = wide.reshape(-1, wide.shape[-1])
    else:
        ids = masked_ids()
        own = pl.pallas_call(
            functools.partial(presence_kernel, local_rows),
            out_shape=jax.ShapeDtypeStruct((devices, GRID, 128), bf16),
            compiler_params=params(),
            name="presence",
        )(ids)
        mate = own
        asked = lax.all_to_all(own, BOTH, 0, 0, tiled=True).reshape(devices, 1, GRID, 128)
        rows, most = select(asked, token_embedding_table, first, CAPACITY)
        most = lax.pmax(most, BOTH)
        received = lax.all_to_all(rows, BOTH, 0, 0, tiled=True)
        slot = slots(ids, own, mate, first, CAPACITY, local_rows)
        vec = lax.all_gather(vectors.astype(f32), BOTH, axis=0, tiled=True).reshape(-1, width)
        wide = jnp.concatenate([query_key_value_matrix, positions], axis=1)
        wide = lax.all_gather(wide, BOTH, axis=0, tiled=True)
    by_micro = lambda v: v.reshape(micros, 1, slot_count)
    most = most.reshape(-1)[0]
    flat = lambda v: v.reshape(-1, width)

    def rest(more, collective):
        layer = attend(
            ATTENTION_HEADS, adapter_scale, lengths.T, by_micro(slot), received.reshape(-1, width), more, wide, vec,
            loss_positions, adapter_down_weight.T, adapter_up_weight,
            *(([output_weight, up_weight, down_weight], collective) if direct else ([], None)),
        )
        layer, layer_w = layer[:10], layer[10:]
        h1, low, keys, values, probs, h1_p, low_p, x_p, wanted, attended = layer
        if direct:
            out_w, up_w, down_w, x_pair, attended_pair = (w.reshape(-1, w.shape[-1]) for w in layer_w)
            d_attended, loss = middle(
                lengths.T, loss_positions, flat(attended), flat(x_p), attended_pair, x_pair, flat(wanted), vec,
                out_w, up_w, down_w, token_embedding_table, collective + 1,
            )
        else:
            out_w, up_w, down_w = (
                lax.all_gather(w, BOTH, axis=0, tiled=True) for w in (output_weight, up_weight, down_weight)
            )
            bias = vec[UP_BIAS:-1].reshape(1, ff)
            valid = (loss_positions[:, 0] + 1 < lengths).astype(f32).reshape(-1, 1)
            hidden, before, two, three, inverse = forward(
                flat(attended), flat(x_p), out_w, up_w, down_w, vec, bias
            )
            own_rows = hidden.shape[0]
            every = lax.all_gather(hidden, BOTH, axis=0, tiled=True)
            means, totals = vocabulary(every, token_embedding_table, own_rows, 4 * own_rows)
            part = totals[:, 0, :own_rows].reshape(-1)
            top = lax.pmax(part, BOTH)
            total = top + jnp.log(lax.psum(jnp.exp(part - top), BOTH))
            mean_row = lax.psum_scatter(
                means.astype(f32) * jnp.exp(part - total)[:, None], BOTH, scatter_dimension=0, tiled=True
            )
            total = lax.dynamic_slice_in_dim(total, me * own_rows, own_rows, 0)
            total = jnp.broadcast_to(jnp.pad(total, (0, 128 - own_rows)), (8, 128))
            d_attended, loss = backward(
                mean_row, total, hidden, flat(wanted), valid, before, two, three, inverse, out_w, up_w, down_w, vec
            )
        back = back_parts(
            ATTENTION_HEADS, adapter_scale, rank, d_attended.reshape(micros, picks, width),
            h1, low, keys, values, probs, h1_p, low_p, adapter_up_weight, loss,
        )
        if direct:
            return finished(
                back, adapter_down_weight.T, adapter_up_weight, left_statistics, right_statistics, collective + 2
            )
        gradient = lax.psum(attend_back(back), BOTH)
        _, new = renewed(gradient, adapter_down_weight.T, adapter_up_weight, left_statistics, right_statistics)
        blocks = lax.all_gather(new, ("fsdp", "dp"))
        blocks = blocks.reshape(lax.axis_size("fsdp"), -1, 8, new.shape[1])
        return [gradient, blocks[:, : left_statistics.shape[0]].reshape(-1, 8, new.shape[1])]

    def another(state):
        step, rows_sum = state
        ids = masked_ids()
        which = step.reshape(1)
        rows, most = select(asked, token_embedding_table, which, CAPACITY)
        if direct:
            received = send_rows(rows, most, 1)[0]
        else:
            received = lax.all_to_all(rows, BOTH, 0, 0, tiled=True)
        slot = slots(ids, own, mate, which, CAPACITY, local_rows)
        found = jnp.take(received.reshape(-1, width), jnp.maximum(slot[0], 0), axis=0)
        found = jnp.where(slot[0][:, None] >= 0, found, jnp.zeros((), bf16))
        return step + 1, rows_sum + found.reshape(micros, slot_count, width)

    def in_rounds():
        more = lax.while_loop(
            lambda state: (state[0] * CAPACITY).astype(f32) < most,
            another,
            (jnp.ones((), jnp.int32), jnp.zeros((micros, slot_count, width), bf16)),
        )[1]
        return rest(more, 5)

    plain = rest(None, 2)
    gradient, blocks = lax.cond(most > CAPACITY, in_rounds, lambda: plain)
    losses, norm, down_g, up_g, left_new, right_new, down_new, up_new = settled(
        gradient, blocks, left_statistics, right_statistics
    )
    return losses, norm[0], down_g.T, up_g, left_new, right_new, down_new.T, up_new


def solution(mesh):
    direct = dict(mesh.shape) == {"dp": 8, "fsdp": 4}
    rows = P(BOTH, None)
    placed = (
        P(None, BOTH, None),
        P(None, BOTH),
        P(None, BOTH, None),
        rows,
        rows,
        rows,
        rows,
        rows,
        rows,
        P(BOTH),
        P(),
        P(),
        P("fsdp", None, None),
        P("fsdp", None, None),
    )
    return jax.shard_map(
        functools.partial(on_device, direct),
        mesh=mesh,
        in_specs=placed,
        out_specs=(P(), P(), P(), P(), P("fsdp", None, None), P("fsdp", None, None), P(), P()),
        check_vma=False,
    )
```
